32 devices in a mesh: dp: 4 (over y, x), section: 2 (over core), tensor: 4 (over z).
Axes of the slice: x: 2, y: 2, z: 4, core: 2. Of those that a mesh axis runs over, the one named last changes fastest.
Arguments:
- inputs: bfloat16 [8, 1024, 1152], P('dp', 'tensor'), may hold values from -6 to 6
- time_emb: bfloat16 [8, 1152], P('dp'), may hold values from -6 to 6
- lengths: int32 [8], P('dp'), may hold values from 256 to 1024, as said below
- key_mask: int32 [8, 1024], P('dp'), may hold values from 0 to 1, as said below
- rel_index: int32 [2, 1024, 1024], replicated, may hold values from 0 to 3968, as said below
- w_qkv: bfloat16 [2, 1152, 3, 1152], P('section', None, None, 'tensor'), may hold values from -0.1875 to 0.1875
- w_time: bfloat16 [2, 1152, 2, 1152], P('section', None, None, 'tensor'), may hold values from -0.046875 to 0.046875
- w_proj: bfloat16 [2, 1152, 1152], P('section', None, 'tensor'), may hold values from -0.5 to 0.5
- w_fc1: bfloat16 [2, 1152, 4608], P('section', None, 'tensor'), may hold values from -0.1875 to 0.1875
- w_fc2: bfloat16 [2, 1152, 4608], P('section', None, 'tensor'), may hold values from -0.125 to 0.125
- rel_table: float32 [2, 16, 3969], P('section', 'tensor'), may hold values from -4 to 4
- norm_gains: float32 [2, 2, 1152], P('section'), may hold values from 0.1 to 1.9
- norm_biases: float32 [2, 2, 1152], P('section'), may hold values from -2 to 2
- cotangent: bfloat16 [8, 1024, 1152], P('dp', 'tensor'), may hold values from -6 to 6
Outputs:
- acts: bfloat16 [2, 8, 1024, 1152], P('section', 'dp', 'tensor')
- input_grads: float32 [2, 8, 1024, 1152], P('section', 'dp', 'tensor')
- grad_qkv: float32 [2, 1152, 3, 1152], P('section', 'dp', None, 'tensor')
- grad_time: float32 [2, 1152, 2, 1152], P('section', 'dp', None, 'tensor')
- grad_proj: float32 [2, 1152, 1152], P('section', 'dp', 'tensor')
- grad_fc1: float32 [2, 1152, 4608], P('section', 'dp', 'tensor')
- grad_fc2: float32 [2, 1152, 4608], P('section', 'dp', 'tensor')
- grad_rel: float32 [2, 16, 3969], P('section', 'tensor')
- grad_gains: float32 [2, 2, 1152], P('section', None, ('dp', 'tensor'))
- grad_biases: float32 [2, 2, 1152], P('section', None, ('dp', 'tensor'))
The draws below stay inside these ranges and needn't reach their ends.
Inputs may be any that keep to these rules, and one draw needn't show every extreme that they name: `lengths`: each length is 256 or 1024; each aligned block of 2 images holds at least one image of length 1024. `key_mask`: zero at every slot at or beyond the image's length; slot 0 is always 1. `rel_index`: table 0 labels the offset between slots a and b of a 32 by 32 grid in row-major order, table 1 that of a 16 by 16 grid for slots below 256 and one label elsewhere; the labels are a permutation of the 3969 offsets.
All inputs are finite; a program needn't handle non-finite values.
Results may differ from the reference program's by a relative error of at most 0.024.
Values may be sent and summed in bfloat16 or wider, within the bound.
A program may use at most 320 MiB of HBM per device.

```python
import jax
import jax.numpy as jnp
from jax import lax

D = 1152
H = 16
HD = 72
FF = 4608
GRID = 32
IMG_DEV = 2
LEN = 1024
SHORT = 256
NB = 3969
IMAGES = 8


def image_lengths(key):
    flags = jax.random.randint(key, (IMAGES,), 0, 5) == 0
    picked = jax.random.randint(jax.random.fold_in(key, 11), (IMAGES // IMG_DEV,), 0, IMG_DEV)
    forced = jnp.arange(IMAGES) % IMG_DEV == jnp.repeat(picked, IMG_DEV)
    return jnp.where(flags | forced, LEN, SHORT).astype(jnp.int32)


def draw_lengths(key, part):
    base_key = key
    return image_lengths(base_key)


def draw_key_mask(key, part):
    sizes_now = image_lengths(key)
    key = jax.random.fold_in(key, 2)
    kept = jax.random.randint(key, (IMAGES, LEN), 0, 4) > 0
    position = jnp.arange(LEN)
    inside = position[None, :] < sizes_now[:, None]
    result = kept & inside | (position[None, :] == 0)
    return result.astype(jnp.int32)


def draw_rel_index(key, part):
    key = jax.random.fold_in(key, 3)
    labels = jax.random.permutation(key, NB).astype(jnp.int32)
    across = 2 * GRID - 1
    position = jnp.arange(LEN)
    row_big = position // GRID
    col_big = position % GRID
    big_table = (row_big[:, None] - row_big[None, :] + GRID - 1) * across + (col_big[:, None] - col_big[None, :] + GRID - 1)
    half_side = GRID // 2
    row_small = position // half_side
    col_small = position % half_side
    inside = position < SHORT
    small_table = (row_small[:, None] - row_small[None, :] + GRID - 1) * across + (col_small[:, None] - col_small[None, :] + GRID - 1)
    small_table = jnp.where(inside[:, None] & inside[None, :], small_table, 0)
    return labels[jnp.stack([big_table, small_table])].astype(jnp.int32)


def steps_of(rng, shape, cuts, least, high):
    level = 1.0
    for dim, blocks in cuts:
        steps = jax.random.uniform(jax.random.fold_in(jax.random.fold_in(rng, 6), dim), (blocks,), jnp.float32, least / len(cuts), high / len(cuts))
        level = level * jnp.repeat(jnp.exp(steps), shape[dim] // blocks).reshape((-1,) + (1,) * (len(shape) - 1 - dim))
    return level


def normal_values(stream_key, shape, scale, most, split=(), held_as=jnp.bfloat16):
    level = steps_of(stream_key, shape, split, -0.22, 0.18) if split else 1.0
    values = jax.random.normal(stream_key, shape, jnp.float32) * scale * level
    return jnp.minimum(jnp.maximum(values, -most), most).astype(held_as)


def setup_inputs(seed: int = 0) -> dict:
    arg_keys = jax.random.split(jax.random.key(seed), 15)
    return {
        "inputs": normal_values(arg_keys[0], (IMAGES, LEN, D), 1.0, 6.0, ((0, 4), (1, 4))),
        "time_emb": normal_values(arg_keys[1], (IMAGES, D), 1.0, 6.0, ((0, 4),)),
        "lengths": draw_lengths(jax.random.fold_in(arg_keys[14], 71), 0),
        "key_mask": draw_key_mask(jax.random.fold_in(arg_keys[14], 71), 0),
        "rel_index": draw_rel_index(jax.random.fold_in(arg_keys[14], 71), 0),
        "w_qkv": normal_values(arg_keys[5], (2, D, 3, D), D ** -0.5, 0.1875, ((0, 2), (3, 4))),
        "w_time": normal_values(arg_keys[6], (2, D, 2, D), (16 * D) ** -0.5, 0.046875, ((0, 2), (3, 4))),
        "w_proj": normal_values(arg_keys[7], (2, D, D), (D // 9) ** -0.5, 0.5, ((0, 2), (2, 4))),
        "w_fc1": normal_values(arg_keys[8], (2, D, FF), D ** -0.5, 0.1875, ((0, 2), (2, 4))),
        "w_fc2": normal_values(arg_keys[9], (2, D, FF), (FF // 2) ** -0.5, 0.125, ((0, 2), (2, 4))),
        "rel_table": normal_values(arg_keys[10], (2, H, NB), 1.0, 4.0, ((0, 2), (1, 4)), jnp.float32),
        "norm_gains": jnp.clip(1.0 + 0.18 * jax.random.normal(arg_keys[11], (2, 2, D), jnp.float32), 0.1, 1.9),
        "norm_biases": normal_values(arg_keys[12], (2, 2, D), 0.3, 2.0, ((0, 2),), jnp.float32),
        "cotangent": normal_values(arg_keys[13], (IMAGES, LEN, D), 1.0, 6.0, ((0, 4), (1, 4))),
    }


@jax.custom_vjp
def low(v):
    return lax.optimization_barrier(v.astype(jnp.bfloat16)).astype(jnp.float32)

@jax.custom_vjp
def low_back(v):
    return v

def low_keep(v):
    return (low(v), None)

def low_pass(kept, grad):
    return (grad,)

def back_keep(v):
    return (v, None)

def back_low(kept, grad):
    return (low(grad),)
low.defvjp(low_keep, low_pass)
low_back.defvjp(back_keep, back_low)

def layer_norm(values, gain, shift):
    center = values - lax.optimization_barrier(jnp.mean(values, axis=-1, keepdims=True))
    spread = lax.optimization_barrier(jnp.mean(center * center, axis=-1, keepdims=True))
    return center * lax.rsqrt(spread + 1e-05) * gain + shift

def one_layer(params, layer, layer_in, time_vec, table_idx, key_valid):
    qkv_weight, time_weight, proj_weight, up_weight, down_weight, bias_table, gains, shifts = params
    highest = lax.Precision.HIGHEST
    q_block = min(512, LEN)
    num_blocks = LEN // q_block
    normed = low(layer_norm(layer_in, gains[layer, 0], shifts[layer, 0]))
    qkv_all = jnp.einsum('rd,dcn->rcn', normed, qkv_weight[layer], precision=highest)
    time_terms = jnp.einsum('d,dcn->cn', time_vec, time_weight[layer], precision=highest)
    queries = low_back(low(qkv_all[:, 0] + time_terms[0])).reshape(LEN, H, HD)
    keys_all = low_back(low(qkv_all[:, 1])).reshape(LEN, H, HD)
    values = low_back(low(qkv_all[:, 2] + time_terms[1])).reshape(LEN, H, HD)
    bias_full = bias_table[layer][:, table_idx]
    query_blocks = queries.reshape(num_blocks, q_block, H, HD)
    bias_blocks = bias_full.reshape(H, num_blocks, q_block, LEN).transpose(1, 0, 2, 3)
    score_scale = 1.0 / jnp.sqrt(jnp.float32(HD))

    def attend(pieces):
        query_part, bias_part = pieces
        scores = jnp.einsum('qhe,khe->hqk', query_part, keys_all, precision=highest) * score_scale + bias_part
        scores = low_back(jnp.where(key_valid[None, None, :], scores, -1e+30))
        attn_probs = low(jax.nn.softmax(scores, axis=-1))
        return jnp.einsum('hqk,khe->qhe', attn_probs, values, precision=highest)
    attended = lax.map(jax.checkpoint(attend), (query_blocks, bias_blocks)).reshape(LEN, D)
    attended = low_back(low(attended))
    branch = low_back(jnp.einsum('rn,dn->rd', attended, proj_weight[layer], precision=highest))
    hidden = layer_in + branch
    normed_mlp = low(layer_norm(hidden, gains[layer, 1], shifts[layer, 1]))
    pre_act = low_back(jnp.dot(normed_mlp, up_weight[layer], precision=highest))
    gelu_out = low(jax.nn.gelu(pre_act, approximate=True))
    return hidden + low_back(jnp.einsum('rf,df->rd', gelu_out, down_weight[layer], precision=highest))

def reference(inputs, time_emb, lengths, key_mask, rel_index, w_qkv, w_time, w_proj, w_fc1, w_fc2, rel_table, norm_gains, norm_biases, cotangent):
    params = (w_qkv.astype(jnp.float32), w_time.astype(jnp.float32), w_proj.astype(jnp.float32), w_fc1.astype(jnp.float32), w_fc2.astype(jnp.float32), rel_table, norm_gains, norm_biases)
    empty_delta = jnp.zeros((LEN, D), jnp.float32)

    def image_step(totals, item):
        image_in, time_vec, length, mask_row, cot_row = item
        key_valid = mask_row > 0
        grid_kind = jnp.where(length < LEN, 1, 0).astype(jnp.int32)
        table_idx = lax.dynamic_index_in_dim(rel_index, grid_kind, 0, keepdims=False)

        def run(param_set, layer_in, delta):
            middle = low_back(low(one_layer(param_set, 0, layer_in, time_vec, table_idx, key_valid))) + delta
            final = low(one_layer(param_set, 1, middle, time_vec, table_idx, key_valid))
            return (final, middle)
        final, pull_back, middle = jax.vjp(run, params, image_in, empty_delta, has_aux=True)
        row_live = (jnp.arange(LEN) < length).astype(jnp.float32)[:, None]
        grad_params, grad_in, grad_mid = pull_back(cot_row * row_live)
        totals = jax.tree.map(jnp.add, totals, grad_params)
        return (totals, (middle, final, grad_in, grad_mid))
    start_totals = jax.tree.map(jnp.zeros_like, params)
    totals, outputs = lax.scan(image_step, start_totals, (inputs.astype(jnp.float32), time_emb.astype(jnp.float32), lengths, key_mask, cotangent.astype(jnp.float32)))
    middles, finals, grads_in, grads_mid = outputs
    acts = jnp.stack([middles, finals]).astype(jnp.bfloat16)
    input_grads = jnp.stack([grads_in, grads_mid])
    return (acts, input_grads, totals[0], totals[1], totals[2], totals[3], totals[4], totals[5], totals[6], totals[7])
```

```python
import functools
import math

import jax
import jax.numpy as jnp
from jax import lax
from jax.experimental import pallas as pl
from jax.experimental.pallas import tpu as pltpu
from jax.sharding import PartitionSpec as P

LOG2E = 1.4426950408889634
HIGHEST = lax.Precision.HIGHEST
BIGL = 1920
SMALL0 = 4 * BIGL
WALL = SMALL0 + 2304


def _labels_hi_lo(lab):
    hi = lax.shift_right_logical(lab, 6)
    lo = jnp.bitwise_and(lab, 63)
    iota = lax.broadcasted_iota(jnp.int32, (64, lab.shape[1]), 0)
    return iota == hi, jnp.where(iota == lo, 1.0, 0.0)


def bias_kernel(out_lab_ref, lab_ref, table_ref, wall_ref):
    lab = lab_ref[...]
    hi_mask, lo_hot = _labels_hi_lo(lab)
    rows = lax.dot_general(table_ref[0], lo_hot, (((1,), (0,)), ((), ())), precision=HIGHEST, preferred_element_type=jnp.float32)
    flat = jnp.sum(jnp.where(hi_mask, rows, 0.0), axis=0, keepdims=True) * LOG2E
    outside = jnp.sum(jnp.where(lab == out_lab_ref[0], flat, 0.0), axis=1, keepdims=True)
    wide = jnp.broadcast_to(flat, (32, 4096))
    wide = pltpu.roll(wide, 4096 - 31, 1, stride=1, stride_axis=0)
    lane = lax.broadcasted_iota(jnp.int32, (32, 128), 1)
    tight = []
    for g in range(16):
        a = wide[:, 256 * g : 256 * g + 128]
        b = wide[:, 256 * g + 128 : 256 * g + 256]
        piece = jnp.where(lane < 32, a, pltpu.roll(a, 96, 1))
        other = jnp.where(lane < 96, pltpu.roll(b, 64, 1), pltpu.roll(b, 32, 1))
        tight.append(jnp.where(lane < 64, piece, other))
    w0 = jnp.concatenate(tight, axis=1)
    for s in range(4):
        shifted = w0 if s == 0 else pltpu.roll(w0, 2048 - 32 * s, 1)
        wall_ref[0, :, s * BIGL : (s + 1) * BIGL] = shifted[:, :BIGL]
    lane16 = lane[:16]
    tight16 = []
    for g in range(8):
        lo_v = w0[:16, 256 * g : 256 * g + 128]
        hi_v = w0[:16, 256 * g + 128 : 256 * g + 256]
        acc = lo_v
        for k in range(1, 4):
            acc = jnp.where(lane16 >= 16 * k, pltpu.roll(lo_v, 128 - 16 * k, 1), acc)
        for k in range(4):
            acc = jnp.where(lane16 >= 64 + 16 * k, pltpu.roll(hi_v, (64 - 16 * k) % 128, 1), acc)
        tight16.append(acc)
    w16 = jnp.concatenate(tight16, axis=1)
    for j in range(16):
        sl = pltpu.roll(w16, 1024 - 16 * (31 - j), 1)[:, :256]
        wall_ref[0, 16 * (j % 2) : 16 * (j % 2) + 16, SMALL0 + 256 * (j // 2) : SMALL0 + 256 * (j // 2) + 256] = sl
    wall_ref[0, :, SMALL0 + 2048 : WALL] = jnp.broadcast_to(outside, (32, 256))


def bias_tables(out_lab, lab, table):
    heads = table.shape[0]
    return pl.pallas_call(
        bias_kernel,
        grid=(heads,),
        in_specs=[
            pl.BlockSpec(memory_space=pltpu.SMEM),
            pl.BlockSpec((1, 4096), lambda h: (0, 0)),
            pl.BlockSpec((1, 64, 64), lambda h: (h, 0, 0)),
        ],
        out_specs=pl.BlockSpec((1, 32, WALL), lambda h: (h, 0, 0)),
        out_shape=jax.ShapeDtypeStruct((heads, 32, WALL), jnp.float32),
        compiler_params=pltpu.CompilerParams(vmem_limit_bytes=40 << 20),
    )(out_lab, lab, table)


def bias_grad_kernel(out_lab_ref, lab_ref, acc_ref, out_ref):
    lab = lab_ref[...]
    hi_mask, lo_hot = _labels_hi_lo(lab)
    acc = acc_ref[0]
    w0 = jnp.zeros((32, 2048), jnp.float32)
    for s in range(4):
        piece = jnp.concatenate([acc[:, s * BIGL : (s + 1) * BIGL], jnp.zeros((32, 128), jnp.float32)], axis=1)
        w0 = w0 + (piece if s == 0 else pltpu.roll(piece, 32 * s, 1))
    w16 = jnp.zeros((16, 1024), jnp.float32)
    for j in range(16):
        piece = acc[16 * (j % 2) : 16 * (j % 2) + 16, SMALL0 + 256 * (j // 2) : SMALL0 + 256 * (j // 2) + 256]
        piece = jnp.concatenate([piece, jnp.zeros((16, 768), jnp.float32)], axis=1)
        w16 = w16 + pltpu.roll(piece, 16 * (31 - j), 1)
    outside = jnp.sum(jnp.sum(acc[:, SMALL0 + 2048 : WALL], axis=0, keepdims=True), axis=1, keepdims=True)
    lane = lax.broadcasted_iota(jnp.int32, (32, 128), 1)
    lane16 = lane[:16]
    wide = []
    for g in range(32):
        src = w0[:, 128 * (g // 2) : 128 * (g // 2) + 128]
        k = 2 * (g % 2)
        first = src if k == 0 else pltpu.roll(src, 128 - 32 * k, 1)
        second = pltpu.roll(src, (64 - 32 * (k + 1)) % 128, 1)
        piece = jnp.where(lane < 32, first, jnp.where((lane >= 64) & (lane < 96), second, 0.0))
        src16 = w16[:, 128 * (g // 4) : 128 * (g // 4) + 128]
        k = 2 * (g % 4)
        first = src16 if k == 0 else pltpu.roll(src16, 128 - 16 * k, 1)
        second = pltpu.roll(src16, (64 - 16 * (k + 1)) % 128, 1)
        piece16 = jnp.where(lane16 < 16, first, jnp.where((lane16 >= 64) & (lane16 < 80), second, 0.0))
        wide.append(piece + jnp.concatenate([piece16, jnp.zeros((16, 128), jnp.float32)], axis=0))
    wide = jnp.concatenate(wide, axis=1)
    back = 31 - lax.broadcasted_iota(jnp.int32, (32, 4096), 0)
    for k in range(5):
        wide = jnp.where(jnp.bitwise_and(back, 1 << k) > 0, pltpu.roll(wide, 1 << k, 1), wide)
    flat = jnp.sum(wide, axis=0, keepdims=True)
    flat = flat + jnp.where(lab == out_lab_ref[0], outside, 0.0)
    spread = jnp.where(hi_mask, jnp.broadcast_to(flat, (64, 4096)), 0.0)
    out_ref[0] = lax.dot_general(spread, lo_hot, (((1,), (1,)), ((), ())), precision=HIGHEST, preferred_element_type=jnp.float32)


def bias_grads(out_lab, lab, acc):
    heads = acc.shape[0]
    return pl.pallas_call(
        bias_grad_kernel,
        grid=(heads,),
        in_specs=[
            pl.BlockSpec(memory_space=pltpu.SMEM),
            pl.BlockSpec((1, 4096), lambda h: (0, 0)),
            pl.BlockSpec((1, 32, WALL), lambda h: (h, 0, 0)),
        ],
        out_specs=pl.BlockSpec((1, 64, 64), lambda h: (h, 0, 0)),
        out_shape=jax.ShapeDtypeStruct((heads, 64, 64), jnp.float32),
        compiler_params=pltpu.CompilerParams(vmem_limit_bytes=40 << 20),
    )(out_lab, lab, acc)


def label_row(rel_index):
    side = 32
    a = rel_index[0, 1023].reshape(side, side)
    b = rel_index[0, 0].reshape(side, side)
    c = rel_index[0, 992].reshape(side, side)
    d = rel_index[0, 31].reshape(side, side)
    top = jnp.concatenate([a, c[:, 1:]], axis=1)
    low = jnp.concatenate([d[1:], b[1:, 1:]], axis=1)
    grid = jnp.flip(jnp.concatenate([top, low], axis=0), (0, 1))
    return jnp.pad(grid, ((0, 1), (0, 1)), constant_values=4095).reshape(1, 4096)


NT = (((1,), (1,)), ((), ()))
TN = (((0,), (0,)), ((), ()))
NN = (((1,), (0,)), ((), ()))
HD = 72
QB = 256


def dot(a, b, dims):
    return lax.dot_general(a, b, dims, preferred_element_type=jnp.float32)


def head_lanes(x, at, extra=None):
    rows = x.shape[0]
    part = x[:, at : at + HD]
    if extra is None:
        pad = jnp.zeros((rows, 128 - HD), x.dtype)
    else:
        pad = extra
    return jnp.concatenate([part, pad], axis=1)


def strip_start(t, small, q_quarter, jj, rel):
    kq = jnp.bitwise_xor(t, rel)
    big = BIGL * ((31 - jj) % 4) + 128 * ((31 - jj) // 4 - 2 * kq + 2 * q_quarter)
    inner = SMALL0 + 256 * jj
    tiny = jnp.where((kq == 0) & (q_quarter == 0), inner, SMALL0 + 2048)
    return pl.multiple_of(jnp.where(small == 1, tiny, big), 128)


def attn_fwd_kernel(order, scale, sc_ref, q_ref, kv_ref, mask_ref, wall_ref, o_ref, lse_ref, s_scr, p_scr):
    t, small = sc_ref[0], sc_ref[1]
    qq = jnp.bitwise_xor(t, sc_ref[2 + pl.program_id(0)])
    heads = wall_ref.shape[0]
    width = heads * HD
    rows = kv_ref.shape[0]
    nstrip = rows // 32
    k_extra = mask_ref[...]
    lane = lax.broadcasted_iota(jnp.int32, (QB, 128 - HD), 1)
    q_extra = jnp.where(lane == 0, 1.0, 0.0).astype(jnp.bfloat16)
    outs = []
    for h in range(heads):
        kh = head_lanes(kv_ref, width + HD * h, k_extra)
        qh = head_lanes(q_ref, HD * h, q_extra)
        vh = head_lanes(kv_ref, 2 * width + HD * h)
        s_scr[h % 2] = dot(kh, qh, NT)
        top = None
        for st in range(nstrip):
            start = strip_start(t, small, qq, st % 8, order[st // 8])
            s = s_scr[h % 2, 32 * st : 32 * st + 32] * (scale * LOG2E) + wall_ref[h, :, pl.ds(start, QB)]
            s_scr[h % 2, 32 * st : 32 * st + 32] = s
            top = s if top is None else jnp.maximum(top, s)
        row_max = jnp.max(top, axis=0, keepdims=True)
        total = None
        for st in range(nstrip):
            p = jnp.exp2(s_scr[h % 2, 32 * st : 32 * st + 32] - row_max)
            p_scr[h % 2, 32 * st : 32 * st + 32] = p.astype(jnp.bfloat16)
            total = p if total is None else total + p
        row_sum = jnp.sum(total, axis=0, keepdims=True)
        o_t = dot(vh, p_scr[h % 2], TN) * (1.0 / row_sum)
        lse_ref[0, h : h + 1, :] = row_max + jnp.log2(row_sum)
        outs.append(o_t.T[:, :HD].astype(jnp.bfloat16))
    o_ref[...] = jnp.concatenate(outs, axis=1)


def attn_fwd(qkv, mask_pad, wall, scalars, order, scale):
    rows, wide = qkv.shape
    nq = rows // QB
    heads = wall.shape[0]
    width = heads * HD
    return pl.pallas_call(
        functools.partial(attn_fwd_kernel, order, scale),
        grid=(nq,),
        in_specs=[
            pl.BlockSpec(memory_space=pltpu.SMEM),
            pl.BlockSpec((QB, wide), lambda i: (i, 0)),
            pl.BlockSpec((rows, wide), lambda i: (0, 0)),
            pl.BlockSpec((rows, 128 - HD), lambda i: (0, 0)),
            pl.BlockSpec((heads, 32, WALL), lambda i: (0, 0, 0), pipeline_mode=pl.Buffered(1)),
        ],
        out_specs=[pl.BlockSpec((QB, width), lambda i: (i, 0)), pl.BlockSpec((1, heads, QB), lambda i: (i, 0, 0))],
        out_shape=[jax.ShapeDtypeStruct((rows, width), jnp.bfloat16), jax.ShapeDtypeStruct((nq, heads, QB), jnp.float32)],
        scratch_shapes=[pltpu.VMEM((2, rows, QB), jnp.float32), pltpu.VMEM((2, rows, QB), jnp.bfloat16)],
        compiler_params=pltpu.CompilerParams(vmem_limit_bytes=40 << 20),
        cost_estimate=pl.CostEstimate(flops=16 << 30, bytes_accessed=12 << 20, transcendentals=0),
    )(scalars, qkv, qkv, mask_pad, wall)


def attn_bwd_kernel(order, scale, sc_ref, q_ref, kv_ref, do_ref, o_ref, lse_ref, mask_ref, wall_ref,
                    dqkv_ref, acc_ref, p_scr, s_scr, dq_scr, dk_scr, dv_scr):
    step = pl.program_id(0)
    t, small = sc_ref[0], sc_ref[1]
    qq = jnp.bitwise_xor(t, sc_ref[2 + step])
    heads = wall_ref.shape[0]
    width = heads * HD
    rows = kv_ref.shape[0]

    @pl.when(step == 0)
    def _():
        acc_ref[...] = jnp.zeros_like(acc_ref)
        dk_scr[...] = jnp.zeros_like(dk_scr)
        dv_scr[...] = jnp.zeros_like(dv_scr)

    k_extra = mask_ref[...]
    lane = lax.broadcasted_iota(jnp.int32, (QB, 128 - HD), 1)
    q_extra = jnp.where(lane == 0, 1.0, 0.0).astype(jnp.bfloat16)
    dqs = []
    for h in range(heads):
        kh = head_lanes(kv_ref, width + HD * h, k_extra)
        qh = head_lanes(q_ref, HD * h, q_extra)
        vh = head_lanes(kv_ref, 2 * width + HD * h)
        doh = head_lanes(do_ref, HD * h)
        oh = head_lanes(o_ref, HD * h)
        inner = jnp.sum((doh.astype(jnp.float32) * oh.astype(jnp.float32)).T, axis=0, keepdims=True)
        lse = lse_ref[0, h : h + 1, :]
        for kb in range(rows // 256):
            s_t = dot(kh[256 * kb : 256 * kb + 256], qh, NT)
            dp_t = dot(vh[256 * kb : 256 * kb + 256], doh, NT)
            for js in range(8):
                st = 8 * kb + js
                start = strip_start(t, small, qq, js, order[kb])
                s = s_t[32 * js : 32 * js + 32] * (scale * LOG2E) + wall_ref[h, :, pl.ds(start, QB)]
                p = jnp.exp2(s - lse)
                ds = p * (dp_t[32 * js : 32 * js + 32] - inner)
                p_scr[h % 2, 32 * st : 32 * st + 32] = p.astype(jnp.bfloat16)
                s_scr[h % 2, 32 * st : 32 * st + 32] = ds.astype(jnp.bfloat16)
                acc_ref[h, :, pl.ds(start, QB)] += ds
        p_b, ds_b = p_scr[h % 2], s_scr[h % 2]
        dv_scr[h] += dot(p_b, doh, NN)
        dk_scr[h] += dot(ds_b, qh, NN)
        dq_t = dot(kh, ds_b, TN) * scale
        dqs.append(dq_t.T[:, :HD].astype(jnp.bfloat16))
    dq_scr[pl.ds(pl.multiple_of(step * QB, QB), QB)] = jnp.concatenate(dqs, axis=1)

    @pl.when(step == pl.num_programs(0) - 1)
    def _():
        parts = [dq_scr[...]]
        parts += [(dk_scr[h, :, :HD] * scale).astype(jnp.bfloat16) for h in range(heads)]
        parts += [dv_scr[h, :, :HD].astype(jnp.bfloat16) for h in range(heads)]
        dqkv_ref[...] = jnp.concatenate(parts, axis=1)


def attn_bwd(qkv, do, o, lse, mask_pad, wall, scalars, order, scale):
    rows, wide = qkv.shape
    nq = rows // QB
    heads = wall.shape[0]
    width = heads * HD
    row_spec = pl.BlockSpec((QB, width), lambda i: (i, 0))
    return pl.pallas_call(
        functools.partial(attn_bwd_kernel, order, scale),
        grid=(nq,),
        in_specs=[
            pl.BlockSpec(memory_space=pltpu.SMEM),
            pl.BlockSpec((QB, wide), lambda i: (i, 0)),
            pl.BlockSpec((rows, wide), lambda i: (0, 0)),
            row_spec,
            row_spec,
            pl.BlockSpec((1, heads, QB), lambda i: (i, 0, 0)),
            pl.BlockSpec((rows, 128 - HD), lambda i: (0, 0)),
            pl.BlockSpec((heads, 32, WALL), lambda i: (0, 0, 0), pipeline_mode=pl.Buffered(1)),
        ],
        out_specs=[pl.BlockSpec((rows, wide), lambda i: (0, 0)), pl.BlockSpec((heads, 32, WALL), lambda i: (0, 0, 0))],
        out_shape=[jax.ShapeDtypeStruct((rows, wide), jnp.bfloat16), jax.ShapeDtypeStruct((heads, 32, WALL), jnp.float32)],
        scratch_shapes=[
            pltpu.VMEM((2, rows, QB), jnp.bfloat16),
            pltpu.VMEM((2, rows, QB), jnp.bfloat16),
            pltpu.VMEM((rows, width), jnp.bfloat16),
            pltpu.VMEM((heads, rows, 128), jnp.float32),
            pltpu.VMEM((heads, rows, 128), jnp.float32),
        ],
        compiler_params=pltpu.CompilerParams(vmem_limit_bytes=48 << 20),
        cost_estimate=pl.CostEstimate(flops=24 << 30, bytes_accessed=20 << 20, transcendentals=0),
    )(scalars, qkv, qkv, do, o, lse, mask_pad, wall)


EPSILON = 1e-05
AXES = ("dp", "section", "tensor")
ORDER = (0, 2, 1, 3)


def normed(x):
    center = x - jnp.mean(x, axis=-1, keepdims=True)
    spread = jnp.mean(center * center, axis=-1, keepdims=True)
    r = lax.rsqrt(spread + EPSILON)
    return center * r, r


def norm_back(x, dy, gain):
    xhat, r = normed(x)
    dxhat = dy * gain
    dx = r * (
        dxhat
        - jnp.mean(dxhat, axis=-1, keepdims=True)
        - xhat * jnp.mean(dxhat * xhat, axis=-1, keepdims=True)
    )
    return dx, jnp.sum(dy * xhat, axis=0), jnp.sum(dy, axis=0)


def gelu_tanh(values):
    return jax.nn.gelu(values, approximate=True)


def local(
    inputs,
    time_emb,
    lengths,
    key_mask,
    rel_index,
    w_qkv,
    w_time,
    w_proj,
    w_fc1,
    w_fc2,
    rel_table,
    norm_gains,
    norm_biases,
    cotangent,
):
    bf16, f32 = jnp.bfloat16, jnp.float32
    _, rows, width = inputs.shape
    seq_len = key_mask.shape[1]
    heads, buckets = rel_table.shape[1:]
    local_width = w_proj.shape[2]
    scale = 1.0 / math.sqrt(HD)
    ndp = lax.axis_size("dp")
    d = lax.axis_index("dp")
    c = lax.axis_index("section")
    z = lax.axis_index("tensor")
    pair = z // 2
    home = c == pair
    first = c == 0
    t = z % 2 + 2 * c

    def move(x, to):
        pairs = []
        for dd in range(ndp):
            for cc in range(2):
                for zz in range(4):
                    dst = to(dd, cc, zz)
                    if dst is not None:
                        pairs.append(((dd * 2 + cc) * 4 + zz, (dst[0] * 2 + dst[1]) * 4 + dst[2]))
        return lax.ppermute(x, AXES, pairs)

    def partner(x):
        return move(x, lambda dd, cc, zz: (dd, cc, zz ^ 1))

    def sibling(x):
        return move(x, lambda dd, cc, zz: (dd, 1 - cc, zz))

    def across(x):
        return move(x, lambda dd, cc, zz: (dd, cc, zz ^ 2))

    def fetch(x):
        rem = across(x)
        keep = jnp.where(home, x, rem)
        recv = sibling(jnp.where(home, rem, x))
        return jnp.where(first, keep, recv), jnp.where(first, recv, keep)

    def fetch_weight(w):
        part = w.shape[0] // ndp
        rem = lax.all_gather(across(lax.dynamic_slice_in_dim(w, d * part, part, 0)), "dp", axis=0, tiled=True)
        keep = jnp.where(home, w, rem)
        recv = sibling(jnp.where(home, rem, w))
        return jnp.where(first, keep, recv), jnp.where(first, recv, keep)

    time_all = jnp.einsum("id,dcn->icn", time_emb, w_time[0], preferred_element_type=f32)
    table = jnp.pad(rel_table[0], ((0, 0), (0, 4096 - buckets)))
    small_pack = jnp.concatenate(
        [
            table.reshape(-1, 128),
            time_all.reshape(-1, 128),
            norm_gains[0].reshape(-1, 128),
            norm_biases[0].reshape(-1, 128),
        ],
        axis=0,
    )
    cuts = []
    at = 0
    for n in (heads * 32, time_all.size // 128, 2 * width // 128, 2 * width // 128):
        cuts.append((at, at + n))
        at += n
    weights_qkv = fetch_weight(w_qkv[0].reshape(width, 3 * local_width))
    packs = fetch(small_pack)
    weights_proj = fetch_weight(w_proj[0])
    weights_fc1 = fetch_weight(w_fc1[0])
    weights_fc2 = fetch_weight(w_fc2[0])

    def home_rows(x):
        other = lax.dynamic_index_in_dim(x, 1 - pair, 0, keepdims=False)
        got = move(other, lambda dd, cc, zz: (dd, cc, zz ^ 2) if cc == zz // 2 else None)
        return jnp.where(home, lax.dynamic_index_in_dim(x, pair, 0, keepdims=False), got)

    label_lanes = label_row(rel_index)
    out_label = rel_index[1, seq_len - 1, seq_len - 1].reshape(1)
    walls, time_terms, gains, shifts = [], [], [], []
    for pack in packs:
        pieces = [pack[a:b] for a, b in cuts]
        walls.append(bias_tables(out_label, label_lanes, pieces[0].reshape(heads, 64, 64)))
        both = pieces[1].reshape(2, 2, local_width)
        mine = lax.dynamic_index_in_dim(both, pair, 0, keepdims=False)
        time_terms.append(jnp.concatenate([mine[0], jnp.zeros((local_width,), f32), mine[1]]))
        gains.append(pieces[2].reshape(2, width))
        shifts.append(pieces[3].reshape(2, width))

    length = lax.dynamic_index_in_dim(lengths, pair, 0, keepdims=False)
    small = (length < seq_len).astype(jnp.int32)
    scalars = jnp.stack([t, small] + [jnp.int32(j) for j in ORDER])
    mask = lax.dynamic_index_in_dim(key_mask, pair, 0, keepdims=False).reshape(4, rows)
    mask = jnp.concatenate([lax.dynamic_index_in_dim(mask, t ^ j, 0, keepdims=False) for j in ORDER])
    lane = jnp.arange(128 - HD)[None, :]
    mask_pad = jnp.where((lane == 0) & (mask[:, None] == 0), -1e30, 0.0).astype(bf16)

    def gather_rows(x):
        far = partner(x)
        near = sibling(x)
        return jnp.concatenate([x, near, far, sibling(far)], axis=0)

    def scatter_rows(far, near):
        a = sibling(far[rows:].astype(bf16))
        rz = partner((far[:rows] + a.astype(f32)).astype(bf16))
        rs = sibling(near[rows:].astype(bf16))
        return near[:rows] + rs.astype(f32) + rz.astype(f32)

    def times_t(x, w):
        return lax.dot_general(x, w, (((1,), (1,)), ((), ())), preferred_element_type=f32)

    def grad_of(x, y):
        return lax.dot_general(x, y, (((0,), (0,)), ((), ())), preferred_element_type=f32).astype(bf16)

    half = 2 * rows

    def forward(layer, x):
        xhat, _ = normed(x)
        n1 = gather_rows((xhat * gains[layer][0] + shifts[layer][0]).astype(bf16))
        qkv = (jnp.dot(n1, weights_qkv[layer], preferred_element_type=f32) + time_terms[layer]).astype(bf16)
        o, lse = attn_fwd(qkv, mask_pad, walls[layer], scalars, ORDER, scale)
        hidden = x + scatter_rows(
            times_t(o[half:], weights_proj[layer]), times_t(o[:half], weights_proj[layer])
        )
        hhat, _ = normed(hidden)
        n2 = gather_rows((hhat * gains[layer][1] + shifts[layer][1]).astype(bf16))
        u = jnp.dot(n2, weights_fc1[layer], preferred_element_type=f32)
        g = gelu_tanh(u).astype(bf16)
        y = hidden + scatter_rows(
            times_t(g[half:], weights_fc2[layer]), times_t(g[:half], weights_fc2[layer])
        )
        return y, (x, n1, qkv, o, lse, hidden, n2, u, g)

    def backward(layer, dy, kept):
        x, n1, qkv, o, lse, hidden, n2, u, g = kept
        dm = gather_rows(dy.astype(bf16))
        grad_fc2 = grad_of(dm, g)
        dg = jnp.dot(dm, weights_fc2[layer], preferred_element_type=f32)
        du = jax.vjp(gelu_tanh, u)[1](dg)[0].astype(bf16)
        dn2 = scatter_rows(times_t(du[half:], weights_fc1[layer]), times_t(du[:half], weights_fc1[layer]))
        grad_fc1 = grad_of(n2, du)
        dx2, dgain2, dshift2 = norm_back(hidden, dn2, gains[layer][1])
        dh = dy + dx2
        da = gather_rows(dh.astype(bf16))
        do = jnp.dot(da, weights_proj[layer], preferred_element_type=f32).astype(bf16)
        grad_proj = grad_of(da, o)
        dqkv, dwall = attn_bwd(qkv, do, o, lse, mask_pad, walls[layer], scalars, ORDER, scale)
        dn1 = scatter_rows(times_t(dqkv[half:], weights_qkv[layer]), times_t(dqkv[:half], weights_qkv[layer]))
        grad_qkv = grad_of(n1, dqkv)
        sums = jnp.sum(dqkv.astype(f32), axis=0)
        sums = jnp.concatenate([sums[:local_width], sums[2 * local_width :]])
        dx1, dgain1, dshift1 = norm_back(x, dn1, gains[layer][0])
        rel = bias_grads(out_label, label_lanes, dwall)
        norms = jnp.stack([dgain1, dgain2, dshift1, dshift2])
        parts = [lax.psum_scatter(w, "dp", scatter_dimension=0, tiled=True) for w in (grad_fc2, grad_fc1, grad_proj, grad_qkv)]
        return dh + dx1, parts, rel, norms, sums

    def by_core(pairs):
        return jnp.where(first, pairs[0], pairs[1])

    def to_home_core(both):
        return move(
            jnp.where(first, both[1], both[0]),
            lambda dd, cc, zz: (dd, 1 - cc, zz) if cc == zz // 2 else None,
        )

    def deliver(both):
        same = jnp.where(home, by_core(both), to_home_core(both))
        got = [
            move(both[layer], lambda dd, cc, zz, to=layer: (dd, to, zz ^ 2) if cc != zz // 2 else None)
            for layer in range(2)
        ]
        return same, by_core(got)

    x0 = home_rows(inputs).astype(f32)
    y0, kept0 = forward(0, x0)
    act0 = y0.astype(bf16)
    y1, kept1 = forward(1, act0.astype(f32))
    act1 = y1.astype(bf16)
    live = (t * rows + jnp.arange(rows)) < length
    dy1 = home_rows(cotangent).astype(f32) * live.astype(f32)[:, None]
    gin1, parts1, rel1, norms1, sums1 = backward(1, dy1, kept1)
    gin0, parts0, rel0, norms0, sums0 = backward(0, gin1.astype(bf16).astype(f32), kept0)

    def by_image(same, other):
        return jnp.stack([jnp.where(pair == 0, same, other), jnp.where(pair == 0, other, same)])[None]

    acts = by_image(*deliver((act0, act1)))
    same, other = deliver((gin0.astype(bf16), gin1.astype(bf16)))
    same = jnp.where(home, by_core((gin0, gin1)), same.astype(f32))
    input_grads = by_image(same, other.astype(f32))
    grads = []
    for a, b in zip(parts0, parts1):
        same, other = deliver((a, b))
        grads.append(same.astype(f32) + other.astype(f32))

    here = (jnp.arange(2 * ndp) == 2 * d + pair).astype(f32)[:, None]
    pack = jnp.concatenate(
        [
            rel0.reshape(-1, 128),
            rel1.reshape(-1, 128),
            (here * jnp.concatenate([sums0, sums1])[None]).reshape(-1, 128),
            jnp.stack([norms0, norms1]).reshape(-1, 128),
        ],
        axis=0,
    )
    bit = 1
    while bit < ndp:
        pack = pack + move(pack, lambda dd, cc, zz, b=bit: (dd ^ b, cc, zz))
        bit *= 2
    pack = pack + across(pack)
    n_rel = heads * 32
    n_sum = 2 * ndp * 4 * local_width // 128
    rel_both = (pack[:n_rel], pack[n_rel : 2 * n_rel])
    sums_all = pack[2 * n_rel : 2 * n_rel + n_sum].reshape(2 * ndp, 2, 2 * local_width)
    norms_all = pack[2 * n_rel + n_sum :]
    norms_all = norms_all + partner(norms_all)
    norms_all = norms_all + sibling(norms_all)
    norms_all = norms_all.reshape(2, 4, width)
    norms_mine = jnp.where(first, norms_all[0], norms_all[1])
    cols = width // (4 * ndp)
    norms_mine = lax.dynamic_slice_in_dim(norms_mine, (d * 4 + z) * cols, cols, 1)
    rel_mine = jnp.where(home, by_core(rel_both), to_home_core(rel_both))
    rel_grad = rel_mine.reshape(heads, 4096)[:, :buckets]
    sums_both = (sums_all[:, 0], sums_all[:, 1])
    sums_mine = jnp.where(home, by_core(sums_both), to_home_core(sums_both))
    emb_all = lax.all_gather(time_emb, "dp", axis=0, tiled=True)
    emb_mine = lax.dynamic_slice_in_dim(emb_all, d * (width // ndp), width // ndp, 1).astype(f32)
    grad_time = lax.dot_general(
        emb_mine, sums_mine, (((0,), (0,)), ((), ())), precision=lax.Precision.HIGHEST, preferred_element_type=f32
    ).reshape(width // ndp, 2, local_width)
    return (
        acts,
        input_grads,
        grads[3].reshape(width // ndp, 3, local_width)[None],
        grad_time[None],
        grads[2][None],
        grads[1][None],
        grads[0][None],
        rel_grad[None],
        norms_mine[:2][None],
        norms_mine[2:][None],
    )


def solution(mesh):
    return jax.shard_map(
        local,
        mesh=mesh,
        in_specs=(
            P("dp", "tensor", None),
            P("dp", None),
            P("dp"),
            P("dp", None),
            P(),
            P("section", None, None, "tensor"),
            P("section", None, None, "tensor"),
            P("section", None, "tensor"),
            P("section", None, "tensor"),
            P("section", None, "tensor"),
            P("section", "tensor", None),
            P("section", None, None),
            P("section", None, None),
            P("dp", "tensor", None),
        ),
        out_specs=(
            P("section", "dp", "tensor", None),
            P("section", "dp", "tensor", None),
            P("section", "dp", None, "tensor"),
            P("section", "dp", None, "tensor"),
            P("section", "dp", "tensor"),
            P("section", "dp", "tensor"),
            P("section", "dp", "tensor"),
            P("section", "tensor", None),
            P("section", None, ("dp", "tensor")),
            P("section", None, ("dp", "tensor")),
        ),
        check_vma=False,
    )
```

```python
import functools
import math

import jax
import jax.numpy as jnp
from jax import lax
from jax.experimental import pallas as pl
from jax.experimental.pallas import tpu as pltpu
from jax.sharding import PartitionSpec as P

LOG2E = 1.4426950408889634
HIGHEST = lax.Precision.HIGHEST
BIGL = 1920
SMALL0 = 4 * BIGL
WALL = SMALL0 + 2304


def _labels_hi_lo(lab):
    hi = lax.shift_right_logical(lab, 6)
    lo = jnp.bitwise_and(lab, 63)
    iota = lax.broadcasted_iota(jnp.int32, (64, lab.shape[1]), 0)
    return iota == hi, jnp.where(iota == lo, 1.0, 0.0)


def bias_kernel(out_lab_ref, lab_ref, table_ref, wall_ref):
    lab = lab_ref[...]
    hi_mask, lo_hot = _labels_hi_lo(lab)
    rows = lax.dot_general(table_ref[0], lo_hot, (((1,), (0,)), ((), ())), precision=HIGHEST, preferred_element_type=jnp.float32)
    flat = jnp.sum(jnp.where(hi_mask, rows, 0.0), axis=0, keepdims=True) * LOG2E
    outside = jnp.sum(jnp.where(lab == out_lab_ref[0], flat, 0.0), axis=1, keepdims=True)
    wide = jnp.broadcast_to(flat, (32, 4096))
    wide = pltpu.roll(wide, 4096 - 31, 1, stride=1, stride_axis=0)
    lane = lax.broadcasted_iota(jnp.int32, (32, 128), 1)
    tight = []
    for g in range(16):
        a = wide[:, 256 * g : 256 * g + 128]
        b = wide[:, 256 * g + 128 : 256 * g + 256]
        piece = jnp.where(lane < 32, a, pltpu.roll(a, 96, 1))
        other = jnp.where(lane < 96, pltpu.roll(b, 64, 1), pltpu.roll(b, 32, 1))
        tight.append(jnp.where(lane < 64, piece, other))
    w0 = jnp.concatenate(tight, axis=1)
    for s in range(4):
        shifted = w0 if s == 0 else pltpu.roll(w0, 2048 - 32 * s, 1)
        wall_ref[0, :, s * BIGL : (s + 1) * BIGL] = shifted[:, :BIGL]
    lane16 = lane[:16]
    tight16 = []
    for g in range(8):
        lo_v = w0[:16, 256 * g : 256 * g + 128]
        hi_v = w0[:16, 256 * g + 128 : 256 * g + 256]
        acc = lo_v
        for k in range(1, 4):
            acc = jnp.where(lane16 >= 16 * k, pltpu.roll(lo_v, 128 - 16 * k, 1), acc)
        for k in range(4):
            acc = jnp.where(lane16 >= 64 + 16 * k, pltpu.roll(hi_v, (64 - 16 * k) % 128, 1), acc)
        tight16.append(acc)
    w16 = jnp.concatenate(tight16, axis=1)
    for j in range(16):
        sl = pltpu.roll(w16, 1024 - 16 * (31 - j), 1)[:, :256]
        wall_ref[0, 16 * (j % 2) : 16 * (j % 2) + 16, SMALL0 + 256 * (j // 2) : SMALL0 + 256 * (j // 2) + 256] = sl
    wall_ref[0, :, SMALL0 + 2048 : WALL] = jnp.broadcast_to(outside, (32, 256))


def bias_tables(out_lab, lab, table):
    heads = table.shape[0]
    return pl.pallas_call(
        bias_kernel,
        grid=(heads,),
        in_specs=[
            pl.BlockSpec(memory_space=pltpu.SMEM),
            pl.BlockSpec((1, 4096), lambda h: (0, 0)),
            pl.BlockSpec((1, 64, 64), lambda h: (h, 0, 0)),
        ],
        out_specs=pl.BlockSpec((1, 32, WALL), lambda h: (h, 0, 0)),
        out_shape=jax.ShapeDtypeStruct((heads, 32, WALL), jnp.float32),
        compiler_params=pltpu.CompilerParams(vmem_limit_bytes=40 << 20),
    )(out_lab, lab, table)


def bias_grad_kernel(out_lab_ref, lab_ref, acc_ref, out_ref):
    lab = lab_ref[...]
    hi_mask, lo_hot = _labels_hi_lo(lab)
    acc = acc_ref[0]
    w0 = jnp.zeros((32, 2048), jnp.float32)
    for s in range(4):
        piece = jnp.concatenate([acc[:, s * BIGL : (s + 1) * BIGL], jnp.zeros((32, 128), jnp.float32)], axis=1)
        w0 = w0 + (piece if s == 0 else pltpu.roll(piece, 32 * s, 1))
    w16 = jnp.zeros((16, 1024), jnp.float32)
    for j in range(16):
        piece = acc[16 * (j % 2) : 16 * (j % 2) + 16, SMALL0 + 256 * (j // 2) : SMALL0 + 256 * (j // 2) + 256]
        piece = jnp.concatenate([piece, jnp.zeros((16, 768), jnp.float32)], axis=1)
        w16 = w16 + pltpu.roll(piece, 16 * (31 - j), 1)
    outside = jnp.sum(jnp.sum(acc[:, SMALL0 + 2048 : WALL], axis=0, keepdims=True), axis=1, keepdims=True)
    lane = lax.broadcasted_iota(jnp.int32, (32, 128), 1)
    lane16 = lane[:16]
    wide = []
    for g in range(32):
        src = w0[:, 128 * (g // 2) : 128 * (g // 2) + 128]
        k = 2 * (g % 2)
        first = src if k == 0 else pltpu.roll(src, 128 - 32 * k, 1)
        second = pltpu.roll(src, (64 - 32 * (k + 1)) % 128, 1)
        piece = jnp.where(lane < 32, first, jnp.where((lane >= 64) & (lane < 96), second, 0.0))
        src16 = w16[:, 128 * (g // 4) : 128 * (g // 4) + 128]
        k = 2 * (g % 4)
        first = src16 if k == 0 else pltpu.roll(src16, 128 - 16 * k, 1)
        second = pltpu.roll(src16, (64 - 16 * (k + 1)) % 128, 1)
        piece16 = jnp.where(lane16 < 16, first, jnp.where((lane16 >= 64) & (lane16 < 80), second, 0.0))
        wide.append(piece + jnp.concatenate([piece16, jnp.zeros((16, 128), jnp.float32)], axis=0))
    wide = jnp.concatenate(wide, axis=1)
    back = 31 - lax.broadcasted_iota(jnp.int32, (32, 4096), 0)
    for k in range(5):
        wide = jnp.where(jnp.bitwise_and(back, 1 << k) > 0, pltpu.roll(wide, 1 << k, 1), wide)
    flat = jnp.sum(wide, axis=0, keepdims=True)
    flat = flat + jnp.where(lab == out_lab_ref[0], outside, 0.0)
    spread = jnp.where(hi_mask, jnp.broadcast_to(flat, (64, 4096)), 0.0)
    out_ref[0] = lax.dot_general(spread, lo_hot, (((1,), (1,)), ((), ())), precision=HIGHEST, preferred_element_type=jnp.float32)


def bias_grads(out_lab, lab, acc):
    heads = acc.shape[0]
    return pl.pallas_call(
        bias_grad_kernel,
        grid=(heads,),
        in_specs=[
            pl.BlockSpec(memory_space=pltpu.SMEM),
            pl.BlockSpec((1, 4096), lambda h: (0, 0)),
            pl.BlockSpec((1, 32, WALL), lambda h: (h, 0, 0)),
        ],
        out_specs=pl.BlockSpec((1, 64, 64), lambda h: (h, 0, 0)),
        out_shape=jax.ShapeDtypeStruct((heads, 64, 64), jnp.float32),
        compiler_params=pltpu.CompilerParams(vmem_limit_bytes=40 << 20),
    )(out_lab, lab, acc)


def label_row(rel_index):
    side = 32
    a = rel_index[0, 1023].reshape(side, side)
    b = rel_index[0, 0].reshape(side, side)
    c = rel_index[0, 992].reshape(side, side)
    d = rel_index[0, 31].reshape(side, side)
    top = jnp.concatenate([a, c[:, 1:]], axis=1)
    low = jnp.concatenate([d[1:], b[1:, 1:]], axis=1)
    grid = jnp.flip(jnp.concatenate([top, low], axis=0), (0, 1))
    return jnp.pad(grid, ((0, 1), (0, 1)), constant_values=4095).reshape(1, 4096)


NT = (((1,), (1,)), ((), ()))
TN = (((0,), (0,)), ((), ()))
NN = (((1,), (0,)), ((), ()))
HD = 72
QB = 256


def dot(a, b, dims):
    return lax.dot_general(a, b, dims, preferred_element_type=jnp.float32)


def head_lanes(x, at, extra=None):
    rows = x.shape[0]
    part = x[:, at : at + HD]
    if extra is None:
        pad = jnp.zeros((rows, 128 - HD), x.dtype)
    else:
        pad = extra
    return jnp.concatenate([part, pad], axis=1)


def strip_start(t, small, q_quarter, jj, rel):
    kq = jnp.bitwise_xor(t, rel)
    big = BIGL * ((31 - jj) % 4) + 128 * ((31 - jj) // 4 - 2 * kq + 2 * q_quarter)
    inner = SMALL0 + 256 * jj
    tiny = jnp.where((kq == 0) & (q_quarter == 0), inner, SMALL0 + 2048)
    return pl.multiple_of(jnp.where(small == 1, tiny, big), 128)


def attn_fwd_kernel(order, scale, sc_ref, q_ref, kv_ref, mask_ref, wall_ref, o_ref, lse_ref, s_scr, p_scr):
    t, small = sc_ref[0], sc_ref[1]
    qq = jnp.bitwise_xor(t, sc_ref[2 + pl.program_id(0)])
    heads = wall_ref.shape[0]
    width = heads * HD
    rows = kv_ref.shape[0]
    nstrip = rows // 32
    k_extra = mask_ref[...]
    lane = lax.broadcasted_iota(jnp.int32, (QB, 128 - HD), 1)
    q_extra = jnp.where(lane == 0, 1.0, 0.0).astype(jnp.bfloat16)
    outs = []
    for h in range(heads):
        kh = head_lanes(kv_ref, width + HD * h, k_extra)
        qh = head_lanes(q_ref, HD * h, q_extra)
        vh = head_lanes(kv_ref, 2 * width + HD * h)
        s_scr[h % 2] = dot(kh, qh, NT)
        top = None
        for st in range(nstrip):
            start = strip_start(t, small, qq, st % 8, order[st // 8])
            s = s_scr[h % 2, 32 * st : 32 * st + 32] * (scale * LOG2E) + wall_ref[h, :, pl.ds(start, QB)]
            s_scr[h % 2, 32 * st : 32 * st + 32] = s
            top = s if top is None else jnp.maximum(top, s)
        row_max = jnp.max(top, axis=0, keepdims=True)
        total = None
        for st in range(nstrip):
            p = jnp.exp2(s_scr[h % 2, 32 * st : 32 * st + 32] - row_max)
            p_scr[h % 2, 32 * st : 32 * st + 32] = p.astype(jnp.bfloat16)
            total = p if total is None else total + p
        row_sum = jnp.sum(total, axis=0, keepdims=True)
        o_t = dot(vh, p_scr[h % 2], TN) * (1.0 / row_sum)
        lse_ref[0, h : h + 1, :] = row_max + jnp.log2(row_sum)
        outs.append(o_t.T[:, :HD].astype(jnp.bfloat16))
    o_ref[...] = jnp.concatenate(outs, axis=1)


def attn_fwd(qkv, mask_pad, wall, scalars, order, scale):
    rows, wide = qkv.shape
    nq = rows // QB
    heads = wall.shape[0]
    width = heads * HD
    return pl.pallas_call(
        functools.partial(attn_fwd_kernel, order, scale),
        grid=(nq,),
        in_specs=[
            pl.BlockSpec(memory_space=pltpu.SMEM),
            pl.BlockSpec((QB, wide), lambda i: (i, 0)),
            pl.BlockSpec((rows, wide), lambda i: (0, 0)),
            pl.BlockSpec((rows, 128 - HD), lambda i: (0, 0)),
            pl.BlockSpec((heads, 32, WALL), lambda i: (0, 0, 0), pipeline_mode=pl.Buffered(1)),
        ],
        out_specs=[pl.BlockSpec((QB, width), lambda i: (i, 0)), pl.BlockSpec((1, heads, QB), lambda i: (i, 0, 0))],
        out_shape=[jax.ShapeDtypeStruct((rows, width), jnp.bfloat16), jax.ShapeDtypeStruct((nq, heads, QB), jnp.float32)],
        scratch_shapes=[pltpu.VMEM((2, rows, QB), jnp.float32), pltpu.VMEM((2, rows, QB), jnp.bfloat16)],
        compiler_params=pltpu.CompilerParams(vmem_limit_bytes=40 << 20),
        cost_estimate=pl.CostEstimate(flops=16 << 30, bytes_accessed=12 << 20, transcendentals=0),
    )(scalars, qkv, qkv, mask_pad, wall)


def attn_bwd_kernel(order, scale, sc_ref, q_ref, kv_ref, do_ref, o_ref, lse_ref, mask_ref, wall_ref,
                    dqkv_ref, acc_ref, p_scr, s_scr, dq_scr, dk_scr, dv_scr):
    step = pl.program_id(0)
    t, small = sc_ref[0], sc_ref[1]
    qq = jnp.bitwise_xor(t, sc_ref[2 + step])
    heads = wall_ref.shape[0]
    width = heads * HD
    rows = kv_ref.shape[0]

    @pl.when(step == 0)
    def _():
        acc_ref[...] = jnp.zeros_like(acc_ref)
        dk_scr[...] = jnp.zeros_like(dk_scr)
        dv_scr[...] = jnp.zeros_like(dv_scr)

    k_extra = mask_ref[...]
    lane = lax.broadcasted_iota(jnp.int32, (QB, 128 - HD), 1)
    q_extra = jnp.where(lane == 0, 1.0, 0.0).astype(jnp.bfloat16)
    dqs = []
    for h in range(heads):
        kh = head_lanes(kv_ref, width + HD * h, k_extra)
        qh = head_lanes(q_ref, HD * h, q_extra)
        vh = head_lanes(kv_ref, 2 * width + HD * h)
        doh = head_lanes(do_ref, HD * h)
        oh = head_lanes(o_ref, HD * h)
        inner = jnp.sum((doh.astype(jnp.float32) * oh.astype(jnp.float32)).T, axis=0, keepdims=True)
        lse = lse_ref[0, h : h + 1, :]
        for kb in range(rows // 256):
            s_t = dot(kh[256 * kb : 256 * kb + 256], qh, NT)
            dp_t = dot(vh[256 * kb : 256 * kb + 256], doh, NT)
            for js in range(8):
                st = 8 * kb + js
                start = strip_start(t, small, qq, js, order[kb])
                s = s_t[32 * js : 32 * js + 32] * (scale * LOG2E) + wall_ref[h, :, pl.ds(start, QB)]
                p = jnp.exp2(s - lse)
                ds = p * (dp_t[32 * js : 32 * js + 32] - inner)
                p_scr[h % 2, 32 * st : 32 * st + 32] = p.astype(jnp.bfloat16)
                s_scr[h % 2, 32 * st : 32 * st + 32] = ds.astype(jnp.bfloat16)
                acc_ref[h, :, pl.ds(start, QB)] += ds
        p_b, ds_b = p_scr[h % 2], s_scr[h % 2]
        dv_scr[h] += dot(p_b, doh, NN)
        dk_scr[h] += dot(ds_b, qh, NN)
        dq_t = dot(kh, ds_b, TN) * scale
        dqs.append(dq_t.T[:, :HD].astype(jnp.bfloat16))
    dq_scr[pl.ds(pl.multiple_of(step * QB, QB), QB)] = jnp.concatenate(dqs, axis=1)

    @pl.when(step == pl.num_programs(0) - 1)
    def _():
        parts = [dq_scr[...]]
        parts += [(dk_scr[h, :, :HD] * scale).astype(jnp.bfloat16) for h in range(heads)]
        parts += [dv_scr[h, :, :HD].astype(jnp.bfloat16) for h in range(heads)]
        dqkv_ref[...] = jnp.concatenate(parts, axis=1)


def attn_bwd(qkv, do, o, lse, mask_pad, wall, scalars, order, scale):
    rows, wide = qkv.shape
    nq = rows // QB
    heads = wall.shape[0]
    width = heads * HD
    row_spec = pl.BlockSpec((QB, width), lambda i: (i, 0))
    return pl.pallas_call(
        functools.partial(attn_bwd_kernel, order, scale),
        grid=(nq,),
        in_specs=[
            pl.BlockSpec(memory_space=pltpu.SMEM),
            pl.BlockSpec((QB, wide), lambda i: (i, 0)),
            pl.BlockSpec((rows, wide), lambda i: (0, 0)),
            row_spec,
            row_spec,
            pl.BlockSpec((1, heads, QB), lambda i: (i, 0, 0)),
            pl.BlockSpec((rows, 128 - HD), lambda i: (0, 0)),
            pl.BlockSpec((heads, 32, WALL), lambda i: (0, 0, 0), pipeline_mode=pl.Buffered(1)),
        ],
        out_specs=[pl.BlockSpec((rows, wide), lambda i: (0, 0)), pl.BlockSpec((heads, 32, WALL), lambda i: (0, 0, 0))],
        out_shape=[jax.ShapeDtypeStruct((rows, wide), jnp.bfloat16), jax.ShapeDtypeStruct((heads, 32, WALL), jnp.float32)],
        scratch_shapes=[
            pltpu.VMEM((2, rows, QB), jnp.bfloat16),
            pltpu.VMEM((2, rows, QB), jnp.bfloat16),
            pltpu.VMEM((rows, width), jnp.bfloat16),
            pltpu.VMEM((heads, rows, 128), jnp.float32),
            pltpu.VMEM((heads, rows, 128), jnp.float32),
        ],
        compiler_params=pltpu.CompilerParams(vmem_limit_bytes=48 << 20),
        cost_estimate=pl.CostEstimate(flops=24 << 30, bytes_accessed=20 << 20, transcendentals=0),
    )(scalars, qkv, qkv, do, o, lse, mask_pad, wall)


EPSILON = 1e-05
NCH = 2
GELU_C = math.sqrt(2.0 / math.pi)


def normed(x):
    center = x - jnp.mean(x, axis=-1, keepdims=True)
    spread = jnp.mean(center * center, axis=-1, keepdims=True)
    r = lax.rsqrt(spread + EPSILON)
    return center * r, r


def norm_back(x, dy, gain):
    xhat, r = normed(x)
    dxhat = dy * gain
    dx = r * (
        dxhat
        - jnp.mean(dxhat, axis=-1, keepdims=True)
        - xhat * jnp.mean(dxhat * xhat, axis=-1, keepdims=True)
    )
    return dx, jnp.sum(dy * xhat, axis=0, keepdims=True), jnp.sum(dy, axis=0, keepdims=True)


def gelu_both(u):
    th = jnp.tanh(GELU_C * (u + 0.044715 * u * u * u))
    half = 0.5 * (1.0 + th)
    slope = half + 0.5 * u * (1.0 - th * th) * GELU_C * (1.0 + 3 * 0.044715 * u * u)
    return u * half, slope


class Links:
    def __init__(self, send_sem, recv_sem):
        z, c = lax.axis_index("tensor"), lax.axis_index("section")
        self.ids = ({"tensor": z + 1 - 2 * lax.rem(z, 2)}, {"section": 1 - c})
        self.send_sem, self.recv_sem = send_sem, recv_sem
        self.used = 0
        self.started = []

    def enter(self):
        barrier = pltpu.get_barrier_semaphore()
        for where in self.ids:
            pl.semaphore_signal(barrier, inc=1, device_id=where, device_id_type=pl.DeviceIdType.MESH)
        pl.semaphore_wait(barrier, 2)

    def send(self, src, dst, to):
        k = self.used
        self.used += 1
        copy = pltpu.make_async_remote_copy(
            src_ref=src,
            dst_ref=dst,
            send_sem=self.send_sem.at[k],
            recv_sem=self.recv_sem.at[k],
            device_id=self.ids[to],
            device_id_type=pl.DeviceIdType.MESH,
        )
        copy.start()
        self.started.append(copy)
        return copy

    def leave(self):
        for copy in self.started:
            copy.wait_send()


PARTNER, SIBLING = 0, 1


def chunk(i, rows):
    return pl.ds(i * (rows // NCH), rows // NCH)


class Scatter:
    COPIES = 3 * NCH

    def __init__(self, links, low, wide):
        self.links, self.low, self.wide = links, low, wide
        self.rows = low.shape[1]
        self.copies = {}

    def far(self, i, p2, p3):
        at = chunk(i, self.rows)
        self.low[0, at] = p3.astype(jnp.bfloat16)
        self.copies["a", i] = self.links.send(self.low.at[0, at], self.low.at[3, at], SIBLING)
        self.wide[0, at] = p2

    def middle(self, i):
        at = chunk(i, self.rows)
        self.copies["a", i].wait_recv()
        self.low[1, at] = (self.wide[0, at] + self.low[3, at].astype(jnp.float32)).astype(jnp.bfloat16)
        self.copies["z", i] = self.links.send(self.low.at[1, at], self.low.at[4, at], PARTNER)

    def near(self, i, p0, p1):
        at = chunk(i, self.rows)
        self.low[2, at] = p1.astype(jnp.bfloat16)
        self.copies["b", i] = self.links.send(self.low.at[2, at], self.low.at[5, at], SIBLING)
        self.wide[1, at] = p0

    def done(self, i):
        at = chunk(i, self.rows)
        self.copies["b", i].wait_recv()
        self.copies["z", i].wait_recv()
        return self.wide[1, at] + self.low[5, at].astype(jnp.float32) + self.low[4, at].astype(jnp.float32)


class Gather:
    COPIES = 3 * NCH

    def __init__(self, links, buf):
        self.links, self.buf = links, buf
        self.rows = buf.shape[1]
        self.copies = {}

    def send(self, i, x):
        at = chunk(i, self.rows)
        self.buf[0, at] = x
        self.copies["z", i] = self.links.send(self.buf.at[0, at], self.buf.at[2, at], PARTNER)
        self.copies["s", i] = self.links.send(self.buf.at[0, at], self.buf.at[1, at], SIBLING)

    def forward(self, i):
        at = chunk(i, self.rows)
        self.copies["z", i].wait_recv()
        self.copies["f", i] = self.links.send(self.buf.at[2, at], self.buf.at[3, at], SIBLING)

    def done(self, i):
        self.copies["s", i].wait_recv()
        self.copies["f", i].wait_recv()
        at = chunk(i, self.rows)
        n = self.rows // NCH
        return jnp.concatenate([self.buf[b, at] for b in range(4)], axis=0)


def start_load(src, dst, sem):
    copy = pltpu.make_async_copy(src, dst, sem)
    copy.start()
    return copy


def block_rows(ref, b, i, rows):
    n = rows // NCH
    return ref[pl.ds(b * rows + i * n, n)]


def put_rows(ref, value, i, rows):
    n = rows // NCH
    for b in range(4):
        ref[pl.ds(b * rows + i * n, n)] = value[b * n : (b + 1) * n]


def weight_grad(out, col, x, y):
    width = x.shape[1]
    step = 384
    for k in range(0, width, step):
        out[k : k + step, col : col + y.shape[1]] = dot(x[:, k : k + step], y, TN).astype(out.dtype)


def flat(ref):
    return ref[...].reshape(-1, ref.shape[-1])


def scatter_product(scatter, i, lhs, weight, rows):
    p = dot(jnp.concatenate([lhs(2), lhs(3)], axis=0), weight, NT)
    n = rows // NCH
    scatter.far(i, p[:n], p[n:])
    p = dot(jnp.concatenate([lhs(0), lhs(1)], axis=0), weight, NT)
    scatter.near(i, p[:n], p[n:])


def mid_kernel(x_ref, o_ref, ln_ref, wp_hbm, wf_hbm,
               hid_ref, act_ref, n2_hbm, u_hbm, g_hbm, n1_hbm,
               wp, wf, u_buf, g_buf, gat1, gat2, low1, wide1, low2, wide2, load_sem, store_sem, send_sem, recv_sem):
    rows = x_ref.shape[0]
    n = rows // NCH
    hidden = wf.shape[1] // 2
    loads = [start_load(wp_hbm, wp, load_sem.at[0]), start_load(wf_hbm, wf, load_sem.at[1])]
    links = Links(send_sem, recv_sem)
    links.enter()
    s1, s2 = Scatter(links, low1, wide1), Scatter(links, low2, wide2)
    g1, g2 = Gather(links, gat1), Gather(links, gat2)
    loads[0].wait()
    for i in range(NCH):
        scatter_product(s1, i, lambda b: block_rows(o_ref, b, i, rows), wp[...], rows)
    for i in range(NCH):
        s1.middle(i)
    for i in range(NCH):
        h = x_ref[chunk(i, rows)] + s1.done(i)
        hid_ref[chunk(i, rows)] = h
        g1.send(i, (normed(h)[0] * ln_ref[0:1] + ln_ref[1:2]).astype(jnp.bfloat16))
    loads[1].wait()

    def mlp(i):
        u = dot(g1.done(i), wf[:, :hidden], NN)
        put_rows(u_buf, u.astype(jnp.bfloat16), i, rows)
        g = gelu_both(u)[0].astype(jnp.bfloat16)
        put_rows(g_buf, g, i, rows)
        scatter_product(s2, i, lambda b: g[b * n : (b + 1) * n], wf[:, hidden:], rows)

    g1.forward(0)
    mlp(0)
    g1.forward(1)
    s2.middle(0)
    mlp(1)
    s2.middle(1)
    stores = [
        start_load(gat1, n2_hbm, store_sem.at[0]),
        start_load(u_buf, u_hbm, store_sem.at[1]),
        start_load(g_buf, g_hbm, store_sem.at[2]),
    ]
    for i in range(NCH):
        act = (hid_ref[chunk(i, rows)] + s2.done(i)).astype(jnp.bfloat16)
        act_ref[chunk(i, rows)] = act
        g2.send(i, (normed(act.astype(jnp.float32))[0] * ln_ref[2:3] + ln_ref[3:4]).astype(jnp.bfloat16))
    for i in range(NCH):
        g2.forward(i)
    for i in range(NCH):
        g2.copies["s", i].wait_recv()
        g2.copies["f", i].wait_recv()
    stores.append(start_load(gat2, n1_hbm, store_sem.at[3]))
    links.leave()
    for store in stores:
        store.wait()


VM = pl.BlockSpec(memory_space=pltpu.VMEM)
HB = pl.BlockSpec(memory_space=pl.ANY)


def comm_scratch(copies):
    return [pltpu.SemaphoreType.DMA((copies,)), pltpu.SemaphoreType.DMA((copies,))]


def scatter_scratch(rows, width):
    return [pltpu.VMEM((6, rows, width), jnp.bfloat16), pltpu.VMEM((2, rows, width), jnp.float32)]


def params(ident):
    return pltpu.CompilerParams(collective_id=ident, has_side_effects=True, vmem_limit_bytes=60 << 20)


def mid_chain(x, o, ln, wp, wf):
    rows, width = x.shape
    hidden = wf.shape[1] // 2
    bf16, f32 = jnp.bfloat16, jnp.float32
    out = jax.ShapeDtypeStruct
    res = pl.pallas_call(
        mid_kernel,
        in_specs=[VM, VM, VM, HB, HB],
        out_specs=[VM, VM, HB, HB, HB, HB],
        out_shape=[
            out((rows, width), f32),
            out((rows, width), bf16),
            out((4, rows, width), bf16),
            out((4 * rows, hidden), bf16),
            out((4 * rows, hidden), bf16),
            out((4, rows, width), bf16),
        ],
        scratch_shapes=[
            pltpu.VMEM(wp.shape, bf16),
            pltpu.VMEM(wf.shape, bf16),
            pltpu.VMEM((4 * rows, hidden), bf16),
            pltpu.VMEM((4 * rows, hidden), bf16),
            pltpu.VMEM((4, rows, width), bf16),
            pltpu.VMEM((4, rows, width), bf16),
            *scatter_scratch(rows, width),
            *scatter_scratch(rows, width),
            pltpu.SemaphoreType.DMA((2,)),
            pltpu.SemaphoreType.DMA((4,)),
            *comm_scratch(2 * Scatter.COPIES + 2 * Gather.COPIES),
        ],
        compiler_params=params(1),
        cost_estimate=pl.CostEstimate(flops=60 << 30, bytes_accessed=24 << 20, transcendentals=0),
    )(x, o, ln, wp, wf)
    hid, act, n2, u, g, n1 = res
    return hid, act, n2.reshape(4 * rows, width), u, g, n1.reshape(4 * rows, width)


def turn_kernel(x_ref, o_ref, dy_ref, ln_ref, dm_hbm, wp_hbm, wf_hbm,
                dh_ref, norm_ref, y_hbm, hid_ref, do_ref, da_hbm, gfc_hbm,
                wp, wf, dm, g_buf, du_buf, y_buf, gfc, gat1, gat2, low1, wide1, low2, wide2,
                load_sem, store_sem, send_sem, recv_sem):
    rows = x_ref.shape[0]
    n = rows // NCH
    hidden = wf.shape[1] // 2
    loads = [
        start_load(wp_hbm, wp, load_sem.at[0]),
        start_load(wf_hbm, wf, load_sem.at[1]),
        start_load(dm_hbm, dm, load_sem.at[2]),
    ]
    links = Links(send_sem, recv_sem)
    links.enter()
    s1, s2 = Scatter(links, low1, wide1), Scatter(links, low2, wide2)
    g1, g2 = Gather(links, gat1), Gather(links, gat2)
    loads[0].wait()
    for i in range(NCH):
        scatter_product(s1, i, lambda b: block_rows(o_ref, b, i, rows), wp[...], rows)
    for i in range(NCH):
        s1.middle(i)
    for i in range(NCH):
        h = x_ref[chunk(i, rows)].astype(jnp.float32) + s1.done(i)
        hid_ref[chunk(i, rows)] = h
        g1.send(i, (normed(h)[0] * ln_ref[0:1] + ln_ref[1:2]).astype(jnp.bfloat16))
    loads[1].wait()
    loads[2].wait()

    def mlp(i):
        u = dot(g1.done(i), wf[:, :hidden], NN)
        g, slope = gelu_both(u)
        put_rows(g_buf, g.astype(jnp.bfloat16), i, rows)
        dmi = jnp.concatenate([block_rows(dm, b, i, rows) for b in range(4)], axis=0)
        du = (dot(dmi, wf[:, hidden:], NN) * slope).astype(jnp.bfloat16)
        put_rows(du_buf, du, i, rows)
        scatter_product(s2, i, lambda b: du[b * n : (b + 1) * n], wf[:, :hidden], rows)

    g1.forward(0)
    mlp(0)
    g1.forward(1)
    s2.middle(0)
    mlp(1)
    s2.middle(1)
    weight_grad(gfc, hidden, dm[...], g_buf[...])
    sums = None
    for i in range(NCH):
        at = chunk(i, rows)
        dx, dgain, dshift = norm_back(hid_ref[at], s2.done(i), ln_ref[0:1])
        dh = dy_ref[at] + dx
        dh_ref[at] = dh
        g2.send(i, dh.astype(jnp.bfloat16))
        both = jnp.concatenate([dgain, dshift], axis=0)
        sums = both if sums is None else sums + both
    norm_ref[...] = sums
    weight_grad(gfc, 0, flat(gat1), du_buf[...])
    stores = [start_load(gfc, gfc_hbm, store_sem.at[0])]
    for b in range(4):
        y_buf[pl.ds(b * rows, rows)] = dot(g_buf[pl.ds(b * rows, rows)], wf[:, hidden:], NT).astype(jnp.bfloat16)
    stores.append(start_load(y_buf, y_hbm, store_sem.at[1]))
    for i in range(NCH):
        g2.forward(i)
        put_rows(do_ref, dot(g2.done(i), wp[...], NN).astype(jnp.bfloat16), i, rows)
    stores.append(start_load(gat2, da_hbm, store_sem.at[2]))
    links.leave()
    for store in stores:
        store.wait()


def turn_chain(x, o, dy, ln, dm, wp, wf):
    rows, width = x.shape
    hidden = wf.shape[1] // 2
    lw = wp.shape[1]
    bf16, f32 = jnp.bfloat16, jnp.float32
    out = jax.ShapeDtypeStruct
    res = pl.pallas_call(
        turn_kernel,
        in_specs=[VM, VM, VM, VM, HB, HB, HB],
        out_specs=[VM, VM, HB, VM, VM, HB, HB],
        out_shape=[
            out((rows, width), f32),
            out((2, width), f32),
            out((4 * rows, width), bf16),
            out((rows, width), f32),
            out((4 * rows, lw), bf16),
            out((4, rows, width), bf16),
            out((width, 2 * hidden), bf16),
        ],
        scratch_shapes=[
            pltpu.VMEM(wp.shape, bf16),
            pltpu.VMEM(wf.shape, bf16),
            pltpu.VMEM((4 * rows, width), bf16),
            pltpu.VMEM((4 * rows, hidden), bf16),
            pltpu.VMEM((4 * rows, hidden), bf16),
            pltpu.VMEM((4 * rows, width), bf16),
            pltpu.VMEM((width, 2 * hidden), bf16),
            pltpu.VMEM((4, rows, width), bf16),
            pltpu.VMEM((4, rows, width), bf16),
            *scatter_scratch(rows, width),
            *scatter_scratch(rows, width),
            pltpu.SemaphoreType.DMA((3,)),
            pltpu.SemaphoreType.DMA((3,)),
            *comm_scratch(2 * Scatter.COPIES + 2 * Gather.COPIES),
        ],
        compiler_params=params(2),
        cost_estimate=pl.CostEstimate(flops=60 << 30, bytes_accessed=24 << 20, transcendentals=0),
    )(x, o, dy, ln, dm, wp, wf)
    dh, norms, y, hid, do, da, gfc = res
    return dh, norms, y, hid, do, da.reshape(4 * rows, width), gfc


def back_kernel(x_ref, dh1_ref, hid_ref, ln_ref, dqkv_ref, wq_hbm, wp_hbm, wf_hbm, u_hbm, g_hbm, n2_hbm,
                gin_ref, dh_ref, norm_ref, do_ref, da_hbm, gfc_hbm,
                wq, wp, wf, u_buf, g_buf, n2, du_buf, gfc, gat1, gat2, low1, wide1, low2, wide2,
                load_sem, store_sem, send_sem, recv_sem):
    rows = x_ref.shape[0]
    n = rows // NCH
    hidden = wf.shape[1] // 2
    loads = [
        start_load(src, dst, load_sem.at[k])
        for k, (src, dst) in enumerate(
            ((wq_hbm, wq), (wf_hbm, wf), (u_hbm, u_buf), (g_hbm, g_buf), (n2_hbm, n2), (wp_hbm, wp))
        )
    ]
    links = Links(send_sem, recv_sem)
    links.enter()
    s1, s2 = Scatter(links, low1, wide1), Scatter(links, low2, wide2)
    g1, g2 = Gather(links, gat1), Gather(links, gat2)
    loads[0].wait()
    for i in range(NCH):
        scatter_product(s1, i, lambda b: block_rows(dqkv_ref, b, i, rows), wq[...], rows)
        if i:
            s1.middle(i - 1)
    s1.middle(NCH - 1)
    sums1 = None
    for i in range(NCH):
        at = chunk(i, rows)
        dx, dgain, dshift = norm_back(x_ref[at].astype(jnp.float32), s1.done(i), ln_ref[0:1])
        gin = dh1_ref[at] + dx
        gin_ref[at] = gin
        g1.send(i, gin.astype(jnp.bfloat16))
        both = jnp.concatenate([dgain, dshift], axis=0)
        sums1 = both if sums1 is None else sums1 + both
    for load in loads[1:]:
        load.wait()

    def mlp(i):
        dmi = g1.done(i)
        ui = jnp.concatenate([block_rows(u_buf, b, i, rows) for b in range(4)], axis=0).astype(jnp.float32)
        du = (dot(dmi, wf[:, hidden:], NN) * gelu_both(ui)[1]).astype(jnp.bfloat16)
        put_rows(du_buf, du, i, rows)
        scatter_product(s2, i, lambda b: du[b * n : (b + 1) * n], wf[:, :hidden], rows)

    g1.forward(0)
    mlp(0)
    g1.forward(1)
    s2.middle(0)
    mlp(1)
    s2.middle(1)
    weight_grad(gfc, hidden, flat(gat1), g_buf[...])
    sums2 = None
    for i in range(NCH):
        at = chunk(i, rows)
        dx, dgain, dshift = norm_back(hid_ref[at], s2.done(i), ln_ref[1:2])
        dh = gin_ref[at].astype(jnp.bfloat16).astype(jnp.float32) + dx
        dh_ref[at] = dh
        g2.send(i, dh.astype(jnp.bfloat16))
        both = jnp.concatenate([dgain, dshift], axis=0)
        sums2 = both if sums2 is None else sums2 + both
    norm_ref[...] = jnp.concatenate([sums1, sums2], axis=0)
    weight_grad(gfc, 0, flat(n2), du_buf[...])
    stores = [start_load(gfc, gfc_hbm, store_sem.at[0])]
    for i in range(NCH):
        g2.forward(i)
        put_rows(do_ref, dot(g2.done(i), wp[...], NN).astype(jnp.bfloat16), i, rows)
    stores.append(start_load(gat2, da_hbm, store_sem.at[1]))
    links.leave()
    for store in stores:
        store.wait()


def back_chain(x, dh1, hid, ln, dqkv, wq, wp, wf, u, g, n2):
    rows, width = x.shape
    hidden = wf.shape[1] // 2
    lw = wp.shape[1]
    bf16, f32 = jnp.bfloat16, jnp.float32
    out = jax.ShapeDtypeStruct
    res = pl.pallas_call(
        back_kernel,
        in_specs=[VM] * 5 + [HB] * 6,
        out_specs=[VM, VM, VM, VM, HB, HB],
        out_shape=[
            out((rows, width), f32),
            out((rows, width), f32),
            out((4, width), f32),
            out((4 * rows, lw), bf16),
            out((4, rows, width), bf16),
            out((width, 2 * hidden), bf16),
        ],
        scratch_shapes=[
            pltpu.VMEM(wq.shape, bf16),
            pltpu.VMEM(wp.shape, bf16),
            pltpu.VMEM(wf.shape, bf16),
            pltpu.VMEM((4 * rows, hidden), bf16),
            pltpu.VMEM((4 * rows, hidden), bf16),
            pltpu.VMEM((4 * rows, width), bf16),
            pltpu.VMEM((4 * rows, hidden), bf16),
            pltpu.VMEM((width, 2 * hidden), bf16),
            pltpu.VMEM((4, rows, width), bf16),
            pltpu.VMEM((4, rows, width), bf16),
            *scatter_scratch(rows, width),
            *scatter_scratch(rows, width),
            pltpu.SemaphoreType.DMA((6,)),
            pltpu.SemaphoreType.DMA((2,)),
            *comm_scratch(2 * Scatter.COPIES + 2 * Gather.COPIES),
        ],
        compiler_params=params(3),
        cost_estimate=pl.CostEstimate(flops=60 << 30, bytes_accessed=24 << 20, transcendentals=0),
    )(x, dh1, hid, ln, dqkv, wq, wp, wf, u, g, n2)
    gin, dh, norms, do, da, gfc = res
    return gin, dh, norms, do, da.reshape(4 * rows, width), gfc


AXES = ("dp", "section", "tensor")
ORDER = (0, 2, 1, 3)


def local(
    inputs,
    time_emb,
    lengths,
    key_mask,
    rel_index,
    w_qkv,
    w_time,
    w_proj,
    w_fc1,
    w_fc2,
    rel_table,
    norm_gains,
    norm_biases,
    cotangent,
):
    bf16, f32 = jnp.bfloat16, jnp.float32
    _, rows, width = inputs.shape
    seq_len = key_mask.shape[1]
    heads, buckets = rel_table.shape[1:]
    local_width = w_proj.shape[2]
    scale = 1.0 / math.sqrt(HD)
    ndp = lax.axis_size("dp")
    d = lax.axis_index("dp")
    c = lax.axis_index("section")
    z = lax.axis_index("tensor")
    pair = z // 2
    home = c == pair
    first = c == 0
    t = z % 2 + 2 * c

    def move(x, to, name="move"):
        pairs = []
        for dd in range(ndp):
            for cc in range(2):
                for zz in range(4):
                    dst = to(dd, cc, zz)
                    if dst is not None:
                        pairs.append(((dd * 2 + cc) * 4 + zz, (dst[0] * 2 + dst[1]) * 4 + dst[2]))
        with jax.named_scope(name):
            return lax.ppermute(x, AXES, pairs)

    def partner(x):
        return move(x, lambda dd, cc, zz: (dd, cc, zz ^ 1), "partner")

    def sibling(x):
        return move(x, lambda dd, cc, zz: (dd, 1 - cc, zz), "sibling")

    def across(x):
        return move(x, lambda dd, cc, zz: (dd, cc, zz ^ 2), "across")

    def fetch(x):
        rem = across(x)
        keep = jnp.where(home, x, rem)
        recv = sibling(jnp.where(home, rem, x))
        return jnp.where(first, keep, recv), jnp.where(first, recv, keep)

    def dp_gather(piece):
        if ndp != 4:
            return lax.all_gather(piece, "dp", axis=0, tiled=True)
        n = piece.shape[0]
        p1 = move(piece, lambda dd, cc, zz: (dd ^ 1, cc, zz), "w_x")
        p2 = move(piece, lambda dd, cc, zz: (dd ^ 2, cc, zz), "w_y")
        p3a = move(p2[: n // 2], lambda dd, cc, zz: (dd ^ 1, cc, zz), "w_yx")
        p3b = move(p1[n // 2 :], lambda dd, cc, zz: (dd ^ 2, cc, zz), "w_xy")
        out = jnp.zeros((ndp * n, piece.shape[1]), piece.dtype)
        for part, at in ((piece, d * n), (p1, (d ^ 1) * n), (p2, (d ^ 2) * n), (p3a, (d ^ 3) * n), (p3b, (d ^ 3) * n + n // 2)):
            out = lax.dynamic_update_slice_in_dim(out, part, at, 0)
        return out

    def dp_scatter(x, bits):
        n = x.shape[1]
        left = sorted(bits, reverse=True)
        v = x.reshape((2,) * len(left) + (-1, n))
        for b in bits:
            axis = left.index(b)
            left.remove(b)
            mine = (d >> b) & 1
            send = lax.dynamic_index_in_dim(v, 1 - mine, axis, keepdims=False)
            keep = lax.dynamic_index_in_dim(v, mine, axis, keepdims=False)
            got = move(send, lambda dd, cc, zz, b=b: (dd ^ (1 << b), cc, zz), "g_dp")
            v = keep.astype(f32) + got.astype(f32)
            if left:
                v = v.astype(bf16)
        return v

    def piece_of(w, layer):
        part = w.shape[0] // ndp
        src = lax.dynamic_slice_in_dim(w, d * part, part, 0)
        far = move(src, lambda dd, cc, zz: (dd, 1 - (zz ^ 2) // 2, zz ^ 2) if cc == layer else None, "w_far")
        near = move(src, lambda dd, cc, zz: (dd, zz // 2, zz) if cc == layer else None, "w_near")
        return jnp.where(home, near, far)

    time_all = jnp.einsum("id,dcn->icn", time_emb, w_time[0], preferred_element_type=f32)
    table = jnp.pad(rel_table[0], ((0, 0), (0, 4096 - buckets)))
    small_pack = jnp.concatenate(
        [
            table.reshape(-1, 128),
            time_all.reshape(-1, 128),
            norm_gains[0].reshape(-1, 128),
            norm_biases[0].reshape(-1, 128),
        ],
        axis=0,
    )
    cuts = []
    at = 0
    for n in (heads * 32, time_all.size // 128, 2 * width // 128, 2 * width // 128):
        cuts.append((at, at + n))
        at += n
    packs = fetch(small_pack)
    def home_rows(x):
        other = lax.dynamic_index_in_dim(x, 1 - pair, 0, keepdims=False)
        got = move(other, lambda dd, cc, zz: (dd, cc, zz ^ 2) if cc == zz // 2 else None, "x_rows")
        return jnp.where(home, lax.dynamic_index_in_dim(x, pair, 0, keepdims=False), got)

    def after(x, *first_things):
        return lax.optimization_barrier((x,) + first_things)[0]

    x0 = home_rows(inputs).astype(f32)
    own_qp = (w_qkv[0].reshape(width, 3 * local_width), w_proj[0])
    own_fc = jnp.concatenate([w_fc1[0], w_fc2[0]], axis=1)
    piece_q0 = piece_of(own_qp[0], 0)
    piece_p0 = piece_of(after(own_qp[1], piece_q0), 0)
    piece_f0 = piece_of(after(own_fc, piece_p0), 0)
    piece_qp1 = piece_of(after(jnp.concatenate(own_qp, axis=1), piece_f0), 1)
    piece_f1 = piece_of(after(own_fc, piece_qp1), 1)
    hidden_units = w_fc1.shape[2]

    def sc_gather(piece):
        return lax.all_gather(piece, "dp", axis=0, tiled=True)

    fc = [sc_gather(piece_f0)]
    qp1 = sc_gather(after(piece_qp1, fc[0]))
    fc.append(sc_gather(after(piece_f1, qp1)))
    weights_qkv = (dp_gather(piece_q0), qp1[:, : 3 * local_width])
    weights_proj = (dp_gather(piece_p0), qp1[:, 3 * local_width :])
    weights_fc = fc

    label_lanes = label_row(rel_index)
    out_label = rel_index[1, seq_len - 1, seq_len - 1].reshape(1)
    walls, time_terms, gains, shifts = [], [], [], []
    for pack in packs:
        pieces = [pack[a:b] for a, b in cuts]
        walls.append(bias_tables(out_label, label_lanes, pieces[0].reshape(heads, 64, 64)))
        both = pieces[1].reshape(2, 2, local_width)
        mine = lax.dynamic_index_in_dim(both, pair, 0, keepdims=False)
        time_terms.append(jnp.concatenate([mine[0], jnp.zeros((local_width,), f32), mine[1]]))
        gains.append(pieces[2].reshape(2, width))
        shifts.append(pieces[3].reshape(2, width))

    length = lax.dynamic_index_in_dim(lengths, pair, 0, keepdims=False)
    small = (length < seq_len).astype(jnp.int32)
    scalars = jnp.stack([t, small] + [jnp.int32(j) for j in ORDER])
    mask = lax.dynamic_index_in_dim(key_mask, pair, 0, keepdims=False).reshape(4, rows)
    mask = jnp.concatenate([lax.dynamic_index_in_dim(mask, t ^ j, 0, keepdims=False) for j in ORDER])
    lane = jnp.arange(128 - HD)[None, :]
    mask_pad = jnp.where((lane == 0) & (mask[:, None] == 0), -1e30, 0.0).astype(bf16)

    def gather_rows(x):
        far = partner(x)
        near = sibling(x)
        return jnp.concatenate([x, near, far, sibling(far)], axis=0)

    def scatter_rows(far, near):
        a = sibling(far[rows:].astype(bf16))
        rz = partner((far[:rows] + a.astype(f32)).astype(bf16))
        rs = sibling(near[rows:].astype(bf16))
        return near[:rows] + rs.astype(f32) + rz.astype(f32)

    def times_t(x, w):
        return lax.dot_general(x, w, (((1,), (1,)), ((), ())), preferred_element_type=f32)

    def grad_of(x, y):
        return lax.dot_general(x, y, (((0,), (0,)), ((), ())), preferred_element_type=f32).astype(bf16)

    half = 2 * rows

    def reduced(x):
        with jax.named_scope("g_sum"):
            return lax.psum_scatter(x, "dp", scatter_dimension=0, tiled=True)

    def reduced_late(x):
        if ndp & (ndp - 1):
            return reduced(x)
        bits = list(range(ndp.bit_length() - 1))
        cut = 4 * 128
        return jnp.concatenate(
            [dp_scatter(x[:, :cut], bits), dp_scatter(x[:, cut:], bits[::-1])], axis=1
        ).astype(bf16)

    def scores_in(n1, layer):
        return (jnp.dot(n1, weights_qkv[layer], preferred_element_type=f32) + time_terms[layer]).astype(bf16)

    def column_sums(dqkv):
        sums = jnp.sum(dqkv.astype(f32), axis=0)
        return jnp.concatenate([sums[:local_width], sums[2 * local_width :]])

    def tie(*values):
        return lax.optimization_barrier(values)

    def by_core(pairs):
        return jnp.where(first, pairs[0], pairs[1])

    def near_of(x, layer):
        return move(x, lambda dd, cc, zz: (dd, layer, zz) if cc == zz // 2 and cc != layer else None, "d_near")

    def far_of(x, layer):
        return move(x, lambda dd, cc, zz: (dd, layer, zz ^ 2) if cc != zz // 2 else None, "d_far")

    live = (t * rows + jnp.arange(rows)) < length

    n1_0 = gather_rows((normed(x0)[0] * gains[0][0] + shifts[0][0]).astype(bf16))
    qkv0 = scores_in(n1_0, 0)
    qkv0, cotangent = tie(qkv0, cotangent)
    cot = home_rows(cotangent)
    o0, lse0 = attn_fwd(qkv0, mask_pad, walls[0], scalars, ORDER, scale)
    o0, cot = tie(o0, cot)
    ln_mid = jnp.stack([gains[0][1], shifts[0][1], gains[1][0], shifts[1][0]])
    hid0, act0, n2_0, u0, g0, n1_1 = mid_chain(x0, o0, ln_mid, weights_proj[0], weights_fc[0])
    qkv1 = scores_in(n1_1, 1)
    dy1 = cot.astype(f32) * live.astype(f32)[:, None]
    qkv1, dm1 = tie(qkv1, dy1.astype(bf16))
    dm1 = gather_rows(dm1)
    o1, lse1 = attn_fwd(qkv1, mask_pad, walls[1], scalars, ORDER, scale)
    o1, dm1 = tie(o1, dm1)

    ln_turn = jnp.stack([gains[1][1], shifts[1][1]])
    dh1, norms1, y1, hid1, do1, da1, gfc1 = turn_chain(act0, o1, dy1, ln_turn, dm1, weights_proj[1], weights_fc[1])
    sum_fc1 = reduced(gfc1)
    do1, y1, a0 = tie(do1, y1, act0)
    act1 = (hid1 + scatter_rows(y1[half:], y1[:half])).astype(bf16)
    got_acts = [near_of(a0, 0) + near_of(act1, 1), far_of(a0, 0) + far_of(act1, 1)]
    dqkv1, dwall1 = attn_bwd(qkv1, do1, o1, lse1, mask_pad, walls[1], scalars, ORDER, scale)
    dqkv1, got_acts = tie(dqkv1, got_acts)
    ln_back = jnp.stack([gains[1][0], gains[0][1]])
    gin1, dh0, norms10, do0, da0, gfc0 = back_chain(
        act0, dh1, hid0, ln_back, dqkv1, weights_qkv[1], weights_proj[0], weights_fc[0], u0, g0, n2_0
    )
    sum_fc0 = reduced(gfc0)
    sum_qp1 = reduced(jnp.concatenate([grad_of(n1_1, dqkv1), grad_of(da1, o1)], axis=1))
    rel1 = bias_grads(out_label, label_lanes, dwall1)
    sums1 = column_sums(dqkv1)
    do0, sum_qp1, rel1, sums1 = tie(do0, sum_qp1, rel1, sums1)
    g1 = gin1.astype(bf16)
    w1 = jnp.concatenate([sum_qp1, sum_fc1], axis=1)
    do0, g1, w1 = tie(do0, g1, w1)
    got1 = [near_of(g1, 1), far_of(g1, 1), near_of(w1, 1), far_of(w1, 1)]
    dqkv0, dwall0 = attn_bwd(qkv0, do0, o0, lse0, mask_pad, walls[0], scalars, ORDER, scale)
    dqkv0, got1 = tie(dqkv0, got1)
    dn1 = scatter_rows(times_t(dqkv0[half:], weights_qkv[0]), times_t(dqkv0[:half], weights_qkv[0]))
    grad_qp0 = jnp.concatenate([grad_of(n1_0, dqkv0), grad_of(da0, o0)], axis=1)
    sum_qp0 = reduced_late(grad_qp0)
    rel0 = bias_grads(out_label, label_lanes, dwall0)
    sums0 = column_sums(dqkv0)
    dn1, grad_qp0, rel0, sums0 = tie(dn1, grad_qp0, rel0, sums0)
    dx, dgain, dshift = norm_back(x0, dn1, gains[0][0])
    gin0 = dh0 + dx
    early0, early1, late1 = norms10[2:], norms1, norms10[:2]
    late0 = jnp.concatenate([dgain, dshift], axis=0)
    sums_w0, sums_w1 = (sum_qp0, sum_fc0), (sum_qp1, sum_fc1)

    def by_image(same, other):
        return jnp.stack([jnp.where(pair == 0, same, other), jnp.where(pair == 0, other, same)])[None]

    acts = by_image(jnp.where(home, by_core((act0, act1)), got_acts[0]), got_acts[1])
    low0 = gin0.astype(bf16)
    same = jnp.where(home, by_core((gin0, gin1)), (near_of(low0, 0) + got1[0]).astype(f32))
    input_grads = by_image(same, (far_of(low0, 0) + got1[1]).astype(f32))

    def total(mine, parts):
        out = jnp.where(home, mine, jnp.zeros_like(mine)).astype(f32)
        for part in parts:
            out = out + part.astype(f32)
        return out

    n_qp = 4 * local_width
    grad_fc = total(
        by_core((sums_w0[1], sums_w1[1])),
        (near_of(sums_w0[1], 0), far_of(sums_w0[1], 0), got1[2][:, n_qp:], got1[3][:, n_qp:]),
    )
    grad_qp = total(
        by_core((sums_w0[0], sums_w1[0])),
        (near_of(sums_w0[0], 0), far_of(sums_w0[0], 0), got1[2][:, :n_qp], got1[3][:, :n_qp]),
    )

    here = (jnp.arange(2 * ndp) == 2 * d + pair).astype(f32)[:, None]
    pack = jnp.concatenate(
        [
            rel0.reshape(-1, 128),
            rel1.reshape(-1, 128),
            (here * jnp.concatenate([sums0, sums1])[None]).reshape(-1, 128),
            jnp.stack([early0, early1, late1]).reshape(-1, 128),
        ],
        axis=0,
    )
    late = late0.reshape(-1, 128)

    def summed(x):
        bit = 1
        while bit < ndp:
            x = x + move(x, lambda dd, cc, zz, b=bit: (dd ^ b, cc, zz), "pack_dp")
            bit *= 2
        return x + across(x)

    pack = summed(pack)
    n_rel = heads * 32
    n_sum = 2 * ndp * 4 * local_width // 128
    rel_both = (pack[:n_rel], pack[n_rel : 2 * n_rel])
    sums_all = pack[2 * n_rel : 2 * n_rel + n_sum].reshape(2 * ndp, 2, 2 * local_width)
    norms = pack[2 * n_rel + n_sum :]
    norms = norms + partner(norms)
    norms = norms + sibling(norms)
    late = summed(late)
    late = late + partner(late)
    late = late + sibling(late)
    early0, early1, late1 = norms.reshape(3, 2, width)
    late0 = late.reshape(2, width)
    norms_mine = jnp.stack([by_core((late0, late1)), by_core((early0, early1))], axis=1)
    cols = width // (4 * ndp)
    norms_mine = lax.dynamic_slice_in_dim(norms_mine, (d * 4 + z) * cols, cols, 2)

    def to_home_core(both):
        return move(
            jnp.where(first, both[1], both[0]),
            lambda dd, cc, zz: (dd, 1 - cc, zz) if cc == zz // 2 else None,
            "pack_near",
        )

    rel_mine = jnp.where(home, by_core(rel_both), to_home_core(rel_both))
    rel_grad = rel_mine.reshape(heads, 4096)[:, :buckets]
    sums_both = (sums_all[:, 0], sums_all[:, 1])
    sums_mine = jnp.where(home, by_core(sums_both), to_home_core(sums_both))
    emb_all = lax.all_gather(time_emb, "dp", axis=0, tiled=True)
    emb_mine = lax.dynamic_slice_in_dim(emb_all, d * (width // ndp), width // ndp, 1).astype(f32)
    grad_time = lax.dot_general(
        emb_mine, sums_mine, (((0,), (0,)), ((), ())), precision=lax.Precision.HIGHEST, preferred_element_type=f32
    ).reshape(width // ndp, 2, local_width)
    return (
        acts,
        input_grads,
        grad_qp[:, : 3 * local_width].reshape(width // ndp, 3, local_width)[None],
        grad_time[None],
        grad_qp[:, 3 * local_width :][None],
        grad_fc[:, :hidden_units][None],
        grad_fc[:, hidden_units:][None],
        rel_grad[None],
        norms_mine[0][None],
        norms_mine[1][None],
    )


def solution(mesh):
    return jax.shard_map(
        local,
        mesh=mesh,
        in_specs=(
            P("dp", "tensor", None),
            P("dp", None),
            P("dp"),
            P("dp", None),
            P(),
            P("section", None, None, "tensor"),
            P("section", None, None, "tensor"),
            P("section", None, "tensor"),
            P("section", None, "tensor"),
            P("section", None, "tensor"),
            P("section", "tensor", None),
            P("section", None, None),
            P("section", None, None),
            P("dp", "tensor", None),
        ),
        out_specs=(
            P("section", "dp", "tensor", None),
            P("section", "dp", "tensor", None),
            P("section", "dp", None, "tensor"),
            P("section", "dp", None, "tensor"),
            P("section", "dp", "tensor"),
            P("section", "dp", "tensor"),
            P("section", "dp", "tensor"),
            P("section", "tensor", None),
            P("section", None, ("dp", "tensor")),
            P("section", None, ("dp", "tensor")),
        ),
        check_vma=False,
    )
```

```python
import functools
import math

import jax
import jax.numpy as jnp
from jax import lax
from jax.experimental import pallas as pl
from jax.experimental.pallas import tpu as pltpu
from jax.sharding import PartitionSpec as P

LOG2E = 1.4426950408889634
HIGHEST = lax.Precision.HIGHEST
PLANE = 7 * 256
WALL = 8 * PLANE


def _labels_hi_lo(lab):
    hi = lax.shift_right_logical(lab, 6)
    lo = jnp.bitwise_and(lab, 63)
    iota = lax.broadcasted_iota(jnp.int32, (64, lab.shape[1]), 0)
    return iota == hi, jnp.where(iota == lo, 1.0, 0.0)


def build_wall(small, out_lab, lab, hi_mask, lo_hot, table, wall_ref):
    rows = lax.dot_general(table, lo_hot, (((1,), (0,)), ((), ())), precision=HIGHEST, preferred_element_type=jnp.float32)
    flat = jnp.sum(jnp.where(hi_mask, rows, 0.0), axis=0, keepdims=True) * LOG2E
    outside = jnp.sum(jnp.where(lab == out_lab, flat, 0.0), axis=1, keepdims=True)
    wide = jnp.broadcast_to(flat, (32, 4096))
    wide = pltpu.roll(wide, 4096 - 31, 1, stride=1, stride_axis=0)
    lane = lax.broadcasted_iota(jnp.int32, (32, 128), 1)
    tight = []
    for g in range(16):
        a = wide[:, 256 * g : 256 * g + 128]
        b = wide[:, 256 * g + 128 : 256 * g + 256]
        piece = jnp.where(lane < 32, a, pltpu.roll(a, 96, 1))
        other = jnp.where(lane < 96, pltpu.roll(b, 64, 1), pltpu.roll(b, 32, 1))
        tight.append(jnp.where(lane < 64, piece, other))
    w0 = jnp.concatenate(tight, axis=1)
    lane16 = lane[:16]
    tight16 = []
    for g in range(8):
        lo_v = w0[:16, 256 * g : 256 * g + 128]
        hi_v = w0[:16, 256 * g + 128 : 256 * g + 256]
        acc = lo_v
        for k in range(1, 4):
            acc = jnp.where(lane16 >= 16 * k, pltpu.roll(lo_v, 128 - 16 * k, 1), acc)
        for k in range(4):
            acc = jnp.where(lane16 >= 64 + 16 * k, pltpu.roll(hi_v, (64 - 16 * k) % 128, 1), acc)
        tight16.append(acc)
    w16 = jnp.concatenate(tight16, axis=1)
    beyond = jnp.broadcast_to(outside, (32, 768))
    tiny = small == 1
    for j in range(8):
        big = w0 if j == 7 else pltpu.roll(w0, 2048 - 32 * (7 - j), 1)
        inner = [pltpu.roll(w16, 1024 - 16 * (31 - 2 * j - k), 1)[:, :256] for k in range(2)]
        inner = jnp.concatenate(inner, axis=0)
        at = j * PLANE
        wall_ref[:, at : at + 768] = jnp.where(tiny, beyond, big[:, :768])
        wall_ref[:, at + 768 : at + 1024] = jnp.where(tiny, inner, big[:, 768:1024])
        wall_ref[:, at + 1024 : at + PLANE] = jnp.where(tiny, beyond, big[:, 1024:PLANE])


def bias_kernel(flags_ref, lab_ref, table_ref, wall_ref):
    lab = lab_ref[...]
    hi_mask, lo_hot = _labels_hi_lo(lab)
    build_wall(flags_ref[0], flags_ref[1], lab, hi_mask, lo_hot, table_ref[0], wall_ref.at[0])


def bias_tables(flags, lab, table):
    heads = table.shape[0]
    return pl.pallas_call(
        bias_kernel,
        grid=(heads,),
        in_specs=[
            pl.BlockSpec(memory_space=pltpu.SMEM),
            pl.BlockSpec((1, 4096), lambda h: (0, 0)),
            pl.BlockSpec((1, 64, 64), lambda h: (h, 0, 0)),
        ],
        out_specs=pl.BlockSpec((1, 32, WALL), lambda h: (h, 0, 0)),
        out_shape=jax.ShapeDtypeStruct((heads, 32, WALL), jnp.float32),
        compiler_params=pltpu.CompilerParams(vmem_limit_bytes=40 << 20),
    )(flags, lab, table)


def wall_grad(small, out_lab, lab, hi_mask, lo_hot, acc_ref):
    tiny = small == 1
    w0 = jnp.zeros((32, 2048), jnp.float32)
    w16 = jnp.zeros((16, 1024), jnp.float32)
    beyond = jnp.zeros((32, 768), jnp.float32)
    for j in range(8):
        at = j * PLANE
        piece = jnp.concatenate([acc_ref[:, at : at + PLANE], jnp.zeros((32, 256), jnp.float32)], axis=1)
        w0 = w0 + (piece if j == 7 else pltpu.roll(piece, 32 * (7 - j), 1))
        beyond = beyond + acc_ref[:, at + 1024 : at + PLANE]
        for k in range(2):
            inner = acc_ref[16 * k : 16 * k + 16, at + 768 : at + 1024]
            inner = jnp.concatenate([inner, jnp.zeros((16, 768), jnp.float32)], axis=1)
            w16 = w16 + pltpu.roll(inner, 16 * (31 - 2 * j - k), 1)
    w0 = jnp.where(tiny, 0.0, w0)
    w16 = jnp.where(tiny, w16, 0.0)
    outside = jnp.sum(jnp.sum(jnp.where(tiny, beyond, 0.0), axis=0, keepdims=True), axis=1, keepdims=True)
    lane = lax.broadcasted_iota(jnp.int32, (32, 128), 1)
    lane16 = lane[:16]
    wide = []
    for g in range(32):
        src = w0[:, 128 * (g // 2) : 128 * (g // 2) + 128]
        k = 2 * (g % 2)
        first = src if k == 0 else pltpu.roll(src, 128 - 32 * k, 1)
        second = pltpu.roll(src, (64 - 32 * (k + 1)) % 128, 1)
        piece = jnp.where(lane < 32, first, jnp.where((lane >= 64) & (lane < 96), second, 0.0))
        src16 = w16[:, 128 * (g // 4) : 128 * (g // 4) + 128]
        k = 2 * (g % 4)
        first = src16 if k == 0 else pltpu.roll(src16, 128 - 16 * k, 1)
        second = pltpu.roll(src16, (64 - 16 * (k + 1)) % 128, 1)
        piece16 = jnp.where(lane16 < 16, first, jnp.where((lane16 >= 64) & (lane16 < 80), second, 0.0))
        wide.append(piece + jnp.concatenate([piece16, jnp.zeros((16, 128), jnp.float32)], axis=0))
    wide = jnp.concatenate(wide, axis=1)
    back = 31 - lax.broadcasted_iota(jnp.int32, (32, 4096), 0)
    for k in range(5):
        wide = jnp.where(jnp.bitwise_and(back, 1 << k) > 0, pltpu.roll(wide, 1 << k, 1), wide)
    flat = jnp.sum(wide, axis=0, keepdims=True)
    flat = flat + jnp.where(lab == out_lab, outside, 0.0)
    spread = jnp.where(hi_mask, jnp.broadcast_to(flat, (64, 4096)), 0.0)
    return lax.dot_general(spread, lo_hot, (((1,), (1,)), ((), ())), precision=HIGHEST, preferred_element_type=jnp.float32)


def bias_grad_kernel(flags_ref, lab_ref, acc_ref, out_ref):
    lab = lab_ref[...]
    hi_mask, lo_hot = _labels_hi_lo(lab)
    out_ref[0] = wall_grad(flags_ref[0], flags_ref[1], lab, hi_mask, lo_hot, acc_ref.at[0])


def bias_grads(flags, lab, acc):
    heads = acc.shape[0]
    return pl.pallas_call(
        bias_grad_kernel,
        grid=(heads,),
        in_specs=[
            pl.BlockSpec(memory_space=pltpu.SMEM),
            pl.BlockSpec((1, 4096), lambda h: (0, 0)),
            pl.BlockSpec((1, 32, WALL), lambda h: (h, 0, 0)),
        ],
        out_specs=pl.BlockSpec((1, 64, 64), lambda h: (h, 0, 0)),
        out_shape=jax.ShapeDtypeStruct((heads, 64, 64), jnp.float32),
        compiler_params=pltpu.CompilerParams(vmem_limit_bytes=40 << 20),
    )(flags, lab, acc)


def label_row(rel_index):
    side = 32
    a = rel_index[0, 1023].reshape(side, side)
    b = rel_index[0, 0].reshape(side, side)
    c = rel_index[0, 992].reshape(side, side)
    d = rel_index[0, 31].reshape(side, side)
    top = jnp.concatenate([a, c[:, 1:]], axis=1)
    low = jnp.concatenate([d[1:], b[1:, 1:]], axis=1)
    grid = jnp.flip(jnp.concatenate([top, low], axis=0), (0, 1))
    return jnp.pad(grid, ((0, 1), (0, 1)), constant_values=4095).reshape(1, 4096)


NT = (((1,), (1,)), ((), ()))
TN = (((0,), (0,)), ((), ()))
NN = (((1,), (0,)), ((), ()))
HD = 72
QB = 256


def dot(a, b, dims):
    return lax.dot_general(a, b, dims, preferred_element_type=jnp.float32)


def head_lanes(x, at, extra=None):
    rows = x.shape[0]
    part = x[:, at : at + HD]
    if extra is None:
        pad = jnp.zeros((rows, 128 - HD), x.dtype)
    else:
        pad = extra
    return jnp.concatenate([part, pad], axis=1)


def quarter(r, c, rel):
    return lax.rem(r + rel % 2, 2) + 2 * lax.rem(c + rel // 2, 2)


def strip_start(q_quarter, jj, kq):
    return pl.multiple_of(PLANE * jj + 256 * (q_quarter - kq + 3), 256)


def attn_block(q_quarter, key_quarters, scale, q_ref, kv_ref, k_extra, wall_ref, lse_ref, s_scr, p_scr):
    heads = wall_ref.shape[0]
    width = heads * HD
    nstrip = kv_ref.shape[0] // 32
    lane = lax.broadcasted_iota(jnp.int32, (QB, 128 - HD), 1)
    q_extra = jnp.where(lane == 0, 1.0, 0.0).astype(jnp.bfloat16)
    outs = []
    for h in range(heads):
        kh = head_lanes(kv_ref, width + HD * h, k_extra)
        qh = head_lanes(q_ref, HD * h, q_extra)
        vh = head_lanes(kv_ref, 2 * width + HD * h)
        s_scr[h % 2] = dot(kh, qh, NT)
        top = None
        for st in range(nstrip):
            start = strip_start(q_quarter, st % 8, key_quarters[st // 8])
            s = s_scr[h % 2, 32 * st : 32 * st + 32] * (scale * LOG2E) + wall_ref[h, :, pl.ds(start, QB)]
            s_scr[h % 2, 32 * st : 32 * st + 32] = s
            top = s if top is None else jnp.maximum(top, s)
        row_max = jnp.max(top, axis=0, keepdims=True)
        total = None
        for st in range(nstrip):
            p = jnp.exp2(s_scr[h % 2, 32 * st : 32 * st + 32] - row_max)
            p_scr[h % 2, 32 * st : 32 * st + 32] = p.astype(jnp.bfloat16)
            total = p if total is None else total + p
        row_sum = jnp.sum(total, axis=0, keepdims=True)
        o_t = dot(vh, p_scr[h % 2], TN) * (1.0 / row_sum)
        lse_ref[h : h + 1, :] = row_max + jnp.log2(row_sum)
        outs.append(o_t.T[:, :HD].astype(jnp.bfloat16))
    return jnp.concatenate(outs, axis=1)


def attn_fwd_kernel(order, scale, sc_ref, q_ref, kv_ref, mask_ref, wall_ref, o_ref, lse_ref, s_scr, p_scr):
    r, c = sc_ref[0], sc_ref[1]
    qq = quarter(r, c, sc_ref[2 + pl.program_id(0)])
    keys = [quarter(r, c, j) for j in order]
    o_ref[...] = attn_block(
        qq, keys, scale, q_ref, kv_ref, mask_ref[...], wall_ref, lse_ref.at[0], s_scr, p_scr
    )


def attn_fwd(qkv, mask_pad, wall, scalars, order, scale):
    rows, wide = qkv.shape
    nq = rows // QB
    heads = wall.shape[0]
    width = heads * HD
    return pl.pallas_call(
        functools.partial(attn_fwd_kernel, order, scale),
        grid=(nq,),
        in_specs=[
            pl.BlockSpec(memory_space=pltpu.SMEM),
            pl.BlockSpec((QB, wide), lambda i: (i, 0)),
            pl.BlockSpec((rows, wide), lambda i: (0, 0)),
            pl.BlockSpec((rows, 128 - HD), lambda i: (0, 0)),
            pl.BlockSpec((heads, 32, WALL), lambda i: (0, 0, 0), pipeline_mode=pl.Buffered(1)),
        ],
        out_specs=[pl.BlockSpec((QB, width), lambda i: (i, 0)), pl.BlockSpec((1, heads, QB), lambda i: (i, 0, 0))],
        out_shape=[jax.ShapeDtypeStruct((rows, width), jnp.bfloat16), jax.ShapeDtypeStruct((nq, heads, QB), jnp.float32)],
        scratch_shapes=[pltpu.VMEM((2, rows, QB), jnp.float32), pltpu.VMEM((2, rows, QB), jnp.bfloat16)],
        compiler_params=pltpu.CompilerParams(vmem_limit_bytes=40 << 20),
        cost_estimate=pl.CostEstimate(flops=16 << 30, bytes_accessed=12 << 20, transcendentals=0),
    )(scalars, qkv, qkv, mask_pad, wall)


def attn_bwd_kernel(order, scale, sc_ref, q_ref, kv_ref, do_ref, o_ref, lse_ref, mask_ref, wall_ref,
                    dqkv_ref, acc_ref, p_scr, s_scr, dq_scr, dk_scr, dv_scr):
    step = pl.program_id(0)
    r, c = sc_ref[0], sc_ref[1]
    qq = quarter(r, c, sc_ref[2 + step])
    keys = [quarter(r, c, j) for j in order]
    heads = wall_ref.shape[0]
    width = heads * HD
    rows = kv_ref.shape[0]

    @pl.when(step == 0)
    def _():
        acc_ref[...] = jnp.zeros_like(acc_ref)
        dk_scr[...] = jnp.zeros_like(dk_scr)
        dv_scr[...] = jnp.zeros_like(dv_scr)

    k_extra = mask_ref[...]
    lane = lax.broadcasted_iota(jnp.int32, (QB, 128 - HD), 1)
    q_extra = jnp.where(lane == 0, 1.0, 0.0).astype(jnp.bfloat16)
    dqs = []
    for h in range(heads):
        kh = head_lanes(kv_ref, width + HD * h, k_extra)
        qh = head_lanes(q_ref, HD * h, q_extra)
        vh = head_lanes(kv_ref, 2 * width + HD * h)
        doh = head_lanes(do_ref, HD * h)
        oh = head_lanes(o_ref, HD * h)
        inner = jnp.sum((doh.astype(jnp.float32) * oh.astype(jnp.float32)).T, axis=0, keepdims=True)
        lse = lse_ref[0, h : h + 1, :]
        for kb in range(rows // 256):
            s_t = dot(kh[256 * kb : 256 * kb + 256], qh, NT)
            dp_t = dot(vh[256 * kb : 256 * kb + 256], doh, NT)
            for js in range(8):
                st = 8 * kb + js
                start = strip_start(qq, js, keys[kb])
                s = s_t[32 * js : 32 * js + 32] * (scale * LOG2E) + wall_ref[h, :, pl.ds(start, QB)]
                p = jnp.exp2(s - lse)
                ds = p * (dp_t[32 * js : 32 * js + 32] - inner)
                p_scr[h % 2, 32 * st : 32 * st + 32] = p.astype(jnp.bfloat16)
                s_scr[h % 2, 32 * st : 32 * st + 32] = ds.astype(jnp.bfloat16)
                acc_ref[h, :, pl.ds(start, QB)] += ds
        p_b, ds_b = p_scr[h % 2], s_scr[h % 2]
        dv_scr[h] += dot(p_b, doh, NN)
        dk_scr[h] += dot(ds_b, qh, NN)
        dq_t = dot(kh, ds_b, TN) * scale
        dqs.append(dq_t.T[:, :HD].astype(jnp.bfloat16))
    dq_scr[pl.ds(pl.multiple_of(step * QB, QB), QB)] = jnp.concatenate(dqs, axis=1)

    @pl.when(step == pl.num_programs(0) - 1)
    def _():
        parts = [dq_scr[...]]
        parts += [(dk_scr[h, :, :HD] * scale).astype(jnp.bfloat16) for h in range(heads)]
        parts += [dv_scr[h, :, :HD].astype(jnp.bfloat16) for h in range(heads)]
        dqkv_ref[...] = jnp.concatenate(parts, axis=1)


def attn_bwd(qkv, do, o, lse, mask_pad, wall, scalars, order, scale):
    rows, wide = qkv.shape
    nq = rows // QB
    heads = wall.shape[0]
    width = heads * HD
    row_spec = pl.BlockSpec((QB, width), lambda i: (i, 0))
    return pl.pallas_call(
        functools.partial(attn_bwd_kernel, order, scale),
        grid=(nq,),
        in_specs=[
            pl.BlockSpec(memory_space=pltpu.SMEM),
            pl.BlockSpec((QB, wide), lambda i: (i, 0)),
            pl.BlockSpec((rows, wide), lambda i: (0, 0)),
            row_spec,
            row_spec,
            pl.BlockSpec((1, heads, QB), lambda i: (i, 0, 0)),
            pl.BlockSpec((rows, 128 - HD), lambda i: (0, 0)),
            pl.BlockSpec((heads, 32, WALL), lambda i: (0, 0, 0), pipeline_mode=pl.Buffered(1)),
        ],
        out_specs=[pl.BlockSpec((rows, wide), lambda i: (0, 0)), pl.BlockSpec((heads, 32, WALL), lambda i: (0, 0, 0))],
        out_shape=[jax.ShapeDtypeStruct((rows, wide), jnp.bfloat16), jax.ShapeDtypeStruct((heads, 32, WALL), jnp.float32)],
        scratch_shapes=[
            pltpu.VMEM((2, rows, QB), jnp.bfloat16),
            pltpu.VMEM((2, rows, QB), jnp.bfloat16),
            pltpu.VMEM((rows, width), jnp.bfloat16),
            pltpu.VMEM((heads, rows, 128), jnp.float32),
            pltpu.VMEM((heads, rows, 128), jnp.float32),
        ],
        compiler_params=pltpu.CompilerParams(vmem_limit_bytes=48 << 20),
        cost_estimate=pl.CostEstimate(flops=24 << 30, bytes_accessed=20 << 20, transcendentals=0),
    )(scalars, qkv, qkv, do, o, lse, mask_pad, wall)


EPSILON = 1e-05
NCH = 2
GELU_C = math.sqrt(2.0 / math.pi)


def normed(x):
    center = x - jnp.mean(x, axis=-1, keepdims=True)
    spread = jnp.mean(center * center, axis=-1, keepdims=True)
    r = lax.rsqrt(spread + EPSILON)
    return center * r, r


def norm_back(x, dy, gain):
    xhat, r = normed(x)
    dxhat = dy * gain
    dx = r * (
        dxhat
        - jnp.mean(dxhat, axis=-1, keepdims=True)
        - xhat * jnp.mean(dxhat * xhat, axis=-1, keepdims=True)
    )
    return dx, jnp.sum(dy * xhat, axis=0, keepdims=True), jnp.sum(dy, axis=0, keepdims=True)


def gelu_both(u):
    th = jnp.tanh(GELU_C * (u + 0.044715 * u * u * u))
    half = 0.5 * (1.0 + th)
    slope = half + 0.5 * u * (1.0 - th * th) * GELU_C * (1.0 + 3 * 0.044715 * u * u)
    return u * half, slope


class Links:
    def __init__(self, send_sem, recv_sem, bits=0):
        z, c = lax.axis_index("tensor"), lax.axis_index("section")
        self.z, self.c = z, c
        self.pair = z // 2
        self.r = lax.rem(z, 2)
        self.home = c == self.pair
        across = z + 2 - 4 * self.pair
        self.ids = {
            PARTNER: {"tensor": z + 1 - 2 * self.r},
            SIBLING: {"section": 1 - c},
            FAR: {"tensor": across, "section": self.pair},
            HOME: {"section": self.pair},
        }
        self.greet = [self.ids[PARTNER], self.ids[SIBLING]]
        self.dp_bit = []
        if bits:
            d = lax.axis_index("dp")
            for b in range(bits):
                bit = lax.rem(d // (1 << b), 2)
                self.dp_bit.append(bit)
                self.ids["dp", b] = {"dp": d + (1 - 2 * bit) * (1 << b)}
                self.greet.append(self.ids["dp", b])
            self.greet += [{"tensor": across}, {"tensor": across, "section": 1 - c}]
        self.send_sem, self.recv_sem = send_sem, recv_sem
        self.used = 0
        self.started = []

    def enter(self):
        barrier = pltpu.get_barrier_semaphore()
        for where in self.greet:
            pl.semaphore_signal(barrier, inc=1, device_id=where, device_id_type=pl.DeviceIdType.MESH)
        pl.semaphore_wait(barrier, len(self.greet))

    def send(self, src, dst, to, cond=None):
        k = self.used
        self.used += 1
        copy = pltpu.make_async_remote_copy(
            src_ref=src,
            dst_ref=dst,
            send_sem=self.send_sem.at[k],
            recv_sem=self.recv_sem.at[k],
            device_id=self.ids[to],
            device_id_type=pl.DeviceIdType.MESH,
        )
        when(cond, copy.start)
        self.started.append((copy, cond))
        return copy

    def leave(self):
        for copy, cond in self.started:
            when(cond, copy.wait_send)


def when(cond, do):
    if cond is None:
        do()
    else:
        pl.when(cond)(lambda: do())


PARTNER, SIBLING, FAR, HOME = "partner", "sibling", "far", "home"


class Spread:
    COPIES = 2

    def __init__(self, links, layer, src, out, sem):
        self.links, self.layer, self.src, self.out, self.sem = links, layer, src, out, sem

    def start(self):
        links = self.links
        mine = links.c == self.layer
        keeps = links.pair == self.layer
        self.local = pltpu.make_async_copy(self.src, self.out, self.sem)
        when(mine & keeps, self.local.start)
        self.near = links.send(self.src, self.out, HOME, mine & jnp.logical_not(keeps))
        self.far = links.send(self.src, self.out, FAR, mine)

    def done(self):
        links = self.links
        keeps = links.pair == self.layer
        when(links.home & keeps, self.local.wait)
        when(links.home & jnp.logical_not(keeps), self.near.wait_recv)
        when(jnp.logical_not(links.home), self.far.wait_recv)


def bits_region(links, gathered, cols=None):
    index = []
    for b in reversed(range(len(links.dp_bit))):
        index.append(pl.ds(0, 2) if b in gathered else links.dp_bit[b])
    return tuple(index) + (() if cols is None else (slice(None), cols))


class Deliver:
    COPIES = 2

    def __init__(self, links, layer, src, out, sem):
        self.links, self.layer, self.src, self.out, self.sem = links, layer, src, out, sem

    def start(self):
        links = self.links
        mine = links.c == self.layer
        keeps = links.pair == self.layer
        self.local = pltpu.make_async_copy(self.src, self.out, self.sem)
        when(mine & keeps, self.local.start)
        at = bits_region(links, ())
        self.far = links.send(self.src.at[at], self.out.at[at], FAR, mine)
        self.near = links.send(self.src, self.out, HOME, mine & jnp.logical_not(keeps))

    def done(self):
        links = self.links
        keeps = links.pair == self.layer
        when(links.home & keeps, self.local.wait)
        when(links.home & jnp.logical_not(keeps), self.near.wait_recv)
        when(jnp.logical_not(links.home), self.far.wait_recv)


class Exchange:
    def __init__(self, links, buf):
        self.links, self.buf = links, buf
        columns = buf.shape[-1]
        cut = columns // 256 * 128
        order = list(range(len(links.dp_bit)))
        self.halves = [(pl.ds(0, cut), order), (pl.ds(cut, columns - cut), order[::-1])]
        self.away = jnp.logical_not(links.home)
        self.last = None

    @staticmethod
    def copies(bits):
        return 2 * bits

    def step(self, s):
        self.done()
        self.last = []
        for cols, order in self.halves:
            at = bits_region(self.links, order[:s], cols)
            self.last.append(self.links.send(self.buf.at[at], self.buf.at[at], ("dp", order[s]), self.away))

    def done(self):
        for copy in self.last or ():
            when(self.away, copy.wait_recv)


class Part:
    def __init__(self, links, src, dst, sem):
        at = bits_region(links, ())
        self.whole = pltpu.make_async_copy(src, dst, sem)
        self.piece = pltpu.make_async_copy(src.at[at], dst.at[at], sem)
        self.home, self.away = links.home, jnp.logical_not(links.home)

    def start(self):
        when(self.home, self.whole.start)
        when(self.away, self.piece.start)
        return self

    def wait(self):
        when(self.home, self.whole.wait)
        when(self.away, self.piece.wait)


def chunk(i, rows):
    return pl.ds(i * (rows // NCH), rows // NCH)


class Scatter:
    COPIES = 3 * NCH

    def __init__(self, links, low, wide):
        self.links, self.low, self.wide = links, low, wide
        self.rows = low.shape[1]
        self.copies = {}

    def far(self, i, p2, p3):
        at = chunk(i, self.rows)
        self.low[0, at] = p3.astype(jnp.bfloat16)
        self.copies["a", i] = self.links.send(self.low.at[0, at], self.low.at[3, at], SIBLING)
        self.wide[0, at] = p2

    def middle(self, i):
        at = chunk(i, self.rows)
        self.copies["a", i].wait_recv()
        self.low[1, at] = (self.wide[0, at] + self.low[3, at].astype(jnp.float32)).astype(jnp.bfloat16)
        self.copies["z", i] = self.links.send(self.low.at[1, at], self.low.at[4, at], PARTNER)

    def near(self, i, p0, p1):
        at = chunk(i, self.rows)
        self.low[2, at] = p1.astype(jnp.bfloat16)
        self.copies["b", i] = self.links.send(self.low.at[2, at], self.low.at[5, at], SIBLING)
        self.wide[1, at] = p0

    def done(self, i):
        at = chunk(i, self.rows)
        self.copies["b", i].wait_recv()
        self.copies["z", i].wait_recv()
        return self.wide[1, at] + self.low[5, at].astype(jnp.float32) + self.low[4, at].astype(jnp.float32)


class Gather:
    COPIES = 3 * NCH

    def __init__(self, links, buf):
        self.links, self.buf = links, buf
        self.rows = buf.shape[1]
        self.copies = {}

    def send(self, i, x):
        at = chunk(i, self.rows)
        self.buf[0, at] = x
        self.copies["z", i] = self.links.send(self.buf.at[0, at], self.buf.at[2, at], PARTNER)
        self.copies["s", i] = self.links.send(self.buf.at[0, at], self.buf.at[1, at], SIBLING)

    def forward(self, i):
        at = chunk(i, self.rows)
        self.copies["z", i].wait_recv()
        self.copies["f", i] = self.links.send(self.buf.at[2, at], self.buf.at[3, at], SIBLING)

    def done(self, i):
        self.copies["s", i].wait_recv()
        self.copies["f", i].wait_recv()
        at = chunk(i, self.rows)
        n = self.rows // NCH
        return jnp.concatenate([self.buf[b, at] for b in range(4)], axis=0)


def start_load(src, dst, sem):
    copy = pltpu.make_async_copy(src, dst, sem)
    copy.start()
    return copy


def block_rows(ref, b, i, rows):
    n = rows // NCH
    return ref[pl.ds(b * rows + i * n, n)]


def put_rows(ref, value, i, rows):
    n = rows // NCH
    for b in range(4):
        ref[pl.ds(b * rows + i * n, n)] = value[b * n : (b + 1) * n]


def weight_grad(out, col, x, y):
    width = x.shape[1]
    step = 384
    for k in range(0, width, step):
        out[k : k + step, col : col + y.shape[1]] = dot(x[:, k : k + step], y, TN).astype(out.dtype)


def flat(ref):
    return ref[...].reshape(-1, ref.shape[-1])


def scatter_product(scatter, i, lhs, weight, rows):
    p = dot(jnp.concatenate([lhs(2), lhs(3)], axis=0), weight, NT)
    n = rows // NCH
    scatter.far(i, p[:n], p[n:])
    p = dot(jnp.concatenate([lhs(0), lhs(1)], axis=0), weight, NT)
    scatter.near(i, p[:n], p[n:])


def mid_kernel(bits, x_ref, o_ref, ln_ref, live_ref, cot_hbm, wp_hbm, w1_hbm, w2_hbm, own_q, own_p, own_1, own_2,
               hid_ref, act_ref, dy_ref, n2_hbm, u_hbm, g_hbm, n1_hbm, w1_out, w2_out, next_q, next_p, next_1, next_2,
               wp, w1, w2, got_q, got_p, got_1, got_2, cot, u_buf, g_buf, gat1, gat2, low1, wide1, low2, wide2,
               load_sem, store_sem, send_sem, recv_sem):
    rows, width = x_ref.shape
    n = rows // NCH
    links = Links(send_sem, recv_sem, bits)
    load_p = start_load(wp_hbm, wp, load_sem.at[0])
    load_1 = Part(links, w1_hbm, w1, load_sem.at[1]).start()
    load_2 = Part(links, w2_hbm, w2, load_sem.at[2]).start()
    own_cot = pltpu.make_async_copy(cot_hbm.at[links.pair], cot, load_sem.at[3])
    when(links.home, own_cot.start)
    links.enter()
    ex1, ex2 = Exchange(links, w1), Exchange(links, w2)
    got = (got_q, got_p, got_1, got_2)
    delivers = [
        Deliver(links, 1, src, dst, load_sem.at[4 + k]) for k, (src, dst) in enumerate(zip((own_q, own_p, own_1, own_2), got))
    ]
    s1, s2 = Scatter(links, low1, wide1), Scatter(links, low2, wide2)
    g1, g2 = Gather(links, gat1), Gather(links, gat2)
    load_p.wait()
    for i in range(NCH):
        scatter_product(s1, i, lambda b: block_rows(o_ref, b, i, rows), wp[...], rows)
    load_1.wait()
    ex1.step(0)
    load_2.wait()
    ex2.step(0)
    for i in range(NCH):
        s1.middle(i)
    for s in range(1, bits):
        ex1.step(s)
    for i in range(NCH):
        h = x_ref[chunk(i, rows)].astype(jnp.float32) + s1.done(i)
        hid_ref[chunk(i, rows)] = h
        g1.send(i, (normed(h)[0] * ln_ref[0:1] + ln_ref[1:2]).astype(jnp.bfloat16))
        if i == 0:
            for s in range(1, bits):
                ex2.step(s)
    for deliver in delivers:
        deliver.start()
    far_cot = links.send(cot_hbm.at[1 - links.pair], cot, FAR, links.home)

    def mlp(i):
        u = dot(g1.done(i), w1[...].reshape(width, -1), NN)
        put_rows(u_buf, u.astype(jnp.bfloat16), i, rows)
        g = gelu_both(u)[0].astype(jnp.bfloat16)
        put_rows(g_buf, g, i, rows)
        if i == 0:
            ex2.done()
        scatter_product(s2, i, lambda b: g[b * n : (b + 1) * n], w2[...].reshape(width, -1), rows)

    g1.forward(0)
    ex1.done()
    mlp(0)
    g1.forward(1)
    s2.middle(0)
    mlp(1)
    s2.middle(1)
    stores = [
        start_load(src, dst, store_sem.at[k])
        for k, (src, dst) in enumerate(((gat1, n2_hbm), (u_buf, u_hbm), (g_buf, g_hbm), (w1, w1_out), (w2, w2_out)))
    ]
    exq, exp = Exchange(links, got_q), Exchange(links, got_p)
    for i in range(NCH):
        act = (hid_ref[chunk(i, rows)] + s2.done(i)).astype(jnp.bfloat16)
        act_ref[chunk(i, rows)] = act
        g2.send(i, (normed(act.astype(jnp.float32))[0] * ln_ref[2:3] + ln_ref[3:4]).astype(jnp.bfloat16))
    delivers[0].done()
    exq.step(0)
    delivers[1].done()
    exp.step(0)
    for i in range(NCH):
        g2.forward(i)
    for s in range(1, bits):
        exq.step(s)
        exp.step(s)
    for i in range(NCH):
        g2.copies["s", i].wait_recv()
        g2.copies["f", i].wait_recv()
    stores.append(start_load(gat2, n1_hbm, store_sem.at[5]))
    for k, (ex, buf, dst) in enumerate(((exq, got_q, next_q), (exp, got_p, next_p))):
        ex.done()
        stores.append(start_load(buf, dst, store_sem.at[6 + k]))
    for k, (buf, dst) in enumerate(((got_1, next_1), (got_2, next_2))):
        delivers[2 + k].done()
        stores.append(Part(links, buf, dst, store_sem.at[8 + k]).start())
    when(links.home, own_cot.wait)
    when(jnp.logical_not(links.home), far_cot.wait_recv)
    dy_ref[...] = cot[...].astype(jnp.float32) * live_ref[...]
    links.leave()
    for store in stores:
        store.wait()


VM = pl.BlockSpec(memory_space=pltpu.VMEM)
HB = pl.BlockSpec(memory_space=pl.ANY)


def comm_scratch(copies):
    return [pltpu.SemaphoreType.DMA((copies,)), pltpu.SemaphoreType.DMA((copies,))]


def scatter_scratch(rows, width):
    return [pltpu.VMEM((6, rows, width), jnp.bfloat16), pltpu.VMEM((2, rows, width), jnp.float32)]


def params(ident):
    return pltpu.CompilerParams(collective_id=ident, has_side_effects=True, vmem_limit_bytes=60 << 20)


def mid_chain(x, o, ln, live, cot, wp, w1, w2, own):
    rows, width = x.shape
    hidden = w1.shape[-1]
    bits = w1.ndim - 2
    bf16, f32 = jnp.bfloat16, jnp.float32
    out = jax.ShapeDtypeStruct
    res = pl.pallas_call(
        functools.partial(mid_kernel, bits),
        in_specs=[VM] * 4 + [HB] * 8,
        out_specs=[VM] * 3 + [HB] * 10,
        out_shape=[
            out((rows, width), f32),
            out((rows, width), bf16),
            out((rows, width), f32),
            out((4, rows, width), bf16),
            out((4 * rows, hidden), bf16),
            out((4 * rows, hidden), bf16),
            out((4, rows, width), bf16),
        ]
        + [out(w.shape, bf16) for w in (w1, w2, *own)],
        scratch_shapes=[
            *[pltpu.VMEM(w.shape, bf16) for w in (wp, w1, w2, *own)],
            pltpu.VMEM((rows, width), bf16),
            pltpu.VMEM((4 * rows, hidden), bf16),
            pltpu.VMEM((4 * rows, hidden), bf16),
            pltpu.VMEM((4, rows, width), bf16),
            pltpu.VMEM((4, rows, width), bf16),
            *scatter_scratch(rows, width),
            *scatter_scratch(rows, width),
            pltpu.SemaphoreType.DMA((8,)),
            pltpu.SemaphoreType.DMA((10,)),
            *comm_scratch(
                2 * Scatter.COPIES + 2 * Gather.COPIES + 4 * Deliver.COPIES + 4 * Exchange.copies(bits) + 1
            ),
        ],
        compiler_params=params(1),
        cost_estimate=pl.CostEstimate(flops=60 << 30, bytes_accessed=24 << 20, transcendentals=0),
    )(x, o, ln, live, cot, wp, w1, w2, *own)
    hid, act, dy, n2, u, g, n1 = res[:7]
    return hid, act, dy, n2.reshape(4 * rows, width), u, g, n1.reshape(4 * rows, width), res[7:9], res[9:]


def turn_kernel(bits, x_ref, o_ref, dy_ref, ln_ref, dm_hbm, wp_hbm, w1_hbm, w2_hbm,
                dh_ref, norm_ref, y_hbm, hid_ref, do_ref, da_hbm, gfc_hbm,
                wp, w1, w2, dm, g_buf, du_buf, y_buf, gfc, gat1, gat2, low1, wide1, low2, wide2,
                load_sem, store_sem, send_sem, recv_sem):
    rows, width = x_ref.shape
    n = rows // NCH
    hidden = w1.shape[-1]
    links = Links(send_sem, recv_sem, bits)
    loads = [
        start_load(wp_hbm, wp, load_sem.at[0]),
        Part(links, w1_hbm, w1, load_sem.at[1]).start(),
        Part(links, w2_hbm, w2, load_sem.at[2]).start(),
        start_load(dm_hbm, dm, load_sem.at[3]),
    ]
    links.enter()
    ex1, ex2 = Exchange(links, w1), Exchange(links, w2)
    s1, s2 = Scatter(links, low1, wide1), Scatter(links, low2, wide2)
    g1, g2 = Gather(links, gat1), Gather(links, gat2)
    loads[0].wait()
    for i in range(NCH):
        scatter_product(s1, i, lambda b: block_rows(o_ref, b, i, rows), wp[...], rows)
    loads[1].wait()
    ex1.step(0)
    loads[2].wait()
    ex2.step(0)
    for i in range(NCH):
        s1.middle(i)
    for s in range(1, bits):
        ex1.step(s)
    for i in range(NCH):
        h = x_ref[chunk(i, rows)].astype(jnp.float32) + s1.done(i)
        hid_ref[chunk(i, rows)] = h
        g1.send(i, (normed(h)[0] * ln_ref[0:1] + ln_ref[1:2]).astype(jnp.bfloat16))
        if i == 0:
            for s in range(1, bits):
                ex2.step(s)
    loads[3].wait()

    def mlp(i):
        u = dot(g1.done(i), w1[...].reshape(width, -1), NN)
        g, slope = gelu_both(u)
        put_rows(g_buf, g.astype(jnp.bfloat16), i, rows)
        dmi = jnp.concatenate([block_rows(dm, b, i, rows) for b in range(4)], axis=0)
        du = (dot(dmi, w2[...].reshape(width, -1), NN) * slope).astype(jnp.bfloat16)
        put_rows(du_buf, du, i, rows)
        scatter_product(s2, i, lambda b: du[b * n : (b + 1) * n], w1[...].reshape(width, -1), rows)

    g1.forward(0)
    ex1.done()
    ex2.done()
    mlp(0)
    g1.forward(1)
    s2.middle(0)
    mlp(1)
    s2.middle(1)
    weight_grad(gfc, hidden, dm[...], g_buf[...])
    sums = None
    for i in range(NCH):
        at = chunk(i, rows)
        dx, dgain, dshift = norm_back(hid_ref[at], s2.done(i), ln_ref[0:1])
        dh = dy_ref[at] + dx
        dh_ref[at] = dh
        g2.send(i, dh.astype(jnp.bfloat16))
        both = jnp.concatenate([dgain, dshift], axis=0)
        sums = both if sums is None else sums + both
    norm_ref[...] = sums
    weight_grad(gfc, 0, flat(gat1), du_buf[...])
    stores = [start_load(gfc, gfc_hbm, store_sem.at[0])]
    for b in range(4):
        y_buf[pl.ds(b * rows, rows)] = dot(g_buf[pl.ds(b * rows, rows)], w2[...].reshape(width, -1), NT).astype(jnp.bfloat16)
    stores.append(start_load(y_buf, y_hbm, store_sem.at[1]))
    for i in range(NCH):
        g2.forward(i)
        put_rows(do_ref, dot(g2.done(i), wp[...], NN).astype(jnp.bfloat16), i, rows)
    stores.append(start_load(gat2, da_hbm, store_sem.at[2]))
    links.leave()
    for store in stores:
        store.wait()


def turn_chain(x, o, dy, ln, dm, wp, w1, w2):
    rows, width = x.shape
    hidden = w1.shape[-1]
    bits = w1.ndim - 2
    lw = wp.shape[1]
    bf16, f32 = jnp.bfloat16, jnp.float32
    out = jax.ShapeDtypeStruct
    res = pl.pallas_call(
        functools.partial(turn_kernel, bits),
        in_specs=[VM, VM, VM, VM, HB, HB, HB, HB],
        out_specs=[VM, VM, HB, VM, VM, HB, HB],
        out_shape=[
            out((rows, width), f32),
            out((2, width), f32),
            out((4 * rows, width), bf16),
            out((rows, width), f32),
            out((4 * rows, lw), bf16),
            out((4, rows, width), bf16),
            out((width, 2 * hidden), bf16),
        ],
        scratch_shapes=[
            pltpu.VMEM(wp.shape, bf16),
            pltpu.VMEM(w1.shape, bf16),
            pltpu.VMEM(w2.shape, bf16),
            pltpu.VMEM((4 * rows, width), bf16),
            pltpu.VMEM((4 * rows, hidden), bf16),
            pltpu.VMEM((4 * rows, hidden), bf16),
            pltpu.VMEM((4 * rows, width), bf16),
            pltpu.VMEM((width, 2 * hidden), bf16),
            pltpu.VMEM((4, rows, width), bf16),
            pltpu.VMEM((4, rows, width), bf16),
            *scatter_scratch(rows, width),
            *scatter_scratch(rows, width),
            pltpu.SemaphoreType.DMA((4,)),
            pltpu.SemaphoreType.DMA((3,)),
            *comm_scratch(2 * Scatter.COPIES + 2 * Gather.COPIES + 2 * Exchange.copies(bits)),
        ],
        compiler_params=params(2),
        cost_estimate=pl.CostEstimate(flops=60 << 30, bytes_accessed=24 << 20, transcendentals=0),
    )(x, o, dy, ln, dm, wp, w1, w2)
    dh, norms, y, hid, do, da, gfc = res
    return dh, norms, y, hid, do, da.reshape(4 * rows, width), gfc


def back_kernel(x_ref, dh1_ref, hid_ref, ln_ref, dqkv_ref, wq_hbm, wp_hbm, w1_hbm, w2_hbm, u_hbm, g_hbm, n2_hbm,
                gin_ref, dh_ref, norm_ref, do_ref, da_hbm, gfc_hbm,
                wq, wp, w1, w2, u_buf, g_buf, n2, du_buf, gfc, gat1, gat2, low1, wide1, low2, wide2,
                load_sem, store_sem, send_sem, recv_sem):
    rows = x_ref.shape[0]
    n = rows // NCH
    hidden = w1.shape[1]
    loads = [
        start_load(src, dst, load_sem.at[k])
        for k, (src, dst) in enumerate(
            ((wq_hbm, wq), (w1_hbm, w1), (w2_hbm, w2), (u_hbm, u_buf), (g_hbm, g_buf), (n2_hbm, n2), (wp_hbm, wp))
        )
    ]
    links = Links(send_sem, recv_sem)
    links.enter()
    s1, s2 = Scatter(links, low1, wide1), Scatter(links, low2, wide2)
    g1, g2 = Gather(links, gat1), Gather(links, gat2)
    loads[0].wait()
    for i in range(NCH):
        scatter_product(s1, i, lambda b: block_rows(dqkv_ref, b, i, rows), wq[...], rows)
        if i:
            s1.middle(i - 1)
    s1.middle(NCH - 1)
    sums1 = None
    for i in range(NCH):
        at = chunk(i, rows)
        dx, dgain, dshift = norm_back(x_ref[at].astype(jnp.float32), s1.done(i), ln_ref[0:1])
        gin = dh1_ref[at] + dx
        gin_ref[at] = gin
        g1.send(i, gin.astype(jnp.bfloat16))
        both = jnp.concatenate([dgain, dshift], axis=0)
        sums1 = both if sums1 is None else sums1 + both
    for load in loads[1:]:
        load.wait()

    def mlp(i):
        dmi = g1.done(i)
        ui = jnp.concatenate([block_rows(u_buf, b, i, rows) for b in range(4)], axis=0).astype(jnp.float32)
        du = (dot(dmi, w2[...], NN) * gelu_both(ui)[1]).astype(jnp.bfloat16)
        put_rows(du_buf, du, i, rows)
        scatter_product(s2, i, lambda b: du[b * n : (b + 1) * n], w1[...], rows)

    g1.forward(0)
    mlp(0)
    g1.forward(1)
    s2.middle(0)
    mlp(1)
    s2.middle(1)
    weight_grad(gfc, hidden, flat(gat1), g_buf[...])
    sums2 = None
    for i in range(NCH):
        at = chunk(i, rows)
        dx, dgain, dshift = norm_back(hid_ref[at], s2.done(i), ln_ref[1:2])
        dh = gin_ref[at].astype(jnp.bfloat16).astype(jnp.float32) + dx
        dh_ref[at] = dh
        g2.send(i, dh.astype(jnp.bfloat16))
        both = jnp.concatenate([dgain, dshift], axis=0)
        sums2 = both if sums2 is None else sums2 + both
    norm_ref[...] = jnp.concatenate([sums1, sums2], axis=0)
    weight_grad(gfc, 0, flat(n2), du_buf[...])
    stores = [start_load(gfc, gfc_hbm, store_sem.at[0])]
    for i in range(NCH):
        g2.forward(i)
        put_rows(do_ref, dot(g2.done(i), wp[...], NN).astype(jnp.bfloat16), i, rows)
    stores.append(start_load(gat2, da_hbm, store_sem.at[1]))
    links.leave()
    for store in stores:
        store.wait()


def back_chain(x, dh1, hid, ln, dqkv, wq, wp, w1, w2, u, g, n2):
    rows, width = x.shape
    hidden = w1.shape[1]
    lw = wp.shape[1]
    bf16, f32 = jnp.bfloat16, jnp.float32
    out = jax.ShapeDtypeStruct
    res = pl.pallas_call(
        back_kernel,
        in_specs=[VM] * 5 + [HB] * 7,
        out_specs=[VM, VM, VM, VM, HB, HB],
        out_shape=[
            out((rows, width), f32),
            out((rows, width), f32),
            out((4, width), f32),
            out((4 * rows, lw), bf16),
            out((4, rows, width), bf16),
            out((width, 2 * hidden), bf16),
        ],
        scratch_shapes=[
            pltpu.VMEM(wq.shape, bf16),
            pltpu.VMEM(wp.shape, bf16),
            pltpu.VMEM(w1.shape, bf16),
            pltpu.VMEM(w2.shape, bf16),
            pltpu.VMEM((4 * rows, hidden), bf16),
            pltpu.VMEM((4 * rows, hidden), bf16),
            pltpu.VMEM((4 * rows, width), bf16),
            pltpu.VMEM((4 * rows, hidden), bf16),
            pltpu.VMEM((width, 2 * hidden), bf16),
            pltpu.VMEM((4, rows, width), bf16),
            pltpu.VMEM((4, rows, width), bf16),
            *scatter_scratch(rows, width),
            *scatter_scratch(rows, width),
            pltpu.SemaphoreType.DMA((7,)),
            pltpu.SemaphoreType.DMA((2,)),
            *comm_scratch(2 * Scatter.COPIES + 2 * Gather.COPIES),
        ],
        compiler_params=params(3),
        cost_estimate=pl.CostEstimate(flops=60 << 30, bytes_accessed=24 << 20, transcendentals=0),
    )(x, dh1, hid, ln, dqkv, wq, wp, w1, w2, u, g, n2)
    gin, dh, norms, do, da, gfc = res
    return gin, dh, norms, do, da.reshape(4 * rows, width), gfc


def start_kernel(order, scale, bits, flags_ref, x_hbm, mask_ref, lab_ref, tab_hbm, pack_hbm,
                 wq_hbm, wp_hbm, w1_hbm, w2_hbm,
                 x_ref, pack_ref, lse_ref, o_ref, n1_hbm, qkv_hbm, wall0_hbm, wall1_hbm,
                 wq0_hbm, wp0_hbm, w10_hbm, w20_hbm,
                 tab, wq, wp, w1, w2, qkv, wall, gat1, s_scr, p_scr, load_sem, store_sem, send_sem, recv_sem):
    small, out_lab = flags_ref[0], flags_ref[1]
    rows, width = x_ref.shape
    wide = qkv.shape[1]
    heads = wall.shape[1]
    links = Links(send_sem, recv_sem, bits)
    pair, home = links.pair, links.home
    own_x = pltpu.make_async_copy(x_hbm.at[pair], x_ref, load_sem.at[0])
    when(home, own_x.start)
    links.enter()
    far_x = links.send(x_hbm.at[1 - pair], x_ref, FAR, home)
    packs = [Spread(links, l, pack_hbm, pack_ref.at[l], load_sem.at[1 + l]) for l in range(2)]
    tabs = [Spread(links, l, tab_hbm, tab.at[l], load_sem.at[3 + l]) for l in range(2)]
    for spread in packs + tabs:
        spread.start()
    get_q = Deliver(links, 0, wq_hbm, wq, load_sem.at[5])
    get_p = Deliver(links, 0, wp_hbm, wp, load_sem.at[6])
    get_1 = Deliver(links, 0, w1_hbm, w1, load_sem.at[7])
    get_2 = Deliver(links, 0, w2_hbm, w2, load_sem.at[8])
    ex_q, ex_p = Exchange(links, wq), Exchange(links, wp)
    get_q.start()
    packs[0].done()
    when(home, own_x.wait)
    when(jnp.logical_not(home), far_x.wait_recv)
    g1 = Gather(links, gat1)
    for i in range(NCH):
        at = chunk(i, rows)
        xhat = normed(x_ref[at].astype(jnp.float32))[0]
        g1.send(i, (xhat * pack_ref[0, 0:1] + pack_ref[0, 2:3]).astype(jnp.bfloat16))
    get_p.start()
    get_1.start()
    get_2.start()
    lab = lab_ref[...]
    hi_mask, lo_hot = _labels_hi_lo(lab)

    def build(l):
        def one(h, carry):
            build_wall(small, out_lab, lab, hi_mask, lo_hot, tab[l, h], wall.at[l, h])
            return carry

        lax.fori_loop(0, heads, one, 0)

    tabs[0].done()
    build(0)
    stores = [start_load(wall.at[0], wall0_hbm, store_sem.at[0])]
    get_q.done()
    ex_q.step(0)
    for i in range(NCH):
        g1.forward(i)
    for s in range(1, bits):
        ex_q.step(s)
    for i in range(NCH):
        g1.copies["s", i].wait_recv()
        g1.copies["f", i].wait_recv()
    stores.append(start_load(gat1, n1_hbm, store_sem.at[1]))
    packs[1].done()
    get_p.done()
    ex_q.done()
    ex_p.step(0)
    stores.append(start_load(wq, wq0_hbm, store_sem.at[2]))
    term = pack_ref[0, pl.ds(4 + pair, 1)][:, :wide]
    weight = wq[...].reshape(width, wide)
    for b in range(4):
        qkv[pl.ds(b * rows, rows)] = (dot(gat1[b], weight, NN) + term).astype(jnp.bfloat16)
    stores.append(start_load(qkv, qkv_hbm, store_sem.at[3]))
    for s in range(1, bits):
        ex_p.step(s)
    keys = [quarter(links.r, links.c, j) for j in order]

    def block(i, carry):
        at = pl.ds(pl.multiple_of(i * QB, QB), QB)
        qq = lax.rem(links.r + i // 2, 2) + 2 * lax.rem(links.c + lax.rem(i, 2), 2)
        o_ref[at] = attn_block(
            qq, keys, scale, qkv.at[at], qkv, mask_ref[...], wall.at[0], lse_ref.at[i], s_scr, p_scr
        )
        return carry

    lax.fori_loop(0, 4, block, 0)
    ex_p.done()
    stores.append(start_load(wp, wp0_hbm, store_sem.at[4]))
    tabs[1].done()
    build(1)
    stores.append(start_load(wall.at[1], wall1_hbm, store_sem.at[5]))
    for k, (get, src, dst) in enumerate(((get_1, w1, w10_hbm), (get_2, w2, w20_hbm))):
        get.done()
        stores.append(Part(links, src, dst, store_sem.at[6 + k]).start())
    links.leave()
    for store in stores:
        store.wait()


def start_chain(flags, x, mask_pad, lab, table, pack, wq, wp, w1, w2, order, scale):
    bits = wq.ndim - 2
    _, rows, width = x.shape
    heads = table.shape[0]
    wide = wq.shape[-1]
    bf16, f32 = jnp.bfloat16, jnp.float32
    out = jax.ShapeDtypeStruct
    copies = 1 + 4 * Spread.COPIES + 4 * Deliver.COPIES + 2 * Exchange.copies(bits) + Gather.COPIES
    return pl.pallas_call(
        functools.partial(start_kernel, order, scale, bits),
        in_specs=[pl.BlockSpec(memory_space=pltpu.SMEM), HB, VM, VM, HB, HB, HB, HB, HB, HB],
        out_specs=[VM] * 4 + [HB] * 8,
        out_shape=[
            out((rows, width), bf16),
            out((2,) + pack.shape, f32),
            out((4, heads, QB), f32),
            out((4 * rows, heads * HD), bf16),
            out((4, rows, width), bf16),
            out((4 * rows, wide), bf16),
            out((heads, 32, WALL), f32),
            out((heads, 32, WALL), f32),
            *[out(w.shape, bf16) for w in (wq, wp, w1, w2)],
        ],
        scratch_shapes=[
            pltpu.VMEM((2,) + table.shape, f32),
            *[pltpu.VMEM(w.shape, bf16) for w in (wq, wp, w1, w2)],
            pltpu.VMEM((4 * rows, wide), bf16),
            pltpu.VMEM((2, heads, 32, WALL), f32),
            pltpu.VMEM((4, rows, width), bf16),
            pltpu.VMEM((2, 4 * rows, QB), f32),
            pltpu.VMEM((2, 4 * rows, QB), bf16),
            pltpu.SemaphoreType.DMA((9,)),
            pltpu.SemaphoreType.DMA((8,)),
            *comm_scratch(copies),
        ],
        compiler_params=params(0),
        cost_estimate=pl.CostEstimate(flops=80 << 30, bytes_accessed=24 << 20, transcendentals=0),
    )(flags, x, mask_pad, lab, table, pack, wq, wp, w1, w2)


AXES = ("dp", "section", "tensor")
ORDER = (0, 2, 1, 3)


def local(
    inputs,
    time_emb,
    lengths,
    key_mask,
    rel_index,
    w_qkv,
    w_time,
    w_proj,
    w_fc1,
    w_fc2,
    rel_table,
    norm_gains,
    norm_biases,
    cotangent,
):
    bf16, f32 = jnp.bfloat16, jnp.float32
    _, rows, width = inputs.shape
    seq_len = key_mask.shape[1]
    heads, buckets = rel_table.shape[1:]
    local_width = w_proj.shape[2]
    scale = 1.0 / math.sqrt(HD)
    ndp = lax.axis_size("dp")
    d = lax.axis_index("dp")
    c = lax.axis_index("section")
    z = lax.axis_index("tensor")
    pair = z // 2
    home = c == pair
    first = c == 0
    t = z % 2 + 2 * c

    def move(x, to, name="move"):
        pairs = []
        for dd in range(ndp):
            for cc in range(2):
                for zz in range(4):
                    dst = to(dd, cc, zz)
                    if dst is not None:
                        pairs.append(((dd * 2 + cc) * 4 + zz, (dst[0] * 2 + dst[1]) * 4 + dst[2]))
        with jax.named_scope(name):
            return lax.ppermute(x, AXES, pairs)

    def partner(x):
        return move(x, lambda dd, cc, zz: (dd, cc, zz ^ 1), "partner")

    def sibling(x):
        return move(x, lambda dd, cc, zz: (dd, 1 - cc, zz), "sibling")

    def across(x):
        return move(x, lambda dd, cc, zz: (dd, cc, zz ^ 2), "across")

    def dp_scatter(x, bits):
        n = x.shape[1]
        left = sorted(bits, reverse=True)
        v = x.reshape((2,) * len(left) + (-1, n))
        for b in bits:
            axis = left.index(b)
            left.remove(b)
            mine = (d >> b) & 1
            send = lax.dynamic_index_in_dim(v, 1 - mine, axis, keepdims=False)
            keep = lax.dynamic_index_in_dim(v, mine, axis, keepdims=False)
            got = move(send, lambda dd, cc, zz, b=b: (dd ^ (1 << b), cc, zz), "g_dp")
            v = keep.astype(f32) + got.astype(f32)
            if left:
                v = v.astype(bf16)
        return v

    def by_bits(w):
        return w.reshape(2, 2, -1, w.shape[-1])

    table = jnp.pad(rel_table[0], ((0, 0), (0, 4096 - buckets))).reshape(heads, 64, 64)
    time_all = jnp.einsum("id,dcn->icn", time_emb, w_time[0], preferred_element_type=f32)
    gap = jnp.zeros((2, local_width), f32)
    time_rows = jnp.concatenate([time_all[:, 0], gap, time_all[:, 1], gap], axis=1)
    small_pack = jnp.concatenate([norm_gains[0], norm_biases[0], time_rows, jnp.zeros((2, width), f32)], axis=0)
    own = [by_bits(w) for w in (jnp.concatenate([w_qkv[0, :, j] for j in range(3)], axis=1), w_proj[0], w_fc1[0], w_fc2[0])]
    label_lanes = label_row(rel_index)
    out_label = rel_index[1, seq_len - 1, seq_len - 1].reshape(1)

    length = lax.dynamic_index_in_dim(lengths, pair, 0, keepdims=False)
    small = (length < seq_len).astype(jnp.int32)
    scalars = jnp.stack([z % 2, c] + [jnp.int32(j) for j in ORDER])
    flags = jnp.concatenate([small.reshape(1), out_label])
    mask = lax.dynamic_index_in_dim(key_mask, pair, 0, keepdims=False).reshape(4, rows)
    mask = jnp.concatenate([lax.dynamic_index_in_dim(mask, t ^ j, 0, keepdims=False) for j in ORDER])
    lane = jnp.arange(128 - HD)[None, :]
    mask_pad = jnp.where((lane == 0) & (mask[:, None] == 0), -1e30, 0.0).astype(bf16)

    def gather_rows(x):
        far = partner(x)
        near = sibling(x)
        return jnp.concatenate([x, near, far, sibling(far)], axis=0)

    def scatter_rows(far, near):
        a = sibling(far[rows:].astype(bf16))
        rz = partner((far[:rows] + a.astype(f32)).astype(bf16))
        rs = sibling(near[rows:].astype(bf16))
        return near[:rows] + rs.astype(f32) + rz.astype(f32)

    def times_t(x, w):
        return lax.dot_general(x, w, (((1,), (1,)), ((), ())), preferred_element_type=f32)

    def grad_of(x, y):
        return lax.dot_general(x, y, (((0,), (0,)), ((), ())), preferred_element_type=f32).astype(bf16)

    half = 2 * rows

    def reduced(x):
        with jax.named_scope("g_sum"):
            return lax.psum_scatter(x, "dp", scatter_dimension=0, tiled=True)

    def reduced_late(x):
        if ndp & (ndp - 1):
            return reduced(x)
        bits = list(range(ndp.bit_length() - 1))
        cut = 4 * 128
        return jnp.concatenate(
            [dp_scatter(x[:, :cut], bits), dp_scatter(x[:, cut:], bits[::-1])], axis=1
        ).astype(bf16)

    def column_sums(dqkv):
        sums = jnp.sum(dqkv.astype(f32), axis=0)
        return jnp.concatenate([sums[:local_width], sums[2 * local_width :]])

    def tie(*values):
        return lax.optimization_barrier(values)

    def by_core(pairs):
        return jnp.where(first, pairs[0], pairs[1])

    def near_of(x, layer):
        return move(x, lambda dd, cc, zz: (dd, layer, zz) if cc == zz // 2 and cc != layer else None, "d_near")

    def far_of(x, layer):
        return move(x, lambda dd, cc, zz: (dd, layer, zz ^ 2) if cc != zz // 2 else None, "d_far")

    live = ((t * rows + jnp.arange(rows)) < length).astype(f32)[:, None]
    res = start_chain(flags, inputs, mask_pad, label_lanes, table, small_pack, *own, ORDER, scale)
    x0, packs, lse0, o0, n1_0, qkv0 = res[:6]
    walls, weights0 = res[6:8], res[8:]
    n1_0 = n1_0.reshape(seq_len, width)

    def whole(w):
        return w.reshape(width, w.shape[-1])

    gains = [packs[l, 0:2] for l in range(2)]
    shifts = [packs[l, 2:4] for l in range(2)]
    ln_mid = jnp.stack([gains[0][1], shifts[0][1], gains[1][0], shifts[1][0]])
    wq0, wp0 = whole(weights0[0]), whole(weights0[1])
    hid0, act0, dy1, n2_0, u0, g0, n1_1, weights0, weights1 = mid_chain(
        x0, o0, ln_mid, live, cotangent, wp0, weights0[2], weights0[3], own
    )
    w10, w20 = whole(weights0[0]), whole(weights0[1])
    wq1, wp1 = whole(weights1[0]), whole(weights1[1])
    term1 = lax.dynamic_index_in_dim(packs[1], 4 + pair, 0, keepdims=False)[: 3 * local_width]
    qkv1 = (jnp.dot(n1_1, wq1, preferred_element_type=f32) + term1).astype(bf16)
    qkv1, dm1 = tie(qkv1, dy1.astype(bf16))
    dm_far, dm_near = partner(dm1), sibling(dm1)
    o1, lse1 = attn_fwd(qkv1, mask_pad, walls[1], scalars, ORDER, scale)
    o1, dm1, dm_far, dm_near = tie(o1, dm1, dm_far, dm_near)
    dm1 = jnp.concatenate([dm1, dm_near, dm_far, sibling(dm_far)], axis=0)

    ln_turn = jnp.stack([gains[1][1], shifts[1][1]])
    dh1, norms1, y1, hid1, do1, da1, gfc1 = turn_chain(act0, o1, dy1, ln_turn, dm1, wp1, weights1[2], weights1[3])
    sum_fc1 = reduced(gfc1)
    do1, y1, a0 = tie(do1, y1, act0)
    act1 = (hid1 + scatter_rows(y1[half:], y1[:half])).astype(bf16)
    got_acts = [near_of(a0, 0) + near_of(act1, 1), far_of(a0, 0) + far_of(act1, 1)]
    dqkv1, dwall1 = attn_bwd(qkv1, do1, o1, lse1, mask_pad, walls[1], scalars, ORDER, scale)
    dqkv1, got_acts = tie(dqkv1, got_acts)
    ln_back = jnp.stack([gains[1][0], gains[0][1]])
    gin1, dh0, norms10, do0, da0, gfc0 = back_chain(
        act0, dh1, hid0, ln_back, dqkv1, wq1, wp0, w10, w20, u0, g0, n2_0
    )
    sum_fc0 = reduced(gfc0)
    sum_qp1 = reduced(jnp.concatenate([grad_of(n1_1, dqkv1), grad_of(da1, o1)], axis=1))
    rel1 = bias_grads(flags, label_lanes, dwall1)
    sums1 = column_sums(dqkv1)
    do0, sum_qp1, rel1, sums1 = tie(do0, sum_qp1, rel1, sums1)
    g1 = gin1.astype(bf16)
    w1 = jnp.concatenate([sum_qp1, sum_fc1], axis=1)
    do0, g1, w1 = tie(do0, g1, w1)
    got1 = [near_of(g1, 1), far_of(g1, 1), near_of(w1, 1), far_of(w1, 1)]
    dqkv0, dwall0 = attn_bwd(qkv0, do0, o0, lse0, mask_pad, walls[0], scalars, ORDER, scale)
    dqkv0, got1 = tie(dqkv0, got1)
    dn1 = scatter_rows(times_t(dqkv0[half:], wq0), times_t(dqkv0[:half], wq0))
    grad_qp0 = jnp.concatenate([grad_of(n1_0, dqkv0), grad_of(da0, o0)], axis=1)
    sum_qp0 = reduced_late(grad_qp0)
    rel0 = bias_grads(flags, label_lanes, dwall0)
    sums0 = column_sums(dqkv0)
    dn1, grad_qp0, rel0, sums0 = tie(dn1, grad_qp0, rel0, sums0)
    dx, dgain, dshift = norm_back(x0.astype(f32), dn1, gains[0][0])
    gin0 = dh0 + dx
    early0, early1, late1 = norms10[2:], norms1, norms10[:2]
    late0 = jnp.concatenate([dgain, dshift], axis=0)
    sums_w0, sums_w1 = (sum_qp0, sum_fc0), (sum_qp1, sum_fc1)

    def by_image(same, other):
        return jnp.stack([jnp.where(pair == 0, same, other), jnp.where(pair == 0, other, same)])[None]

    acts = by_image(jnp.where(home, by_core((act0, act1)), got_acts[0]), got_acts[1])
    low0 = gin0.astype(bf16)
    same = jnp.where(home, by_core((gin0, gin1)), (near_of(low0, 0) + got1[0]).astype(f32))
    input_grads = by_image(same, (far_of(low0, 0) + got1[1]).astype(f32))

    def total(mine, parts):
        out = jnp.where(home, mine, jnp.zeros_like(mine)).astype(f32)
        for part in parts:
            out = out + part.astype(f32)
        return out

    n_qp = 4 * local_width
    hidden_units = w_fc1.shape[2]
    grad_fc = total(
        by_core((sums_w0[1], sums_w1[1])),
        (near_of(sums_w0[1], 0), far_of(sums_w0[1], 0), got1[2][:, n_qp:], got1[3][:, n_qp:]),
    )
    grad_qp = total(
        by_core((sums_w0[0], sums_w1[0])),
        (near_of(sums_w0[0], 0), far_of(sums_w0[0], 0), got1[2][:, :n_qp], got1[3][:, :n_qp]),
    )

    here = (jnp.arange(2 * ndp) == 2 * d + pair).astype(f32)[:, None]
    pack = jnp.concatenate(
        [
            rel0.reshape(-1, 128),
            rel1.reshape(-1, 128),
            (here * jnp.concatenate([sums0, sums1])[None]).reshape(-1, 128),
            jnp.stack([early0, early1, late1]).reshape(-1, 128),
        ],
        axis=0,
    )
    late = late0.reshape(-1, 128)

    def summed(x):
        bit = 1
        while bit < ndp:
            x = x + move(x, lambda dd, cc, zz, b=bit: (dd ^ b, cc, zz), "pack_dp")
            bit *= 2
        return x + across(x)

    pack = summed(pack)
    n_rel = heads * 32
    n_sum = 2 * ndp * 4 * local_width // 128
    rel_both = (pack[:n_rel], pack[n_rel : 2 * n_rel])
    sums_all = pack[2 * n_rel : 2 * n_rel + n_sum].reshape(2 * ndp, 2, 2 * local_width)
    norms = pack[2 * n_rel + n_sum :]
    norms = norms + partner(norms)
    norms = norms + sibling(norms)
    late = summed(late)
    late = late + partner(late)
    late = late + sibling(late)
    early0, early1, late1 = norms.reshape(3, 2, width)
    late0 = late.reshape(2, width)
    norms_mine = jnp.stack([by_core((late0, late1)), by_core((early0, early1))], axis=1)
    cols = width // (4 * ndp)
    norms_mine = lax.dynamic_slice_in_dim(norms_mine, (d * 4 + z) * cols, cols, 2)

    def to_home_core(both):
        return move(
            jnp.where(first, both[1], both[0]),
            lambda dd, cc, zz: (dd, 1 - cc, zz) if cc == zz // 2 else None,
            "pack_near",
        )

    rel_mine = jnp.where(home, by_core(rel_both), to_home_core(rel_both))
    rel_grad = rel_mine.reshape(heads, 4096)[:, :buckets]
    sums_both = (sums_all[:, 0], sums_all[:, 1])
    sums_mine = jnp.where(home, by_core(sums_both), to_home_core(sums_both))
    emb_all = lax.all_gather(time_emb, "dp", axis=0, tiled=True)
    emb_mine = lax.dynamic_slice_in_dim(emb_all, d * (width // ndp), width // ndp, 1).astype(f32)
    grad_time = lax.dot_general(
        emb_mine, sums_mine, (((0,), (0,)), ((), ())), precision=lax.Precision.HIGHEST, preferred_element_type=f32
    ).reshape(width // ndp, 2, local_width)
    return (
        acts,
        input_grads,
        grad_qp[:, : 3 * local_width].reshape(width // ndp, 3, local_width)[None],
        grad_time[None],
        grad_qp[:, 3 * local_width :][None],
        grad_fc[:, :hidden_units][None],
        grad_fc[:, hidden_units:][None],
        rel_grad[None],
        norms_mine[0][None],
        norms_mine[1][None],
    )


def solution(mesh):
    return jax.shard_map(
        local,
        mesh=mesh,
        in_specs=(
            P("dp", "tensor", None),
            P("dp", None),
            P("dp"),
            P("dp", None),
            P(),
            P("section", None, None, "tensor"),
            P("section", None, None, "tensor"),
            P("section", None, "tensor"),
            P("section", None, "tensor"),
            P("section", None, "tensor"),
            P("section", "tensor", None),
            P("section", None, None),
            P("section", None, None),
            P("dp", "tensor", None),
        ),
        out_specs=(
            P("section", "dp", "tensor", None),
            P("section", "dp", "tensor", None),
            P("section", "dp", None, "tensor"),
            P("section", "dp", None, "tensor"),
            P("section", "dp", "tensor"),
            P("section", "dp", "tensor"),
            P("section", "dp", "tensor"),
            P("section", "tensor", None),
            P("section", None, ("dp", "tensor")),
            P("section", None, ("dp", "tensor")),
        ),
        check_vma=False,
    )
```

```python
import functools
import math

import jax
import jax.numpy as jnp
from jax import lax
from jax.experimental import pallas as pl
from jax.experimental.pallas import tpu as pltpu
from jax.sharding import PartitionSpec as P

LOG2E = 1.4426950408889634
HIGHEST = lax.Precision.HIGHEST
PLANE = 7 * 256
WALL = 8 * PLANE


def _labels_hi_lo(lab):
    hi = lax.shift_right_logical(lab, 6)
    lo = jnp.bitwise_and(lab, 63)
    iota = lax.broadcasted_iota(jnp.int32, (64, lab.shape[1]), 0)
    return iota == hi, jnp.where(iota == lo, 1.0, 0.0)


def build_wall(small, out_lab, lab, hi_mask, lo_hot, table, wall_ref):
    rows = lax.dot_general(table, lo_hot, (((1,), (0,)), ((), ())), precision=HIGHEST, preferred_element_type=jnp.float32)
    flat = jnp.sum(jnp.where(hi_mask, rows, 0.0), axis=0, keepdims=True) * LOG2E
    outside = jnp.sum(jnp.where(lab == out_lab, flat, 0.0), axis=1, keepdims=True)
    wide = jnp.broadcast_to(flat, (32, 4096))
    wide = pltpu.roll(wide, 4096 - 31, 1, stride=1, stride_axis=0)
    lane = lax.broadcasted_iota(jnp.int32, (32, 128), 1)
    tight = []
    for g in range(16):
        a = wide[:, 256 * g : 256 * g + 128]
        b = wide[:, 256 * g + 128 : 256 * g + 256]
        piece = jnp.where(lane < 32, a, pltpu.roll(a, 96, 1))
        other = jnp.where(lane < 96, pltpu.roll(b, 64, 1), pltpu.roll(b, 32, 1))
        tight.append(jnp.where(lane < 64, piece, other))
    w0 = jnp.concatenate(tight, axis=1)
    lane16 = lane[:16]
    tight16 = []
    for g in range(8):
        lo_v = w0[:16, 256 * g : 256 * g + 128]
        hi_v = w0[:16, 256 * g + 128 : 256 * g + 256]
        acc = lo_v
        for k in range(1, 4):
            acc = jnp.where(lane16 >= 16 * k, pltpu.roll(lo_v, 128 - 16 * k, 1), acc)
        for k in range(4):
            acc = jnp.where(lane16 >= 64 + 16 * k, pltpu.roll(hi_v, (64 - 16 * k) % 128, 1), acc)
        tight16.append(acc)
    w16 = jnp.concatenate(tight16, axis=1)
    beyond = jnp.broadcast_to(outside, (32, 768))
    tiny = small == 1
    for j in range(8):
        big = w0 if j == 7 else pltpu.roll(w0, 2048 - 32 * (7 - j), 1)
        inner = [pltpu.roll(w16, 1024 - 16 * (31 - 2 * j - k), 1)[:, :256] for k in range(2)]
        inner = jnp.concatenate(inner, axis=0)
        at = j * PLANE
        wall_ref[:, at : at + 768] = jnp.where(tiny, beyond, big[:, :768])
        wall_ref[:, at + 768 : at + 1024] = jnp.where(tiny, inner, big[:, 768:1024])
        wall_ref[:, at + 1024 : at + PLANE] = jnp.where(tiny, beyond, big[:, 1024:PLANE])


def bias_kernel(flags_ref, lab_ref, table_ref, wall_ref):
    lab = lab_ref[...]
    hi_mask, lo_hot = _labels_hi_lo(lab)
    build_wall(flags_ref[0], flags_ref[1], lab, hi_mask, lo_hot, table_ref[0], wall_ref.at[0])


def bias_tables(flags, lab, table):
    heads = table.shape[0]
    return pl.pallas_call(
        bias_kernel,
        grid=(heads,),
        in_specs=[
            pl.BlockSpec(memory_space=pltpu.SMEM),
            pl.BlockSpec((1, 4096), lambda h: (0, 0)),
            pl.BlockSpec((1, 64, 64), lambda h: (h, 0, 0)),
        ],
        out_specs=pl.BlockSpec((1, 32, WALL), lambda h: (h, 0, 0)),
        out_shape=jax.ShapeDtypeStruct((heads, 32, WALL), jnp.float32),
        compiler_params=pltpu.CompilerParams(vmem_limit_bytes=40 << 20),
    )(flags, lab, table)


def wall_grad(small, out_lab, lab, hi_mask, lo_hot, acc_ref):
    tiny = small == 1
    w0 = jnp.zeros((32, 2048), jnp.float32)
    w16 = jnp.zeros((16, 1024), jnp.float32)
    beyond = jnp.zeros((32, 768), jnp.float32)
    for j in range(8):
        at = j * PLANE
        piece = jnp.concatenate([acc_ref[:, at : at + PLANE], jnp.zeros((32, 256), jnp.float32)], axis=1)
        w0 = w0 + (piece if j == 7 else pltpu.roll(piece, 32 * (7 - j), 1))
        beyond = beyond + acc_ref[:, at + 1024 : at + PLANE]
        for k in range(2):
            inner = acc_ref[16 * k : 16 * k + 16, at + 768 : at + 1024]
            inner = jnp.concatenate([inner, jnp.zeros((16, 768), jnp.float32)], axis=1)
            w16 = w16 + pltpu.roll(inner, 16 * (31 - 2 * j - k), 1)
    w0 = jnp.where(tiny, 0.0, w0)
    w16 = jnp.where(tiny, w16, 0.0)
    outside = jnp.sum(jnp.sum(jnp.where(tiny, beyond, 0.0), axis=0, keepdims=True), axis=1, keepdims=True)
    lane = lax.broadcasted_iota(jnp.int32, (32, 128), 1)
    lane16 = lane[:16]
    wide = []
    for g in range(32):
        src = w0[:, 128 * (g // 2) : 128 * (g // 2) + 128]
        k = 2 * (g % 2)
        first = src if k == 0 else pltpu.roll(src, 128 - 32 * k, 1)
        second = pltpu.roll(src, (64 - 32 * (k + 1)) % 128, 1)
        piece = jnp.where(lane < 32, first, jnp.where((lane >= 64) & (lane < 96), second, 0.0))
        src16 = w16[:, 128 * (g // 4) : 128 * (g // 4) + 128]
        k = 2 * (g % 4)
        first = src16 if k == 0 else pltpu.roll(src16, 128 - 16 * k, 1)
        second = pltpu.roll(src16, (64 - 16 * (k + 1)) % 128, 1)
        piece16 = jnp.where(lane16 < 16, first, jnp.where((lane16 >= 64) & (lane16 < 80), second, 0.0))
        wide.append(piece + jnp.concatenate([piece16, jnp.zeros((16, 128), jnp.float32)], axis=0))
    wide = jnp.concatenate(wide, axis=1)
    back = 31 - lax.broadcasted_iota(jnp.int32, (32, 4096), 0)
    for k in range(5):
        wide = jnp.where(jnp.bitwise_and(back, 1 << k) > 0, pltpu.roll(wide, 1 << k, 1), wide)
    flat = jnp.sum(wide, axis=0, keepdims=True)
    flat = flat + jnp.where(lab == out_lab, outside, 0.0)
    spread = jnp.where(hi_mask, jnp.broadcast_to(flat, (64, 4096)), 0.0)
    return lax.dot_general(spread, lo_hot, (((1,), (1,)), ((), ())), precision=HIGHEST, preferred_element_type=jnp.float32)


def bias_grad_kernel(flags_ref, lab_ref, acc_ref, out_ref):
    lab = lab_ref[...]
    hi_mask, lo_hot = _labels_hi_lo(lab)
    out_ref[0] = wall_grad(flags_ref[0], flags_ref[1], lab, hi_mask, lo_hot, acc_ref.at[0])


def bias_grads(flags, lab, acc):
    heads = acc.shape[0]
    return pl.pallas_call(
        bias_grad_kernel,
        grid=(heads,),
        in_specs=[
            pl.BlockSpec(memory_space=pltpu.SMEM),
            pl.BlockSpec((1, 4096), lambda h: (0, 0)),
            pl.BlockSpec((1, 32, WALL), lambda h: (h, 0, 0)),
        ],
        out_specs=pl.BlockSpec((1, 64, 64), lambda h: (h, 0, 0)),
        out_shape=jax.ShapeDtypeStruct((heads, 64, 64), jnp.float32),
        compiler_params=pltpu.CompilerParams(vmem_limit_bytes=40 << 20),
    )(flags, lab, acc)


def label_row(rel_index):
    side = 32
    a = rel_index[0, 1023].reshape(side, side)
    b = rel_index[0, 0].reshape(side, side)
    c = rel_index[0, 992].reshape(side, side)
    d = rel_index[0, 31].reshape(side, side)
    top = jnp.concatenate([a, c[:, 1:]], axis=1)
    low = jnp.concatenate([d[1:], b[1:, 1:]], axis=1)
    grid = jnp.flip(jnp.concatenate([top, low], axis=0), (0, 1))
    return jnp.pad(grid, ((0, 1), (0, 1)), constant_values=4095).reshape(1, 4096)


NT = (((1,), (1,)), ((), ()))
TN = (((0,), (0,)), ((), ()))
NN = (((1,), (0,)), ((), ()))
HD = 72
QB = 256


def dot(a, b, dims):
    return lax.dot_general(a, b, dims, preferred_element_type=jnp.float32)


def head_lanes(x, at, extra=None):
    rows = x.shape[0]
    part = x[:, at : at + HD]
    if extra is None:
        pad = jnp.zeros((rows, 128 - HD), x.dtype)
    else:
        pad = extra
    return jnp.concatenate([part, pad], axis=1)


def quarter(r, c, rel):
    return lax.rem(r + rel % 2, 2) + 2 * lax.rem(c + rel // 2, 2)


def strip_start(q_quarter, jj, kq):
    return pl.multiple_of(PLANE * jj + 256 * (q_quarter - kq + 3), 256)


def attn_block(q_quarter, key_quarters, scale, q_ref, kv_ref, k_extra, wall_ref, lse_ref, s_scr, p_scr):
    heads = wall_ref.shape[0]
    width = heads * HD
    nstrip = kv_ref.shape[0] // 32
    lane = lax.broadcasted_iota(jnp.int32, (QB, 128 - HD), 1)
    q_extra = jnp.where(lane == 0, 1.0, 0.0).astype(jnp.bfloat16)
    outs = []
    for h in range(heads):
        kh = head_lanes(kv_ref, width + HD * h, k_extra)
        qh = head_lanes(q_ref, HD * h, q_extra)
        vh = head_lanes(kv_ref, 2 * width + HD * h)
        s_scr[h % 2] = dot(kh, qh, NT)
        top = None
        for st in range(nstrip):
            start = strip_start(q_quarter, st % 8, key_quarters[st // 8])
            s = s_scr[h % 2, 32 * st : 32 * st + 32] * (scale * LOG2E) + wall_ref[h, :, pl.ds(start, QB)]
            s_scr[h % 2, 32 * st : 32 * st + 32] = s
            top = s if top is None else jnp.maximum(top, s)
        row_max = jnp.max(top, axis=0, keepdims=True)
        total = None
        for st in range(nstrip):
            p = jnp.exp2(s_scr[h % 2, 32 * st : 32 * st + 32] - row_max)
            p_scr[h % 2, 32 * st : 32 * st + 32] = p.astype(jnp.bfloat16)
            total = p if total is None else total + p
        row_sum = jnp.sum(total, axis=0, keepdims=True)
        o_t = dot(vh, p_scr[h % 2], TN) * (1.0 / row_sum)
        lse_ref[h : h + 1, :] = row_max + jnp.log2(row_sum)
        outs.append(o_t.T[:, :HD].astype(jnp.bfloat16))
    return jnp.concatenate(outs, axis=1)


def attn_fwd_kernel(order, scale, sc_ref, q_ref, kv_ref, mask_ref, wall_ref, o_ref, lse_ref, s_scr, p_scr):
    r, c = sc_ref[0], sc_ref[1]
    qq = quarter(r, c, sc_ref[2 + pl.program_id(0)])
    keys = [quarter(r, c, j) for j in order]
    o_ref[...] = attn_block(
        qq, keys, scale, q_ref, kv_ref, mask_ref[...], wall_ref, lse_ref.at[0], s_scr, p_scr
    )


def attn_fwd(qkv, mask_pad, wall, scalars, order, scale):
    rows, wide = qkv.shape
    nq = rows // QB
    heads = wall.shape[0]
    width = heads * HD
    return pl.pallas_call(
        functools.partial(attn_fwd_kernel, order, scale),
        grid=(nq,),
        in_specs=[
            pl.BlockSpec(memory_space=pltpu.SMEM),
            pl.BlockSpec((QB, wide), lambda i: (i, 0)),
            pl.BlockSpec((rows, wide), lambda i: (0, 0)),
            pl.BlockSpec((rows, 128 - HD), lambda i: (0, 0)),
            pl.BlockSpec((heads, 32, WALL), lambda i: (0, 0, 0), pipeline_mode=pl.Buffered(1)),
        ],
        out_specs=[pl.BlockSpec((QB, width), lambda i: (i, 0)), pl.BlockSpec((1, heads, QB), lambda i: (i, 0, 0))],
        out_shape=[jax.ShapeDtypeStruct((rows, width), jnp.bfloat16), jax.ShapeDtypeStruct((nq, heads, QB), jnp.float32)],
        scratch_shapes=[pltpu.VMEM((2, rows, QB), jnp.float32), pltpu.VMEM((2, rows, QB), jnp.bfloat16)],
        compiler_params=pltpu.CompilerParams(vmem_limit_bytes=40 << 20),
        cost_estimate=pl.CostEstimate(flops=16 << 30, bytes_accessed=12 << 20, transcendentals=0),
    )(scalars, qkv, qkv, mask_pad, wall)


def attn_bwd_kernel(order, scale, sc_ref, q_ref, kv_ref, do_ref, o_ref, lse_ref, mask_ref, wall_ref,
                    dqkv_ref, acc_ref, p_scr, s_scr, dq_scr, dk_scr, dv_scr):
    step = pl.program_id(0)
    r, c = sc_ref[0], sc_ref[1]
    qq = quarter(r, c, sc_ref[2 + step])
    keys = [quarter(r, c, j) for j in order]
    heads = wall_ref.shape[0]
    width = heads * HD
    rows = kv_ref.shape[0]

    @pl.when(step == 0)
    def _():
        acc_ref[...] = jnp.zeros_like(acc_ref)
        dk_scr[...] = jnp.zeros_like(dk_scr)
        dv_scr[...] = jnp.zeros_like(dv_scr)

    k_extra = mask_ref[...]
    lane = lax.broadcasted_iota(jnp.int32, (QB, 128 - HD), 1)
    q_extra = jnp.where(lane == 0, 1.0, 0.0).astype(jnp.bfloat16)
    dqs = []
    for h in range(heads):
        kh = head_lanes(kv_ref, width + HD * h, k_extra)
        qh = head_lanes(q_ref, HD * h, q_extra)
        vh = head_lanes(kv_ref, 2 * width + HD * h)
        doh = head_lanes(do_ref, HD * h)
        oh = head_lanes(o_ref, HD * h)
        inner = jnp.sum((doh.astype(jnp.float32) * oh.astype(jnp.float32)).T, axis=0, keepdims=True)
        lse = lse_ref[0, h : h + 1, :]
        for kb in range(rows // 256):
            s_t = dot(kh[256 * kb : 256 * kb + 256], qh, NT)
            dp_t = dot(vh[256 * kb : 256 * kb + 256], doh, NT)
            for js in range(8):
                st = 8 * kb + js
                start = strip_start(qq, js, keys[kb])
                s = s_t[32 * js : 32 * js + 32] * (scale * LOG2E) + wall_ref[h, :, pl.ds(start, QB)]
                p = jnp.exp2(s - lse)
                ds = p * (dp_t[32 * js : 32 * js + 32] - inner)
                p_scr[h % 2, 32 * st : 32 * st + 32] = p.astype(jnp.bfloat16)
                s_scr[h % 2, 32 * st : 32 * st + 32] = ds.astype(jnp.bfloat16)
                acc_ref[h, :, pl.ds(start, QB)] += ds
        p_b, ds_b = p_scr[h % 2], s_scr[h % 2]
        dv_scr[h] += dot(p_b, doh, NN)
        dk_scr[h] += dot(ds_b, qh, NN)
        dq_t = dot(kh, ds_b, TN) * scale
        dqs.append(dq_t.T[:, :HD].astype(jnp.bfloat16))
    dq_scr[pl.ds(pl.multiple_of(step * QB, QB), QB)] = jnp.concatenate(dqs, axis=1)

    @pl.when(step == pl.num_programs(0) - 1)
    def _():
        parts = [dq_scr[...]]
        parts += [(dk_scr[h, :, :HD] * scale).astype(jnp.bfloat16) for h in range(heads)]
        parts += [dv_scr[h, :, :HD].astype(jnp.bfloat16) for h in range(heads)]
        dqkv_ref[...] = jnp.concatenate(parts, axis=1)


def attn_bwd(qkv, do, o, lse, mask_pad, wall, scalars, order, scale):
    rows, wide = qkv.shape
    nq = rows // QB
    heads = wall.shape[0]
    width = heads * HD
    row_spec = pl.BlockSpec((QB, width), lambda i: (i, 0))
    return pl.pallas_call(
        functools.partial(attn_bwd_kernel, order, scale),
        grid=(nq,),
        in_specs=[
            pl.BlockSpec(memory_space=pltpu.SMEM),
            pl.BlockSpec((QB, wide), lambda i: (i, 0)),
            pl.BlockSpec((rows, wide), lambda i: (0, 0)),
            row_spec,
            row_spec,
            pl.BlockSpec((1, heads, QB), lambda i: (i, 0, 0)),
            pl.BlockSpec((rows, 128 - HD), lambda i: (0, 0)),
            pl.BlockSpec((heads, 32, WALL), lambda i: (0, 0, 0), pipeline_mode=pl.Buffered(1)),
        ],
        out_specs=[pl.BlockSpec((rows, wide), lambda i: (0, 0)), pl.BlockSpec((heads, 32, WALL), lambda i: (0, 0, 0))],
        out_shape=[jax.ShapeDtypeStruct((rows, wide), jnp.bfloat16), jax.ShapeDtypeStruct((heads, 32, WALL), jnp.float32)],
        scratch_shapes=[
            pltpu.VMEM((2, rows, QB), jnp.bfloat16),
            pltpu.VMEM((2, rows, QB), jnp.bfloat16),
            pltpu.VMEM((rows, width), jnp.bfloat16),
            pltpu.VMEM((heads, rows, 128), jnp.float32),
            pltpu.VMEM((heads, rows, 128), jnp.float32),
        ],
        compiler_params=pltpu.CompilerParams(vmem_limit_bytes=48 << 20),
        cost_estimate=pl.CostEstimate(flops=24 << 30, bytes_accessed=20 << 20, transcendentals=0),
    )(scalars, qkv, qkv, do, o, lse, mask_pad, wall)


EPSILON = 1e-05
NCH = 2
GELU_C = math.sqrt(2.0 / math.pi)


def normed(x):
    center = x - jnp.mean(x, axis=-1, keepdims=True)
    spread = jnp.mean(center * center, axis=-1, keepdims=True)
    r = lax.rsqrt(spread + EPSILON)
    return center * r, r


def norm_back(x, dy, gain):
    xhat, r = normed(x)
    dxhat = dy * gain
    dx = r * (
        dxhat
        - jnp.mean(dxhat, axis=-1, keepdims=True)
        - xhat * jnp.mean(dxhat * xhat, axis=-1, keepdims=True)
    )
    return dx, jnp.sum(dy * xhat, axis=0, keepdims=True), jnp.sum(dy, axis=0, keepdims=True)


def gelu_both(u):
    th = jnp.tanh(GELU_C * (u + 0.044715 * u * u * u))
    half = 0.5 * (1.0 + th)
    slope = half + 0.5 * u * (1.0 - th * th) * GELU_C * (1.0 + 3 * 0.044715 * u * u)
    return u * half, slope


class Links:
    def __init__(self, send_sem, recv_sem, bits=0):
        z, c = lax.axis_index("tensor"), lax.axis_index("section")
        self.z, self.c = z, c
        self.pair = z // 2
        self.r = lax.rem(z, 2)
        self.home = c == self.pair
        across = z + 2 - 4 * self.pair
        self.ids = {
            PARTNER: {"tensor": z + 1 - 2 * self.r},
            SIBLING: {"section": 1 - c},
            FAR: {"tensor": across, "section": self.pair},
            HOME: {"section": self.pair},
        }
        self.greet = [self.ids[PARTNER], self.ids[SIBLING]]
        self.dp_bit = []
        if bits:
            d = lax.axis_index("dp")
            for b in range(bits):
                bit = lax.rem(d // (1 << b), 2)
                self.dp_bit.append(bit)
                self.ids["dp", b] = {"dp": d + (1 - 2 * bit) * (1 << b)}
                self.greet.append(self.ids["dp", b])
            self.greet += [{"tensor": across}, {"tensor": across, "section": 1 - c}]
        self.ids[ACROSS] = {"tensor": across}
        for layer in range(2):
            self.ids["return", layer] = {"tensor": across, "section": layer}
        self.send_sem, self.recv_sem = send_sem, recv_sem
        self.used = 0
        self.started = []

    def enter(self):
        barrier = pltpu.get_barrier_semaphore()
        for where in self.greet:
            pl.semaphore_signal(barrier, inc=1, device_id=where, device_id_type=pl.DeviceIdType.MESH)
        pl.semaphore_wait(barrier, len(self.greet))

    def make(self, src, dst, to, cond=None, track=True):
        k = self.used
        self.used += 1
        copy = pltpu.make_async_remote_copy(
            src_ref=src,
            dst_ref=dst,
            send_sem=self.send_sem.at[k],
            recv_sem=self.recv_sem.at[k],
            device_id=self.ids[to],
            device_id_type=pl.DeviceIdType.MESH,
        )
        if track:
            self.started.append((copy, cond))
        return copy

    def send(self, src, dst, to, cond=None, track=True):
        copy = self.make(src, dst, to, cond, track)
        when(cond, copy.start)
        return copy

    def leave(self):
        for copy, cond in self.started:
            when(cond, copy.wait_send)


def when(cond, do):
    if cond is None:
        do()
    else:
        pl.when(cond)(lambda: do())


PARTNER, SIBLING, FAR, HOME, ACROSS = "partner", "sibling", "far", "home", "across"


class Spread:
    COPIES = 2

    def __init__(self, links, layer, src, out, sem):
        self.links, self.layer, self.src, self.out, self.sem = links, layer, src, out, sem

    def start(self):
        links = self.links
        mine = links.c == self.layer
        keeps = links.pair == self.layer
        self.local = pltpu.make_async_copy(self.src, self.out, self.sem)
        when(mine & keeps, self.local.start)
        self.near = links.send(self.src, self.out, HOME, mine & jnp.logical_not(keeps))
        self.far = links.send(self.src, self.out, FAR, mine)

    def done(self):
        links = self.links
        keeps = links.pair == self.layer
        when(links.home & keeps, self.local.wait)
        when(links.home & jnp.logical_not(keeps), self.near.wait_recv)
        when(jnp.logical_not(links.home), self.far.wait_recv)


def bits_region(links, gathered, cols=None):
    index = []
    for b in reversed(range(len(links.dp_bit))):
        index.append(pl.ds(0, 2) if b in gathered else links.dp_bit[b])
    return tuple(index) + (() if cols is None else (slice(None), cols))


class Deliver:
    COPIES = 2

    def __init__(self, links, layer, src, out, sem=None):
        self.links, self.layer, self.src, self.out, self.sem = links, layer, src, out, sem

    def start(self):
        links = self.links
        mine = links.c == self.layer
        keeps = links.pair == self.layer
        if self.sem is not None:
            self.local = pltpu.make_async_copy(self.src, self.out, self.sem)
            when(mine & keeps, self.local.start)
        at = bits_region(links, ())
        self.far = links.send(self.src.at[at], self.out.at[at], FAR, mine)
        self.near = links.send(self.src, self.out, HOME, mine & jnp.logical_not(keeps))

    def done(self):
        links = self.links
        keeps = links.pair == self.layer
        if self.sem is not None:
            when(links.home & keeps, self.local.wait)
        when(links.home & jnp.logical_not(keeps), self.near.wait_recv)
        when(jnp.logical_not(links.home), self.far.wait_recv)


class Exchange:
    def __init__(self, links, buf):
        self.links, self.buf = links, buf
        columns = buf.shape[-1]
        cut = columns // 256 * 128
        order = list(range(len(links.dp_bit)))
        self.halves = [(pl.ds(0, cut), order), (pl.ds(cut, columns - cut), order[::-1])]
        self.away = jnp.logical_not(links.home)
        self.last = None

    @staticmethod
    def copies(bits):
        return 2 * bits

    def step(self, s):
        self.done()
        self.last = []
        for cols, order in self.halves:
            at = bits_region(self.links, order[:s], cols)
            self.last.append(self.links.send(self.buf.at[at], self.buf.at[at], ("dp", order[s]), self.away))

    def done(self):
        for copy in self.last or ():
            when(self.away, copy.wait_recv)


class Part:
    def __init__(self, links, layer, own, got, dst, sem):
        at = bits_region(links, ())
        keeps = links.pair == layer
        self.ways = (
            (links.home & keeps, pltpu.make_async_copy(own, dst, sem)),
            (links.home & jnp.logical_not(keeps), pltpu.make_async_copy(got, dst, sem)),
            (jnp.logical_not(links.home), pltpu.make_async_copy(got.at[at], dst.at[at], sem)),
        )

    def start(self):
        for cond, copy in self.ways:
            when(cond, copy.start)
        return self

    def wait(self):
        for cond, copy in self.ways:
            when(cond, copy.wait)


def chunk(i, rows):
    return pl.ds(i * (rows // NCH), rows // NCH)


class Scatter:
    COPIES = 3 * NCH

    def __init__(self, links, low, wide):
        self.links, self.low, self.wide = links, low, wide
        self.rows = low.shape[1]
        self.copies = {}

    def far(self, i, p2, p3):
        at = chunk(i, self.rows)
        self.low[0, at] = p3.astype(jnp.bfloat16)
        self.copies["a", i] = self.links.send(self.low.at[0, at], self.low.at[3, at], SIBLING)
        self.wide[0, at] = p2

    def middle(self, i):
        at = chunk(i, self.rows)
        self.copies["a", i].wait_recv()
        self.low[1, at] = (self.wide[0, at] + self.low[3, at].astype(jnp.float32)).astype(jnp.bfloat16)
        self.copies["z", i] = self.links.send(self.low.at[1, at], self.low.at[4, at], PARTNER)

    def near(self, i, p0, p1):
        at = chunk(i, self.rows)
        self.low[2, at] = p1.astype(jnp.bfloat16)
        self.copies["b", i] = self.links.send(self.low.at[2, at], self.low.at[5, at], SIBLING)
        self.wide[1, at] = p0

    def release(self):
        for copy in self.copies.values():
            copy.wait_send()
        self.links.started = [s for s in self.links.started if all(s[0] is not c for c in self.copies.values())]
        self.copies = {}

    def done(self, i):
        at = chunk(i, self.rows)
        self.copies["b", i].wait_recv()
        self.copies["z", i].wait_recv()
        return self.wide[1, at] + self.low[5, at].astype(jnp.float32) + self.low[4, at].astype(jnp.float32)


class Gather:
    COPIES = 3 * NCH

    def __init__(self, links, buf):
        self.links, self.buf = links, buf
        self.rows = buf.shape[1]
        self.copies = {}

    def send(self, i, x):
        at = chunk(i, self.rows)
        self.buf[0, at] = x
        self.copies["z", i] = self.links.send(self.buf.at[0, at], self.buf.at[2, at], PARTNER)
        self.copies["s", i] = self.links.send(self.buf.at[0, at], self.buf.at[1, at], SIBLING)

    def forward(self, i):
        at = chunk(i, self.rows)
        self.copies["z", i].wait_recv()
        self.copies["f", i] = self.links.send(self.buf.at[2, at], self.buf.at[3, at], SIBLING)

    def done(self, i):
        self.copies["s", i].wait_recv()
        self.copies["f", i].wait_recv()
        at = chunk(i, self.rows)
        n = self.rows // NCH
        return jnp.concatenate([self.buf[b, at] for b in range(4)], axis=0)


class DpReduce:
    COPIES = 4

    def __init__(self, links, buf, land0, land1, sent):
        self.links, self.buf, self.land0, self.land1, self.sent = links, buf, land0, land1, sent
        columns = buf.shape[-1]
        cut = columns // 256 * 128
        self.cols = (pl.ds(0, cut), pl.ds(cut, columns - cut))
        self.orders = ((0, 1), (1, 0))
        self.mine = links.dp_bit
        self.other = [1 - bit for bit in links.dp_bit]
        self.first, self.second = [], []
        for (b0, b1), h, cols in zip(self.orders, range(2), self.cols):
            at = self.place(h, self.other[b0], pl.ds(0, 2))
            self.first.append(links.make(buf.at[at + (slice(None), cols)], land0.at[:, :, cols], ("dp", b0)))
            self.second.append(links.make(sent.at[0, :, cols], land1.at[0, :, cols], ("dp", b1)))

    @staticmethod
    def scratch(n, columns):
        return [pltpu.VMEM((k, n, columns), jnp.bfloat16) for k in (2, 1, 1)]

    def place(self, h, first, second):
        return (second, first) if self.orders[h][0] == 0 else (first, second)

    def start(self):
        for copy in self.first:
            copy.start()

    def middle(self):
        for h, cols in enumerate(self.cols):
            b0, b1 = self.orders[h]
            self.first[h].wait_recv()
            sums = []
            for second in (self.other[b1], self.mine[b1]):
                own = self.buf[self.place(h, self.mine[b0], second) + (slice(None), cols)]
                sums.append(own.astype(jnp.float32) + self.land0[second, :, cols].astype(jnp.float32))
            self.sent[0, :, cols] = sums[0].astype(jnp.bfloat16)
            self.buf[self.place(h, self.mine[b0], self.mine[b1]) + (slice(None), cols)] = sums[1].astype(jnp.bfloat16)
            self.second[h].start()

    def done(self, out):
        for h, cols in enumerate(self.cols):
            self.second[h].wait_recv()
            b0, b1 = self.orders[h]
            own = self.buf[self.place(h, self.mine[b0], self.mine[b1]) + (slice(None), cols)]
            out[:, cols] = (own.astype(jnp.float32) + self.land1[0, :, cols].astype(jnp.float32)).astype(out.dtype)


class Return:
    COPIES = 2

    def __init__(self, links, layer, src, near, far):
        self.links, self.layer = links, layer
        self.home, self.away = links.home, jnp.logical_not(links.home)
        self.here = links.c == layer
        self.near_cond = self.home & jnp.logical_not(self.here)
        self.near = links.make(src, near, SIBLING, self.near_cond)
        self.far = links.make(src, far, ("return", layer), self.away)

    def start(self):
        when(self.near_cond, self.near.start)
        when(self.away, self.far.start)

    def done(self):
        when(self.here & self.away, self.near.wait_recv)
        when(self.here, self.far.wait_recv)


def start_load(src, dst, sem):
    copy = pltpu.make_async_copy(src, dst, sem)
    copy.start()
    return copy


def block_rows(ref, b, i, rows):
    n = rows // NCH
    return ref[pl.ds(b * rows + i * n, n)]


def put_rows(ref, value, i, rows):
    n = rows // NCH
    for b in range(4):
        ref[pl.ds(b * rows + i * n, n)] = value[b * n : (b + 1) * n]


def weight_grad(out, col, x, y):
    width = x.shape[1]
    step = 384
    for k in range(0, width, step):
        out[k : k + step, col : col + y.shape[1]] = dot(x[:, k : k + step], y, TN).astype(out.dtype)


def flat(ref):
    return ref[...].reshape(-1, ref.shape[-1])


def scatter_product(scatter, i, lhs, weight, rows):
    p = dot(jnp.concatenate([lhs(2), lhs(3)], axis=0), weight, NT)
    n = rows // NCH
    scatter.far(i, p[:n], p[n:])
    p = dot(jnp.concatenate([lhs(0), lhs(1)], axis=0), weight, NT)
    scatter.near(i, p[:n], p[n:])


def slab_grad(out, col, x, y):
    n = out.shape[2]
    width = x.shape[1]
    step = 384
    for k in range(0, width, step):
        res = dot(x[:, k : k + step], y, TN).astype(out.dtype)
        at = k
        while at < k + step:
            slab = at // n
            stop = min(k + step, (slab + 1) * n)
            out[slab // 2, slab % 2, at - slab * n : stop - slab * n, col : col + y.shape[1]] = res[at - k : stop - k]
            at = stop


def block_quarter(links, i):
    return lax.rem(links.r + i // 2, 2) + 2 * lax.rem(links.c + lax.rem(i, 2), 2)


def mid_kernel(order, scale, bits, x_ref, o_ref, ln_ref, cot_ref, live_ref, term_ref, mask_ref,
               wp_hbm, got1_hbm, got2_hbm, wall_hbm, own_q, own_p, own_1, own_2,
               hid_ref, act_ref, dy_ref, o1_ref, lse_ref,
               n2_hbm, u_hbm, g_hbm, n1_hbm, qkv_hbm, dm_hbm, w1_out, w2_out, next_q, next_p, next_1, next_2,
               wp, w1, w2, got_q, got_p, wall, u_buf, g_buf, qkv, gat1, gat2, gat3, low, wide, s_scr, p_scr,
               load_sem, store_sem, send_sem, recv_sem):
    rows, width = x_ref.shape
    n = rows // NCH
    links = Links(send_sem, recv_sem, bits)
    load_p = start_load(wp_hbm, wp, load_sem.at[0])
    load_1 = Part(links, 0, own_1, got1_hbm, w1, load_sem.at[1]).start()
    load_2 = Part(links, 0, own_2, got2_hbm, w2, load_sem.at[2]).start()
    load_w = start_load(wall_hbm, wall, load_sem.at[3])
    links.enter()
    ex1, ex2 = Exchange(links, w1), Exchange(links, w2)
    exq, exp = Exchange(links, got_q), Exchange(links, got_p)
    get_q, get_p = Deliver(links, 1, own_q, got_q, load_sem.at[4]), Deliver(links, 1, own_p, got_p, load_sem.at[5])
    get_1, get_2 = Deliver(links, 1, own_1, next_1), Deliver(links, 1, own_2, next_2)
    s1, s2 = Scatter(links, low, wide), Scatter(links, low, wide)
    g1, g2, g3 = Gather(links, gat1), Gather(links, gat2), Gather(links, gat3)
    load_p.wait()
    for i in range(NCH):
        scatter_product(s1, i, lambda b: block_rows(o_ref, b, i, rows), wp[...], rows)
    load_1.wait()
    ex1.step(0)
    load_2.wait()
    ex2.step(0)
    for i in range(NCH):
        s1.middle(i)
    for s in range(1, bits):
        ex1.step(s)
    get_q.start()
    get_p.start()
    for i in range(NCH):
        h = x_ref[chunk(i, rows)].astype(jnp.float32) + s1.done(i)
        hid_ref[chunk(i, rows)] = h
        g1.send(i, (normed(h)[0] * ln_ref[0:1] + ln_ref[1:2]).astype(jnp.bfloat16))
        if i == 0:
            for s in range(1, bits):
                ex2.step(s)
    s1.release()

    def mlp(i):
        u = dot(g1.done(i), w1[...].reshape(width, -1), NN)
        put_rows(u_buf, u.astype(jnp.bfloat16), i, rows)
        g = gelu_both(u)[0].astype(jnp.bfloat16)
        put_rows(g_buf, g, i, rows)
        if i == 0:
            ex2.done()
        scatter_product(s2, i, lambda b: g[b * n : (b + 1) * n], w2[...].reshape(width, -1), rows)

    g1.forward(0)
    ex1.done()
    mlp(0)
    g1.forward(1)
    s2.middle(0)
    mlp(1)
    s2.middle(1)
    stores = [
        start_load(src, dst, store_sem.at[k])
        for k, (src, dst) in enumerate(((gat1, n2_hbm), (u_buf, u_hbm), (g_buf, g_hbm), (w1, w1_out), (w2, w2_out)))
    ]
    get_q.done()
    exq.step(0)
    for i in range(NCH):
        act = (hid_ref[chunk(i, rows)] + s2.done(i)).astype(jnp.bfloat16)
        act_ref[chunk(i, rows)] = act
        g2.send(i, (normed(act.astype(jnp.float32))[0] * ln_ref[2:3] + ln_ref[3:4]).astype(jnp.bfloat16))
    for i in range(NCH):
        at = chunk(i, rows)
        dy = cot_ref[at].astype(jnp.float32) * live_ref[at]
        dy_ref[at] = dy
        g3.send(i, dy.astype(jnp.bfloat16))
    get_1.start()
    get_2.start()
    for s in range(1, bits):
        exq.step(s)
    get_p.done()
    exp.step(0)
    for i in range(NCH):
        g2.forward(i)
    exq.done()
    weight = got_q[...].reshape(width, -1)
    for i in range(NCH):
        part = (dot(g2.done(i), weight, NN) + term_ref[0:1]).astype(jnp.bfloat16)
        put_rows(qkv, part, i, rows)
    for s in range(1, bits):
        exp.step(s)
    stores += [
        start_load(src, dst, store_sem.at[5 + k])
        for k, (src, dst) in enumerate(((gat2, n1_hbm), (qkv, qkv_hbm), (got_q, next_q)))
    ]
    load_w.wait()
    keys = [quarter(links.r, links.c, j) for j in order]

    def block(i, carry):
        at = pl.ds(pl.multiple_of(i * QB, QB), QB)
        o1_ref[at] = attn_block(
            block_quarter(links, i), keys, scale, qkv.at[at], qkv, mask_ref[...], wall, lse_ref.at[i], s_scr, p_scr
        )
        return carry

    lax.fori_loop(0, 4, block, 0)
    for i in range(NCH):
        g3.forward(i)
    exp.done()
    stores.append(start_load(got_p, next_p, store_sem.at[8]))
    for i in range(NCH):
        g3.copies["s", i].wait_recv()
        g3.copies["f", i].wait_recv()
    stores.append(start_load(gat3, dm_hbm, store_sem.at[9]))
    get_1.done()
    get_2.done()
    links.leave()
    for store in stores:
        store.wait()


VM = pl.BlockSpec(memory_space=pltpu.VMEM)
HB = pl.BlockSpec(memory_space=pl.ANY)


def comm_scratch(copies):
    return [pltpu.SemaphoreType.DMA((copies,)), pltpu.SemaphoreType.DMA((copies,))]


def scatter_scratch(rows, width):
    return [pltpu.VMEM((6, rows, width), jnp.bfloat16), pltpu.VMEM((2, rows, width), jnp.float32)]


def params(ident):
    return pltpu.CompilerParams(collective_id=ident, has_side_effects=True, vmem_limit_bytes=52 << 20)


def mid_chain(x, o, ln, cot, live, term, mask_pad, wp, w1, w2, wall, own, order, scale):
    rows, width = x.shape
    hidden = w1.shape[-1]
    bits = w1.ndim - 2
    heads = wall.shape[0]
    wide = own[0].shape[-1]
    bf16, f32 = jnp.bfloat16, jnp.float32
    out = jax.ShapeDtypeStruct
    res = pl.pallas_call(
        functools.partial(mid_kernel, order, scale, bits),
        in_specs=[VM] * 7 + [HB] * 8,
        out_specs=[VM] * 5 + [HB] * 12,
        out_shape=[
            out((rows, width), f32),
            out((rows, width), bf16),
            out((rows, width), f32),
            out((4 * rows, heads * HD), bf16),
            out((4, heads, QB), f32),
            out((4, rows, width), bf16),
            out((4 * rows, hidden), bf16),
            out((4 * rows, hidden), bf16),
            out((4, rows, width), bf16),
            out((4 * rows, wide), bf16),
            out((4, rows, width), bf16),
        ]
        + [out(w.shape, bf16) for w in (w1, w2, *own)],
        scratch_shapes=[
            *[pltpu.VMEM(w.shape, bf16) for w in (wp, w1, w2, *own[:2])],
            pltpu.VMEM(wall.shape, f32),
            pltpu.VMEM((4 * rows, hidden), bf16),
            pltpu.VMEM((4 * rows, hidden), bf16),
            pltpu.VMEM((4 * rows, wide), bf16),
            pltpu.VMEM((4, rows, width), bf16),
            pltpu.VMEM((4, rows, width), bf16),
            pltpu.VMEM((4, rows, width), bf16),
            *scatter_scratch(rows, width),
            pltpu.VMEM((2, 4 * rows, QB), f32),
            pltpu.VMEM((2, 4 * rows, QB), bf16),
            pltpu.SemaphoreType.DMA((6,)),
            pltpu.SemaphoreType.DMA((10,)),
            *comm_scratch(2 * Scatter.COPIES + 3 * Gather.COPIES + 4 * Deliver.COPIES + 4 * Exchange.copies(bits)),
        ],
        compiler_params=params(1),
        cost_estimate=pl.CostEstimate(flops=60 << 30, bytes_accessed=24 << 20, transcendentals=0),
    )(x, o, ln, cot, live, term, mask_pad, wp, w1, w2, wall, *own)
    hid, act, dy, o1, lse, n2, u, g, n1, qkv, dm = res[:11]
    rest = lambda v: v.reshape(4 * rows, width)
    return hid, act, dy, o1, lse, rest(n2), u, g, rest(n1), qkv, rest(dm), res[11:13], res[13:]


def turn_kernel(bits, fold, x_ref, o_ref, dy_ref, ln_ref, dm_hbm, wp_hbm, own1, own2, got1, got2,
                dh_ref, norm_ref, hid_ref, do_ref, fc2_ref, y_hbm, da_hbm, fc1_hbm,
                wp, w1, w2, dm, g_buf, du_buf, y_buf, fc1, fc2, gat1, gat2, low, wide, *refs):
    lands, (load_sem, store_sem, send_sem, recv_sem) = refs[:-4], refs[-4:]
    rows, width = x_ref.shape
    n = rows // NCH
    links = Links(send_sem, recv_sem, bits)
    loads = [
        start_load(wp_hbm, wp, load_sem.at[0]),
        Part(links, 1, own1, got1, w1, load_sem.at[1]).start(),
        Part(links, 1, own2, got2, w2, load_sem.at[2]).start(),
        start_load(dm_hbm, dm, load_sem.at[3]),
    ]
    links.enter()
    ex1, ex2 = Exchange(links, w1), Exchange(links, w2)
    s1, s2 = Scatter(links, low, wide), Scatter(links, low, wide)
    g1, g2 = Gather(links, gat1), Gather(links, gat2)
    loads[0].wait()
    for i in range(NCH):
        scatter_product(s1, i, lambda b: block_rows(o_ref, b, i, rows), wp[...], rows)
    loads[1].wait()
    ex1.step(0)
    loads[2].wait()
    ex2.step(0)
    for i in range(NCH):
        s1.middle(i)
    for s in range(1, bits):
        ex1.step(s)
    for i in range(NCH):
        h = x_ref[chunk(i, rows)].astype(jnp.float32) + s1.done(i)
        hid_ref[chunk(i, rows)] = h
        g1.send(i, (normed(h)[0] * ln_ref[0:1] + ln_ref[1:2]).astype(jnp.bfloat16))
        if i == 0:
            for s in range(1, bits):
                ex2.step(s)
    s1.release()
    loads[3].wait()

    def mlp(i):
        u = dot(g1.done(i), w1[...].reshape(width, -1), NN)
        g, slope = gelu_both(u)
        put_rows(g_buf, g.astype(jnp.bfloat16), i, rows)
        dmi = jnp.concatenate([block_rows(dm, b, i, rows) for b in range(4)], axis=0)
        du = (dot(dmi, w2[...].reshape(width, -1), NN) * slope).astype(jnp.bfloat16)
        put_rows(du_buf, du, i, rows)
        scatter_product(s2, i, lambda b: du[b * n : (b + 1) * n], w1[...].reshape(width, -1), rows)

    g1.forward(0)
    ex1.done()
    ex2.done()
    mlp(0)
    g1.forward(1)
    s2.middle(0)
    mlp(1)
    s2.middle(1)
    slab_grad(fc2, 0, dm[...], g_buf[...])
    if fold:
        reduce = DpReduce(links, fc2, *lands)
        reduce.start()
    sums = None
    for i in range(NCH):
        at = chunk(i, rows)
        dx, dgain, dshift = norm_back(hid_ref[at], s2.done(i), ln_ref[0:1])
        dh = dy_ref[at] + dx
        dh_ref[at] = dh
        g2.send(i, dh.astype(jnp.bfloat16))
        both = jnp.concatenate([dgain, dshift], axis=0)
        sums = both if sums is None else sums + both
    norm_ref[...] = sums
    slab_grad(fc1, 0, flat(gat1), du_buf[...])
    stores = [start_load(fc1, fc1_hbm, store_sem.at[0])]
    g2.forward(0)
    for b in range(4):
        y = dot(g_buf[pl.ds(b * rows, rows)], w2[...].reshape(width, -1), NT)
        y_buf[pl.ds(b * rows, rows)] = y.astype(jnp.bfloat16)
    stores.append(start_load(y_buf, y_hbm, store_sem.at[1]))
    if fold:
        reduce.middle()
    g2.forward(1)
    for i in range(NCH):
        put_rows(do_ref, dot(g2.done(i), wp[...], NN).astype(jnp.bfloat16), i, rows)
    stores.append(start_load(gat2, da_hbm, store_sem.at[2]))
    if fold:
        reduce.done(fc2_ref)
    else:
        fc2_ref[...] = fc2[...]
    links.leave()
    for store in stores:
        store.wait()


def turn_chain(ndp, x, o, dy, ln, dm, wp, own, got):
    rows, width = x.shape
    hidden = own[0].shape[-1]
    bits = own[0].ndim - 2
    fold = ndp == 4
    lw = wp.shape[1]
    n = width // 4
    bf16, f32 = jnp.bfloat16, jnp.float32
    out = jax.ShapeDtypeStruct
    res = pl.pallas_call(
        functools.partial(turn_kernel, bits, fold),
        in_specs=[VM, VM, VM, VM] + [HB] * 6,
        out_specs=[VM] * 5 + [HB] * 3,
        out_shape=[
            out((rows, width), f32),
            out((2, width), f32),
            out((rows, width), f32),
            out((4 * rows, lw), bf16),
            out((n, hidden) if fold else (2, 2, n, hidden), bf16),
            out((4 * rows, width), bf16),
            out((4, rows, width), bf16),
            out((2, 2, n, hidden), bf16),
        ],
        scratch_shapes=[
            pltpu.VMEM(wp.shape, bf16),
            pltpu.VMEM(own[0].shape, bf16),
            pltpu.VMEM(own[1].shape, bf16),
            pltpu.VMEM((4 * rows, width), bf16),
            pltpu.VMEM((4 * rows, hidden), bf16),
            pltpu.VMEM((4 * rows, hidden), bf16),
            pltpu.VMEM((4 * rows, width), bf16),
            pltpu.VMEM((2, 2, n, hidden), bf16),
            pltpu.VMEM((2, 2, n, hidden), bf16),
            pltpu.VMEM((4, rows, width), bf16),
            pltpu.VMEM((4, rows, width), bf16),
            *scatter_scratch(rows, width),
            *(DpReduce.scratch(n, hidden) if fold else []),
            pltpu.SemaphoreType.DMA((4,)),
            pltpu.SemaphoreType.DMA((3,)),
            *comm_scratch(2 * Scatter.COPIES + 2 * Gather.COPIES + 2 * Exchange.copies(bits) + DpReduce.COPIES),
        ],
        compiler_params=params(2),
        cost_estimate=pl.CostEstimate(flops=60 << 30, bytes_accessed=24 << 20, transcendentals=0),
    )(x, o, dy, ln, dm, wp, *own, *got)
    dh, norms, hid, do, fc2, y, da, fc1 = res
    return dh, norms, y, hid, do, da.reshape(4 * rows, width), fc1, fc2


def back_kernel(bits, fold, layers, flags_ref, x_ref, dh1_ref, hid_ref, ln_ref, dqkv_ref, o1_ref, lab_ref,
                wq_hbm, wp_hbm, w1_hbm, w2_hbm, u_hbm, g_hbm, n2_hbm, n1_hbm, da1_hbm, dwall_hbm, *refs):
    refs = list(refs)
    take = lambda k: [refs.pop(0) for _ in range(k)]
    blocks = take(len(layers))
    gin_ref, dh_ref, norm_ref, do_ref, da_hbm, fc1_hbm, fc2_out, qp_out, rel_out, sum_out = take(10)
    places = [take(2) for _ in range(len(layers) + 1)]
    wq, wp, w1, w2, u_buf, g_buf, fc2, gqp, strips, gin_low, gat1, gat2, low, wide = take(14)
    if fold:
        lands_qp, lands_fc = take(3), take(3)
    load_sem, store_sem, send_sem, recv_sem = refs
    small, out_lab = flags_ref[0], flags_ref[1]
    rows, width = x_ref.shape
    n = rows // NCH
    hidden = w1.shape[1]
    heads = rel_out.shape[0]
    lw = o1_ref.shape[1]
    load = lambda k, src, dst: start_load(src, dst, load_sem.at[k])
    load_q, load_n1, load_da = load(0, wq_hbm, wq), load(1, n1_hbm, u_buf), load(2, da1_hbm, g_buf)
    load_1, load_2, load_p = load(3, w1_hbm, w1), load(4, w2_hbm, w2), load(5, wp_hbm, wp)
    load_strip = load(6, dwall_hbm.at[0], strips)
    links = Links(send_sem, recv_sem, bits)
    links.enter()
    blocks.append(gin_low)
    layers = layers + [1]
    returns = [Return(links, layer, src, *at) for layer, src, at in zip(layers, blocks, places)]
    for back in returns[:-1]:
        back.start()
    s1, s2 = Scatter(links, low, wide), Scatter(links, low, wide)
    g1, g2 = Gather(links, gat1), Gather(links, gat2)
    load_q.wait()
    for i in range(NCH):
        scatter_product(s1, i, lambda b: block_rows(dqkv_ref, b, i, rows), wq[...], rows)
        if i:
            s1.middle(i - 1)
    s1.middle(NCH - 1)
    load_n1.wait()
    slab_grad(gqp, 0, u_buf[...], dqkv_ref[...])
    load_da.wait()
    slab_grad(gqp, dqkv_ref.shape[1], g_buf[...], o1_ref[...])
    load_u, load_g = load(8, u_hbm, u_buf), load(9, g_hbm, g_buf)
    if fold:
        reduce = DpReduce(links, gqp, *lands_qp)
        reduce.start()
    cols = jnp.sum(dqkv_ref[...].astype(jnp.float32), axis=0, keepdims=True)
    sum_out[...] = jnp.concatenate([cols[:, :lw], cols[:, 2 * lw :]], axis=1)
    sums1 = None
    for i in range(NCH):
        at = chunk(i, rows)
        dx, dgain, dshift = norm_back(x_ref[at].astype(jnp.float32), s1.done(i), ln_ref[0:1])
        gin = dh1_ref[at] + dx
        gin_ref[at] = gin
        gin_low[at] = gin.astype(jnp.bfloat16)
        g1.send(i, gin_low[at])
        both = jnp.concatenate([dgain, dshift], axis=0)
        sums1 = both if sums1 is None else sums1 + both
    returns[-1].start()
    lab = lab_ref[...]
    hi_mask, lo_hot = _labels_hi_lo(lab)

    def bias_head(h, load_strip):
        load_strip.wait()
        rel_out[h] = wall_grad(small, out_lab, lab, hi_mask, lo_hot, strips)
        return load(6, dwall_hbm.at[h + 1], strips) if h + 1 < heads else None

    load_strip = bias_head(0, load_strip)
    load_strip = bias_head(1, load_strip)
    s1.release()
    load_1.wait()
    load_2.wait()
    load_u.wait()

    def mlp(i):
        dmi = g1.done(i)
        ui = jnp.concatenate([block_rows(u_buf, b, i, rows) for b in range(4)], axis=0).astype(jnp.float32)
        du = (dot(dmi, w2[...], NN) * gelu_both(ui)[1]).astype(jnp.bfloat16)
        put_rows(u_buf, du, i, rows)
        scatter_product(s2, i, lambda b: du[b * n : (b + 1) * n], w1[...], rows)

    g1.forward(0)
    mlp(0)
    g1.forward(1)
    s2.middle(0)
    mlp(1)
    s2.middle(1)
    if fold:
        reduce.middle()
    load_g.wait()
    slab_grad(fc2, 0, flat(gat1), g_buf[...])
    if fold:
        reduce_2 = DpReduce(links, fc2, *lands_fc)
        reduce_2.start()
    load_n2 = load(10, n2_hbm, g_buf)
    sums2 = None
    for i in range(NCH):
        at = chunk(i, rows)
        dx, dgain, dshift = norm_back(hid_ref[at], s2.done(i), ln_ref[1:2])
        dh = gin_ref[at].astype(jnp.bfloat16).astype(jnp.float32) + dx
        dh_ref[at] = dh
        g2.send(i, dh.astype(jnp.bfloat16))
        both = jnp.concatenate([dgain, dshift], axis=0)
        sums2 = both if sums2 is None else sums2 + both
    norm_ref[...] = jnp.concatenate([sums1, sums2], axis=0)
    load_n2.wait()
    weight_grad(w2, 0, g_buf[...], u_buf[...])
    stores = [start_load(w2, fc1_hbm, store_sem.at[0])]
    load_strip = bias_head(2, load_strip)
    load_p.wait()
    g2.forward(0)
    bias_head(3, load_strip)
    g2.forward(1)
    for i in range(NCH):
        put_rows(do_ref, dot(g2.done(i), wp[...], NN).astype(jnp.bfloat16), i, rows)
    stores.append(start_load(gat2, da_hbm, store_sem.at[2]))
    if fold:
        reduce_2.middle()
        reduce.done(qp_out)
        reduce_2.done(fc2_out)
    else:
        qp_out[...] = gqp[...]
        fc2_out[...] = fc2[...]
    for back in returns:
        back.done()
    links.leave()
    for store in stores:
        store.wait()


def back_chain(ndp, flags, x, dh1, hid, ln, dqkv, o1, lab, wq, wp, w1, w2, u, g, n2, n1, da1, dwall, returns):
    rows, width = x.shape
    hidden = w1.shape[1]
    lw = wp.shape[1]
    heads = dwall.shape[0]
    fold = ndp == 4
    bits = 2
    n = width // 4
    qp_cols = wq.shape[1] + lw
    bf16, f32 = jnp.bfloat16, jnp.float32
    out = jax.ShapeDtypeStruct
    layers = [layer for layer, _ in returns]
    blocks = [block for _, block in returns]
    copies = 2 * Scatter.COPIES + 2 * Gather.COPIES + 2 * DpReduce.COPIES + (len(layers) + 1) * Return.COPIES
    res = pl.pallas_call(
        functools.partial(back_kernel, bits, fold, layers),
        in_specs=[pl.BlockSpec(memory_space=pltpu.SMEM)] + [VM] * 7 + [HB] * (10 + len(blocks)),
        out_specs=[VM, VM, VM, VM, HB, HB, VM, VM, VM, VM] + [HB] * (2 * len(blocks) + 2),
        out_shape=[
            out((rows, width), f32),
            out((rows, width), f32),
            out((4, width), f32),
            out((4 * rows, lw), bf16),
            out((4, rows, width), bf16),
            out((width, hidden), bf16),
            out((n, hidden) if fold else (2, 2, n, hidden), bf16),
            out((n, qp_cols) if fold else (2, 2, n, qp_cols), bf16),
            out((heads, 64, 64), f32),
            out((1, 2 * lw), f32),
        ]
        + [out(block.shape, block.dtype) for block in blocks for _ in range(2)]
        + [out((rows, width), bf16)] * 2,
        scratch_shapes=[
            pltpu.VMEM(wq.shape, bf16),
            pltpu.VMEM(wp.shape, bf16),
            pltpu.VMEM(w1.shape, bf16),
            pltpu.VMEM(w2.shape, bf16),
            pltpu.VMEM((4 * rows, hidden), bf16),
            pltpu.VMEM((4 * rows, hidden), bf16),
            pltpu.VMEM((2, 2, n, hidden), bf16),
            pltpu.VMEM((2, 2, n, qp_cols), bf16),
            pltpu.VMEM(dwall.shape[1:], f32),
            pltpu.VMEM((rows, width), bf16),
            pltpu.VMEM((4, rows, width), bf16),
            pltpu.VMEM((4, rows, width), bf16),
            *scatter_scratch(rows, width),
            *(DpReduce.scratch(n, qp_cols) + DpReduce.scratch(n, hidden) if fold else []),
            pltpu.SemaphoreType.DMA((11,)),
            pltpu.SemaphoreType.DMA((3,)),
            *comm_scratch(copies),
        ],
        compiler_params=params(3),
        cost_estimate=pl.CostEstimate(flops=60 << 30, bytes_accessed=24 << 20, transcendentals=0),
    )(flags, x, dh1, hid, ln, dqkv, o1, lab, wq, wp, w1, w2, u, g, n2, n1, da1, dwall, *blocks)
    gin, dh, norms, do, da, fc1, fc2, qp, rel, sums = res[:10]
    got = [(res[10 + 2 * k], res[11 + 2 * k]) for k in range(len(layers) + 1)]
    return gin, dh, norms, do, da.reshape(4 * rows, width), fc1, fc2, qp, rel, sums, got


def start_kernel(order, scale, bits, flags_ref, x_hbm, cot_hbm, mask_ref, lab_ref, tab_hbm, pack_hbm,
                 wq_hbm, wp_hbm, w1_hbm, w2_hbm,
                 x_ref, cot_ref, pack_ref, lse_ref, o_ref, n1_hbm, qkv_hbm, wall0_hbm, wall1_hbm,
                 wq0_hbm, wp0_hbm, w10_hbm, w20_hbm,
                 tab, wq, wp, qkv, wall, gat1, s_scr, p_scr, load_sem, store_sem, send_sem, recv_sem):
    small, out_lab = flags_ref[0], flags_ref[1]
    rows, width = x_ref.shape
    wide = qkv.shape[1]
    heads = wall.shape[1]
    links = Links(send_sem, recv_sem, bits)
    pair, home = links.pair, links.home
    own_x = pltpu.make_async_copy(x_hbm.at[pair], x_ref, load_sem.at[0])
    when(home, own_x.start)
    own_cot = pltpu.make_async_copy(cot_hbm.at[pair], cot_ref, load_sem.at[7])
    when(home, own_cot.start)
    links.enter()
    packs = [Spread(links, l, pack_hbm, pack_ref.at[l], load_sem.at[1 + l]) for l in range(2)]
    tabs = [Spread(links, l, tab_hbm, tab.at[l], load_sem.at[3 + l]) for l in range(2)]
    tabs[0].start()
    packs[0].start()
    far_x = links.send(x_hbm.at[1 - pair], x_ref, FAR, home)
    tabs[1].start()
    packs[1].start()
    get_q = Deliver(links, 0, wq_hbm, wq, load_sem.at[5])
    get_p = Deliver(links, 0, wp_hbm, wp, load_sem.at[6])
    get_1, get_2 = Deliver(links, 0, w1_hbm, w10_hbm), Deliver(links, 0, w2_hbm, w20_hbm)
    ex_q, ex_p = Exchange(links, wq), Exchange(links, wp)
    get_q.start()
    lab = lab_ref[...]
    hi_mask, lo_hot = _labels_hi_lo(lab)

    def build(l):
        def one(h, carry):
            build_wall(small, out_lab, lab, hi_mask, lo_hot, tab[l, h], wall.at[l, h])
            return carry

        lax.fori_loop(0, heads, one, 0)

    tabs[0].done()
    build(0)
    stores = [start_load(wall.at[0], wall0_hbm, store_sem.at[0])]
    packs[0].done()
    when(home, own_x.wait)
    when(jnp.logical_not(home), far_x.wait_recv)
    g1 = Gather(links, gat1)
    for i in range(NCH):
        at = chunk(i, rows)
        xhat = normed(x_ref[at].astype(jnp.float32))[0]
        g1.send(i, (xhat * pack_ref[0, 0:1] + pack_ref[0, 2:3]).astype(jnp.bfloat16))
    get_p.start()
    get_1.start()
    get_2.start()
    far_cot = links.send(cot_hbm.at[1 - pair], cot_ref, FAR, home)
    tabs[1].done()
    build(1)
    stores.append(start_load(wall.at[1], wall1_hbm, store_sem.at[5]))
    get_q.done()
    ex_q.step(0)
    for i in range(NCH):
        g1.forward(i)
    for s in range(1, bits):
        ex_q.step(s)
    for i in range(NCH):
        g1.copies["s", i].wait_recv()
        g1.copies["f", i].wait_recv()
    stores.append(start_load(gat1, n1_hbm, store_sem.at[1]))
    packs[1].done()
    get_p.done()
    ex_q.done()
    ex_p.step(0)
    stores.append(start_load(wq, wq0_hbm, store_sem.at[2]))
    term = pack_ref[0, pl.ds(4 + pair, 1)][:, :wide]
    weight = wq[...].reshape(width, wide)
    for b in range(4):
        qkv[pl.ds(b * rows, rows)] = (dot(gat1[b], weight, NN) + term).astype(jnp.bfloat16)
    stores.append(start_load(qkv, qkv_hbm, store_sem.at[3]))
    for s in range(1, bits):
        ex_p.step(s)
    keys = [quarter(links.r, links.c, j) for j in order]

    def block(i, carry):
        at = pl.ds(pl.multiple_of(i * QB, QB), QB)
        qq = lax.rem(links.r + i // 2, 2) + 2 * lax.rem(links.c + lax.rem(i, 2), 2)
        o_ref[at] = attn_block(
            qq, keys, scale, qkv.at[at], qkv, mask_ref[...], wall.at[0], lse_ref.at[i], s_scr, p_scr
        )
        return carry

    lax.fori_loop(0, 4, block, 0)
    ex_p.done()
    stores.append(start_load(wp, wp0_hbm, store_sem.at[4]))
    get_1.done()
    get_2.done()
    when(home, own_cot.wait)
    when(jnp.logical_not(home), far_cot.wait_recv)
    links.leave()
    for store in stores:
        store.wait()


def start_chain(flags, x, cot, mask_pad, lab, table, pack, wq, wp, w1, w2, order, scale):
    bits = wq.ndim - 2
    _, rows, width = x.shape
    heads = table.shape[0]
    wide = wq.shape[-1]
    bf16, f32 = jnp.bfloat16, jnp.float32
    out = jax.ShapeDtypeStruct
    copies = 2 + 4 * Spread.COPIES + 4 * Deliver.COPIES + 2 * Exchange.copies(bits) + Gather.COPIES
    return pl.pallas_call(
        functools.partial(start_kernel, order, scale, bits),
        in_specs=[pl.BlockSpec(memory_space=pltpu.SMEM), HB, HB, VM, VM, HB, HB, HB, HB, HB, HB],
        out_specs=[VM] * 5 + [HB] * 8,
        out_shape=[
            out((rows, width), bf16),
            out((rows, width), bf16),
            out((2,) + pack.shape, f32),
            out((4, heads, QB), f32),
            out((4 * rows, heads * HD), bf16),
            out((4, rows, width), bf16),
            out((4 * rows, wide), bf16),
            out((heads, 32, WALL), f32),
            out((heads, 32, WALL), f32),
            *[out(w.shape, bf16) for w in (wq, wp, w1, w2)],
        ],
        scratch_shapes=[
            pltpu.VMEM((2,) + table.shape, f32),
            *[pltpu.VMEM(w.shape, bf16) for w in (wq, wp)],
            pltpu.VMEM((4 * rows, wide), bf16),
            pltpu.VMEM((2, heads, 32, WALL), f32),
            pltpu.VMEM((4, rows, width), bf16),
            pltpu.VMEM((2, 4 * rows, QB), f32),
            pltpu.VMEM((2, 4 * rows, QB), bf16),
            pltpu.SemaphoreType.DMA((8,)),
            pltpu.SemaphoreType.DMA((6,)),
            *comm_scratch(copies),
        ],
        compiler_params=params(0),
        cost_estimate=pl.CostEstimate(flops=80 << 30, bytes_accessed=24 << 20, transcendentals=0),
    )(flags, x, cot, mask_pad, lab, table, pack, wq, wp, w1, w2)


def attn_back(links, order, scale, qkv_ref, do_ref, o_ref, lse_ref, k_extra, wall, acc, p_scr, s_scr, dq_scr, dk_scr, dv_scr,
              dqkv_ref, event):
    heads = wall.shape[0]
    width = heads * HD
    total = qkv_ref.shape[0]
    keys = [quarter(links.r, links.c, j) for j in order]
    lane = lax.broadcasted_iota(jnp.int32, (QB, 128 - HD), 1)
    q_extra = jnp.where(lane == 0, 1.0, 0.0).astype(jnp.bfloat16)

    def block(i, carry):
        at = pl.ds(pl.multiple_of(i * QB, QB), QB)
        q_ref, d_ref, out_ref = qkv_ref.at[at], do_ref.at[at], o_ref.at[at]
        qq = block_quarter(links, i)
        dqs = []
        for h in range(heads):
            kh = head_lanes(qkv_ref, width + HD * h, k_extra)
            qh = head_lanes(q_ref, HD * h, q_extra)
            vh = head_lanes(qkv_ref, 2 * width + HD * h)
            doh = head_lanes(d_ref, HD * h)
            oh = head_lanes(out_ref, HD * h)
            inner = jnp.sum((doh.astype(jnp.float32) * oh.astype(jnp.float32)).T, axis=0, keepdims=True)
            lse = lse_ref[i, h : h + 1, :]
            for kb in range(total // 256):
                s_t = dot(kh[256 * kb : 256 * kb + 256], qh, NT)
                dp_t = dot(vh[256 * kb : 256 * kb + 256], doh, NT)
                for js in range(8):
                    st = 8 * kb + js
                    start = strip_start(qq, js, keys[kb])
                    s = s_t[32 * js : 32 * js + 32] * (scale * LOG2E) + wall[h, :, pl.ds(start, QB)]
                    p = jnp.exp2(s - lse)
                    ds = p * (dp_t[32 * js : 32 * js + 32] - inner)
                    p_scr[h % 2, 32 * st : 32 * st + 32] = p.astype(jnp.bfloat16)
                    s_scr[h % 2, 32 * st : 32 * st + 32] = ds.astype(jnp.bfloat16)
                    acc[h, :, pl.ds(start, QB)] += ds
            p_b, ds_b = p_scr[h % 2], s_scr[h % 2]
            dv_scr[h] += dot(p_b, doh, NN)
            dk_scr[h] += dot(ds_b, qh, NN)
            dq_t = dot(kh, ds_b, TN) * scale
            dqs.append(dq_t.T[:, :HD].astype(jnp.bfloat16))
        dq_scr[at] = jnp.concatenate(dqs, axis=1)
        event(i)
        return carry

    lax.fori_loop(0, total // QB, block, 0)
    parts = [dq_scr[...]]
    parts += [(dk_scr[h, :, :HD] * scale).astype(jnp.bfloat16) for h in range(heads)]
    parts += [dv_scr[h, :, :HD].astype(jnp.bfloat16) for h in range(heads)]
    dqkv_ref[...] = jnp.concatenate(parts, axis=1)


def bwd_kernel(order, scale, bits, fold, layers, summed, qkv_ref, do_ref, o_ref, lse_ref, mask_ref, wall_hbm, gfc_hbm, *refs):
    refs = list(refs)
    take = lambda k: [refs.pop(0) for _ in range(k)]
    blocks = take(len(layers))
    y_ref, hid_ref = take(2) if summed else (None, None)
    dqkv_ref, acc_hbm = take(2)
    (fc_out,) = take(1) if fold else (None,)
    places = [take(2) for _ in layers]
    (act_ref,) = take(1) if summed else (None,)
    wall, acc, p_scr, s_scr, dq_scr, dk_scr, dv_scr = take(7)
    if fold:
        gfc, land0, land1, sent = take(4)
    if summed:
        (low,) = take(1)
    load_sem, store_sem, send_sem, recv_sem = refs
    loads = [start_load(wall_hbm, wall, load_sem.at[0])]
    if fold:
        loads.append(start_load(gfc_hbm, gfc, load_sem.at[1]))
    links = Links(send_sem, recv_sem, bits)
    links.enter()
    returns = [Return(links, layer, src, *at) for layer, src, at in zip(layers, blocks, places)]
    if fold:
        reduce = DpReduce(links, gfc, land0, land1, sent)
    if summed:
        rows = hid_ref.shape[0]
        part = lambda b: y_ref.at[pl.ds(b * rows, rows)]
        to_sib = links.make(part(3), low.at[0], SIBLING)
        near = links.make(part(1), low.at[1], SIBLING)
        to_partner = links.make(low.at[2], low.at[3], PARTNER)
        to_sib.start()
        near.start()
    acc[...] = jnp.zeros_like(acc)
    dk_scr[...] = jnp.zeros_like(dk_scr)
    dv_scr[...] = jnp.zeros_like(dv_scr)
    if fold:
        loads[1].wait()
        reduce.start()
    if summed:
        to_sib.wait_recv()
        low[2] = (part(2)[...].astype(jnp.float32) + low[0].astype(jnp.float32)).astype(jnp.bfloat16)
        to_partner.start()
    for back in returns:
        back.start()
    loads[0].wait()

    def event(i):
        if fold:
            pl.when(i == 2)(lambda: reduce.middle())

    attn_back(
        links, order, scale, qkv_ref, do_ref, o_ref, lse_ref, mask_ref[...], wall, acc, p_scr, s_scr, dq_scr, dk_scr, dv_scr,
        dqkv_ref, event,
    )
    stores = [start_load(acc, acc_hbm, store_sem.at[0])]
    if summed:
        near.wait_recv()
        to_partner.wait_recv()
        act = hid_ref[...] + part(0)[...].astype(jnp.float32) + low[1].astype(jnp.float32) + low[3].astype(jnp.float32)
        act_ref[...] = act.astype(jnp.bfloat16)
    if fold:
        reduce.done(fc_out)
    for back in returns:
        back.done()
    links.leave()
    for store in stores:
        store.wait()


def bwd_chain(ident, fold, qkv, do, o, lse, mask_pad, wall, gfc, returns, order, scale, summed=None):
    total, wide = qkv.shape
    heads = wall.shape[0]
    bits = 2
    n, columns = gfc.shape[2:]
    bf16, f32 = jnp.bfloat16, jnp.float32
    out = jax.ShapeDtypeStruct
    layers = [layer for layer, _ in returns]
    blocks = [block for _, block in returns]
    outs = [out((total, wide), bf16), out(wall.shape, f32)]
    specs = [VM, HB]
    if fold:
        outs.append(out((n, columns), bf16))
        specs.append(VM)
    for block in blocks:
        outs += [out(block.shape, block.dtype)] * 2
        specs += [VM] * 2
    scratch = [
        pltpu.VMEM(wall.shape, f32),
        pltpu.VMEM(wall.shape, f32),
        pltpu.VMEM((2, total, QB), bf16),
        pltpu.VMEM((2, total, QB), bf16),
        pltpu.VMEM((total, heads * HD), bf16),
        pltpu.VMEM((heads, total, 128), f32),
        pltpu.VMEM((heads, total, 128), f32),
    ]
    if fold:
        scratch += [pltpu.VMEM(gfc.shape, bf16), *DpReduce.scratch(n, columns)]
    more = []
    if summed is not None:
        more = list(summed)
        rows, width = summed[1].shape
        outs.append(out((rows, width), bf16))
        specs.append(VM)
        scratch.append(pltpu.VMEM((4, rows, width), bf16))
    copies = len(layers) * Return.COPIES + (DpReduce.COPIES if fold else 0) + (3 if more else 0)
    res = pl.pallas_call(
        functools.partial(bwd_kernel, order, scale, bits, fold, layers, bool(more)),
        in_specs=[VM] * 5 + [HB] * 2 + [VM] * (len(blocks) + len(more)),
        out_specs=specs,
        out_shape=outs,
        scratch_shapes=scratch
        + [pltpu.SemaphoreType.DMA((2,)), pltpu.SemaphoreType.DMA((1,)), *comm_scratch(max(copies, 1))],
        compiler_params=params(ident),
        cost_estimate=pl.CostEstimate(flops=24 << 30, bytes_accessed=20 << 20, transcendentals=0),
    )(qkv, do, o, lse, mask_pad, wall, gfc, *blocks, *more)
    res = list(res)
    dqkv, acc = res[:2]
    res = res[2:]
    fc = res.pop(0) if fold else None
    got = [(res[2 * k], res[2 * k + 1]) for k in range(len(layers))]
    act = res[-1] if more else None
    return dqkv, acc, fc, got, act


class SumHops:
    def __init__(self, links, buf, land, hops):
        self.links, self.buf, self.land, self.hops, self.k = links, buf, land, hops, 0

    def send(self):
        if self.k < len(self.hops):
            self.copy = self.links.send(self.buf, self.land.at[self.k], self.hops[self.k], track=False)

    def take(self):
        self.copy.wait_recv()
        self.copy.wait_send()
        self.buf[...] = self.buf[...] + self.land[self.k]
        self.k += 1
        self.send()


def end_kernel(order, scale, bits, fold, layers, flags_ref, qkv_ref, do_ref, o_ref, lse_ref, mask_ref,
               x_ref, dh_ref, ln_ref, lab_ref, small_ref, rel1_ref,
               wall_hbm, wq_hbm, n1_hbm, da_hbm, fc_hbm, *refs):
    refs = list(refs)
    take = lambda k: [refs.pop(0) for _ in range(k)]
    blocks = take(len(layers))
    gin_ref, norm_out, rel_out, sum_out, qp_out = take(5)
    (fc_out,) = take(1) if fold else (None,)
    places = [take(2) for _ in range(len(layers) + (3 if fold else 1))]
    acc, dqkv_ref, gqp, gin_low, low1 = take(5)
    rel, rel_land, rel_near, norms, norm_land, sums, sum_land, sum_near = take(8)
    if fold:
        fc, lands_q, lands_f = take(1)[0], take(3), take(3)
    load_sem, send_sem, recv_sem = refs
    small, out_lab = flags_ref[0], flags_ref[1]
    rows, width = x_ref.shape
    heads = rel.shape[1]
    if fold:
        load_f = start_load(fc_hbm, fc, load_sem.at[1])
    links = Links(send_sem, recv_sem, bits)
    home, away = links.home, jnp.logical_not(links.home)
    links.enter()
    give = list(zip(layers, blocks)) + [(0, gin_low)] + ([(0, fc_out), (0, qp_out)] if fold else [])
    returns = [Return(links, layer, src, *at) for (layer, src), at in zip(give, places)]
    early = len(layers)
    for back in returns[:early]:
        back.start()
    if fold:
        reduce_f = DpReduce(links, fc, *lands_f)
        reduce_q = DpReduce(links, gqp, *lands_q)
        load_f.wait()
        reduce_f.start()
    acc[...] = jnp.zeros_like(acc)

    def event(i):
        if fold:
            pl.when(i == 2)(lambda: reduce_f.middle())

    def attention(wall, p_scr, s_scr, dq_scr, dk_scr, dv_scr):
        load_w = start_load(wall_hbm, wall, load_sem.at[0])
        dk_scr[...] = jnp.zeros_like(dk_scr)
        dv_scr[...] = jnp.zeros_like(dv_scr)
        load_w.wait()
        attn_back(
            links, order, scale, qkv_ref, do_ref, o_ref, lse_ref, mask_ref[...], wall, acc, p_scr, s_scr, dq_scr, dk_scr,
            dv_scr, dqkv_ref, event,
        )

    total = qkv_ref.shape[0]
    vmem, bf16, f32 = pltpu.VMEM, jnp.bfloat16, jnp.float32
    pl.run_scoped(
        attention,
        vmem(wall_hbm.shape, f32),
        vmem((2, total, QB), bf16),
        vmem((2, total, QB), bf16),
        vmem((total, heads * HD), bf16),
        vmem((heads, total, 128), f32),
        vmem((heads, total, 128), f32),
    )
    lw = o_ref.shape[1]

    def rest(wq, rows_buf, wide1):
        s1 = Scatter(links, low1, wide1)
        load_q = start_load(wq_hbm, wq, load_sem.at[2])
        load_n = start_load(n1_hbm, rows_buf, load_sem.at[3])
        load_q.wait()
        for i in range(NCH):
            scatter_product(s1, i, lambda b: block_rows(dqkv_ref, b, i, rows), wq[...], rows)
            if i:
                s1.middle(i - 1)
        s1.middle(NCH - 1)
        if fold:
            reduce_f.done(fc_out)
            returns[early + 1].start()
        load_n.wait()
        slab_grad(gqp, 0, rows_buf[...], dqkv_ref[...])
        load_d = start_load(da_hbm, rows_buf, load_sem.at[4])
        load_d.wait()
        slab_grad(gqp, dqkv_ref.shape[1], rows_buf[...], o_ref[...])

        if fold:
            reduce_q.start()
        hops = [("dp", b) for b in range(bits)] + [ACROSS]
        cols = jnp.sum(dqkv_ref[...].astype(jnp.float32), axis=0, keepdims=True)
        mine = jnp.concatenate([cols[:, :lw], cols[:, 2 * lw :]], axis=1)
        images = sums.shape[0] // 2
        number = 2 * lax.axis_index("dp") + links.pair
        here = lax.broadcasted_iota(jnp.int32, (images, 2 * lw), 0) == number
        sums[...] = small_ref[8:]
        sums[0:images, 0 : 2 * lw] = jnp.where(here, jnp.broadcast_to(mine, (images, 2 * lw)), 0.0)
        sum_hops = SumHops(links, sums, sum_land, hops)
        sum_hops.send()
        late = None
        for i in range(NCH):
            at = chunk(i, rows)
            dx, dgain, dshift = norm_back(x_ref[at].astype(jnp.float32), s1.done(i), ln_ref[0:1])
            gin = dh_ref[at] + dx
            gin_ref[at] = gin
            gin_low[at] = gin.astype(jnp.bfloat16)
            both = jnp.concatenate([dgain, dshift], axis=0)
            late = both if late is None else late + both
        returns[early].start()
        norms[...] = small_ref[0:8]
        norms[0:2] = late
        norm_hops = SumHops(links, norms, norm_land, hops + [PARTNER, SIBLING])
        norm_hops.send()
        lab = lab_ref[...]
        hi_mask, lo_hot = _labels_hi_lo(lab)
        rel[1] = rel1_ref[...]

        def heads_of(a, b):
            def one(h, carry):
                rel[0, h] = wall_grad(small, out_lab, lab, hi_mask, lo_hot, acc.at[h])
                return carry

            lax.fori_loop(a, b, one, 0)

        heads_of(0, heads // 2)
        sum_hops.take()
        norm_hops.take()
        heads_of(heads // 2, heads)
        rel_hops = SumHops(links, rel, rel_land, hops)
        rel_hops.send()
        if fold:
            reduce_q.middle()
        norm_hops.take()
        sum_hops.take()
        rel_hops.take()
        if fold:
            reduce_q.done(qp_out)
            returns[early + 2].start()
        else:
            qp_out[...] = gqp[...]
        for k in range(1, len(hops)):
            if k + 1 < len(hops):
                sum_hops.take()
            rel_hops.take()
            norm_hops.take()
        norm_hops.take()
        norm_out[...] = norms[...]
        rel_copy = links.send(rel.at[1 - links.c], rel_near, SIBLING, home)
        sum_copy = links.send(sums, sum_near, SIBLING, home)

        @pl.when(home)
        def _():
            rel_out[...] = rel[links.c]
            sum_out[...] = sums[...]

        @pl.when(away)
        def _():
            rel_copy.wait_recv()
            sum_copy.wait_recv()
            rel_out[...] = rel_near[...]
            sum_out[...] = sum_near[...]

        for back in returns:
            back.done()
        links.leave()

    pl.run_scoped(rest, vmem(wq_hbm.shape, bf16), vmem(n1_hbm.shape, bf16), vmem((2, rows, width), f32))


def end_chain(ndp, flags, qkv, do, o, lse, mask_pad, x, dh, ln, lab, smalls, rel1, wall, wq, n1, da, fc, returns, order, scale):
    rows, width = x.shape
    heads = wall.shape[0]
    total, wide = qkv.shape
    bits = ndp.bit_length() - 1
    fold = bits == 2
    n, fc_cols = fc.shape[2:]
    qp_cols = wide + o.shape[1]
    images = smalls.shape[0] - 8
    hops = bits + 1
    bf16, f32 = jnp.bfloat16, jnp.float32
    out = jax.ShapeDtypeStruct
    layers = [layer for layer, _ in returns]
    blocks = [block for _, block in returns]
    landed = [out(block.shape, bf16) for block in blocks] + [out((rows, width), bf16)]
    outs = [
        out((rows, width), f32),
        out((8, width), f32),
        out((heads, 64, 64), f32),
        out((images, width), f32),
        out((n, qp_cols) if fold else (2, 2, n, qp_cols), bf16),
    ]
    if fold:
        outs.append(out((n, fc_cols), bf16))
        landed += [out((n, fc_cols), bf16), out((n, qp_cols), bf16)]
    copies = Scatter.COPIES + (len(landed)) * Return.COPIES + 2 * DpReduce.COPIES + 3 * hops + 4
    res = pl.pallas_call(
        functools.partial(end_kernel, order, scale, bits, fold, layers),
        in_specs=[pl.BlockSpec(memory_space=pltpu.SMEM)] + [VM] * 11 + [HB] * (5 + len(blocks)),
        out_specs=[VM] * len(outs) + [HB] * (2 * len(landed)),
        out_shape=outs + [shape for shape in landed for _ in range(2)],
        scratch_shapes=[
            pltpu.VMEM(wall.shape, f32),
            pltpu.VMEM((total, wide), bf16),
            pltpu.VMEM((2, 2, n, qp_cols), bf16),
            pltpu.VMEM((rows, width), bf16),
            pltpu.VMEM((6, rows, width), bf16),
            pltpu.VMEM((2, heads, 64, 64), f32),
            pltpu.VMEM((hops, 2, heads, 64, 64), f32),
            pltpu.VMEM((heads, 64, 64), f32),
            pltpu.VMEM((8, width), f32),
            pltpu.VMEM((hops + 2, 8, width), f32),
            pltpu.VMEM((images, width), f32),
            pltpu.VMEM((hops, images, width), f32),
            pltpu.VMEM((images, width), f32),
            *([pltpu.VMEM(fc.shape, bf16)] if fold else []),
            *(DpReduce.scratch(n, qp_cols) + DpReduce.scratch(n, fc_cols) if fold else []),
            pltpu.SemaphoreType.DMA((5,)),
            *comm_scratch(copies),
        ],
        compiler_params=params(4),
        cost_estimate=pl.CostEstimate(flops=90 << 30, bytes_accessed=24 << 20, transcendentals=0),
    )(flags, qkv, do, o, lse, mask_pad, x, dh, ln, lab, smalls, rel1, wall, wq, n1, da, fc, *blocks)
    res = list(res)
    got = [(res[len(outs) + 2 * k], res[len(outs) + 2 * k + 1]) for k in range(len(landed))]
    return res[: len(outs)], got


AXES = ("dp", "section", "tensor")
ORDER = (0, 2, 1, 3)


def local(
    inputs,
    time_emb,
    lengths,
    key_mask,
    rel_index,
    w_qkv,
    w_time,
    w_proj,
    w_fc1,
    w_fc2,
    rel_table,
    norm_gains,
    norm_biases,
    cotangent,
):
    bf16, f32 = jnp.bfloat16, jnp.float32
    _, rows, width = inputs.shape
    seq_len = key_mask.shape[1]
    heads, buckets = rel_table.shape[1:]
    local_width = w_proj.shape[2]
    scale = 1.0 / math.sqrt(HD)
    ndp = lax.axis_size("dp")
    d = lax.axis_index("dp")
    c = lax.axis_index("section")
    z = lax.axis_index("tensor")
    pair = z // 2
    home = c == pair
    first = c == 0
    t = z % 2 + 2 * c

    def move(x, to, name="move"):
        pairs = []
        for dd in range(ndp):
            for cc in range(2):
                for zz in range(4):
                    dst = to(dd, cc, zz)
                    if dst is not None:
                        pairs.append(((dd * 2 + cc) * 4 + zz, (dst[0] * 2 + dst[1]) * 4 + dst[2]))
        with jax.named_scope(name):
            return lax.ppermute(x, AXES, pairs)

    def partner(x):
        return move(x, lambda dd, cc, zz: (dd, cc, zz ^ 1), "partner")

    def sibling(x):
        return move(x, lambda dd, cc, zz: (dd, 1 - cc, zz), "sibling")

    def across(x):
        return move(x, lambda dd, cc, zz: (dd, cc, zz ^ 2), "across")

    def dp_scatter(x, bits):
        n = x.shape[1]
        left = sorted(bits, reverse=True)
        v = x.reshape((2,) * len(left) + (-1, n))
        for b in bits:
            axis = left.index(b)
            left.remove(b)
            mine = (d >> b) & 1
            send = lax.dynamic_index_in_dim(v, 1 - mine, axis, keepdims=False)
            keep = lax.dynamic_index_in_dim(v, mine, axis, keepdims=False)
            got = move(send, lambda dd, cc, zz, b=b: (dd ^ (1 << b), cc, zz), "g_dp")
            v = keep.astype(f32) + got.astype(f32)
            if left:
                v = v.astype(bf16)
        return v

    def by_bits(w):
        return w.reshape(2, 2, -1, w.shape[-1])

    table = jnp.pad(rel_table[0], ((0, 0), (0, 4096 - buckets))).reshape(heads, 64, 64)
    time_all = jnp.einsum("id,dcn->icn", time_emb, w_time[0], preferred_element_type=f32)
    gap = jnp.zeros((2, local_width), f32)
    time_rows = jnp.concatenate([time_all[:, 0], gap, time_all[:, 1], gap], axis=1)
    small_pack = jnp.concatenate([norm_gains[0], norm_biases[0], time_rows, jnp.zeros((2, width), f32)], axis=0)
    own = [by_bits(w) for w in (jnp.concatenate([w_qkv[0, :, j] for j in range(3)], axis=1), w_proj[0], w_fc1[0], w_fc2[0])]
    label_lanes = label_row(rel_index)
    out_label = rel_index[1, seq_len - 1, seq_len - 1].reshape(1)

    length = lax.dynamic_index_in_dim(lengths, pair, 0, keepdims=False)
    small = (length < seq_len).astype(jnp.int32)
    scalars = jnp.stack([z % 2, c] + [jnp.int32(j) for j in ORDER])
    flags = jnp.concatenate([small.reshape(1), out_label])
    mask = lax.dynamic_index_in_dim(key_mask, pair, 0, keepdims=False).reshape(4, rows)
    mask = jnp.concatenate([lax.dynamic_index_in_dim(mask, t ^ j, 0, keepdims=False) for j in ORDER])
    lane = jnp.arange(128 - HD)[None, :]
    mask_pad = jnp.where((lane == 0) & (mask[:, None] == 0), -1e30, 0.0).astype(bf16)

    def gather_rows(x):
        far = partner(x)
        near = sibling(x)
        return jnp.concatenate([x, near, far, sibling(far)], axis=0)

    def scatter_rows(far, near):
        a = sibling(far[rows:].astype(bf16))
        rz = partner((far[:rows] + a.astype(f32)).astype(bf16))
        rs = sibling(near[rows:].astype(bf16))
        return near[:rows] + rs.astype(f32) + rz.astype(f32)

    def times_t(x, w):
        return lax.dot_general(x, w, (((1,), (1,)), ((), ())), preferred_element_type=f32)

    def grad_of(x, y):
        return lax.dot_general(x, y, (((0,), (0,)), ((), ())), preferred_element_type=f32).astype(bf16)

    half = 2 * rows

    def reduced(x):
        with jax.named_scope("g_sum"):
            return lax.psum_scatter(x, "dp", scatter_dimension=0, tiled=True)

    def reduced_late(x):
        if ndp & (ndp - 1):
            return reduced(x)
        bits = list(range(ndp.bit_length() - 1))
        cut = 4 * 128
        return jnp.concatenate(
            [dp_scatter(x[:, :cut], bits), dp_scatter(x[:, cut:], bits[::-1])], axis=1
        ).astype(bf16)

    def column_sums(dqkv):
        sums = jnp.sum(dqkv.astype(f32), axis=0)
        return jnp.concatenate([sums[:local_width], sums[2 * local_width :]])

    def tie(*values):
        return lax.optimization_barrier(values)

    def by_core(pairs):
        return jnp.where(first, pairs[0], pairs[1])

    def near_of(x, layer):
        return move(x, lambda dd, cc, zz: (dd, layer, zz) if cc == zz // 2 and cc != layer else None, "d_near")

    def far_of(x, layer):
        return move(x, lambda dd, cc, zz: (dd, layer, zz ^ 2) if cc != zz // 2 else None, "d_far")

    live = ((t * rows + jnp.arange(rows)) < length).astype(f32)[:, None]
    res = start_chain(flags, inputs, cotangent, mask_pad, label_lanes, table, small_pack, *own, ORDER, scale)
    x0, cot, packs, lse0, o0, n1_0, qkv0 = res[:7]
    walls, got0 = res[7:9], res[9:]
    n1_0 = n1_0.reshape(seq_len, width)

    def whole(w):
        return w.reshape(width, w.shape[-1])

    gains = [packs[l, 0:2] for l in range(2)]
    shifts = [packs[l, 2:4] for l in range(2)]
    ln_mid = jnp.stack([gains[0][1], shifts[0][1], gains[1][0], shifts[1][0]])
    wq0, wp0 = whole(got0[0]), whole(got0[1])
    term1 = lax.dynamic_index_in_dim(packs[1], 4 + pair, 0, keepdims=True)[:, : 3 * local_width]
    hid0, act0, dy1, o1, lse1, n2_0, u0, g0, n1_1, qkv1, dm1, fc_w0, got1 = mid_chain(
        x0, o0, ln_mid, cot, live, term1, mask_pad, wp0, got0[2], got0[3], walls[1], own, ORDER, scale
    )
    w10, w20 = whole(fc_w0[0]), whole(fc_w0[1])
    wq1, wp1 = whole(got1[0]), whole(got1[1])

    fold = ndp == 4
    ln_turn = jnp.stack([gains[1][1], shifts[1][1]])
    dh1, norms1, y1, hid1, do1, da1, fc1_1, fc2_1 = turn_chain(
        ndp, act0, o1, dy1, ln_turn, dm1, wp1, own[2:], got1[2:]
    )
    give = [(0, act0)] + ([(1, fc2_1)] if fold else [])
    dqkv1, dwall1, sum_fc1_1, landed, act1 = bwd_chain(
        6, fold, qkv1, do1, o1, lse1, mask_pad, walls[1], fc1_1, give, ORDER, scale, (y1, hid1)
    )
    got_act0, got_fc2_1 = landed[0], landed[-1]
    ln_back = jnp.stack([gains[1][0], gains[0][1]])
    give = [(1, act1)] + ([(1, sum_fc1_1)] if fold else [])
    gin1, dh0, norms10, do0, da0, fc1_0, fc2_0, qp1, rel1, sums1, landed = back_chain(
        ndp, flags, act0, dh1, hid0, ln_back, dqkv1, o1, label_lanes,
        wq1, wp0, w10, w20, u0, g0, n2_0, n1_1, da1, dwall1, give,
    )
    got_act1, got_fc1_1, got_gin1 = landed[0], landed[len(landed) - 2], landed[-1]
    number = 2 * d + pair
    sums_rows = lax.dynamic_update_slice(
        jnp.zeros((2 * ndp, width), f32), sums1, (number, jnp.int32(width - 2 * local_width))
    )
    mine = lax.dynamic_index_in_dim(time_emb, pair, 0, keepdims=True).astype(f32)
    emb_rows = lax.dynamic_update_slice(jnp.zeros((2 * ndp, width), f32), mine, (number, jnp.int32(0)))
    smalls = jnp.concatenate(
        [jnp.zeros((2, width), f32), norms10[2:], norms10[:2], norms1, sums_rows, emb_rows], axis=0
    )
    give = [(1, qp1), (0, fc2_0)] if fold else []
    (gin0, norms, rel, sums_all, qp0, *more), landed = end_chain(
        ndp, flags, qkv0, do0, o0, lse0, mask_pad, x0, dh0, gains[0][0:1], label_lanes, smalls, rel1,
        walls[0], wq0, n1_0, da0, by_bits(fc1_0), give, ORDER, scale,
    )
    if fold:
        got_qp1, got_fc2_0, got_gin0, got_fc1_0, got_qp0 = landed
        parts = (
            (qp0, got_qp0, qp1, got_qp1),
            (more[0], got_fc1_0, sum_fc1_1, got_fc1_1),
            (fc2_0, got_fc2_0, fc2_1, got_fc2_1),
        )
    else:
        (got_gin0,) = landed
        parts = []
        for x0_, x1_ in ((qp0, qp1), (by_bits(fc1_0), fc1_1), (fc2_0, fc2_1)):
            a, b = reduced(whole(x0_)), reduced(whole(x1_))
            parts.append((a, (near_of(a, 0), far_of(a, 0)), b, (near_of(b, 1), far_of(b, 1))))

    def by_image(same, other):
        return jnp.stack([jnp.where(pair == 0, same, other), jnp.where(pair == 0, other, same)])[None]

    acts = by_image(
        jnp.where(home, by_core((act0, act1)), by_core((got_act0[0], got_act1[0]))), by_core((got_act0[1], got_act1[1]))
    )
    same = jnp.where(home, by_core((gin0, gin1)), by_core((got_gin0[0], got_gin1[0])).astype(f32))
    input_grads = by_image(same, by_core((got_gin0[1], got_gin1[1])).astype(f32))

    def total(mine, got):
        return jnp.where(home, mine, got[0]).astype(f32) + got[1].astype(f32)

    grad_qp, grad_fc1, grad_fc2 = [by_core((total(a, x), total(b, y))) for a, x, b, y in parts]

    rel_grad = rel.reshape(heads, 4096)[:, :buckets]
    norms_mine = jnp.where(first, norms[:4], norms[4:]).reshape(2, 2, width)
    cols = width // (4 * ndp)
    norms_mine = lax.dynamic_slice_in_dim(norms_mine, (d * 4 + z) * cols, cols, 2)
    sums_of, emb_of = sums_all[: 2 * ndp], sums_all[2 * ndp :]
    sums_mine = jnp.where(first, sums_of[:, : 2 * local_width], sums_of[:, 2 * local_width :])
    emb_mine = lax.dynamic_slice_in_dim(emb_of, d * (width // ndp), width // ndp, 1)
    grad_time = lax.dot_general(
        emb_mine, sums_mine, (((0,), (0,)), ((), ())), precision=lax.Precision.HIGHEST, preferred_element_type=f32
    ).reshape(width // ndp, 2, local_width)
    return (
        acts,
        input_grads,
        grad_qp[:, : 3 * local_width].reshape(width // ndp, 3, local_width)[None],
        grad_time[None],
        grad_qp[:, 3 * local_width :][None],
        grad_fc1[None],
        grad_fc2[None],
        rel_grad[None],
        norms_mine[:, 0][None],
        norms_mine[:, 1][None],
    )


def solution(mesh):
    return jax.shard_map(
        local,
        mesh=mesh,
        in_specs=(
            P("dp", "tensor", None),
            P("dp", None),
            P("dp"),
            P("dp", None),
            P(),
            P("section", None, None, "tensor"),
            P("section", None, None, "tensor"),
            P("section", None, "tensor"),
            P("section", None, "tensor"),
            P("section", None, "tensor"),
            P("section", "tensor", None),
            P("section", None, None),
            P("section", None, None),
            P("dp", "tensor", None),
        ),
        out_specs=(
            P("section", "dp", "tensor", None),
            P("section", "dp", "tensor", None),
            P("section", "dp", None, "tensor"),
            P("section", "dp", None, "tensor"),
            P("section", "dp", "tensor"),
            P("section", "dp", "tensor"),
            P("section", "dp", "tensor"),
            P("section", "tensor", None),
            P("section", None, ("dp", "tensor")),
            P("section", None, ("dp", "tensor")),
        ),
        check_vma=False,
    )
```

```python
import functools
import math

import jax
import jax.numpy as jnp
from jax import lax
from jax.experimental import pallas as pl
from jax.experimental.pallas import tpu as pltpu
from jax.sharding import PartitionSpec as P

LOG2E = 1.4426950408889634
HIGHEST = lax.Precision.HIGHEST
PLANE = 7 * 256
WALL = 8 * PLANE


def _labels_hi_lo(lab):
    hi = lax.shift_right_logical(lab, 6)
    lo = jnp.bitwise_and(lab, 63)
    iota = lax.broadcasted_iota(jnp.int32, (64, lab.shape[1]), 0)
    return iota == hi, jnp.where(iota == lo, 1.0, 0.0)


def build_wall(small, out_lab, lab, hi_mask, lo_hot, table, wall_ref):
    rows = lax.dot_general(table, lo_hot, (((1,), (0,)), ((), ())), precision=HIGHEST, preferred_element_type=jnp.float32)
    flat = jnp.sum(jnp.where(hi_mask, rows, 0.0), axis=0, keepdims=True) * LOG2E
    outside = jnp.sum(jnp.where(lab == out_lab, flat, 0.0), axis=1, keepdims=True)
    wide = jnp.broadcast_to(flat, (32, 4096))
    wide = pltpu.roll(wide, 4096 - 31, 1, stride=1, stride_axis=0)
    lane = lax.broadcasted_iota(jnp.int32, (32, 128), 1)
    tight = []
    for g in range(16):
        a = wide[:, 256 * g : 256 * g + 128]
        b = wide[:, 256 * g + 128 : 256 * g + 256]
        piece = jnp.where(lane < 32, a, pltpu.roll(a, 96, 1))
        other = jnp.where(lane < 96, pltpu.roll(b, 64, 1), pltpu.roll(b, 32, 1))
        tight.append(jnp.where(lane < 64, piece, other))
    w0 = jnp.concatenate(tight, axis=1)
    lane16 = lane[:16]
    tight16 = []
    for g in range(8):
        lo_v = w0[:16, 256 * g : 256 * g + 128]
        hi_v = w0[:16, 256 * g + 128 : 256 * g + 256]
        acc = lo_v
        for k in range(1, 4):
            acc = jnp.where(lane16 >= 16 * k, pltpu.roll(lo_v, 128 - 16 * k, 1), acc)
        for k in range(4):
            acc = jnp.where(lane16 >= 64 + 16 * k, pltpu.roll(hi_v, (64 - 16 * k) % 128, 1), acc)
        tight16.append(acc)
    w16 = jnp.concatenate(tight16, axis=1)
    beyond = jnp.broadcast_to(outside, (32, 768))
    tiny = small == 1
    for j in range(8):
        big = w0 if j == 7 else pltpu.roll(w0, 2048 - 32 * (7 - j), 1)
        inner = [pltpu.roll(w16, 1024 - 16 * (31 - 2 * j - k), 1)[:, :256] for k in range(2)]
        inner = jnp.concatenate(inner, axis=0)
        at = j * PLANE
        wall_ref[:, at : at + 768] = jnp.where(tiny, beyond, big[:, :768])
        wall_ref[:, at + 768 : at + 1024] = jnp.where(tiny, inner, big[:, 768:1024])
        wall_ref[:, at + 1024 : at + PLANE] = jnp.where(tiny, beyond, big[:, 1024:PLANE])


def bias_kernel(flags_ref, lab_ref, table_ref, wall_ref):
    lab = lab_ref[...]
    hi_mask, lo_hot = _labels_hi_lo(lab)
    build_wall(flags_ref[0], flags_ref[1], lab, hi_mask, lo_hot, table_ref[0], wall_ref.at[0])


def bias_tables(flags, lab, table):
    heads = table.shape[0]
    return pl.pallas_call(
        bias_kernel,
        grid=(heads,),
        in_specs=[
            pl.BlockSpec(memory_space=pltpu.SMEM),
            pl.BlockSpec((1, 4096), lambda h: (0, 0)),
            pl.BlockSpec((1, 64, 64), lambda h: (h, 0, 0)),
        ],
        out_specs=pl.BlockSpec((1, 32, WALL), lambda h: (h, 0, 0)),
        out_shape=jax.ShapeDtypeStruct((heads, 32, WALL), jnp.float32),
        compiler_params=pltpu.CompilerParams(vmem_limit_bytes=40 << 20),
    )(flags, lab, table)


def wall_grad(small, out_lab, lab, hi_mask, lo_hot, acc_ref):
    tiny = small == 1
    w0 = jnp.zeros((32, 2048), jnp.float32)
    w16 = jnp.zeros((16, 1024), jnp.float32)
    beyond = jnp.zeros((32, 768), jnp.float32)
    for j in range(8):
        at = j * PLANE
        piece = jnp.concatenate([acc_ref[:, at : at + PLANE], jnp.zeros((32, 256), jnp.float32)], axis=1)
        w0 = w0 + (piece if j == 7 else pltpu.roll(piece, 32 * (7 - j), 1))
        beyond = beyond + acc_ref[:, at + 1024 : at + PLANE]
        for k in range(2):
            inner = acc_ref[16 * k : 16 * k + 16, at + 768 : at + 1024]
            inner = jnp.concatenate([inner, jnp.zeros((16, 768), jnp.float32)], axis=1)
            w16 = w16 + pltpu.roll(inner, 16 * (31 - 2 * j - k), 1)
    w0 = jnp.where(tiny, 0.0, w0)
    w16 = jnp.where(tiny, w16, 0.0)
    outside = jnp.sum(jnp.sum(jnp.where(tiny, beyond, 0.0), axis=0, keepdims=True), axis=1, keepdims=True)
    lane = lax.broadcasted_iota(jnp.int32, (32, 128), 1)
    lane16 = lane[:16]
    wide = []
    for g in range(32):
        src = w0[:, 128 * (g // 2) : 128 * (g // 2) + 128]
        k = 2 * (g % 2)
        first = src if k == 0 else pltpu.roll(src, 128 - 32 * k, 1)
        second = pltpu.roll(src, (64 - 32 * (k + 1)) % 128, 1)
        piece = jnp.where(lane < 32, first, jnp.where((lane >= 64) & (lane < 96), second, 0.0))
        src16 = w16[:, 128 * (g // 4) : 128 * (g // 4) + 128]
        k = 2 * (g % 4)
        first = src16 if k == 0 else pltpu.roll(src16, 128 - 16 * k, 1)
        second = pltpu.roll(src16, (64 - 16 * (k + 1)) % 128, 1)
        piece16 = jnp.where(lane16 < 16, first, jnp.where((lane16 >= 64) & (lane16 < 80), second, 0.0))
        wide.append(piece + jnp.concatenate([piece16, jnp.zeros((16, 128), jnp.float32)], axis=0))
    wide = jnp.concatenate(wide, axis=1)
    back = 31 - lax.broadcasted_iota(jnp.int32, (32, 4096), 0)
    for k in range(5):
        wide = jnp.where(jnp.bitwise_and(back, 1 << k) > 0, pltpu.roll(wide, 1 << k, 1), wide)
    flat = jnp.sum(wide, axis=0, keepdims=True)
    flat = flat + jnp.where(lab == out_lab, outside, 0.0)
    spread = jnp.where(hi_mask, jnp.broadcast_to(flat, (64, 4096)), 0.0)
    return lax.dot_general(spread, lo_hot, (((1,), (1,)), ((), ())), precision=HIGHEST, preferred_element_type=jnp.float32)


def bias_grad_kernel(flags_ref, lab_ref, acc_ref, out_ref):
    lab = lab_ref[...]
    hi_mask, lo_hot = _labels_hi_lo(lab)
    out_ref[0] = wall_grad(flags_ref[0], flags_ref[1], lab, hi_mask, lo_hot, acc_ref.at[0])


def bias_grads(flags, lab, acc):
    heads = acc.shape[0]
    return pl.pallas_call(
        bias_grad_kernel,
        grid=(heads,),
        in_specs=[
            pl.BlockSpec(memory_space=pltpu.SMEM),
            pl.BlockSpec((1, 4096), lambda h: (0, 0)),
            pl.BlockSpec((1, 32, WALL), lambda h: (h, 0, 0)),
        ],
        out_specs=pl.BlockSpec((1, 64, 64), lambda h: (h, 0, 0)),
        out_shape=jax.ShapeDtypeStruct((heads, 64, 64), jnp.float32),
        compiler_params=pltpu.CompilerParams(vmem_limit_bytes=40 << 20),
    )(flags, lab, acc)


def label_row(rel_index):
    side = 32
    a = rel_index[0, 1023].reshape(side, side)
    b = rel_index[0, 0].reshape(side, side)
    c = rel_index[0, 992].reshape(side, side)
    d = rel_index[0, 31].reshape(side, side)
    top = jnp.concatenate([a, c[:, 1:]], axis=1)
    low = jnp.concatenate([d[1:], b[1:, 1:]], axis=1)
    grid = jnp.flip(jnp.concatenate([top, low], axis=0), (0, 1))
    return jnp.pad(grid, ((0, 1), (0, 1)), constant_values=4095).reshape(1, 4096)


NT = (((1,), (1,)), ((), ()))
TN = (((0,), (0,)), ((), ()))
NN = (((1,), (0,)), ((), ()))
HD = 72
QB = 256


def dot(a, b, dims):
    return lax.dot_general(a, b, dims, preferred_element_type=jnp.float32)


def head_lanes(x, at, extra=None):
    rows = x.shape[0]
    part = x[:, at : at + HD]
    if extra is None:
        pad = jnp.zeros((rows, 128 - HD), x.dtype)
    else:
        pad = extra
    return jnp.concatenate([part, pad], axis=1)


def quarter(r, c, rel):
    return lax.rem(r + rel % 2, 2) + 2 * lax.rem(c + rel // 2, 2)


def strip_start(q_quarter, jj, kq):
    return pl.multiple_of(PLANE * jj + 256 * (q_quarter - kq + 3), 256)


def attn_block(q_quarter, key_quarters, scale, q_ref, kv_ref, k_extra, wall_ref, lse_ref, s_scr, p_scr):
    heads = wall_ref.shape[0]
    width = heads * HD
    nstrip = kv_ref.shape[0] // 32
    lane = lax.broadcasted_iota(jnp.int32, (QB, 128 - HD), 1)
    q_extra = jnp.where(lane == 0, 1.0, 0.0).astype(jnp.bfloat16)
    outs = []
    for h in range(heads):
        kh = head_lanes(kv_ref, width + HD * h, k_extra)
        qh = head_lanes(q_ref, HD * h, q_extra)
        vh = head_lanes(kv_ref, 2 * width + HD * h)
        s_scr[h % 2] = dot(kh, qh, NT)
        top = None
        for st in range(nstrip):
            start = strip_start(q_quarter, st % 8, key_quarters[st // 8])
            s = s_scr[h % 2, 32 * st : 32 * st + 32] * (scale * LOG2E) + wall_ref[h, :, pl.ds(start, QB)]
            s_scr[h % 2, 32 * st : 32 * st + 32] = s
            top = s if top is None else jnp.maximum(top, s)
        row_max = jnp.max(top, axis=0, keepdims=True)
        total = None
        for st in range(nstrip):
            p = jnp.exp2(s_scr[h % 2, 32 * st : 32 * st + 32] - row_max)
            p_scr[h % 2, 32 * st : 32 * st + 32] = p.astype(jnp.bfloat16)
            total = p if total is None else total + p
        row_sum = jnp.sum(total, axis=0, keepdims=True)
        o_t = dot(vh, p_scr[h % 2], TN) * (1.0 / row_sum)
        lse_ref[h : h + 1, :] = row_max + jnp.log2(row_sum)
        outs.append(o_t.T[:, :HD].astype(jnp.bfloat16))
    return jnp.concatenate(outs, axis=1)


def attn_fwd_kernel(order, scale, sc_ref, q_ref, kv_ref, mask_ref, wall_ref, o_ref, lse_ref, s_scr, p_scr):
    r, c = sc_ref[0], sc_ref[1]
    qq = quarter(r, c, sc_ref[2 + pl.program_id(0)])
    keys = [quarter(r, c, j) for j in order]
    o_ref[...] = attn_block(
        qq, keys, scale, q_ref, kv_ref, mask_ref[...], wall_ref, lse_ref.at[0], s_scr, p_scr
    )


def attn_fwd(qkv, mask_pad, wall, scalars, order, scale):
    rows, wide = qkv.shape
    nq = rows // QB
    heads = wall.shape[0]
    width = heads * HD
    return pl.pallas_call(
        functools.partial(attn_fwd_kernel, order, scale),
        grid=(nq,),
        in_specs=[
            pl.BlockSpec(memory_space=pltpu.SMEM),
            pl.BlockSpec((QB, wide), lambda i: (i, 0)),
            pl.BlockSpec((rows, wide), lambda i: (0, 0)),
            pl.BlockSpec((rows, 128 - HD), lambda i: (0, 0)),
            pl.BlockSpec((heads, 32, WALL), lambda i: (0, 0, 0), pipeline_mode=pl.Buffered(1)),
        ],
        out_specs=[pl.BlockSpec((QB, width), lambda i: (i, 0)), pl.BlockSpec((1, heads, QB), lambda i: (i, 0, 0))],
        out_shape=[jax.ShapeDtypeStruct((rows, width), jnp.bfloat16), jax.ShapeDtypeStruct((nq, heads, QB), jnp.float32)],
        scratch_shapes=[pltpu.VMEM((2, rows, QB), jnp.float32), pltpu.VMEM((2, rows, QB), jnp.bfloat16)],
        compiler_params=pltpu.CompilerParams(vmem_limit_bytes=40 << 20),
        cost_estimate=pl.CostEstimate(flops=16 << 30, bytes_accessed=12 << 20, transcendentals=0),
    )(scalars, qkv, qkv, mask_pad, wall)


def attn_bwd_kernel(order, scale, sc_ref, q_ref, kv_ref, do_ref, o_ref, lse_ref, mask_ref, wall_ref,
                    dqkv_ref, acc_ref, p_scr, s_scr, dq_scr, dk_scr, dv_scr):
    step = pl.program_id(0)
    r, c = sc_ref[0], sc_ref[1]
    qq = quarter(r, c, sc_ref[2 + step])
    keys = [quarter(r, c, j) for j in order]
    heads = wall_ref.shape[0]
    width = heads * HD
    rows = kv_ref.shape[0]

    @pl.when(step == 0)
    def _():
        acc_ref[...] = jnp.zeros_like(acc_ref)
        dk_scr[...] = jnp.zeros_like(dk_scr)
        dv_scr[...] = jnp.zeros_like(dv_scr)

    k_extra = mask_ref[...]
    lane = lax.broadcasted_iota(jnp.int32, (QB, 128 - HD), 1)
    q_extra = jnp.where(lane == 0, 1.0, 0.0).astype(jnp.bfloat16)
    dqs = []
    for h in range(heads):
        kh = head_lanes(kv_ref, width + HD * h, k_extra)
        qh = head_lanes(q_ref, HD * h, q_extra)
        vh = head_lanes(kv_ref, 2 * width + HD * h)
        doh = head_lanes(do_ref, HD * h)
        oh = head_lanes(o_ref, HD * h)
        inner = jnp.sum((doh.astype(jnp.float32) * oh.astype(jnp.float32)).T, axis=0, keepdims=True)
        lse = lse_ref[0, h : h + 1, :]
        for kb in range(rows // 256):
            s_t = dot(kh[256 * kb : 256 * kb + 256], qh, NT)
            dp_t = dot(vh[256 * kb : 256 * kb + 256], doh, NT)
            for js in range(8):
                st = 8 * kb + js
                start = strip_start(qq, js, keys[kb])
                s = s_t[32 * js : 32 * js + 32] * (scale * LOG2E) + wall_ref[h, :, pl.ds(start, QB)]
                p = jnp.exp2(s - lse)
                ds = p * (dp_t[32 * js : 32 * js + 32] - inner)
                p_scr[h % 2, 32 * st : 32 * st + 32] = p.astype(jnp.bfloat16)
                s_scr[h % 2, 32 * st : 32 * st + 32] = ds.astype(jnp.bfloat16)
                acc_ref[h, :, pl.ds(start, QB)] += ds
        p_b, ds_b = p_scr[h % 2], s_scr[h % 2]
        dv_scr[h] += dot(p_b, doh, NN)
        dk_scr[h] += dot(ds_b, qh, NN)
        dq_t = dot(kh, ds_b, TN) * scale
        dqs.append(dq_t.T[:, :HD].astype(jnp.bfloat16))
    dq_scr[pl.ds(pl.multiple_of(step * QB, QB), QB)] = jnp.concatenate(dqs, axis=1)

    @pl.when(step == pl.num_programs(0) - 1)
    def _():
        parts = [dq_scr[...]]
        parts += [(dk_scr[h, :, :HD] * scale).astype(jnp.bfloat16) for h in range(heads)]
        parts += [dv_scr[h, :, :HD].astype(jnp.bfloat16) for h in range(heads)]
        dqkv_ref[...] = jnp.concatenate(parts, axis=1)


def attn_bwd(qkv, do, o, lse, mask_pad, wall, scalars, order, scale):
    rows, wide = qkv.shape
    nq = rows // QB
    heads = wall.shape[0]
    width = heads * HD
    row_spec = pl.BlockSpec((QB, width), lambda i: (i, 0))
    return pl.pallas_call(
        functools.partial(attn_bwd_kernel, order, scale),
        grid=(nq,),
        in_specs=[
            pl.BlockSpec(memory_space=pltpu.SMEM),
            pl.BlockSpec((QB, wide), lambda i: (i, 0)),
            pl.BlockSpec((rows, wide), lambda i: (0, 0)),
            row_spec,
            row_spec,
            pl.BlockSpec((1, heads, QB), lambda i: (i, 0, 0)),
            pl.BlockSpec((rows, 128 - HD), lambda i: (0, 0)),
            pl.BlockSpec((heads, 32, WALL), lambda i: (0, 0, 0), pipeline_mode=pl.Buffered(1)),
        ],
        out_specs=[pl.BlockSpec((rows, wide), lambda i: (0, 0)), pl.BlockSpec((heads, 32, WALL), lambda i: (0, 0, 0))],
        out_shape=[jax.ShapeDtypeStruct((rows, wide), jnp.bfloat16), jax.ShapeDtypeStruct((heads, 32, WALL), jnp.float32)],
        scratch_shapes=[
            pltpu.VMEM((2, rows, QB), jnp.bfloat16),
            pltpu.VMEM((2, rows, QB), jnp.bfloat16),
            pltpu.VMEM((rows, width), jnp.bfloat16),
            pltpu.VMEM((heads, rows, 128), jnp.float32),
            pltpu.VMEM((heads, rows, 128), jnp.float32),
        ],
        compiler_params=pltpu.CompilerParams(vmem_limit_bytes=48 << 20),
        cost_estimate=pl.CostEstimate(flops=24 << 30, bytes_accessed=20 << 20, transcendentals=0),
    )(scalars, qkv, qkv, do, o, lse, mask_pad, wall)


EPSILON = 1e-05
NCH = 2
GELU_C = math.sqrt(2.0 / math.pi)


def normed(x):
    center = x - jnp.mean(x, axis=-1, keepdims=True)
    spread = jnp.mean(center * center, axis=-1, keepdims=True)
    r = lax.rsqrt(spread + EPSILON)
    return center * r, r


def norm_back(x, dy, gain):
    xhat, r = normed(x)
    dxhat = dy * gain
    dx = r * (
        dxhat
        - jnp.mean(dxhat, axis=-1, keepdims=True)
        - xhat * jnp.mean(dxhat * xhat, axis=-1, keepdims=True)
    )
    return dx, jnp.sum(dy * xhat, axis=0, keepdims=True), jnp.sum(dy, axis=0, keepdims=True)


def gelu_both(u):
    th = jnp.tanh(GELU_C * (u + 0.044715 * u * u * u))
    half = 0.5 * (1.0 + th)
    slope = half + 0.5 * u * (1.0 - th * th) * GELU_C * (1.0 + 3 * 0.044715 * u * u)
    return u * half, slope


class Links:
    def __init__(self, send_sem, recv_sem, bits=0):
        z, c = lax.axis_index("tensor"), lax.axis_index("section")
        self.z, self.c = z, c
        self.pair = z // 2
        self.r = lax.rem(z, 2)
        self.home = c == self.pair
        across = z + 2 - 4 * self.pair
        self.ids = {
            PARTNER: {"tensor": z + 1 - 2 * self.r},
            SIBLING: {"section": 1 - c},
            FAR: {"tensor": across, "section": self.pair},
            HOME: {"section": self.pair},
        }
        self.greet = [self.ids[PARTNER], self.ids[SIBLING]]
        self.dp_bit = []
        if bits:
            d = lax.axis_index("dp")
            for b in range(bits):
                bit = lax.rem(d // (1 << b), 2)
                self.dp_bit.append(bit)
                self.ids["dp", b] = {"dp": d + (1 - 2 * bit) * (1 << b)}
                self.greet.append(self.ids["dp", b])
            self.greet += [{"tensor": across}, {"tensor": across, "section": 1 - c}]
        self.ids[ACROSS] = {"tensor": across}
        for layer in range(2):
            self.ids["return", layer] = {"tensor": across, "section": layer}
        self.send_sem, self.recv_sem = send_sem, recv_sem
        self.used = 0
        self.started = []

    def enter(self):
        barrier = pltpu.get_barrier_semaphore()
        for where in self.greet:
            pl.semaphore_signal(barrier, inc=1, device_id=where, device_id_type=pl.DeviceIdType.MESH)
        pl.semaphore_wait(barrier, len(self.greet))

    def make(self, src, dst, to, cond=None, track=True):
        k = self.used
        self.used += 1
        copy = pltpu.make_async_remote_copy(
            src_ref=src,
            dst_ref=dst,
            send_sem=self.send_sem.at[k],
            recv_sem=self.recv_sem.at[k],
            device_id=self.ids[to],
            device_id_type=pl.DeviceIdType.MESH,
        )
        if track:
            self.started.append((copy, cond))
        return copy

    def send(self, src, dst, to, cond=None, track=True):
        copy = self.make(src, dst, to, cond, track)
        when(cond, copy.start)
        return copy

    def leave(self):
        for copy, cond in self.started:
            when(cond, copy.wait_send)


def when(cond, do):
    if cond is None:
        do()
    else:
        pl.when(cond)(lambda: do())


PARTNER, SIBLING, FAR, HOME, ACROSS = "partner", "sibling", "far", "home", "across"


class Spread:
    COPIES = 2

    def __init__(self, links, layer, src, out, sem):
        self.links, self.layer, self.src, self.out, self.sem = links, layer, src, out, sem

    def start(self):
        links = self.links
        mine = links.c == self.layer
        keeps = links.pair == self.layer
        self.local = pltpu.make_async_copy(self.src, self.out, self.sem)
        when(mine & keeps, self.local.start)
        self.near = links.send(self.src, self.out, HOME, mine & jnp.logical_not(keeps))
        self.far = links.send(self.src, self.out, FAR, mine)

    def done(self):
        links = self.links
        keeps = links.pair == self.layer
        when(links.home & keeps, self.local.wait)
        when(links.home & jnp.logical_not(keeps), self.near.wait_recv)
        when(jnp.logical_not(links.home), self.far.wait_recv)


def bits_region(links, gathered, cols=None):
    index = []
    for b in reversed(range(len(links.dp_bit))):
        index.append(pl.ds(0, 2) if b in gathered else links.dp_bit[b])
    return tuple(index) + (() if cols is None else (slice(None), cols))


class Deliver:
    COPIES = 2

    def __init__(self, links, layer, src, out, sem=None):
        self.links, self.layer, self.src, self.out, self.sem = links, layer, src, out, sem

    def start(self):
        links = self.links
        mine = links.c == self.layer
        keeps = links.pair == self.layer
        if self.sem is not None:
            self.local = pltpu.make_async_copy(self.src, self.out, self.sem)
            when(mine & keeps, self.local.start)
        at = bits_region(links, ())
        self.far = links.send(self.src.at[at], self.out.at[at], FAR, mine)
        self.near = links.send(self.src, self.out, HOME, mine & jnp.logical_not(keeps))

    def done(self):
        links = self.links
        keeps = links.pair == self.layer
        if self.sem is not None:
            when(links.home & keeps, self.local.wait)
        when(links.home & jnp.logical_not(keeps), self.near.wait_recv)
        when(jnp.logical_not(links.home), self.far.wait_recv)


class Exchange:
    def __init__(self, links, buf):
        self.links, self.buf = links, buf
        columns = buf.shape[-1]
        cut = columns // 256 * 128
        order = list(range(len(links.dp_bit)))
        self.halves = [(pl.ds(0, cut), order), (pl.ds(cut, columns - cut), order[::-1])]
        self.away = jnp.logical_not(links.home)
        self.last = None

    @staticmethod
    def copies(bits):
        return 2 * bits

    def step(self, s):
        self.done()
        self.last = []
        for cols, order in self.halves:
            at = bits_region(self.links, order[:s], cols)
            self.last.append(self.links.send(self.buf.at[at], self.buf.at[at], ("dp", order[s]), self.away))

    def done(self):
        for copy in self.last or ():
            when(self.away, copy.wait_recv)


class Part:
    def __init__(self, links, layer, own, got, dst, sem):
        at = bits_region(links, ())
        keeps = links.pair == layer
        self.ways = (
            (links.home & keeps, pltpu.make_async_copy(own, dst, sem)),
            (links.home & jnp.logical_not(keeps), pltpu.make_async_copy(got, dst, sem)),
            (jnp.logical_not(links.home), pltpu.make_async_copy(got.at[at], dst.at[at], sem)),
        )

    def start(self):
        for cond, copy in self.ways:
            when(cond, copy.start)
        return self

    def wait(self):
        for cond, copy in self.ways:
            when(cond, copy.wait)


def chunk(i, rows):
    return pl.ds(i * (rows // NCH), rows // NCH)


class Scatter:
    COPIES = 3 * NCH

    def __init__(self, links, low, wide):
        self.links, self.low, self.wide = links, low, wide
        self.rows = low.shape[1]
        self.copies = {}

    def far(self, i, p2, p3):
        at = chunk(i, self.rows)
        self.low[0, at] = p3.astype(jnp.bfloat16)
        self.copies["a", i] = self.links.send(self.low.at[0, at], self.low.at[3, at], SIBLING)
        self.wide[0, at] = p2

    def middle(self, i):
        at = chunk(i, self.rows)
        self.copies["a", i].wait_recv()
        self.low[1, at] = (self.wide[0, at] + self.low[3, at].astype(jnp.float32)).astype(jnp.bfloat16)
        self.copies["z", i] = self.links.send(self.low.at[1, at], self.low.at[4, at], PARTNER)

    def near(self, i, p0, p1):
        at = chunk(i, self.rows)
        self.low[2, at] = p1.astype(jnp.bfloat16)
        self.copies["b", i] = self.links.send(self.low.at[2, at], self.low.at[5, at], SIBLING)
        self.wide[1, at] = p0

    def release(self):
        for copy in self.copies.values():
            copy.wait_send()
        self.links.started = [s for s in self.links.started if all(s[0] is not c for c in self.copies.values())]
        self.copies = {}

    def done(self, i):
        at = chunk(i, self.rows)
        self.copies["b", i].wait_recv()
        self.copies["z", i].wait_recv()
        return self.wide[1, at] + self.low[5, at].astype(jnp.float32) + self.low[4, at].astype(jnp.float32)


class Gather:
    COPIES = 3 * NCH

    def __init__(self, links, buf):
        self.links, self.buf = links, buf
        self.rows = buf.shape[1]
        self.copies = {}

    def send(self, i, x):
        at = chunk(i, self.rows)
        self.buf[0, at] = x
        self.copies["z", i] = self.links.send(self.buf.at[0, at], self.buf.at[2, at], PARTNER)
        self.copies["s", i] = self.links.send(self.buf.at[0, at], self.buf.at[1, at], SIBLING)

    def forward(self, i):
        at = chunk(i, self.rows)
        self.copies["z", i].wait_recv()
        self.copies["f", i] = self.links.send(self.buf.at[2, at], self.buf.at[3, at], SIBLING)

    def done(self, i):
        self.copies["s", i].wait_recv()
        self.copies["f", i].wait_recv()
        at = chunk(i, self.rows)
        n = self.rows // NCH
        return jnp.concatenate([self.buf[b, at] for b in range(4)], axis=0)


class DpReduce:
    COPIES = 4

    def __init__(self, links, buf, land0, land1=None, sent=None):
        self.links, self.buf, self.land0, self.land1, self.sent = links, buf, land0, land1, sent
        columns = buf.shape[-1]
        cut = columns // 256 * 128
        self.cols = (pl.ds(0, cut), pl.ds(cut, columns - cut))
        self.orders = ((0, 1), (1, 0))
        self.mine = links.dp_bit
        self.other = [1 - bit for bit in links.dp_bit]
        self.first, self.second = [], []
        for (b0, b1), h, cols in zip(self.orders, range(2), self.cols):
            at = self.place(h, self.other[b0], pl.ds(0, 2))
            self.first.append(links.make(buf.at[at + (slice(None), cols)], land0.at[:, :, cols], ("dp", b0)))
            if land1 is not None:
                self.second.append(links.make(sent.at[0, :, cols], land1.at[0, :, cols], ("dp", b1)))

    @staticmethod
    def scratch(n, columns):
        return [pltpu.VMEM((k, n, columns), jnp.bfloat16) for k in (2, 1, 1)]

    def place(self, h, first, second):
        return (second, first) if self.orders[h][0] == 0 else (first, second)

    def start(self):
        for copy in self.first:
            copy.start()

    def half(self, h, cols):
        b0, b1 = self.orders[h]
        self.first[h].wait_recv()
        sums = []
        for second in (self.other[b1], self.mine[b1]):
            own = self.buf[self.place(h, self.mine[b0], second) + (slice(None), cols)]
            sums.append(own.astype(jnp.float32) + self.land0[second, :, cols].astype(jnp.float32))
        return sums

    def split(self, sent, kept):
        for h, cols in enumerate(self.cols):
            sums = self.half(h, cols)
            sent[:, cols] = sums[0].astype(jnp.bfloat16)
            kept[:, cols] = sums[1].astype(jnp.bfloat16)

    def middle(self):
        for h, cols in enumerate(self.cols):
            b0, b1 = self.orders[h]
            sums = self.half(h, cols)
            self.sent[0, :, cols] = sums[0].astype(jnp.bfloat16)
            self.buf[self.place(h, self.mine[b0], self.mine[b1]) + (slice(None), cols)] = sums[1].astype(jnp.bfloat16)
            self.second[h].start()

    def done(self, out):
        for h, cols in enumerate(self.cols):
            self.second[h].wait_recv()
            b0, b1 = self.orders[h]
            own = self.buf[self.place(h, self.mine[b0], self.mine[b1]) + (slice(None), cols)]
            out[:, cols] = (own.astype(jnp.float32) + self.land1[0, :, cols].astype(jnp.float32)).astype(out.dtype)


class DpFinish:
    COPIES = 2

    def __init__(self, links, sent, kept, land):
        self.kept, self.land = kept, land
        columns = sent.shape[-1]
        cut = columns // 256 * 128
        self.cols = (pl.ds(0, cut), pl.ds(cut, columns - cut))
        self.copies = [
            links.make(sent.at[:, cols], land.at[:, cols], ("dp", b)) for cols, b in zip(self.cols, (1, 0))
        ]

    def start(self):
        for copy in self.copies:
            copy.start()

    def done(self, out):
        for copy, cols in zip(self.copies, self.cols):
            copy.wait_recv()
            out[:, cols] = (self.kept[:, cols].astype(jnp.float32) + self.land[:, cols].astype(jnp.float32)).astype(out.dtype)


class Return:
    COPIES = 2

    def __init__(self, links, layer, src, near, far):
        self.links, self.layer = links, layer
        self.home, self.away = links.home, jnp.logical_not(links.home)
        self.here = links.c == layer
        self.near_cond = self.home & jnp.logical_not(self.here)
        self.near = links.make(src, near, SIBLING, self.near_cond)
        self.far = links.make(src, far, ("return", layer), self.away)

    def start(self):
        when(self.near_cond, self.near.start)
        when(self.away, self.far.start)

    def done(self):
        when(self.here & self.away, self.near.wait_recv)
        when(self.here, self.far.wait_recv)


def start_load(src, dst, sem):
    copy = pltpu.make_async_copy(src, dst, sem)
    copy.start()
    return copy


def block_rows(ref, b, i, rows):
    n = rows // NCH
    return ref[pl.ds(b * rows + i * n, n)]


def put_rows(ref, value, i, rows):
    n = rows // NCH
    for b in range(4):
        ref[pl.ds(b * rows + i * n, n)] = value[b * n : (b + 1) * n]


def weight_grad(out, col, x, y):
    width = x.shape[1]
    step = 384
    for k in range(0, width, step):
        out[k : k + step, col : col + y.shape[1]] = dot(x[:, k : k + step], y, TN).astype(out.dtype)


def flat(ref):
    return ref[...].reshape(-1, ref.shape[-1])


def scatter_product(scatter, i, lhs, weight, rows):
    p = dot(jnp.concatenate([lhs(2), lhs(3)], axis=0), weight, NT)
    n = rows // NCH
    scatter.far(i, p[:n], p[n:])
    p = dot(jnp.concatenate([lhs(0), lhs(1)], axis=0), weight, NT)
    scatter.near(i, p[:n], p[n:])


def slab_grad(out, col, x, y):
    n = out.shape[2]
    width = x.shape[1]
    step = 384
    for k in range(0, width, step):
        res = dot(x[:, k : k + step], y, TN).astype(out.dtype)
        at = k
        while at < k + step:
            slab = at // n
            stop = min(k + step, (slab + 1) * n)
            out[slab // 2, slab % 2, at - slab * n : stop - slab * n, col : col + y.shape[1]] = res[at - k : stop - k]
            at = stop


def block_quarter(links, i):
    return lax.rem(links.r + i // 2, 2) + 2 * lax.rem(links.c + lax.rem(i, 2), 2)


def mid_kernel(order, scale, bits, x_ref, o_ref, ln_ref, cot_ref, live_ref, term_ref, mask_ref,
               wp_hbm, got1_hbm, got2_hbm, wall_hbm, own_q, own_p, own_1, own_2,
               hid_ref, act_ref, dy_ref, o1_ref, lse_ref,
               n2_hbm, u_hbm, g_hbm, n1_hbm, qkv_hbm, dm_hbm, w1_out, w2_out, next_q, next_p, next_1, next_2,
               wp, w1, w2, got_q, got_p, wall, u_buf, g_buf, qkv, gat1, gat2, gat3, low, wide, s_scr, p_scr,
               load_sem, store_sem, send_sem, recv_sem):
    rows, width = x_ref.shape
    n = rows // NCH
    links = Links(send_sem, recv_sem, bits)
    load_p = start_load(wp_hbm, wp, load_sem.at[0])
    load_1 = Part(links, 0, own_1, got1_hbm, w1, load_sem.at[1]).start()
    load_2 = Part(links, 0, own_2, got2_hbm, w2, load_sem.at[2]).start()
    load_w = start_load(wall_hbm, wall, load_sem.at[3])
    links.enter()
    ex1, ex2 = Exchange(links, w1), Exchange(links, w2)
    exq, exp = Exchange(links, got_q), Exchange(links, got_p)
    get_q, get_p = Deliver(links, 1, own_q, got_q, load_sem.at[4]), Deliver(links, 1, own_p, got_p, load_sem.at[5])
    get_1, get_2 = Deliver(links, 1, own_1, next_1), Deliver(links, 1, own_2, next_2)
    s1, s2 = Scatter(links, low, wide), Scatter(links, low, wide)
    g1, g2, g3 = Gather(links, gat1), Gather(links, gat2), Gather(links, gat3)
    load_p.wait()
    for i in range(NCH):
        scatter_product(s1, i, lambda b: block_rows(o_ref, b, i, rows), wp[...], rows)
    load_1.wait()
    ex1.step(0)
    load_2.wait()
    ex2.step(0)
    for i in range(NCH):
        s1.middle(i)
    for s in range(1, bits):
        ex1.step(s)
    get_q.start()
    get_p.start()
    for i in range(NCH):
        h = x_ref[chunk(i, rows)].astype(jnp.float32) + s1.done(i)
        hid_ref[chunk(i, rows)] = h
        g1.send(i, (normed(h)[0] * ln_ref[0:1] + ln_ref[1:2]).astype(jnp.bfloat16))
        if i == 0:
            for s in range(1, bits):
                ex2.step(s)
    s1.release()

    def mlp(i):
        u = dot(g1.done(i), w1[...].reshape(width, -1), NN)
        put_rows(u_buf, u.astype(jnp.bfloat16), i, rows)
        g = gelu_both(u)[0].astype(jnp.bfloat16)
        put_rows(g_buf, g, i, rows)
        if i == 0:
            ex2.done()
        scatter_product(s2, i, lambda b: g[b * n : (b + 1) * n], w2[...].reshape(width, -1), rows)

    g1.forward(0)
    ex1.done()
    mlp(0)
    g1.forward(1)
    s2.middle(0)
    mlp(1)
    s2.middle(1)
    stores = [
        start_load(src, dst, store_sem.at[k])
        for k, (src, dst) in enumerate(((gat1, n2_hbm), (u_buf, u_hbm), (g_buf, g_hbm), (w1, w1_out), (w2, w2_out)))
    ]
    get_q.done()
    exq.step(0)
    for i in range(NCH):
        act = (hid_ref[chunk(i, rows)] + s2.done(i)).astype(jnp.bfloat16)
        act_ref[chunk(i, rows)] = act
        g2.send(i, (normed(act.astype(jnp.float32))[0] * ln_ref[2:3] + ln_ref[3:4]).astype(jnp.bfloat16))
    for i in range(NCH):
        at = chunk(i, rows)
        dy = cot_ref[at].astype(jnp.float32) * live_ref[at]
        dy_ref[at] = dy
        g3.send(i, dy.astype(jnp.bfloat16))
    get_1.start()
    get_2.start()
    for s in range(1, bits):
        exq.step(s)
    get_p.done()
    exp.step(0)
    for i in range(NCH):
        g2.forward(i)
    exq.done()
    weight = got_q[...].reshape(width, -1)
    for i in range(NCH):
        part = (dot(g2.done(i), weight, NN) + term_ref[0:1]).astype(jnp.bfloat16)
        put_rows(qkv, part, i, rows)
    for s in range(1, bits):
        exp.step(s)
    stores += [
        start_load(src, dst, store_sem.at[5 + k])
        for k, (src, dst) in enumerate(((gat2, n1_hbm), (qkv, qkv_hbm), (got_q, next_q)))
    ]
    load_w.wait()
    keys = [quarter(links.r, links.c, j) for j in order]

    def block(i, carry):
        at = pl.ds(pl.multiple_of(i * QB, QB), QB)
        o1_ref[at] = attn_block(
            block_quarter(links, i), keys, scale, qkv.at[at], qkv, mask_ref[...], wall, lse_ref.at[i], s_scr, p_scr
        )
        return carry

    lax.fori_loop(0, 4, block, 0)
    for i in range(NCH):
        g3.forward(i)
    exp.done()
    stores.append(start_load(got_p, next_p, store_sem.at[8]))
    for i in range(NCH):
        g3.copies["s", i].wait_recv()
        g3.copies["f", i].wait_recv()
    stores.append(start_load(gat3, dm_hbm, store_sem.at[9]))
    get_1.done()
    get_2.done()
    links.leave()
    for store in stores:
        store.wait()


VM = pl.BlockSpec(memory_space=pltpu.VMEM)
HB = pl.BlockSpec(memory_space=pl.ANY)


def comm_scratch(copies):
    return [pltpu.SemaphoreType.DMA((copies,)), pltpu.SemaphoreType.DMA((copies,))]


def scatter_scratch(rows, width):
    return [pltpu.VMEM((6, rows, width), jnp.bfloat16), pltpu.VMEM((2, rows, width), jnp.float32)]


def params(ident):
    return pltpu.CompilerParams(collective_id=ident, has_side_effects=True, vmem_limit_bytes=52 << 20)


def mid_chain(x, o, ln, cot, live, term, mask_pad, wp, w1, w2, wall, own, order, scale):
    rows, width = x.shape
    hidden = w1.shape[-1]
    bits = w1.ndim - 2
    heads = wall.shape[0]
    wide = own[0].shape[-1]
    bf16, f32 = jnp.bfloat16, jnp.float32
    out = jax.ShapeDtypeStruct
    res = pl.pallas_call(
        functools.partial(mid_kernel, order, scale, bits),
        in_specs=[VM] * 7 + [HB] * 8,
        out_specs=[VM] * 5 + [HB] * 12,
        out_shape=[
            out((rows, width), f32),
            out((rows, width), bf16),
            out((rows, width), f32),
            out((4 * rows, heads * HD), bf16),
            out((4, heads, QB), f32),
            out((4, rows, width), bf16),
            out((4 * rows, hidden), bf16),
            out((4 * rows, hidden), bf16),
            out((4, rows, width), bf16),
            out((4 * rows, wide), bf16),
            out((4, rows, width), bf16),
        ]
        + [out(w.shape, bf16) for w in (w1, w2, *own)],
        scratch_shapes=[
            *[pltpu.VMEM(w.shape, bf16) for w in (wp, w1, w2, *own[:2])],
            pltpu.VMEM(wall.shape, f32),
            pltpu.VMEM((4 * rows, hidden), bf16),
            pltpu.VMEM((4 * rows, hidden), bf16),
            pltpu.VMEM((4 * rows, wide), bf16),
            pltpu.VMEM((4, rows, width), bf16),
            pltpu.VMEM((4, rows, width), bf16),
            pltpu.VMEM((4, rows, width), bf16),
            *scatter_scratch(rows, width),
            pltpu.VMEM((2, 4 * rows, QB), f32),
            pltpu.VMEM((2, 4 * rows, QB), bf16),
            pltpu.SemaphoreType.DMA((6,)),
            pltpu.SemaphoreType.DMA((10,)),
            *comm_scratch(2 * Scatter.COPIES + 3 * Gather.COPIES + 4 * Deliver.COPIES + 4 * Exchange.copies(bits)),
        ],
        compiler_params=params(1),
        cost_estimate=pl.CostEstimate(flops=60 << 30, bytes_accessed=24 << 20, transcendentals=0),
    )(x, o, ln, cot, live, term, mask_pad, wp, w1, w2, wall, *own)
    hid, act, dy, o1, lse, n2, u, g, n1, qkv, dm = res[:11]
    rest = lambda v: v.reshape(4 * rows, width)
    return hid, act, dy, o1, lse, rest(n2), u, g, rest(n1), qkv, rest(dm), res[11:13], res[13:]


def turn_kernel(bits, fold, x_ref, o_ref, dy_ref, ln_ref, dm_hbm, wp_hbm, own1, own2, got1, got2,
                dh_ref, norm_ref, hid_ref, do_ref, fc2_sent, fc2_ref, y_hbm, da_hbm, fc1_hbm,
                wp, w1, w2, dm, g_buf, du_buf, y_buf, fc1, fc2, gat1, gat2, low, wide, *refs):
    lands, (load_sem, store_sem, send_sem, recv_sem) = refs[:-4], refs[-4:]
    rows, width = x_ref.shape
    n = rows // NCH
    links = Links(send_sem, recv_sem, bits)
    loads = [
        start_load(wp_hbm, wp, load_sem.at[0]),
        Part(links, 1, own1, got1, w1, load_sem.at[1]).start(),
        Part(links, 1, own2, got2, w2, load_sem.at[2]).start(),
        start_load(dm_hbm, dm, load_sem.at[3]),
    ]
    links.enter()
    ex1, ex2 = Exchange(links, w1), Exchange(links, w2)
    s1, s2 = Scatter(links, low, wide), Scatter(links, low, wide)
    g1, g2 = Gather(links, gat1), Gather(links, gat2)
    loads[0].wait()
    for i in range(NCH):
        scatter_product(s1, i, lambda b: block_rows(o_ref, b, i, rows), wp[...], rows)
    loads[1].wait()
    ex1.step(0)
    loads[2].wait()
    ex2.step(0)
    for i in range(NCH):
        s1.middle(i)
    for s in range(1, bits):
        ex1.step(s)
    for i in range(NCH):
        h = x_ref[chunk(i, rows)].astype(jnp.float32) + s1.done(i)
        hid_ref[chunk(i, rows)] = h
        g1.send(i, (normed(h)[0] * ln_ref[0:1] + ln_ref[1:2]).astype(jnp.bfloat16))
        if i == 0:
            for s in range(1, bits):
                ex2.step(s)
    s1.release()
    loads[3].wait()

    def mlp(i):
        u = dot(g1.done(i), w1[...].reshape(width, -1), NN)
        g, slope = gelu_both(u)
        put_rows(g_buf, g.astype(jnp.bfloat16), i, rows)
        dmi = jnp.concatenate([block_rows(dm, b, i, rows) for b in range(4)], axis=0)
        du = (dot(dmi, w2[...].reshape(width, -1), NN) * slope).astype(jnp.bfloat16)
        put_rows(du_buf, du, i, rows)
        scatter_product(s2, i, lambda b: du[b * n : (b + 1) * n], w1[...].reshape(width, -1), rows)

    g1.forward(0)
    ex1.done()
    ex2.done()
    mlp(0)
    g1.forward(1)
    s2.middle(0)
    mlp(1)
    s2.middle(1)
    slab_grad(fc2, 0, dm[...], g_buf[...])
    if fold:
        reduce = DpReduce(links, fc2, lands[0])
        reduce.start()
    sums = None
    for i in range(NCH):
        at = chunk(i, rows)
        dx, dgain, dshift = norm_back(hid_ref[at], s2.done(i), ln_ref[0:1])
        dh = dy_ref[at] + dx
        dh_ref[at] = dh
        g2.send(i, dh.astype(jnp.bfloat16))
        both = jnp.concatenate([dgain, dshift], axis=0)
        sums = both if sums is None else sums + both
    norm_ref[...] = sums
    slab_grad(fc1, 0, flat(gat1), du_buf[...])
    stores = [start_load(fc1, fc1_hbm, store_sem.at[0])]
    g2.forward(0)
    for b in range(4):
        y = dot(g_buf[pl.ds(b * rows, rows)], w2[...].reshape(width, -1), NT)
        y_buf[pl.ds(b * rows, rows)] = y.astype(jnp.bfloat16)
    stores.append(start_load(y_buf, y_hbm, store_sem.at[1]))
    g2.forward(1)
    for i in range(NCH):
        put_rows(do_ref, dot(g2.done(i), wp[...], NN).astype(jnp.bfloat16), i, rows)
    stores.append(start_load(gat2, da_hbm, store_sem.at[2]))
    if fold:
        reduce.split(fc2_sent, fc2_ref)
    else:
        fc2_ref[...] = fc2[...]
    links.leave()
    for store in stores:
        store.wait()


def turn_chain(ndp, x, o, dy, ln, dm, wp, own, got):
    rows, width = x.shape
    hidden = own[0].shape[-1]
    bits = own[0].ndim - 2
    fold = ndp == 4
    lw = wp.shape[1]
    n = width // 4
    bf16, f32 = jnp.bfloat16, jnp.float32
    out = jax.ShapeDtypeStruct
    res = pl.pallas_call(
        functools.partial(turn_kernel, bits, fold),
        in_specs=[VM, VM, VM, VM] + [HB] * 6,
        out_specs=[VM] * 6 + [HB] * 3,
        out_shape=[
            out((rows, width), f32),
            out((2, width), f32),
            out((rows, width), f32),
            out((4 * rows, lw), bf16),
            out((n, hidden), bf16),
            out((n, hidden) if fold else (2, 2, n, hidden), bf16),
            out((4 * rows, width), bf16),
            out((4, rows, width), bf16),
            out((2, 2, n, hidden), bf16),
        ],
        scratch_shapes=[
            pltpu.VMEM(wp.shape, bf16),
            pltpu.VMEM(own[0].shape, bf16),
            pltpu.VMEM(own[1].shape, bf16),
            pltpu.VMEM((4 * rows, width), bf16),
            pltpu.VMEM((4 * rows, hidden), bf16),
            pltpu.VMEM((4 * rows, hidden), bf16),
            pltpu.VMEM((4 * rows, width), bf16),
            pltpu.VMEM((2, 2, n, hidden), bf16),
            pltpu.VMEM((2, 2, n, hidden), bf16),
            pltpu.VMEM((4, rows, width), bf16),
            pltpu.VMEM((4, rows, width), bf16),
            *scatter_scratch(rows, width),
            *(DpReduce.scratch(n, hidden)[:1] if fold else []),
            pltpu.SemaphoreType.DMA((4,)),
            pltpu.SemaphoreType.DMA((3,)),
            *comm_scratch(2 * Scatter.COPIES + 2 * Gather.COPIES + 2 * Exchange.copies(bits) + DpReduce.COPIES),
        ],
        compiler_params=params(2),
        cost_estimate=pl.CostEstimate(flops=60 << 30, bytes_accessed=24 << 20, transcendentals=0),
    )(x, o, dy, ln, dm, wp, *own, *got)
    dh, norms, hid, do, sent, fc2, y, da, fc1 = res
    return dh, norms, y, hid, do, da.reshape(4 * rows, width), fc1, (sent, fc2)


def back_kernel(bits, fold, layers, flags_ref, x_ref, dh1_ref, hid_ref, ln_ref, dqkv_ref, o1_ref, lab_ref,
                wq_hbm, wp_hbm, w1_hbm, w2_hbm, u_hbm, g_hbm, n2_hbm, n1_hbm, da1_hbm, dwall_hbm, *refs):
    refs = list(refs)
    take = lambda k: [refs.pop(0) for _ in range(k)]
    blocks = take(len(layers))
    gin_ref, dh_ref, norm_ref, do_ref, da_hbm, fc1_hbm, fc2_sent, fc2_out, qp_out, rel_out, sum_out = take(11)
    places = [take(2) for _ in range(len(layers) + 1)]
    wq, wp, w1, w2, u_buf, g_buf, fc2, gqp, strips, gin_low, gat1, gat2, low, wide = take(14)
    if fold:
        lands_qp, lands_fc = take(3), take(1)
    load_sem, store_sem, send_sem, recv_sem = refs
    small, out_lab = flags_ref[0], flags_ref[1]
    rows, width = x_ref.shape
    n = rows // NCH
    hidden = w1.shape[1]
    heads = rel_out.shape[0]
    lw = o1_ref.shape[1]
    load = lambda k, src, dst: start_load(src, dst, load_sem.at[k])
    load_q, load_n1, load_da = load(0, wq_hbm, wq), load(1, n1_hbm, u_buf), load(2, da1_hbm, g_buf)
    load_1, load_2, load_p = load(3, w1_hbm, w1), load(4, w2_hbm, w2), load(5, wp_hbm, wp)
    load_strip = load(6, dwall_hbm.at[0], strips)
    links = Links(send_sem, recv_sem, bits)
    links.enter()
    blocks.append(gin_low)
    layers = layers + [1]
    returns = [Return(links, layer, src, *at) for layer, src, at in zip(layers, blocks, places)]
    for back in returns[:-1]:
        back.start()
    s1, s2 = Scatter(links, low, wide), Scatter(links, low, wide)
    g1, g2 = Gather(links, gat1), Gather(links, gat2)
    load_q.wait()
    for i in range(NCH):
        scatter_product(s1, i, lambda b: block_rows(dqkv_ref, b, i, rows), wq[...], rows)
        if i:
            s1.middle(i - 1)
    s1.middle(NCH - 1)
    load_n1.wait()
    slab_grad(gqp, 0, u_buf[...], dqkv_ref[...])
    load_da.wait()
    slab_grad(gqp, dqkv_ref.shape[1], g_buf[...], o1_ref[...])
    load_u, load_g = load(8, u_hbm, u_buf), load(9, g_hbm, g_buf)
    if fold:
        reduce = DpReduce(links, gqp, *lands_qp)
        reduce.start()
    cols = jnp.sum(dqkv_ref[...].astype(jnp.float32), axis=0, keepdims=True)
    sum_out[...] = jnp.concatenate([cols[:, :lw], cols[:, 2 * lw :]], axis=1)
    sums1 = None
    for i in range(NCH):
        at = chunk(i, rows)
        dx, dgain, dshift = norm_back(x_ref[at].astype(jnp.float32), s1.done(i), ln_ref[0:1])
        gin = dh1_ref[at] + dx
        gin_ref[at] = gin
        gin_low[at] = gin.astype(jnp.bfloat16)
        g1.send(i, gin_low[at])
        both = jnp.concatenate([dgain, dshift], axis=0)
        sums1 = both if sums1 is None else sums1 + both
    returns[-1].start()
    lab = lab_ref[...]
    hi_mask, lo_hot = _labels_hi_lo(lab)

    def bias_head(h, load_strip):
        load_strip.wait()
        rel_out[h] = wall_grad(small, out_lab, lab, hi_mask, lo_hot, strips)
        return load(6, dwall_hbm.at[h + 1], strips) if h + 1 < heads else None

    load_strip = bias_head(0, load_strip)
    load_strip = bias_head(1, load_strip)
    s1.release()
    load_1.wait()
    load_2.wait()
    load_u.wait()

    def mlp(i):
        dmi = g1.done(i)
        ui = jnp.concatenate([block_rows(u_buf, b, i, rows) for b in range(4)], axis=0).astype(jnp.float32)
        du = (dot(dmi, w2[...], NN) * gelu_both(ui)[1]).astype(jnp.bfloat16)
        put_rows(u_buf, du, i, rows)
        scatter_product(s2, i, lambda b: du[b * n : (b + 1) * n], w1[...], rows)

    g1.forward(0)
    mlp(0)
    g1.forward(1)
    s2.middle(0)
    mlp(1)
    s2.middle(1)
    if fold:
        reduce.middle()
    load_g.wait()
    slab_grad(fc2, 0, flat(gat1), g_buf[...])
    if fold:
        reduce_2 = DpReduce(links, fc2, *lands_fc)
        reduce_2.start()
    load_n2 = load(10, n2_hbm, g_buf)
    sums2 = None
    for i in range(NCH):
        at = chunk(i, rows)
        dx, dgain, dshift = norm_back(hid_ref[at], s2.done(i), ln_ref[1:2])
        dh = gin_ref[at].astype(jnp.bfloat16).astype(jnp.float32) + dx
        dh_ref[at] = dh
        g2.send(i, dh.astype(jnp.bfloat16))
        both = jnp.concatenate([dgain, dshift], axis=0)
        sums2 = both if sums2 is None else sums2 + both
    norm_ref[...] = jnp.concatenate([sums1, sums2], axis=0)
    load_n2.wait()
    weight_grad(w2, 0, g_buf[...], u_buf[...])
    stores = [start_load(w2, fc1_hbm, store_sem.at[0])]
    load_strip = bias_head(2, load_strip)
    load_p.wait()
    g2.forward(0)
    bias_head(3, load_strip)
    g2.forward(1)
    for i in range(NCH):
        put_rows(do_ref, dot(g2.done(i), wp[...], NN).astype(jnp.bfloat16), i, rows)
    stores.append(start_load(gat2, da_hbm, store_sem.at[2]))
    if fold:
        reduce.done(qp_out)
        reduce_2.split(fc2_sent, fc2_out)
    else:
        qp_out[...] = gqp[...]
        fc2_out[...] = fc2[...]
    for back in returns:
        back.done()
    links.leave()
    for store in stores:
        store.wait()


def back_chain(ndp, flags, x, dh1, hid, ln, dqkv, o1, lab, wq, wp, w1, w2, u, g, n2, n1, da1, dwall, returns):
    rows, width = x.shape
    hidden = w1.shape[1]
    lw = wp.shape[1]
    heads = dwall.shape[0]
    fold = ndp == 4
    bits = 2
    n = width // 4
    qp_cols = wq.shape[1] + lw
    bf16, f32 = jnp.bfloat16, jnp.float32
    out = jax.ShapeDtypeStruct
    layers = [layer for layer, _ in returns]
    blocks = [block for _, block in returns]
    copies = 2 * Scatter.COPIES + 2 * Gather.COPIES + 2 * DpReduce.COPIES + (len(layers) + 1) * Return.COPIES
    res = pl.pallas_call(
        functools.partial(back_kernel, bits, fold, layers),
        in_specs=[pl.BlockSpec(memory_space=pltpu.SMEM)] + [VM] * 7 + [HB] * (10 + len(blocks)),
        out_specs=[VM, VM, VM, VM, HB, HB, VM, VM, VM, VM, VM] + [HB] * (2 * len(blocks) + 2),
        out_shape=[
            out((rows, width), f32),
            out((rows, width), f32),
            out((4, width), f32),
            out((4 * rows, lw), bf16),
            out((4, rows, width), bf16),
            out((width, hidden), bf16),
            out((n, hidden), bf16),
            out((n, hidden) if fold else (2, 2, n, hidden), bf16),
            out((n, qp_cols) if fold else (2, 2, n, qp_cols), bf16),
            out((heads, 64, 64), f32),
            out((1, 2 * lw), f32),
        ]
        + [out(block.shape, block.dtype) for block in blocks for _ in range(2)]
        + [out((rows, width), bf16)] * 2,
        scratch_shapes=[
            pltpu.VMEM(wq.shape, bf16),
            pltpu.VMEM(wp.shape, bf16),
            pltpu.VMEM(w1.shape, bf16),
            pltpu.VMEM(w2.shape, bf16),
            pltpu.VMEM((4 * rows, hidden), bf16),
            pltpu.VMEM((4 * rows, hidden), bf16),
            pltpu.VMEM((2, 2, n, hidden), bf16),
            pltpu.VMEM((2, 2, n, qp_cols), bf16),
            pltpu.VMEM(dwall.shape[1:], f32),
            pltpu.VMEM((rows, width), bf16),
            pltpu.VMEM((4, rows, width), bf16),
            pltpu.VMEM((4, rows, width), bf16),
            *scatter_scratch(rows, width),
            *(DpReduce.scratch(n, qp_cols) + DpReduce.scratch(n, hidden)[:1] if fold else []),
            pltpu.SemaphoreType.DMA((11,)),
            pltpu.SemaphoreType.DMA((3,)),
            *comm_scratch(copies),
        ],
        compiler_params=params(3),
        cost_estimate=pl.CostEstimate(flops=60 << 30, bytes_accessed=24 << 20, transcendentals=0),
    )(flags, x, dh1, hid, ln, dqkv, o1, lab, wq, wp, w1, w2, u, g, n2, n1, da1, dwall, *blocks)
    gin, dh, norms, do, da, fc1, sent, fc2, qp, rel, sums = res[:11]
    got = [(res[11 + 2 * k], res[12 + 2 * k]) for k in range(len(layers) + 1)]
    return gin, dh, norms, do, da.reshape(4 * rows, width), fc1, (sent, fc2), qp, rel, sums, got


def start_kernel(order, scale, bits, flags_ref, x_hbm, cot_hbm, mask_ref, lab_ref, tab_hbm, pack_hbm,
                 wq_hbm, wp_hbm, w1_hbm, w2_hbm,
                 x_ref, cot_ref, pack_ref, lse_ref, o_ref, n1_hbm, qkv_hbm, wall0_hbm, wall1_hbm,
                 wq0_hbm, wp0_hbm, w10_hbm, w20_hbm,
                 tab, wq, wp, qkv, wall, gat1, s_scr, p_scr, load_sem, store_sem, send_sem, recv_sem):
    small, out_lab = flags_ref[0], flags_ref[1]
    rows, width = x_ref.shape
    wide = qkv.shape[1]
    heads = wall.shape[1]
    links = Links(send_sem, recv_sem, bits)
    pair, home = links.pair, links.home
    own_x = pltpu.make_async_copy(x_hbm.at[pair], x_ref, load_sem.at[0])
    when(home, own_x.start)
    own_cot = pltpu.make_async_copy(cot_hbm.at[pair], cot_ref, load_sem.at[7])
    when(home, own_cot.start)
    links.enter()
    packs = [Spread(links, l, pack_hbm, pack_ref.at[l], load_sem.at[1 + l]) for l in range(2)]
    tabs = [Spread(links, l, tab_hbm, tab.at[l], load_sem.at[3 + l]) for l in range(2)]
    tabs[0].start()
    packs[0].start()
    far_x = links.send(x_hbm.at[1 - pair], x_ref, FAR, home)
    tabs[1].start()
    packs[1].start()
    get_q = Deliver(links, 0, wq_hbm, wq, load_sem.at[5])
    get_p = Deliver(links, 0, wp_hbm, wp, load_sem.at[6])
    get_1, get_2 = Deliver(links, 0, w1_hbm, w10_hbm), Deliver(links, 0, w2_hbm, w20_hbm)
    ex_q, ex_p = Exchange(links, wq), Exchange(links, wp)
    get_q.start()
    lab = lab_ref[...]
    hi_mask, lo_hot = _labels_hi_lo(lab)

    def build(l):
        def one(h, carry):
            build_wall(small, out_lab, lab, hi_mask, lo_hot, tab[l, h], wall.at[l, h])
            return carry

        lax.fori_loop(0, heads, one, 0)

    tabs[0].done()
    build(0)
    stores = [start_load(wall.at[0], wall0_hbm, store_sem.at[0])]
    packs[0].done()
    when(home, own_x.wait)
    when(jnp.logical_not(home), far_x.wait_recv)
    g1 = Gather(links, gat1)
    for i in range(NCH):
        at = chunk(i, rows)
        xhat = normed(x_ref[at].astype(jnp.float32))[0]
        g1.send(i, (xhat * pack_ref[0, 0:1] + pack_ref[0, 2:3]).astype(jnp.bfloat16))
    get_p.start()
    get_1.start()
    get_2.start()
    far_cot = links.send(cot_hbm.at[1 - pair], cot_ref, FAR, home)
    tabs[1].done()
    build(1)
    stores.append(start_load(wall.at[1], wall1_hbm, store_sem.at[5]))
    get_q.done()
    ex_q.step(0)
    for i in range(NCH):
        g1.forward(i)
    for s in range(1, bits):
        ex_q.step(s)
    for i in range(NCH):
        g1.copies["s", i].wait_recv()
        g1.copies["f", i].wait_recv()
    stores.append(start_load(gat1, n1_hbm, store_sem.at[1]))
    packs[1].done()
    get_p.done()
    ex_q.done()
    ex_p.step(0)
    stores.append(start_load(wq, wq0_hbm, store_sem.at[2]))
    term = pack_ref[0, pl.ds(4 + pair, 1)][:, :wide]
    weight = wq[...].reshape(width, wide)
    for b in range(4):
        qkv[pl.ds(b * rows, rows)] = (dot(gat1[b], weight, NN) + term).astype(jnp.bfloat16)
    stores.append(start_load(qkv, qkv_hbm, store_sem.at[3]))
    for s in range(1, bits):
        ex_p.step(s)
    keys = [quarter(links.r, links.c, j) for j in order]

    def block(i, carry):
        at = pl.ds(pl.multiple_of(i * QB, QB), QB)
        qq = lax.rem(links.r + i // 2, 2) + 2 * lax.rem(links.c + lax.rem(i, 2), 2)
        o_ref[at] = attn_block(
            qq, keys, scale, qkv.at[at], qkv, mask_ref[...], wall.at[0], lse_ref.at[i], s_scr, p_scr
        )
        return carry

    lax.fori_loop(0, 4, block, 0)
    ex_p.done()
    stores.append(start_load(wp, wp0_hbm, store_sem.at[4]))
    get_1.done()
    get_2.done()
    when(home, own_cot.wait)
    when(jnp.logical_not(home), far_cot.wait_recv)
    links.leave()
    for store in stores:
        store.wait()


def start_chain(flags, x, cot, mask_pad, lab, table, pack, wq, wp, w1, w2, order, scale):
    bits = wq.ndim - 2
    _, rows, width = x.shape
    heads = table.shape[0]
    wide = wq.shape[-1]
    bf16, f32 = jnp.bfloat16, jnp.float32
    out = jax.ShapeDtypeStruct
    copies = 2 + 4 * Spread.COPIES + 4 * Deliver.COPIES + 2 * Exchange.copies(bits) + Gather.COPIES
    return pl.pallas_call(
        functools.partial(start_kernel, order, scale, bits),
        in_specs=[pl.BlockSpec(memory_space=pltpu.SMEM), HB, HB, VM, VM, HB, HB, HB, HB, HB, HB],
        out_specs=[VM] * 5 + [HB] * 8,
        out_shape=[
            out((rows, width), bf16),
            out((rows, width), bf16),
            out((2,) + pack.shape, f32),
            out((4, heads, QB), f32),
            out((4 * rows, heads * HD), bf16),
            out((4, rows, width), bf16),
            out((4 * rows, wide), bf16),
            out((heads, 32, WALL), f32),
            out((heads, 32, WALL), f32),
            *[out(w.shape, bf16) for w in (wq, wp, w1, w2)],
        ],
        scratch_shapes=[
            pltpu.VMEM((2,) + table.shape, f32),
            *[pltpu.VMEM(w.shape, bf16) for w in (wq, wp)],
            pltpu.VMEM((4 * rows, wide), bf16),
            pltpu.VMEM((2, heads, 32, WALL), f32),
            pltpu.VMEM((4, rows, width), bf16),
            pltpu.VMEM((2, 4 * rows, QB), f32),
            pltpu.VMEM((2, 4 * rows, QB), bf16),
            pltpu.SemaphoreType.DMA((8,)),
            pltpu.SemaphoreType.DMA((6,)),
            *comm_scratch(copies),
        ],
        compiler_params=params(0),
        cost_estimate=pl.CostEstimate(flops=80 << 30, bytes_accessed=24 << 20, transcendentals=0),
    )(flags, x, cot, mask_pad, lab, table, pack, wq, wp, w1, w2)


def attn_back(links, order, scale, qkv_ref, do_ref, o_ref, lse_ref, k_extra, wall, acc, p_scr, s_scr, dq_scr, dk_scr, dv_scr,
              dqkv_ref, event):
    heads = wall.shape[0]
    width = heads * HD
    total = qkv_ref.shape[0]
    keys = [quarter(links.r, links.c, j) for j in order]
    lane = lax.broadcasted_iota(jnp.int32, (QB, 128 - HD), 1)
    q_extra = jnp.where(lane == 0, 1.0, 0.0).astype(jnp.bfloat16)

    def block(i, carry):
        at = pl.ds(pl.multiple_of(i * QB, QB), QB)
        q_ref, d_ref, out_ref = qkv_ref.at[at], do_ref.at[at], o_ref.at[at]
        qq = block_quarter(links, i)
        dqs = []
        for h in range(heads):
            kh = head_lanes(qkv_ref, width + HD * h, k_extra)
            qh = head_lanes(q_ref, HD * h, q_extra)
            vh = head_lanes(qkv_ref, 2 * width + HD * h)
            doh = head_lanes(d_ref, HD * h)
            oh = head_lanes(out_ref, HD * h)
            inner = jnp.sum((doh.astype(jnp.float32) * oh.astype(jnp.float32)).T, axis=0, keepdims=True)
            lse = lse_ref[i, h : h + 1, :]
            for kb in range(total // 256):
                s_t = dot(kh[256 * kb : 256 * kb + 256], qh, NT)
                dp_t = dot(vh[256 * kb : 256 * kb + 256], doh, NT)
                for js in range(8):
                    st = 8 * kb + js
                    start = strip_start(qq, js, keys[kb])
                    s = s_t[32 * js : 32 * js + 32] * (scale * LOG2E) + wall[h, :, pl.ds(start, QB)]
                    p = jnp.exp2(s - lse)
                    ds = p * (dp_t[32 * js : 32 * js + 32] - inner)
                    p_scr[h % 2, 32 * st : 32 * st + 32] = p.astype(jnp.bfloat16)
                    s_scr[h % 2, 32 * st : 32 * st + 32] = ds.astype(jnp.bfloat16)
                    acc[h, :, pl.ds(start, QB)] += ds
            p_b, ds_b = p_scr[h % 2], s_scr[h % 2]
            dv_scr[h] += dot(p_b, doh, NN)
            dk_scr[h] += dot(ds_b, qh, NN)
            dq_t = dot(kh, ds_b, TN) * scale
            dqs.append(dq_t.T[:, :HD].astype(jnp.bfloat16))
        dq_scr[at] = jnp.concatenate(dqs, axis=1)
        event(i)
        return carry

    lax.fori_loop(0, total // QB, block, 0)
    parts = [dq_scr[...]]
    parts += [(dk_scr[h, :, :HD] * scale).astype(jnp.bfloat16) for h in range(heads)]
    parts += [dv_scr[h, :, :HD].astype(jnp.bfloat16) for h in range(heads)]
    dqkv_ref[...] = jnp.concatenate(parts, axis=1)


def bwd_kernel(order, scale, bits, fold, layers, summed, qkv_ref, do_ref, o_ref, lse_ref, mask_ref, wall_hbm, gfc_hbm, *refs):
    refs = list(refs)
    take = lambda k: [refs.pop(0) for _ in range(k)]
    blocks = take(len(layers))
    sent_2, kept_2 = take(2) if fold else (None, None)
    y_ref, hid_ref = take(2) if summed else (None, None)
    dqkv_ref, acc_hbm = take(2)
    fc_out, fin_out = take(2) if fold else (None, None)
    places = [take(2) for _ in range(len(layers) + (1 if fold else 0))]
    (act_ref,) = take(1) if summed else (None,)
    wall, acc, p_scr, s_scr, dq_scr, dk_scr, dv_scr = take(7)
    if fold:
        gfc, land0, land1, sent, land_2 = take(5)
    if summed:
        (low,) = take(1)
    load_sem, store_sem, send_sem, recv_sem = refs
    loads = [start_load(wall_hbm, wall, load_sem.at[0])]
    if fold:
        loads.append(start_load(gfc_hbm, gfc, load_sem.at[1]))
    links = Links(send_sem, recv_sem, bits)
    links.enter()
    returns = [Return(links, layer, src, *at) for layer, src, at in zip(layers, blocks, places)]
    if fold:
        finish = DpFinish(links, sent_2, kept_2, land_2)
        finish.start()
        last = Return(links, 1, fin_out, *places[-1])
        reduce = DpReduce(links, gfc, land0, land1, sent)
    if summed:
        rows = hid_ref.shape[0]
        part = lambda b: y_ref.at[pl.ds(b * rows, rows)]
        to_sib = links.make(part(3), low.at[0], SIBLING)
        near = links.make(part(1), low.at[1], SIBLING)
        to_partner = links.make(low.at[2], low.at[3], PARTNER)
        to_sib.start()
        near.start()
    acc[...] = jnp.zeros_like(acc)
    dk_scr[...] = jnp.zeros_like(dk_scr)
    dv_scr[...] = jnp.zeros_like(dv_scr)
    if fold:
        loads[1].wait()
        reduce.start()
    if summed:
        to_sib.wait_recv()
        low[2] = (part(2)[...].astype(jnp.float32) + low[0].astype(jnp.float32)).astype(jnp.bfloat16)
        to_partner.start()
    for back in returns:
        back.start()
    loads[0].wait()

    def finished():
        finish.done(fin_out)
        last.start()

    def event(i):
        if fold:
            pl.when(i == 0)(finished)
            pl.when(i == 2)(lambda: reduce.middle())

    attn_back(
        links, order, scale, qkv_ref, do_ref, o_ref, lse_ref, mask_ref[...], wall, acc, p_scr, s_scr, dq_scr, dk_scr, dv_scr,
        dqkv_ref, event,
    )
    stores = [start_load(acc, acc_hbm, store_sem.at[0])]
    if summed:
        near.wait_recv()
        to_partner.wait_recv()
        act = hid_ref[...] + part(0)[...].astype(jnp.float32) + low[1].astype(jnp.float32) + low[3].astype(jnp.float32)
        act_ref[...] = act.astype(jnp.bfloat16)
    if fold:
        reduce.done(fc_out)
        last.done()
    for back in returns:
        back.done()
    links.leave()
    for store in stores:
        store.wait()


def bwd_chain(ident, fold, qkv, do, o, lse, mask_pad, wall, gfc, finish, returns, order, scale, summed=None):
    total, wide = qkv.shape
    heads = wall.shape[0]
    bits = 2
    n, columns = gfc.shape[2:]
    bf16, f32 = jnp.bfloat16, jnp.float32
    out = jax.ShapeDtypeStruct
    layers = [layer for layer, _ in returns]
    blocks = [block for _, block in returns]
    outs = [out((total, wide), bf16), out(wall.shape, f32)]
    specs = [VM, HB]
    if fold:
        outs += [out((n, columns), bf16)] * 2
        specs += [VM] * 2
    for block in blocks + ([finish[0]] if fold else []):
        outs += [out(block.shape, block.dtype)] * 2
        specs += [HB] * 2
    scratch = [
        pltpu.VMEM(wall.shape, f32),
        pltpu.VMEM(wall.shape, f32),
        pltpu.VMEM((2, total, QB), bf16),
        pltpu.VMEM((2, total, QB), bf16),
        pltpu.VMEM((total, heads * HD), bf16),
        pltpu.VMEM((heads, total, 128), f32),
        pltpu.VMEM((heads, total, 128), f32),
    ]
    if fold:
        scratch += [pltpu.VMEM(gfc.shape, bf16), *DpReduce.scratch(n, columns), pltpu.VMEM((n, columns), bf16)]
    more = list(finish) if fold else []
    if summed is not None:
        more += list(summed)
        rows, width = summed[1].shape
        outs.append(out((rows, width), bf16))
        specs.append(VM)
        scratch.append(pltpu.VMEM((4, rows, width), bf16))
    copies = len(layers) * Return.COPIES + (DpReduce.COPIES + DpFinish.COPIES + Return.COPIES if fold else 0) + (3 if summed else 0)
    res = pl.pallas_call(
        functools.partial(bwd_kernel, order, scale, bits, fold, layers, summed is not None),
        in_specs=[VM] * 5 + [HB] * 2 + [VM] * (len(blocks) + len(more)),
        out_specs=specs,
        out_shape=outs,
        scratch_shapes=scratch
        + [pltpu.SemaphoreType.DMA((2,)), pltpu.SemaphoreType.DMA((1,)), *comm_scratch(max(copies, 1))],
        compiler_params=params(ident),
        cost_estimate=pl.CostEstimate(flops=24 << 30, bytes_accessed=20 << 20, transcendentals=0),
    )(qkv, do, o, lse, mask_pad, wall, gfc, *blocks, *more)
    res = list(res)
    dqkv, acc = res[:2]
    res = res[2:]
    fc, fin = (res.pop(0), res.pop(0)) if fold else (None, None)
    got = [(res[2 * k], res[2 * k + 1]) for k in range(len(layers) + (1 if fold else 0))]
    act = res[-1] if summed is not None else None
    return dqkv, acc, fc, fin, got, act


class SumHops:
    def __init__(self, links, buf, land, hops):
        self.links, self.buf, self.land, self.hops, self.k = links, buf, land, hops, 0

    def send(self):
        if self.k < len(self.hops):
            self.copy = self.links.send(self.buf, self.land.at[self.k], self.hops[self.k], track=False)

    def take(self):
        self.copy.wait_recv()
        self.copy.wait_send()
        self.buf[...] = self.buf[...] + self.land[self.k]
        self.k += 1
        self.send()


def end_kernel(order, scale, bits, fold, layers, flags_ref, qkv_ref, do_ref, o_ref, lse_ref, mask_ref,
               x_ref, dh_ref, ln_ref, lab_ref, small_ref, rel1_ref,
               wall_hbm, wq_hbm, n1_hbm, da_hbm, fc_hbm, *refs):
    refs = list(refs)
    take = lambda k: [refs.pop(0) for _ in range(k)]
    blocks = take(len(layers))
    sent_2, kept_2 = take(2) if fold else (None, None)
    gin_ref, small_out, rel_out, q_out = take(4)
    fc_out, fin_out = take(2) if fold else (None, None)
    (all_fc,) = (None,) if fold else take(1)
    places = [take(2) for _ in range(len(layers) + (4 if fold else 1))]
    acc, dqkv_ref, gq, fc, gin_low, low1 = take(6)
    rel, rel_land, rel_near, smalls, small_land, norm_land, small_near = take(7)
    if fold:
        lands_q, lands_f, (land_2,) = take(3), take(3), take(1)
    load_sem, send_sem, recv_sem = refs
    small, out_lab = flags_ref[0], flags_ref[1]
    rows, width = x_ref.shape
    heads = rel.shape[1]
    hidden = fc_hbm.shape[-1]
    load_f = start_load(fc_hbm, fc.at[:, :, :, pl.ds(0, hidden)], load_sem.at[1])
    links = Links(send_sem, recv_sem, bits)
    home, away = links.home, jnp.logical_not(links.home)
    links.enter()
    give = list(zip(layers, blocks)) + [(0, gin_low)] + ([(0, fc_out), (0, q_out), (0, fin_out)] if fold else [])
    returns = [Return(links, layer, src, *at) for (layer, src), at in zip(give, places)]
    early = len(layers)
    for back in returns[:early]:
        back.start()
    if fold:
        finish = DpFinish(links, sent_2, kept_2, land_2)
        finish.start()
        reduce_f = DpReduce(links, fc, *lands_f)
        reduce_q = DpReduce(links, gq, *lands_q)

    def proj_grad(rows_buf):
        start_load(da_hbm, rows_buf, load_sem.at[4]).wait()
        slab_grad(fc, hidden, rows_buf[...], o_ref[...])

    pl.run_scoped(proj_grad, pltpu.VMEM(da_hbm.shape, jnp.bfloat16))
    load_f.wait()
    if fold:
        reduce_f.start()
    acc[...] = jnp.zeros_like(acc)

    def finished():
        finish.done(fin_out)
        returns[early + 3].start()

    def event(i):
        if fold:
            pl.when(i == 0)(finished)
            pl.when(i == 2)(lambda: reduce_f.middle())

    def attention(wall, p_scr, s_scr, dq_scr, dk_scr, dv_scr):
        load_w = start_load(wall_hbm, wall, load_sem.at[0])
        dk_scr[...] = jnp.zeros_like(dk_scr)
        dv_scr[...] = jnp.zeros_like(dv_scr)
        load_w.wait()
        attn_back(
            links, order, scale, qkv_ref, do_ref, o_ref, lse_ref, mask_ref[...], wall, acc, p_scr, s_scr, dq_scr, dk_scr,
            dv_scr, dqkv_ref, event,
        )

    total = qkv_ref.shape[0]
    vmem, bf16, f32 = pltpu.VMEM, jnp.bfloat16, jnp.float32
    pl.run_scoped(
        attention,
        vmem(wall_hbm.shape, f32),
        vmem((2, total, QB), bf16),
        vmem((2, total, QB), bf16),
        vmem((total, heads * HD), bf16),
        vmem((heads, total, 128), f32),
        vmem((heads, total, 128), f32),
    )
    lw = o_ref.shape[1]

    def rest(wq, rows_buf, wide1):
        s1 = Scatter(links, low1, wide1)
        load_n = start_load(n1_hbm, rows_buf, load_sem.at[3])
        load_q = start_load(wq_hbm, wq, load_sem.at[2])
        load_n.wait()
        slab_grad(gq, 0, rows_buf[...], dqkv_ref[...])
        if fold:
            reduce_q.start()
        load_q.wait()
        for i in range(NCH):
            scatter_product(s1, i, lambda b: block_rows(dqkv_ref, b, i, rows), wq[...], rows)
            if i:
                s1.middle(i - 1)
        s1.middle(NCH - 1)
        if fold:
            reduce_f.done(fc_out)
            returns[early + 1].start()
        cols = jnp.sum(dqkv_ref[...].astype(jnp.float32), axis=0, keepdims=True)
        mine = jnp.concatenate([cols[:, :lw], cols[:, 2 * lw :]], axis=1)
        images = (smalls.shape[0] - 8) // 2
        number = 2 * lax.axis_index("dp") + links.pair
        here = lax.broadcasted_iota(jnp.int32, (images, 2 * lw), 0) == number
        smalls[...] = small_ref[...]
        smalls[8 : 8 + images, 0 : 2 * lw] = jnp.where(here, jnp.broadcast_to(mine, (images, 2 * lw)), 0.0)
        lab = lab_ref[...]
        hi_mask, lo_hot = _labels_hi_lo(lab)
        rel[1] = rel1_ref[...]

        def heads_of(a, b):
            def one(h, carry):
                rel[0, h] = wall_grad(small, out_lab, lab, hi_mask, lo_hot, acc.at[h])
                return carry

            lax.fori_loop(a, b, one, 0)

        heads_of(0, heads // 2)
        late = None
        for i in range(NCH):
            at = chunk(i, rows)
            dx, dgain, dshift = norm_back(x_ref[at].astype(jnp.float32), s1.done(i), ln_ref[0:1])
            gin = dh_ref[at] + dx
            gin_ref[at] = gin
            gin_low[at] = gin.astype(jnp.bfloat16)
            both = jnp.concatenate([dgain, dshift], axis=0)
            late = both if late is None else late + both
        smalls[0:2] = late
        hops = [ACROSS] + [("dp", b) for b in range(bits)]
        small_hops = SumHops(links, smalls, small_land, hops)
        small_hops.send()
        returns[early].start()
        heads_of(heads // 2, heads)
        rel_hops = SumHops(links, rel, rel_land, hops)
        rel_hops.send()
        if fold:
            reduce_q.middle()
        small_hops.take()
        rel_hops.take()
        if fold:
            reduce_q.done(q_out)
            returns[early + 2].start()
        else:
            q_out[...] = gq[...]
            all_fc[...] = fc[...]
        for _ in range(bits):
            small_hops.take()
            rel_hops.take()
        images_at = pl.ds(8, smalls.shape[0] - 8)
        rel_copy = links.send(rel.at[1 - links.c], rel_near, SIBLING, home)
        small_copy = links.send(smalls.at[images_at], small_near, SIBLING, home)
        norm_hops = SumHops(links, smalls.at[pl.ds(0, 8)], norm_land, [PARTNER, SIBLING])
        norm_hops.send()

        @pl.when(home)
        def _():
            rel_out[...] = rel[links.c]
            small_out[images_at] = smalls[images_at]

        @pl.when(away)
        def _():
            rel_copy.wait_recv()
            small_copy.wait_recv()
            rel_out[...] = rel_near[...]
            small_out[images_at] = small_near[...]

        norm_hops.take()
        norm_hops.take()
        small_out[0:8] = smalls[0:8]
        for back in returns:
            back.done()
        links.leave()

    pl.run_scoped(rest, vmem(wq_hbm.shape, bf16), vmem(n1_hbm.shape, bf16), vmem((2, rows, width), f32))


def end_chain(ndp, flags, qkv, do, o, lse, mask_pad, x, dh, ln, lab, smalls, rel1, wall, wq, n1, da, fc, finish, returns, order, scale):
    rows, width = x.shape
    heads = wall.shape[0]
    total, wide = qkv.shape
    bits = ndp.bit_length() - 1
    fold = bits == 2
    n, hidden = fc.shape[2:]
    fc_cols = hidden + o.shape[1]
    count = smalls.shape[0]
    hops = bits + 1
    bf16, f32 = jnp.bfloat16, jnp.float32
    out = jax.ShapeDtypeStruct
    layers = [layer for layer, _ in returns]
    blocks = [block for _, block in returns]
    landed = [out(block.shape, bf16) for block in blocks] + [out((rows, width), bf16)]
    outs = [
        out((rows, width), f32),
        out((count, width), f32),
        out((heads, 64, 64), f32),
        out((n, wide) if fold else (2, 2, n, wide), bf16),
    ]
    if fold:
        outs += [out((n, fc_cols), bf16), out((n, hidden), bf16)]
        landed += [out((n, fc_cols), bf16), out((n, wide), bf16), out((n, hidden), bf16)]
        blocks += list(finish)
    else:
        outs.append(out((2, 2, n, fc_cols), bf16))
    copies = Scatter.COPIES + len(landed) * Return.COPIES + 2 * DpReduce.COPIES + DpFinish.COPIES + 2 * hops + 4
    res = pl.pallas_call(
        functools.partial(end_kernel, order, scale, bits, fold, layers),
        in_specs=[pl.BlockSpec(memory_space=pltpu.SMEM)] + [VM] * 11 + [HB] * (5 + len(layers)) + ([VM] * 2 if fold else []),
        out_specs=[VM] * len(outs) + [HB] * (2 * len(landed)),
        out_shape=outs + [shape for shape in landed for _ in range(2)],
        scratch_shapes=[
            pltpu.VMEM(wall.shape, f32),
            pltpu.VMEM((total, wide), bf16),
            pltpu.VMEM((2, 2, n, wide), bf16),
            pltpu.VMEM((2, 2, n, fc_cols), bf16),
            pltpu.VMEM((rows, width), bf16),
            pltpu.VMEM((6, rows, width), bf16),
            pltpu.VMEM((2, heads, 64, 64), f32),
            pltpu.VMEM((hops, 2, heads, 64, 64), f32),
            pltpu.VMEM((heads, 64, 64), f32),
            pltpu.VMEM((count, width), f32),
            pltpu.VMEM((hops, count, width), f32),
            pltpu.VMEM((2, 8, width), f32),
            pltpu.VMEM((count - 8, width), f32),
            *(
                DpReduce.scratch(n, wide) + DpReduce.scratch(n, fc_cols) + [pltpu.VMEM((n, hidden), bf16)]
                if fold
                else []
            ),
            pltpu.SemaphoreType.DMA((5,)),
            *comm_scratch(copies),
        ],
        compiler_params=params(4),
        cost_estimate=pl.CostEstimate(flops=90 << 30, bytes_accessed=24 << 20, transcendentals=0),
    )(flags, qkv, do, o, lse, mask_pad, x, dh, ln, lab, smalls, rel1, wall, wq, n1, da, fc, *blocks)
    res = list(res)
    got = [(res[len(outs) + 2 * k], res[len(outs) + 2 * k + 1]) for k in range(len(landed))]
    return res[: len(outs)], got


AXES = ("dp", "section", "tensor")
ORDER = (0, 2, 1, 3)


def local(
    inputs,
    time_emb,
    lengths,
    key_mask,
    rel_index,
    w_qkv,
    w_time,
    w_proj,
    w_fc1,
    w_fc2,
    rel_table,
    norm_gains,
    norm_biases,
    cotangent,
):
    bf16, f32 = jnp.bfloat16, jnp.float32
    _, rows, width = inputs.shape
    seq_len = key_mask.shape[1]
    heads, buckets = rel_table.shape[1:]
    local_width = w_proj.shape[2]
    scale = 1.0 / math.sqrt(HD)
    ndp = lax.axis_size("dp")
    d = lax.axis_index("dp")
    c = lax.axis_index("section")
    z = lax.axis_index("tensor")
    pair = z // 2
    home = c == pair
    first = c == 0
    t = z % 2 + 2 * c

    def move(x, to, name="move"):
        pairs = []
        for dd in range(ndp):
            for cc in range(2):
                for zz in range(4):
                    dst = to(dd, cc, zz)
                    if dst is not None:
                        pairs.append(((dd * 2 + cc) * 4 + zz, (dst[0] * 2 + dst[1]) * 4 + dst[2]))
        with jax.named_scope(name):
            return lax.ppermute(x, AXES, pairs)

    def partner(x):
        return move(x, lambda dd, cc, zz: (dd, cc, zz ^ 1), "partner")

    def sibling(x):
        return move(x, lambda dd, cc, zz: (dd, 1 - cc, zz), "sibling")

    def across(x):
        return move(x, lambda dd, cc, zz: (dd, cc, zz ^ 2), "across")

    def dp_scatter(x, bits):
        n = x.shape[1]
        left = sorted(bits, reverse=True)
        v = x.reshape((2,) * len(left) + (-1, n))
        for b in bits:
            axis = left.index(b)
            left.remove(b)
            mine = (d >> b) & 1
            send = lax.dynamic_index_in_dim(v, 1 - mine, axis, keepdims=False)
            keep = lax.dynamic_index_in_dim(v, mine, axis, keepdims=False)
            got = move(send, lambda dd, cc, zz, b=b: (dd ^ (1 << b), cc, zz), "g_dp")
            v = keep.astype(f32) + got.astype(f32)
            if left:
                v = v.astype(bf16)
        return v

    def by_bits(w):
        return w.reshape(2, 2, -1, w.shape[-1])

    table = jnp.pad(rel_table[0], ((0, 0), (0, 4096 - buckets))).reshape(heads, 64, 64)
    time_all = jnp.einsum("id,dcn->icn", time_emb, w_time[0], preferred_element_type=f32)
    gap = jnp.zeros((2, local_width), f32)
    time_rows = jnp.concatenate([time_all[:, 0], gap, time_all[:, 1], gap], axis=1)
    small_pack = jnp.concatenate([norm_gains[0], norm_biases[0], time_rows, jnp.zeros((2, width), f32)], axis=0)
    own = [by_bits(w) for w in (jnp.concatenate([w_qkv[0, :, j] for j in range(3)], axis=1), w_proj[0], w_fc1[0], w_fc2[0])]
    label_lanes = label_row(rel_index)
    out_label = rel_index[1, seq_len - 1, seq_len - 1].reshape(1)

    length = lax.dynamic_index_in_dim(lengths, pair, 0, keepdims=False)
    small = (length < seq_len).astype(jnp.int32)
    scalars = jnp.stack([z % 2, c] + [jnp.int32(j) for j in ORDER])
    flags = jnp.concatenate([small.reshape(1), out_label])
    mask = lax.dynamic_index_in_dim(key_mask, pair, 0, keepdims=False).reshape(4, rows)
    mask = jnp.concatenate([lax.dynamic_index_in_dim(mask, t ^ j, 0, keepdims=False) for j in ORDER])
    lane = jnp.arange(128 - HD)[None, :]
    mask_pad = jnp.where((lane == 0) & (mask[:, None] == 0), -1e30, 0.0).astype(bf16)

    def gather_rows(x):
        far = partner(x)
        near = sibling(x)
        return jnp.concatenate([x, near, far, sibling(far)], axis=0)

    def scatter_rows(far, near):
        a = sibling(far[rows:].astype(bf16))
        rz = partner((far[:rows] + a.astype(f32)).astype(bf16))
        rs = sibling(near[rows:].astype(bf16))
        return near[:rows] + rs.astype(f32) + rz.astype(f32)

    def times_t(x, w):
        return lax.dot_general(x, w, (((1,), (1,)), ((), ())), preferred_element_type=f32)

    def grad_of(x, y):
        return lax.dot_general(x, y, (((0,), (0,)), ((), ())), preferred_element_type=f32).astype(bf16)

    half = 2 * rows

    def reduced(x):
        with jax.named_scope("g_sum"):
            return lax.psum_scatter(x, "dp", scatter_dimension=0, tiled=True)

    def reduced_late(x):
        if ndp & (ndp - 1):
            return reduced(x)
        bits = list(range(ndp.bit_length() - 1))
        cut = 4 * 128
        return jnp.concatenate(
            [dp_scatter(x[:, :cut], bits), dp_scatter(x[:, cut:], bits[::-1])], axis=1
        ).astype(bf16)

    def column_sums(dqkv):
        sums = jnp.sum(dqkv.astype(f32), axis=0)
        return jnp.concatenate([sums[:local_width], sums[2 * local_width :]])

    def tie(*values):
        return lax.optimization_barrier(values)

    def by_core(pairs):
        return jnp.where(first, pairs[0], pairs[1])

    def near_of(x, layer):
        return move(x, lambda dd, cc, zz: (dd, layer, zz) if cc == zz // 2 and cc != layer else None, "d_near")

    def far_of(x, layer):
        return move(x, lambda dd, cc, zz: (dd, layer, zz ^ 2) if cc != zz // 2 else None, "d_far")

    live = ((t * rows + jnp.arange(rows)) < length).astype(f32)[:, None]
    res = start_chain(flags, inputs, cotangent, mask_pad, label_lanes, table, small_pack, *own, ORDER, scale)
    x0, cot, packs, lse0, o0, n1_0, qkv0 = res[:7]
    walls, got0 = res[7:9], res[9:]
    n1_0 = n1_0.reshape(seq_len, width)

    def whole(w):
        return w.reshape(width, w.shape[-1])

    gains = [packs[l, 0:2] for l in range(2)]
    shifts = [packs[l, 2:4] for l in range(2)]
    ln_mid = jnp.stack([gains[0][1], shifts[0][1], gains[1][0], shifts[1][0]])
    wq0, wp0 = whole(got0[0]), whole(got0[1])
    term1 = lax.dynamic_index_in_dim(packs[1], 4 + pair, 0, keepdims=True)[:, : 3 * local_width]
    hid0, act0, dy1, o1, lse1, n2_0, u0, g0, n1_1, qkv1, dm1, fc_w0, got1 = mid_chain(
        x0, o0, ln_mid, cot, live, term1, mask_pad, wp0, got0[2], got0[3], walls[1], own, ORDER, scale
    )
    w10, w20 = whole(fc_w0[0]), whole(fc_w0[1])
    wq1, wp1 = whole(got1[0]), whole(got1[1])

    fold = ndp == 4
    ln_turn = jnp.stack([gains[1][1], shifts[1][1]])
    dh1, norms1, y1, hid1, do1, da1, fc1_1, fc2_1 = turn_chain(
        ndp, act0, o1, dy1, ln_turn, dm1, wp1, own[2:], got1[2:]
    )
    dqkv1, dwall1, sum_fc1_1, sum_fc2_1, landed, act1 = bwd_chain(
        6, fold, qkv1, do1, o1, lse1, mask_pad, walls[1], fc1_1, fc2_1, [(0, act0)], ORDER, scale, (y1, hid1)
    )
    got_act0, got_fc2_1 = landed[0], landed[-1]
    ln_back = jnp.stack([gains[1][0], gains[0][1]])
    give = [(1, act1)] + ([(1, sum_fc1_1)] if fold else [])
    gin1, dh0, norms10, do0, da0, fc1_0, fc2_0, qp1, rel1, sums1, landed = back_chain(
        ndp, flags, act0, dh1, hid0, ln_back, dqkv1, o1, label_lanes,
        wq1, wp0, w10, w20, u0, g0, n2_0, n1_1, da1, dwall1, give,
    )
    got_act1, got_fc1_1, got_gin1 = landed[0], landed[len(landed) - 2], landed[-1]
    number = 2 * d + pair
    sums_rows = lax.dynamic_update_slice(
        jnp.zeros((2 * ndp, width), f32), sums1, (number, jnp.int32(width - 2 * local_width))
    )
    mine = lax.dynamic_index_in_dim(time_emb, pair, 0, keepdims=True).astype(f32)
    emb_rows = lax.dynamic_update_slice(jnp.zeros((2 * ndp, width), f32), mine, (number, jnp.int32(0)))
    smalls = jnp.concatenate(
        [jnp.zeros((2, width), f32), norms10[2:], norms10[:2], norms1, sums_rows, emb_rows], axis=0
    )
    give = [(1, qp1)] if fold else []
    (gin0, smalls, rel, q0, *more), landed = end_chain(
        ndp, flags, qkv0, do0, o0, lse0, mask_pad, x0, dh0, gains[0][0:1], label_lanes, smalls, rel1,
        walls[0], wq0, n1_0, da0, by_bits(fc1_0), fc2_0, give, ORDER, scale,
    )
    norms, sums_all = smalls[:8], smalls[8:]

    def total(mine, got):
        return jnp.where(home, mine, got[0]).astype(f32) + got[1].astype(f32)

    hidden_units = w_fc1.shape[2]
    wide = 3 * local_width
    if fold:
        got_qp1, got_gin0, got_f0, got_q0, got_fc2_0 = landed
        f0, sum_fc2_0 = more
        f0, qp1 = total(f0, got_f0), total(qp1, got_qp1)
        layer0 = (total(q0, got_q0), f0[:, hidden_units:], f0[:, :hidden_units], total(sum_fc2_0, got_fc2_0))
        layer1 = (qp1[:, :wide], qp1[:, wide:], total(sum_fc1_1, got_fc1_1), total(sum_fc2_1, got_fc2_1))
    else:
        (got_gin0,) = landed

        def summed(x, layer):
            x = reduced(whole(x))
            return total(x, (near_of(x, layer), far_of(x, layer)))

        f0, qp1 = summed(more[0], 0), summed(qp1, 1)
        layer0 = (summed(q0, 0), f0[:, hidden_units:], f0[:, :hidden_units], summed(fc2_0[1], 0))
        layer1 = (qp1[:, :wide], qp1[:, wide:], summed(fc1_1, 1), summed(fc2_1[1], 1))
    grad_q, grad_p, grad_fc1, grad_fc2 = [by_core(pair_of) for pair_of in zip(layer0, layer1)]

    def by_image(same, other):
        return jnp.stack([jnp.where(pair == 0, same, other), jnp.where(pair == 0, other, same)])[None]

    acts = by_image(
        jnp.where(home, by_core((act0, act1)), by_core((got_act0[0], got_act1[0]))), by_core((got_act0[1], got_act1[1]))
    )
    same = jnp.where(home, by_core((gin0, gin1)), by_core((got_gin0[0], got_gin1[0])).astype(f32))
    input_grads = by_image(same, by_core((got_gin0[1], got_gin1[1])).astype(f32))

    rel_grad = rel.reshape(heads, 4096)[:, :buckets]
    norms_mine = jnp.where(first, norms[:4], norms[4:]).reshape(2, 2, width)
    cols = width // (4 * ndp)
    norms_mine = lax.dynamic_slice_in_dim(norms_mine, (d * 4 + z) * cols, cols, 2)
    sums_of, emb_of = sums_all[: 2 * ndp], sums_all[2 * ndp :]
    sums_mine = jnp.where(first, sums_of[:, : 2 * local_width], sums_of[:, 2 * local_width :])
    emb_mine = lax.dynamic_slice_in_dim(emb_of, d * (width // ndp), width // ndp, 1)
    grad_time = lax.dot_general(
        emb_mine, sums_mine, (((0,), (0,)), ((), ())), precision=lax.Precision.HIGHEST, preferred_element_type=f32
    ).reshape(width // ndp, 2, local_width)
    return (
        acts,
        input_grads,
        grad_q.reshape(width // ndp, 3, local_width)[None],
        grad_time[None],
        grad_p[None],
        grad_fc1[None],
        grad_fc2[None],
        rel_grad[None],
        norms_mine[:, 0][None],
        norms_mine[:, 1][None],
    )


def solution(mesh):
    return jax.shard_map(
        local,
        mesh=mesh,
        in_specs=(
            P("dp", "tensor", None),
            P("dp", None),
            P("dp"),
            P("dp", None),
            P(),
            P("section", None, None, "tensor"),
            P("section", None, None, "tensor"),
            P("section", None, "tensor"),
            P("section", None, "tensor"),
            P("section", None, "tensor"),
            P("section", "tensor", None),
            P("section", None, None),
            P("section", None, None),
            P("dp", "tensor", None),
        ),
        out_specs=(
            P("section", "dp", "tensor", None),
            P("section", "dp", "tensor", None),
            P("section", "dp", None, "tensor"),
            P("section", "dp", None, "tensor"),
            P("section", "dp", "tensor"),
            P("section", "dp", "tensor"),
            P("section", "dp", "tensor"),
            P("section", "tensor", None),
            P("section", None, ("dp", "tensor")),
            P("section", None, ("dp", "tensor")),
        ),
        check_vma=False,
    )
```

```python
import functools
import math

import jax
import jax.numpy as jnp
from jax import lax
from jax.experimental import pallas as pl
from jax.experimental.pallas import tpu as pltpu
from jax.sharding import PartitionSpec as P

LOG2E = 1.4426950408889634
HIGHEST = lax.Precision.HIGHEST
PLANE = 7 * 256
WALL = 8 * PLANE


def _labels_hi_lo(lab):
    hi = lax.shift_right_logical(lab, 6)
    lo = jnp.bitwise_and(lab, 63)
    iota = lax.broadcasted_iota(jnp.int32, (64, lab.shape[1]), 0)
    group = 2 * jnp.bitwise_and(iota, 31) + lax.shift_right_logical(iota, 5)
    return group == hi, jnp.where(iota == lo, 1.0, 0.0)


def build_wall(small, out_lab, lab, hi_mask, lo_hot, table, wall_ref):
    table = jnp.concatenate([table[:, :64], table[:, 64:]], axis=0)
    rows = lax.dot_general(table, lo_hot, (((1,), (0,)), ((), ())), precision=HIGHEST, preferred_element_type=jnp.float32)
    flat = jnp.sum(jnp.where(hi_mask, rows, 0.0), axis=0, keepdims=True) * LOG2E
    outside = jnp.sum(jnp.where(lab == out_lab, flat, 0.0), axis=1, keepdims=True)
    wide = jnp.broadcast_to(flat, (32, 4096))
    wide = pltpu.roll(wide, 4096 - 31, 1, stride=1, stride_axis=0)
    lane = lax.broadcasted_iota(jnp.int32, (32, 128), 1)
    tight = []
    for g in range(16):
        a = wide[:, 256 * g : 256 * g + 128]
        b = wide[:, 256 * g + 128 : 256 * g + 256]
        piece = jnp.where(lane < 32, a, pltpu.roll(a, 96, 1))
        other = jnp.where(lane < 96, pltpu.roll(b, 64, 1), pltpu.roll(b, 32, 1))
        tight.append(jnp.where(lane < 64, piece, other))
    w0 = jnp.concatenate(tight, axis=1)
    lane16 = lane[:16]
    tight16 = []
    for g in range(8):
        lo_v = w0[:16, 256 * g : 256 * g + 128]
        hi_v = w0[:16, 256 * g + 128 : 256 * g + 256]
        acc = lo_v
        for k in range(1, 4):
            acc = jnp.where(lane16 >= 16 * k, pltpu.roll(lo_v, 128 - 16 * k, 1), acc)
        for k in range(4):
            acc = jnp.where(lane16 >= 64 + 16 * k, pltpu.roll(hi_v, (64 - 16 * k) % 128, 1), acc)
        tight16.append(acc)
    w16 = jnp.concatenate(tight16, axis=1)
    beyond = jnp.broadcast_to(outside, (32, 768))
    tiny = small == 1
    for j in range(8):
        big = w0 if j == 7 else pltpu.roll(w0, 2048 - 32 * (7 - j), 1)
        inner = [pltpu.roll(w16, 1024 - 16 * (31 - 2 * j - k), 1)[:, :256] for k in range(2)]
        inner = jnp.concatenate(inner, axis=0)
        at = j * PLANE
        wall_ref[:, at : at + 768] = jnp.where(tiny, beyond, big[:, :768])
        wall_ref[:, at + 768 : at + 1024] = jnp.where(tiny, inner, big[:, 768:1024])
        wall_ref[:, at + 1024 : at + PLANE] = jnp.where(tiny, beyond, big[:, 1024:PLANE])


def wall_grad(small, out_lab, lab, hi_mask, lo_hot, acc_ref):
    tiny = small == 1
    w0 = jnp.zeros((32, 2048), jnp.float32)
    w16 = jnp.zeros((16, 1024), jnp.float32)
    beyond = jnp.zeros((32, 768), jnp.float32)
    for j in range(8):
        at = j * PLANE
        piece = jnp.concatenate([acc_ref[:, at : at + PLANE], jnp.zeros((32, 256), jnp.float32)], axis=1)
        w0 = w0 + (piece if j == 7 else pltpu.roll(piece, 32 * (7 - j), 1))
        beyond = beyond + acc_ref[:, at + 1024 : at + PLANE]
        for k in range(2):
            inner = acc_ref[16 * k : 16 * k + 16, at + 768 : at + 1024]
            inner = jnp.concatenate([inner, jnp.zeros((16, 768), jnp.float32)], axis=1)
            w16 = w16 + pltpu.roll(inner, 16 * (31 - 2 * j - k), 1)
    w0 = jnp.where(tiny, 0.0, w0)
    w16 = jnp.where(tiny, w16, 0.0)
    outside = jnp.sum(jnp.sum(jnp.where(tiny, beyond, 0.0), axis=0, keepdims=True), axis=1, keepdims=True)
    lane = lax.broadcasted_iota(jnp.int32, (32, 128), 1)
    lane16 = lane[:16]
    wide = []
    for g in range(32):
        src = w0[:, 128 * (g // 2) : 128 * (g // 2) + 128]
        k = 2 * (g % 2)
        first = src if k == 0 else pltpu.roll(src, 128 - 32 * k, 1)
        second = pltpu.roll(src, (64 - 32 * (k + 1)) % 128, 1)
        piece = jnp.where(lane < 32, first, jnp.where((lane >= 64) & (lane < 96), second, 0.0))
        src16 = w16[:, 128 * (g // 4) : 128 * (g // 4) + 128]
        k = 2 * (g % 4)
        first = src16 if k == 0 else pltpu.roll(src16, 128 - 16 * k, 1)
        second = pltpu.roll(src16, (64 - 16 * (k + 1)) % 128, 1)
        piece16 = jnp.where(lane16 < 16, first, jnp.where((lane16 >= 64) & (lane16 < 80), second, 0.0))
        wide.append(piece + jnp.concatenate([piece16, jnp.zeros((16, 128), jnp.float32)], axis=0))
    wide = jnp.concatenate(wide, axis=1)
    back = 31 - lax.broadcasted_iota(jnp.int32, (32, 4096), 0)
    for k in range(5):
        wide = jnp.where(jnp.bitwise_and(back, 1 << k) > 0, pltpu.roll(wide, 1 << k, 1), wide)
    flat = jnp.sum(wide, axis=0, keepdims=True)
    flat = flat + jnp.where(lab == out_lab, outside, 0.0)
    spread = jnp.where(hi_mask, jnp.broadcast_to(flat, (64, 4096)), 0.0)
    res = lax.dot_general(spread, lo_hot, (((1,), (1,)), ((), ())), precision=HIGHEST, preferred_element_type=jnp.float32)
    return jnp.concatenate([res[:32], res[32:]], axis=1)


def label_row(rel_index):
    side = 32
    a = rel_index[0, 1023].reshape(side, side)
    b = rel_index[0, 0].reshape(side, side)
    c = rel_index[0, 992].reshape(side, side)
    d = rel_index[0, 31].reshape(side, side)
    top = jnp.concatenate([a, c[:, 1:]], axis=1)
    low = jnp.concatenate([d[1:], b[1:, 1:]], axis=1)
    grid = jnp.flip(jnp.concatenate([top, low], axis=0), (0, 1))
    return jnp.pad(grid, ((0, 1), (0, 1)), constant_values=4095).reshape(1, 4096)


NT = (((1,), (1,)), ((), ()))
TN = (((0,), (0,)), ((), ()))
NN = (((1,), (0,)), ((), ()))
HD = 72
QB = 256


def dot(a, b, dims):
    return lax.dot_general(a, b, dims, preferred_element_type=jnp.float32)


def head_lanes(x, at, extra=None):
    rows = x.shape[0]
    part = x[:, at : at + HD]
    if extra is None:
        pad = jnp.zeros((rows, 128 - HD), x.dtype)
    else:
        pad = extra
    return jnp.concatenate([part, pad], axis=1)


def quarter(r, c, rel):
    return lax.rem(r + rel % 2, 2) + 2 * lax.rem(c + rel // 2, 2)


def strip_start(q_quarter, jj, kq):
    return pl.multiple_of(PLANE * jj + 256 * (q_quarter - kq + 3), 256)


def attn_block(q_quarter, key_quarters, scale, q_ref, kv_ref, k_extra, wall_ref, lse_ref, s_scr, p_scr):
    heads = wall_ref.shape[0]
    width = heads * HD
    nstrip = kv_ref.shape[0] // 32
    lane = lax.broadcasted_iota(jnp.int32, (QB, 128 - HD), 1)
    q_extra = jnp.where(lane == 0, 1.0, 0.0).astype(jnp.bfloat16)
    outs = []
    for h in range(heads):
        kh = head_lanes(kv_ref, width + HD * h, k_extra)
        qh = head_lanes(q_ref, HD * h, q_extra)
        vh = head_lanes(kv_ref, 2 * width + HD * h)
        s_scr[h % 2] = dot(kh, qh, NT)
        top = None
        for st in range(nstrip):
            start = strip_start(q_quarter, st % 8, key_quarters[st // 8])
            s = s_scr[h % 2, 32 * st : 32 * st + 32] * (scale * LOG2E) + wall_ref[h, :, pl.ds(start, QB)]
            s_scr[h % 2, 32 * st : 32 * st + 32] = s
            top = s if top is None else jnp.maximum(top, s)
        row_max = jnp.max(top, axis=0, keepdims=True)
        total = None
        for st in range(nstrip):
            p = jnp.exp2(s_scr[h % 2, 32 * st : 32 * st + 32] - row_max)
            p_scr[h % 2, 32 * st : 32 * st + 32] = p.astype(jnp.bfloat16)
            total = p if total is None else total + p
        row_sum = jnp.sum(total, axis=0, keepdims=True)
        o_t = dot(vh, p_scr[h % 2], TN) * (1.0 / row_sum)
        lse_ref[h : h + 1, :] = row_max + jnp.log2(row_sum)
        outs.append(o_t.T[:, :HD].astype(jnp.bfloat16))
    return jnp.concatenate(outs, axis=1)


EPSILON = 1e-05
NCH = 2
GELU_C = math.sqrt(2.0 / math.pi)


def normed(x):
    center = x - jnp.mean(x, axis=-1, keepdims=True)
    spread = jnp.mean(center * center, axis=-1, keepdims=True)
    r = lax.rsqrt(spread + EPSILON)
    return center * r, r


def norm_back(x, dy, gain):
    xhat, r = normed(x)
    dxhat = dy * gain
    dx = r * (
        dxhat
        - jnp.mean(dxhat, axis=-1, keepdims=True)
        - xhat * jnp.mean(dxhat * xhat, axis=-1, keepdims=True)
    )
    return dx, jnp.sum(dy * xhat, axis=0, keepdims=True), jnp.sum(dy, axis=0, keepdims=True)


def gelu_both(u):
    th = jnp.tanh(GELU_C * (u + 0.044715 * u * u * u))
    half = 0.5 * (1.0 + th)
    slope = half + 0.5 * u * (1.0 - th * th) * GELU_C * (1.0 + 3 * 0.044715 * u * u)
    return u * half, slope


class Links:
    def __init__(self, send_sem, recv_sem, bits=0):
        z, c = lax.axis_index("tensor"), lax.axis_index("section")
        self.z, self.c = z, c
        self.pair = z // 2
        self.r = lax.rem(z, 2)
        self.home = c == self.pair
        across = z + 2 - 4 * self.pair
        self.ids = {
            PARTNER: {"tensor": z + 1 - 2 * self.r},
            SIBLING: {"section": 1 - c},
            FAR: {"tensor": across, "section": self.pair},
            HOME: {"section": self.pair},
        }
        self.greet = [self.ids[PARTNER], self.ids[SIBLING]]
        self.dp_bit = []
        if bits:
            d = lax.axis_index("dp")
            for b in range(bits):
                bit = lax.rem(d // (1 << b), 2)
                self.dp_bit.append(bit)
                self.ids["dp", b] = {"dp": d + (1 - 2 * bit) * (1 << b)}
                self.greet.append(self.ids["dp", b])
            self.greet += [{"tensor": across}, {"tensor": across, "section": 1 - c}]
        self.ids[ACROSS] = {"tensor": across}
        for layer in range(2):
            self.ids["return", layer] = {"tensor": across, "section": layer}
        self.send_sem, self.recv_sem = send_sem, recv_sem
        self.used = 0
        self.started = []

    def enter(self):
        barrier = pltpu.get_barrier_semaphore()
        for where in self.greet:
            pl.semaphore_signal(barrier, inc=1, device_id=where, device_id_type=pl.DeviceIdType.MESH)
        pl.semaphore_wait(barrier, len(self.greet))

    def make(self, src, dst, to, cond=None, track=True):
        k = self.used
        self.used += 1
        assert k < self.send_sem.shape[0]
        copy = pltpu.make_async_remote_copy(
            src_ref=src,
            dst_ref=dst,
            send_sem=self.send_sem.at[k],
            recv_sem=self.recv_sem.at[k],
            device_id=self.ids[to],
            device_id_type=pl.DeviceIdType.MESH,
        )
        if track:
            self.started.append((copy, cond))
        return copy

    def send(self, src, dst, to, cond=None, track=True):
        copy = self.make(src, dst, to, cond, track)
        when(cond, copy.start)
        return copy

    def leave(self):
        for copy, cond in self.started:
            when(cond, copy.wait_send)


def when(cond, do):
    if cond is None:
        do()
    else:
        pl.when(cond)(lambda: do())


PARTNER, SIBLING, FAR, HOME, ACROSS = "partner", "sibling", "far", "home", "across"


class Spread:
    COPIES = 2

    def __init__(self, links, layer, src, out, sem):
        self.links, self.layer, self.src, self.out, self.sem = links, layer, src, out, sem

    def start(self):
        links = self.links
        mine = links.c == self.layer
        keeps = links.pair == self.layer
        self.local = pltpu.make_async_copy(self.src, self.out, self.sem)
        when(mine & keeps, self.local.start)
        self.near = links.send(self.src, self.out, HOME, mine & jnp.logical_not(keeps))
        self.far = links.send(self.src, self.out, FAR, mine)

    def done(self):
        links = self.links
        keeps = links.pair == self.layer
        when(links.home & keeps, self.local.wait)
        when(links.home & jnp.logical_not(keeps), self.near.wait_recv)
        when(jnp.logical_not(links.home), self.far.wait_recv)


def bits_region(links, gathered, cols=None):
    index = []
    for b in reversed(range(len(links.dp_bit))):
        index.append(pl.ds(0, 2) if b in gathered else links.dp_bit[b])
    return tuple(index) + (() if cols is None else (slice(None), cols))


class Deliver:
    COPIES = 2

    def __init__(self, links, layer, src, out, sem=None):
        self.links, self.layer, self.src, self.out, self.sem = links, layer, src, out, sem

    def start(self):
        links = self.links
        mine = links.c == self.layer
        keeps = links.pair == self.layer
        if self.sem is not None:
            self.local = pltpu.make_async_copy(self.src, self.out, self.sem)
            when(mine & keeps, self.local.start)
        at = bits_region(links, ())
        self.far = links.send(self.src.at[at], self.out.at[at], FAR, mine)
        self.near = links.send(self.src, self.out, HOME, mine & jnp.logical_not(keeps))

    def done(self):
        links = self.links
        keeps = links.pair == self.layer
        if self.sem is not None:
            when(links.home & keeps, self.local.wait)
        when(links.home & jnp.logical_not(keeps), self.near.wait_recv)
        when(jnp.logical_not(links.home), self.far.wait_recv)


class Exchange:
    def __init__(self, links, buf):
        self.links, self.buf = links, buf
        columns = buf.shape[-1]
        cut = columns // 256 * 128
        order = list(range(len(links.dp_bit)))
        self.halves = [(pl.ds(0, cut), order), (pl.ds(cut, columns - cut), order[::-1])]
        self.away = jnp.logical_not(links.home)
        self.last = None

    @staticmethod
    def copies(bits):
        return 2 * bits

    def step(self, s):
        self.done()
        self.last = []
        for cols, order in self.halves:
            at = bits_region(self.links, order[:s], cols)
            self.last.append(self.links.send(self.buf.at[at], self.buf.at[at], ("dp", order[s]), self.away))

    def done(self):
        for copy in self.last or ():
            when(self.away, copy.wait_recv)


class Part:
    def __init__(self, links, layer, own, got, dst, sem):
        at = bits_region(links, ())
        keeps = links.pair == layer
        self.ways = (
            (links.home & keeps, pltpu.make_async_copy(own, dst, sem)),
            (links.home & jnp.logical_not(keeps), pltpu.make_async_copy(got, dst, sem)),
            (jnp.logical_not(links.home), pltpu.make_async_copy(got.at[at], dst.at[at], sem)),
        )

    def start(self):
        for cond, copy in self.ways:
            when(cond, copy.start)
        return self

    def wait(self):
        for cond, copy in self.ways:
            when(cond, copy.wait)


def chunk(i, rows):
    return pl.ds(i * (rows // NCH), rows // NCH)


class Scatter:
    COPIES = 3 * NCH

    def __init__(self, links, low, wide):
        self.links, self.low, self.wide = links, low, wide
        self.rows = low.shape[1]
        self.copies = {}

    def far(self, i, p2, p3):
        at = chunk(i, self.rows)
        self.low[0, at] = p3.astype(jnp.bfloat16)
        self.copies["a", i] = self.links.send(self.low.at[0, at], self.low.at[3, at], SIBLING)
        self.wide[0, at] = p2

    def middle(self, i):
        at = chunk(i, self.rows)
        self.copies["a", i].wait_recv()
        self.low[1, at] = (self.wide[0, at] + self.low[3, at].astype(jnp.float32)).astype(jnp.bfloat16)
        self.copies["z", i] = self.links.send(self.low.at[1, at], self.low.at[4, at], PARTNER)

    def near(self, i, p0, p1):
        at = chunk(i, self.rows)
        self.low[2, at] = p1.astype(jnp.bfloat16)
        self.copies["b", i] = self.links.send(self.low.at[2, at], self.low.at[5, at], SIBLING)
        self.wide[1, at] = p0

    def release(self):
        for copy in self.copies.values():
            copy.wait_send()
        self.links.started = [s for s in self.links.started if all(s[0] is not c for c in self.copies.values())]
        self.copies = {}

    def done(self, i):
        at = chunk(i, self.rows)
        self.copies["b", i].wait_recv()
        self.copies["z", i].wait_recv()
        return self.wide[1, at] + self.low[5, at].astype(jnp.float32) + self.low[4, at].astype(jnp.float32)


class Gather:
    COPIES = 3 * NCH

    def __init__(self, links, buf):
        self.links, self.buf = links, buf
        self.rows = buf.shape[1]
        self.copies = {}

    def send(self, i, x):
        at = chunk(i, self.rows)
        self.buf[0, at] = x
        self.copies["z", i] = self.links.send(self.buf.at[0, at], self.buf.at[2, at], PARTNER)
        self.copies["s", i] = self.links.send(self.buf.at[0, at], self.buf.at[1, at], SIBLING)

    def forward(self, i):
        at = chunk(i, self.rows)
        self.copies["z", i].wait_recv()
        self.copies["f", i] = self.links.send(self.buf.at[2, at], self.buf.at[3, at], SIBLING)

    def done(self, i):
        self.copies["s", i].wait_recv()
        self.copies["f", i].wait_recv()
        at = chunk(i, self.rows)
        n = self.rows // NCH
        return jnp.concatenate([self.buf[b, at] for b in range(4)], axis=0)


class DpReduce:
    COPIES = 4

    def __init__(self, links, buf, land0, land1=None, sent=None):
        self.links, self.buf, self.land0, self.land1, self.sent = links, buf, land0, land1, sent
        columns = buf.shape[-1]
        cut = columns // 256 * 128
        self.cols = (pl.ds(0, cut), pl.ds(cut, columns - cut))
        self.orders = ((0, 1), (1, 0))
        self.mine = links.dp_bit
        self.other = [1 - bit for bit in links.dp_bit]
        self.first, self.second = [], []
        for (b0, b1), h, cols in zip(self.orders, range(2), self.cols):
            at = self.place(h, self.other[b0], pl.ds(0, 2))
            self.first.append(links.make(buf.at[at + (slice(None), cols)], land0.at[:, :, cols], ("dp", b0)))
            if land1 is not None:
                self.second.append(links.make(sent.at[0, :, cols], land1.at[0, :, cols], ("dp", b1)))

    @staticmethod
    def scratch(n, columns):
        return [pltpu.VMEM((k, n, columns), jnp.bfloat16) for k in (2, 1, 1)]

    def place(self, h, first, second):
        return (second, first) if self.orders[h][0] == 0 else (first, second)

    def start(self):
        for copy in self.first:
            copy.start()

    def half(self, h, cols):
        b0, b1 = self.orders[h]
        self.first[h].wait_recv()
        sums = []
        for second in (self.other[b1], self.mine[b1]):
            own = self.buf[self.place(h, self.mine[b0], second) + (slice(None), cols)]
            sums.append(own.astype(jnp.float32) + self.land0[second, :, cols].astype(jnp.float32))
        return sums

    def split(self, sent, kept):
        for h, cols in enumerate(self.cols):
            sums = self.half(h, cols)
            sent[:, cols] = sums[0].astype(jnp.bfloat16)
            kept[:, cols] = sums[1].astype(jnp.bfloat16)

    def middle(self):
        for h, cols in enumerate(self.cols):
            b0, b1 = self.orders[h]
            sums = self.half(h, cols)
            self.sent[0, :, cols] = sums[0].astype(jnp.bfloat16)
            self.buf[self.place(h, self.mine[b0], self.mine[b1]) + (slice(None), cols)] = sums[1].astype(jnp.bfloat16)
            self.second[h].start()

    def done(self, out):
        for h, cols in enumerate(self.cols):
            self.second[h].wait_recv()
            b0, b1 = self.orders[h]
            own = self.buf[self.place(h, self.mine[b0], self.mine[b1]) + (slice(None), cols)]
            out[:, cols] = (own.astype(jnp.float32) + self.land1[0, :, cols].astype(jnp.float32)).astype(out.dtype)


class DpFinish:
    COPIES = 2

    def __init__(self, links, sent, kept, land):
        self.kept, self.land = kept, land
        columns = sent.shape[-1]
        cut = columns // 256 * 128
        self.cols = (pl.ds(0, cut), pl.ds(cut, columns - cut))
        self.copies = [
            links.make(sent.at[:, cols], land.at[:, cols], ("dp", b)) for cols, b in zip(self.cols, (1, 0))
        ]

    def start(self):
        for copy in self.copies:
            copy.start()

    def done(self, out):
        for copy, cols in zip(self.copies, self.cols):
            copy.wait_recv()
            out[:, cols] = (self.kept[:, cols].astype(jnp.float32) + self.land[:, cols].astype(jnp.float32)).astype(out.dtype)


class Return:
    COPIES = 2

    def __init__(self, links, layer, src, near, far):
        self.links, self.layer = links, layer
        self.home, self.away = links.home, jnp.logical_not(links.home)
        self.here = links.c == layer
        self.near_cond = self.home & jnp.logical_not(self.here)
        self.near = links.make(src, near, SIBLING, self.near_cond)
        self.far = links.make(src, far, ("return", layer), self.away)

    def start(self):
        when(self.near_cond, self.near.start)
        when(self.away, self.far.start)

    def done(self):
        when(self.here & self.away, self.near.wait_recv)
        when(self.here, self.far.wait_recv)


def start_load(src, dst, sem):
    copy = pltpu.make_async_copy(src, dst, sem)
    copy.start()
    return copy


def block_rows(ref, b, i, rows):
    n = rows // NCH
    return ref[pl.ds(b * rows + i * n, n)]


def put_rows(ref, value, i, rows):
    n = rows // NCH
    for b in range(4):
        ref[pl.ds(b * rows + i * n, n)] = value[b * n : (b + 1) * n]


def weight_grad(out, col, x, y):
    width = x.shape[1]
    step = 384
    for k in range(0, width, step):
        out[k : k + step, col : col + y.shape[1]] = dot(x[:, k : k + step], y, TN).astype(out.dtype)


def flat(ref):
    return ref[...].reshape(-1, ref.shape[-1])


def scatter_product(scatter, i, lhs, weight, rows):
    p = dot(jnp.concatenate([lhs(2), lhs(3)], axis=0), weight, NT)
    n = rows // NCH
    scatter.far(i, p[:n], p[n:])
    p = dot(jnp.concatenate([lhs(0), lhs(1)], axis=0), weight, NT)
    scatter.near(i, p[:n], p[n:])


def slab_grad(out, col, x, y):
    n = out.shape[2]
    width = x.shape[1]
    step = 384
    for k in range(0, width, step):
        res = dot(x[:, k : k + step], y, TN).astype(out.dtype)
        at = k
        while at < k + step:
            slab = at // n
            stop = min(k + step, (slab + 1) * n)
            out[slab // 2, slab % 2, at - slab * n : stop - slab * n, col : col + y.shape[1]] = res[at - k : stop - k]
            at = stop


def block_quarter(links, i):
    return lax.rem(links.r + i // 2, 2) + 2 * lax.rem(links.c + lax.rem(i, 2), 2)


def mid_kernel(order, scale, bits, x_ref, o_ref, ln_ref, cot_ref, live_ref, term_ref, mask_ref,
               wp_hbm, got1_hbm, got2_hbm, wall_hbm, own_q, own_p, own_1, own_2,
               hid_ref, act_ref, dy_ref, o1_ref, lse_ref,
               n2_hbm, u_hbm, g_hbm, n1_hbm, qkv_hbm, dm_hbm, w1_out, w2_out, next_q, next_p, next_1, next_2,
               wp, w1, w2, got_q, got_p, wall, u_buf, g_buf, qkv, gat1, gat2, gat3, low, wide, s_scr, p_scr,
               load_sem, store_sem, send_sem, recv_sem):
    rows, width = x_ref.shape
    n = rows // NCH
    links = Links(send_sem, recv_sem, bits)
    load_p = start_load(wp_hbm, wp, load_sem.at[0])
    load_1 = Part(links, 0, own_1, got1_hbm, w1, load_sem.at[1]).start()
    load_2 = Part(links, 0, own_2, got2_hbm, w2, load_sem.at[2]).start()
    load_w = start_load(wall_hbm, wall, load_sem.at[3])
    links.enter()
    ex1, ex2 = Exchange(links, w1), Exchange(links, w2)
    exq, exp = Exchange(links, got_q), Exchange(links, got_p)
    get_q, get_p = Deliver(links, 1, own_q, got_q, load_sem.at[4]), Deliver(links, 1, own_p, got_p, load_sem.at[5])
    get_1, get_2 = Deliver(links, 1, own_1, next_1), Deliver(links, 1, own_2, next_2)
    s1, s2 = Scatter(links, low, wide), Scatter(links, low, wide)
    g1, g2, g3 = Gather(links, gat1), Gather(links, gat2), Gather(links, gat3)
    load_p.wait()
    for i in range(NCH):
        scatter_product(s1, i, lambda b: block_rows(o_ref, b, i, rows), wp[...], rows)
    load_1.wait()
    ex1.step(0)
    load_2.wait()
    ex2.step(0)
    for i in range(NCH):
        s1.middle(i)
    for s in range(1, bits):
        ex1.step(s)
    get_q.start()
    get_p.start()
    for i in range(NCH):
        h = x_ref[chunk(i, rows)].astype(jnp.float32) + s1.done(i)
        hid_ref[chunk(i, rows)] = h
        g1.send(i, (normed(h)[0] * ln_ref[0:1] + ln_ref[1:2]).astype(jnp.bfloat16))
        if i == 0:
            for s in range(1, bits):
                ex2.step(s)
    s1.release()

    def mlp(i):
        u = dot(g1.done(i), w1[...].reshape(width, -1), NN)
        put_rows(u_buf, u.astype(jnp.bfloat16), i, rows)
        g = gelu_both(u)[0].astype(jnp.bfloat16)
        put_rows(g_buf, g, i, rows)
        if i == 0:
            ex2.done()
        scatter_product(s2, i, lambda b: g[b * n : (b + 1) * n], w2[...].reshape(width, -1), rows)

    g1.forward(0)
    ex1.done()
    for i in range(NCH):
        mlp(i)
        if i + 1 < NCH:
            g1.forward(i + 1)
        s2.middle(i)
    stores = [
        start_load(src, dst, store_sem.at[k])
        for k, (src, dst) in enumerate(((gat1, n2_hbm), (u_buf, u_hbm), (g_buf, g_hbm), (w1, w1_out), (w2, w2_out)))
    ]
    get_q.done()
    exq.step(0)
    for i in range(NCH):
        act = (hid_ref[chunk(i, rows)] + s2.done(i)).astype(jnp.bfloat16)
        act_ref[chunk(i, rows)] = act
        g2.send(i, (normed(act.astype(jnp.float32))[0] * ln_ref[2:3] + ln_ref[3:4]).astype(jnp.bfloat16))
    for i in range(NCH):
        at = chunk(i, rows)
        dy = cot_ref[at].astype(jnp.float32) * live_ref[at]
        dy_ref[at] = dy
        g3.send(i, dy.astype(jnp.bfloat16))
    get_1.start()
    get_2.start()
    for s in range(1, bits):
        exq.step(s)
    get_p.done()
    exp.step(0)
    for i in range(NCH):
        g2.forward(i)
    exq.done()
    weight = got_q[...].reshape(width, -1)
    for i in range(NCH):
        part = (dot(g2.done(i), weight, NN) + term_ref[0:1]).astype(jnp.bfloat16)
        put_rows(qkv, part, i, rows)
    for s in range(1, bits):
        exp.step(s)
    stores += [
        start_load(src, dst, store_sem.at[5 + k])
        for k, (src, dst) in enumerate(((gat2, n1_hbm), (qkv, qkv_hbm), (got_q, next_q)))
    ]
    load_w.wait()
    keys = [quarter(links.r, links.c, j) for j in order]

    def block(i, carry):
        at = pl.ds(pl.multiple_of(i * QB, QB), QB)
        o1_ref[at] = attn_block(
            block_quarter(links, i), keys, scale, qkv.at[at], qkv, mask_ref[...], wall, lse_ref.at[i], s_scr, p_scr
        )
        return carry

    lax.fori_loop(0, 4, block, 0)
    for i in range(NCH):
        g3.forward(i)
    exp.done()
    stores.append(start_load(got_p, next_p, store_sem.at[8]))
    for i in range(NCH):
        g3.copies["s", i].wait_recv()
        g3.copies["f", i].wait_recv()
    stores.append(start_load(gat3, dm_hbm, store_sem.at[9]))
    get_1.done()
    get_2.done()
    links.leave()
    for store in stores:
        store.wait()


VM = pl.BlockSpec(memory_space=pltpu.VMEM)
HB = pl.BlockSpec(memory_space=pl.ANY)


def comm_scratch(copies):
    return [pltpu.SemaphoreType.DMA((copies,)), pltpu.SemaphoreType.DMA((copies,))]


def scatter_scratch(rows, width):
    return [pltpu.VMEM((6, rows, width), jnp.bfloat16), pltpu.VMEM((2, rows, width), jnp.float32)]


def params(ident):
    return pltpu.CompilerParams(collective_id=ident, has_side_effects=True, vmem_limit_bytes=52 << 20)


def mid_chain(x, o, ln, cot, live, term, mask_pad, wp, w1, w2, wall, own, order, scale):
    rows, width = x.shape
    hidden = w1.shape[-1]
    bits = w1.ndim - 2
    heads = wall.shape[0]
    wide = own[0].shape[-1]
    bf16, f32 = jnp.bfloat16, jnp.float32
    out = jax.ShapeDtypeStruct
    res = pl.pallas_call(
        functools.partial(mid_kernel, order, scale, bits),
        in_specs=[VM] * 7 + [HB] * 8,
        out_specs=[VM] * 5 + [HB] * 12,
        out_shape=[
            out((rows, width), f32),
            out((rows, width), bf16),
            out((rows, width), f32),
            out((4 * rows, heads * HD), bf16),
            out((4, heads, QB), f32),
            out((4, rows, width), bf16),
            out((4 * rows, hidden), bf16),
            out((4 * rows, hidden), bf16),
            out((4, rows, width), bf16),
            out((4 * rows, wide), bf16),
            out((4, rows, width), bf16),
        ]
        + [out(w.shape, bf16) for w in (w1, w2, *own)],
        scratch_shapes=[
            *[pltpu.VMEM(w.shape, bf16) for w in (wp, w1, w2, *own[:2])],
            pltpu.VMEM(wall.shape, f32),
            pltpu.VMEM((4 * rows, hidden), bf16),
            pltpu.VMEM((4 * rows, hidden), bf16),
            pltpu.VMEM((4 * rows, wide), bf16),
            pltpu.VMEM((4, rows, width), bf16),
            pltpu.VMEM((4, rows, width), bf16),
            pltpu.VMEM((4, rows, width), bf16),
            *scatter_scratch(rows, width),
            pltpu.VMEM((2, 4 * rows, QB), f32),
            pltpu.VMEM((2, 4 * rows, QB), bf16),
            pltpu.SemaphoreType.DMA((6,)),
            pltpu.SemaphoreType.DMA((10,)),
            *comm_scratch(2 * Scatter.COPIES + 3 * Gather.COPIES + 4 * Deliver.COPIES + 4 * Exchange.copies(bits)),
        ],
        compiler_params=params(1),
        cost_estimate=pl.CostEstimate(flops=60 << 30, bytes_accessed=24 << 20, transcendentals=0),
    )(x, o, ln, cot, live, term, mask_pad, wp, w1, w2, wall, *own)
    hid, act, dy, o1, lse, n2, u, g, n1, qkv, dm = res[:11]
    rest = lambda v: v.reshape(4 * rows, width)
    return hid, act, dy, o1, lse, rest(n2), u, g, rest(n1), qkv, rest(dm), res[11:13], res[13:]


def turn_kernel(bits, fold, x_ref, o_ref, dy_ref, ln_ref, dm_hbm, wp_hbm, own1, own2, got1, got2,
                dh_ref, norm_ref, hid_ref, do_ref, fc2_sent, fc2_ref, y_hbm, da_hbm, fc1_hbm,
                wp, w1, w2, dm, g_buf, du_buf, y_buf, fc1, fc2, gat1, gat2, low, wide, *refs):
    lands, (load_sem, store_sem, send_sem, recv_sem) = refs[:-4], refs[-4:]
    rows, width = x_ref.shape
    n = rows // NCH
    links = Links(send_sem, recv_sem, bits)
    loads = [
        start_load(wp_hbm, wp, load_sem.at[0]),
        Part(links, 1, own1, got1, w1, load_sem.at[1]).start(),
        Part(links, 1, own2, got2, w2, load_sem.at[2]).start(),
        start_load(dm_hbm, dm, load_sem.at[3]),
    ]
    links.enter()
    ex1, ex2 = Exchange(links, w1), Exchange(links, w2)
    s1, s2 = Scatter(links, low, wide), Scatter(links, low, wide)
    g1, g2 = Gather(links, gat1), Gather(links, gat2)
    loads[0].wait()
    for i in range(NCH):
        scatter_product(s1, i, lambda b: block_rows(o_ref, b, i, rows), wp[...], rows)
    loads[1].wait()
    ex1.step(0)
    loads[2].wait()
    ex2.step(0)
    for i in range(NCH):
        s1.middle(i)
    for s in range(1, bits):
        ex1.step(s)
    for i in range(NCH):
        h = x_ref[chunk(i, rows)].astype(jnp.float32) + s1.done(i)
        hid_ref[chunk(i, rows)] = h
        g1.send(i, (normed(h)[0] * ln_ref[0:1] + ln_ref[1:2]).astype(jnp.bfloat16))
        if i == 0:
            for s in range(1, bits):
                ex2.step(s)
    s1.release()
    loads[3].wait()

    def mlp(i):
        u = dot(g1.done(i), w1[...].reshape(width, -1), NN)
        g, slope = gelu_both(u)
        put_rows(g_buf, g.astype(jnp.bfloat16), i, rows)
        dmi = jnp.concatenate([block_rows(dm, b, i, rows) for b in range(4)], axis=0)
        du = (dot(dmi, w2[...].reshape(width, -1), NN) * slope).astype(jnp.bfloat16)
        put_rows(du_buf, du, i, rows)
        scatter_product(s2, i, lambda b: du[b * n : (b + 1) * n], w1[...].reshape(width, -1), rows)

    g1.forward(0)
    ex1.done()
    ex2.done()
    for i in range(NCH):
        mlp(i)
        if i + 1 < NCH:
            g1.forward(i + 1)
        s2.middle(i)
    slab_grad(fc2, 0, dm[...], g_buf[...])
    if fold:
        reduce = DpReduce(links, fc2, lands[0])
        reduce.start()
    sums = None
    for i in range(NCH):
        at = chunk(i, rows)
        dx, dgain, dshift = norm_back(hid_ref[at], s2.done(i), ln_ref[0:1])
        dh = dy_ref[at] + dx
        dh_ref[at] = dh
        g2.send(i, dh.astype(jnp.bfloat16))
        both = jnp.concatenate([dgain, dshift], axis=0)
        sums = both if sums is None else sums + both
    norm_ref[...] = sums
    slab_grad(fc1, 0, flat(gat1), du_buf[...])
    stores = [start_load(fc1, fc1_hbm, store_sem.at[0])]
    g2.forward(0)
    for b in range(4):
        y = dot(g_buf[pl.ds(b * rows, rows)], w2[...].reshape(width, -1), NT)
        y_buf[pl.ds(b * rows, rows)] = y.astype(jnp.bfloat16)
    stores.append(start_load(y_buf, y_hbm, store_sem.at[1]))
    for i in range(1, NCH):
        g2.forward(i)
    for i in range(NCH):
        put_rows(do_ref, dot(g2.done(i), wp[...], NN).astype(jnp.bfloat16), i, rows)
    stores.append(start_load(gat2, da_hbm, store_sem.at[2]))
    if fold:
        reduce.split(fc2_sent, fc2_ref)
    else:
        fc2_ref[...] = fc2[...]
    links.leave()
    for store in stores:
        store.wait()


def turn_chain(ndp, x, o, dy, ln, dm, wp, own, got):
    rows, width = x.shape
    hidden = own[0].shape[-1]
    bits = own[0].ndim - 2
    fold = ndp == 4
    lw = wp.shape[1]
    n = width // 4
    bf16, f32 = jnp.bfloat16, jnp.float32
    out = jax.ShapeDtypeStruct
    res = pl.pallas_call(
        functools.partial(turn_kernel, bits, fold),
        in_specs=[VM, VM, VM, VM] + [HB] * 6,
        out_specs=[VM] * 6 + [HB] * 3,
        out_shape=[
            out((rows, width), f32),
            out((2, width), f32),
            out((rows, width), f32),
            out((4 * rows, lw), bf16),
            out((n, hidden), bf16),
            out((n, hidden) if fold else (2, 2, n, hidden), bf16),
            out((4 * rows, width), bf16),
            out((4, rows, width), bf16),
            out((2, 2, n, hidden), bf16),
        ],
        scratch_shapes=[
            pltpu.VMEM(wp.shape, bf16),
            pltpu.VMEM(own[0].shape, bf16),
            pltpu.VMEM(own[1].shape, bf16),
            pltpu.VMEM((4 * rows, width), bf16),
            pltpu.VMEM((4 * rows, hidden), bf16),
            pltpu.VMEM((4 * rows, hidden), bf16),
            pltpu.VMEM((4 * rows, width), bf16),
            pltpu.VMEM((2, 2, n, hidden), bf16),
            pltpu.VMEM((2, 2, n, hidden), bf16),
            pltpu.VMEM((4, rows, width), bf16),
            pltpu.VMEM((4, rows, width), bf16),
            *scatter_scratch(rows, width),
            *(DpReduce.scratch(n, hidden)[:1] if fold else []),
            pltpu.SemaphoreType.DMA((4,)),
            pltpu.SemaphoreType.DMA((3,)),
            *comm_scratch(2 * Scatter.COPIES + 2 * Gather.COPIES + 2 * Exchange.copies(bits) + DpReduce.COPIES),
        ],
        compiler_params=params(2),
        cost_estimate=pl.CostEstimate(flops=60 << 30, bytes_accessed=24 << 20, transcendentals=0),
    )(x, o, dy, ln, dm, wp, *own, *got)
    dh, norms, hid, do, sent, fc2, y, da, fc1 = res
    return dh, norms, y, hid, do, da.reshape(4 * rows, width), fc1, (sent, fc2)


def back_kernel(bits, fold, layers, flags_ref, x_ref, dh1_ref, hid_ref, ln_ref, dqkv_ref, o1_ref, lab_ref,
                wq_hbm, wp_hbm, w1_hbm, w2_hbm, u_hbm, g_hbm, n2_hbm, n1_hbm, da1_hbm, dwall_hbm, *refs):
    refs = list(refs)
    take = lambda k: [refs.pop(0) for _ in range(k)]
    blocks = take(len(layers))
    gin_ref, dh_ref, norm_ref, do_ref, da_hbm, fc1_hbm, fc2_sent, fc2_out, qp_out, rel_out, sum_out = take(11)
    places = [take(2) for _ in range(len(layers) + 1)]
    wq, wp, w1, w2, u_buf, g_buf, fc2, gqp, strips, gin_low, gat1, gat2, low, wide = take(14)
    if fold:
        lands_qp, lands_fc = take(3), take(1)
    load_sem, store_sem, send_sem, recv_sem = refs
    small, out_lab = flags_ref[0], flags_ref[1]
    rows, width = x_ref.shape
    n = rows // NCH
    hidden = w1.shape[1]
    heads = rel_out.shape[0]
    lw = o1_ref.shape[1]
    load = lambda k, src, dst: start_load(src, dst, load_sem.at[k])
    load_q, load_n1, load_da = load(0, wq_hbm, wq), load(1, n1_hbm, u_buf), load(2, da1_hbm, g_buf)
    load_1, load_2, load_p = load(3, w1_hbm, w1), load(4, w2_hbm, w2), load(5, wp_hbm, wp)
    load_strip = load(6, dwall_hbm.at[0], strips)
    links = Links(send_sem, recv_sem, bits)
    links.enter()
    blocks.append(gin_low)
    layers = layers + [1]
    returns = [Return(links, layer, src, *at) for layer, src, at in zip(layers, blocks, places)]
    for back in returns[:-1]:
        back.start()
    s1, s2 = Scatter(links, low, wide), Scatter(links, low, wide)
    g1, g2 = Gather(links, gat1), Gather(links, gat2)
    load_q.wait()
    for i in range(NCH):
        scatter_product(s1, i, lambda b: block_rows(dqkv_ref, b, i, rows), wq[...], rows)
        if i:
            s1.middle(i - 1)
    s1.middle(NCH - 1)
    load_n1.wait()
    slab_grad(gqp, 0, u_buf[...], dqkv_ref[...])
    load_da.wait()
    slab_grad(gqp, dqkv_ref.shape[1], g_buf[...], o1_ref[...])
    load_u, load_g = load(8, u_hbm, u_buf), load(9, g_hbm, g_buf)
    if fold:
        reduce = DpReduce(links, gqp, *lands_qp)
        reduce.start()
    cols = jnp.sum(dqkv_ref[...].astype(jnp.float32), axis=0, keepdims=True)
    sum_out[...] = jnp.concatenate([cols[:, :lw], cols[:, 2 * lw :]], axis=1)
    sums1 = None
    for i in range(NCH):
        at = chunk(i, rows)
        dx, dgain, dshift = norm_back(x_ref[at].astype(jnp.float32), s1.done(i), ln_ref[0:1])
        gin = dh1_ref[at] + dx
        gin_ref[at] = gin
        gin_low[at] = gin.astype(jnp.bfloat16)
        g1.send(i, gin_low[at])
        both = jnp.concatenate([dgain, dshift], axis=0)
        sums1 = both if sums1 is None else sums1 + both
    returns[-1].start()
    lab = lab_ref[...]
    hi_mask, lo_hot = _labels_hi_lo(lab)

    def bias_head(h, load_strip):
        load_strip.wait()
        rel_out[h] = wall_grad(small, out_lab, lab, hi_mask, lo_hot, strips)
        return load(6, dwall_hbm.at[h + 1], strips) if h + 1 < heads else None

    load_strip = bias_head(0, load_strip)
    load_strip = bias_head(1, load_strip)
    s1.release()
    load_1.wait()
    load_2.wait()
    load_u.wait()

    def mlp(i):
        dmi = g1.done(i)
        ui = jnp.concatenate([block_rows(u_buf, b, i, rows) for b in range(4)], axis=0).astype(jnp.float32)
        du = (dot(dmi, w2[...], NN) * gelu_both(ui)[1]).astype(jnp.bfloat16)
        put_rows(u_buf, du, i, rows)
        scatter_product(s2, i, lambda b: du[b * n : (b + 1) * n], w1[...], rows)

    g1.forward(0)
    for i in range(NCH):
        mlp(i)
        if i + 1 < NCH:
            g1.forward(i + 1)
        s2.middle(i)
    if fold:
        reduce.middle()
    load_g.wait()
    slab_grad(fc2, 0, flat(gat1), g_buf[...])
    if fold:
        reduce_2 = DpReduce(links, fc2, *lands_fc)
        reduce_2.start()
    load_n2 = load(10, n2_hbm, g_buf)
    sums2 = None
    for i in range(NCH):
        at = chunk(i, rows)
        dx, dgain, dshift = norm_back(hid_ref[at], s2.done(i), ln_ref[1:2])
        dh = gin_ref[at].astype(jnp.bfloat16).astype(jnp.float32) + dx
        dh_ref[at] = dh
        g2.send(i, dh.astype(jnp.bfloat16))
        both = jnp.concatenate([dgain, dshift], axis=0)
        sums2 = both if sums2 is None else sums2 + both
    norm_ref[...] = jnp.concatenate([sums1, sums2], axis=0)
    load_n2.wait()
    weight_grad(w2, 0, g_buf[...], u_buf[...])
    stores = [start_load(w2, fc1_hbm, store_sem.at[0])]
    load_strip = bias_head(2, load_strip)
    load_p.wait()
    g2.forward(0)
    bias_head(3, load_strip)
    for i in range(1, NCH):
        g2.forward(i)
    for i in range(NCH):
        put_rows(do_ref, dot(g2.done(i), wp[...], NN).astype(jnp.bfloat16), i, rows)
    stores.append(start_load(gat2, da_hbm, store_sem.at[2]))
    if fold:
        reduce.done(qp_out)
        reduce_2.split(fc2_sent, fc2_out)
    else:
        qp_out[...] = gqp[...]
        fc2_out[...] = fc2[...]
    for back in returns:
        back.done()
    links.leave()
    for store in stores:
        store.wait()


def back_chain(ndp, flags, x, dh1, hid, ln, dqkv, o1, lab, wq, wp, w1, w2, u, g, n2, n1, da1, dwall, returns):
    rows, width = x.shape
    hidden = w1.shape[1]
    lw = wp.shape[1]
    heads = dwall.shape[0]
    fold = ndp == 4
    bits = 2
    n = width // 4
    qp_cols = wq.shape[1] + lw
    bf16, f32 = jnp.bfloat16, jnp.float32
    out = jax.ShapeDtypeStruct
    layers = [layer for layer, _ in returns]
    blocks = [block for _, block in returns]
    copies = 2 * Scatter.COPIES + 2 * Gather.COPIES + 2 * DpReduce.COPIES + (len(layers) + 1) * Return.COPIES
    res = pl.pallas_call(
        functools.partial(back_kernel, bits, fold, layers),
        in_specs=[pl.BlockSpec(memory_space=pltpu.SMEM)] + [VM] * 7 + [HB] * (10 + len(blocks)),
        out_specs=[VM, VM, VM, VM, HB, HB, VM, VM, VM, VM, VM] + [HB] * (2 * len(blocks) + 2),
        out_shape=[
            out((rows, width), f32),
            out((rows, width), f32),
            out((4, width), f32),
            out((4 * rows, lw), bf16),
            out((4, rows, width), bf16),
            out((width, hidden), bf16),
            out((n, hidden), bf16),
            out((n, hidden) if fold else (2, 2, n, hidden), bf16),
            out((n, qp_cols) if fold else (2, 2, n, qp_cols), bf16),
            out((heads, 32, 128), f32),
            out((1, 2 * lw), f32),
        ]
        + [out(block.shape, block.dtype) for block in blocks for _ in range(2)]
        + [out((rows, width), bf16)] * 2,
        scratch_shapes=[
            pltpu.VMEM(wq.shape, bf16),
            pltpu.VMEM(wp.shape, bf16),
            pltpu.VMEM(w1.shape, bf16),
            pltpu.VMEM(w2.shape, bf16),
            pltpu.VMEM((4 * rows, hidden), bf16),
            pltpu.VMEM((4 * rows, hidden), bf16),
            pltpu.VMEM((2, 2, n, hidden), bf16),
            pltpu.VMEM((2, 2, n, qp_cols), bf16),
            pltpu.VMEM(dwall.shape[1:], f32),
            pltpu.VMEM((rows, width), bf16),
            pltpu.VMEM((4, rows, width), bf16),
            pltpu.VMEM((4, rows, width), bf16),
            *scatter_scratch(rows, width),
            *(DpReduce.scratch(n, qp_cols) + DpReduce.scratch(n, hidden)[:1] if fold else []),
            pltpu.SemaphoreType.DMA((11,)),
            pltpu.SemaphoreType.DMA((3,)),
            *comm_scratch(copies),
        ],
        compiler_params=params(3),
        cost_estimate=pl.CostEstimate(flops=60 << 30, bytes_accessed=24 << 20, transcendentals=0),
    )(flags, x, dh1, hid, ln, dqkv, o1, lab, wq, wp, w1, w2, u, g, n2, n1, da1, dwall, *blocks)
    gin, dh, norms, do, da, fc1, sent, fc2, qp, rel, sums = res[:11]
    got = [(res[11 + 2 * k], res[12 + 2 * k]) for k in range(len(layers) + 1)]
    return gin, dh, norms, do, da.reshape(4 * rows, width), fc1, (sent, fc2), qp, rel, sums, got


def start_kernel(order, scale, bits, flags_ref, x_hbm, cot_hbm, mask_ref, lab_ref, tab_hbm, pack_hbm,
                 wq_hbm, wp_hbm, w1_hbm, w2_hbm,
                 x_ref, cot_ref, pack_ref, lse_ref, o_ref, n1_hbm, qkv_hbm, wall0_hbm, wall1_hbm,
                 wq0_hbm, wp0_hbm, w10_hbm, w20_hbm,
                 tab, wq, wp, qkv, wall, gat1, s_scr, p_scr, load_sem, store_sem, send_sem, recv_sem):
    small, out_lab = flags_ref[0], flags_ref[1]
    rows, width = x_ref.shape
    wide = qkv.shape[1]
    heads = wall.shape[1]
    links = Links(send_sem, recv_sem, bits)
    pair, home = links.pair, links.home
    own_x = pltpu.make_async_copy(x_hbm.at[pair], x_ref, load_sem.at[0])
    when(home, own_x.start)
    own_cot = pltpu.make_async_copy(cot_hbm.at[pair], cot_ref, load_sem.at[7])
    when(home, own_cot.start)
    links.enter()
    packs = [Spread(links, l, pack_hbm, pack_ref.at[l], load_sem.at[1 + l]) for l in range(2)]
    tabs = [Spread(links, l, tab_hbm, tab.at[l], load_sem.at[3 + l]) for l in range(2)]
    tabs[0].start()
    packs[0].start()
    far_x = links.send(x_hbm.at[1 - pair], x_ref, FAR, home)
    tabs[1].start()
    packs[1].start()
    get_q = Deliver(links, 0, wq_hbm, wq, load_sem.at[5])
    get_p = Deliver(links, 0, wp_hbm, wp, load_sem.at[6])
    get_1, get_2 = Deliver(links, 0, w1_hbm, w10_hbm), Deliver(links, 0, w2_hbm, w20_hbm)
    ex_q, ex_p = Exchange(links, wq), Exchange(links, wp)
    get_q.start()
    lab = lab_ref[...]
    hi_mask, lo_hot = _labels_hi_lo(lab)

    def build(l):
        def one(h, carry):
            build_wall(small, out_lab, lab, hi_mask, lo_hot, tab[l, h], wall.at[l, h])
            return carry

        lax.fori_loop(0, heads, one, 0)

    tabs[0].done()
    build(0)
    stores = [start_load(wall.at[0], wall0_hbm, store_sem.at[0])]
    packs[0].done()
    when(home, own_x.wait)
    when(jnp.logical_not(home), far_x.wait_recv)
    g1 = Gather(links, gat1)
    for i in range(NCH):
        at = chunk(i, rows)
        xhat = normed(x_ref[at].astype(jnp.float32))[0]
        g1.send(i, (xhat * pack_ref[0, 0:1] + pack_ref[0, 2:3]).astype(jnp.bfloat16))
    get_p.start()
    get_1.start()
    get_2.start()
    far_cot = links.send(cot_hbm.at[1 - pair], cot_ref, FAR, home)
    tabs[1].done()
    build(1)
    stores.append(start_load(wall.at[1], wall1_hbm, store_sem.at[5]))
    get_q.done()
    ex_q.step(0)
    for i in range(NCH):
        g1.forward(i)
    for s in range(1, bits):
        ex_q.step(s)
    for i in range(NCH):
        g1.copies["s", i].wait_recv()
        g1.copies["f", i].wait_recv()
    stores.append(start_load(gat1, n1_hbm, store_sem.at[1]))
    packs[1].done()
    get_p.done()
    ex_q.done()
    ex_p.step(0)
    stores.append(start_load(wq, wq0_hbm, store_sem.at[2]))
    term = pack_ref[0, pl.ds(4 + pair, 1)][:, :wide]
    weight = wq[...].reshape(width, wide)
    for b in range(4):
        qkv[pl.ds(b * rows, rows)] = (dot(gat1[b], weight, NN) + term).astype(jnp.bfloat16)
    stores.append(start_load(qkv, qkv_hbm, store_sem.at[3]))
    for s in range(1, bits):
        ex_p.step(s)
    keys = [quarter(links.r, links.c, j) for j in order]

    def block(i, carry):
        at = pl.ds(pl.multiple_of(i * QB, QB), QB)
        qq = lax.rem(links.r + i // 2, 2) + 2 * lax.rem(links.c + lax.rem(i, 2), 2)
        o_ref[at] = attn_block(
            qq, keys, scale, qkv.at[at], qkv, mask_ref[...], wall.at[0], lse_ref.at[i], s_scr, p_scr
        )
        return carry

    lax.fori_loop(0, 4, block, 0)
    ex_p.done()
    stores.append(start_load(wp, wp0_hbm, store_sem.at[4]))
    get_1.done()
    get_2.done()
    when(home, own_cot.wait)
    when(jnp.logical_not(home), far_cot.wait_recv)
    links.leave()
    for store in stores:
        store.wait()


def start_chain(flags, x, cot, mask_pad, lab, table, pack, wq, wp, w1, w2, order, scale):
    bits = wq.ndim - 2
    _, rows, width = x.shape
    heads = table.shape[0]
    wide = wq.shape[-1]
    bf16, f32 = jnp.bfloat16, jnp.float32
    out = jax.ShapeDtypeStruct
    copies = 2 + 4 * Spread.COPIES + 4 * Deliver.COPIES + 2 * Exchange.copies(bits) + Gather.COPIES
    return pl.pallas_call(
        functools.partial(start_kernel, order, scale, bits),
        in_specs=[pl.BlockSpec(memory_space=pltpu.SMEM), HB, HB, VM, VM, HB, HB, HB, HB, HB, HB],
        out_specs=[VM] * 5 + [HB] * 8,
        out_shape=[
            out((rows, width), bf16),
            out((rows, width), bf16),
            out((2,) + pack.shape, f32),
            out((4, heads, QB), f32),
            out((4 * rows, heads * HD), bf16),
            out((4, rows, width), bf16),
            out((4 * rows, wide), bf16),
            out((heads, 32, WALL), f32),
            out((heads, 32, WALL), f32),
            *[out(w.shape, bf16) for w in (wq, wp, w1, w2)],
        ],
        scratch_shapes=[
            pltpu.VMEM((2,) + table.shape, f32),
            *[pltpu.VMEM(w.shape, bf16) for w in (wq, wp)],
            pltpu.VMEM((4 * rows, wide), bf16),
            pltpu.VMEM((2, heads, 32, WALL), f32),
            pltpu.VMEM((4, rows, width), bf16),
            pltpu.VMEM((2, 4 * rows, QB), f32),
            pltpu.VMEM((2, 4 * rows, QB), bf16),
            pltpu.SemaphoreType.DMA((8,)),
            pltpu.SemaphoreType.DMA((6,)),
            *comm_scratch(copies),
        ],
        compiler_params=params(0),
        cost_estimate=pl.CostEstimate(flops=80 << 30, bytes_accessed=24 << 20, transcendentals=0),
    )(flags, x, cot, mask_pad, lab, table, pack, wq, wp, w1, w2)


def attn_back(links, order, scale, qkv_ref, do_ref, o_ref, lse_ref, k_extra, wall, acc, p_scr, s_scr, dq_scr, dk_scr, dv_scr,
              dqkv_ref, event):
    heads = wall.shape[0]
    width = heads * HD
    total = qkv_ref.shape[0]
    keys = [quarter(links.r, links.c, j) for j in order]
    lane = lax.broadcasted_iota(jnp.int32, (QB, 128 - HD), 1)
    q_extra = jnp.where(lane == 0, 1.0, 0.0).astype(jnp.bfloat16)

    def block(i, carry):
        at = pl.ds(pl.multiple_of(i * QB, QB), QB)
        q_ref, d_ref, out_ref = qkv_ref.at[at], do_ref.at[at], o_ref.at[at]
        qq = block_quarter(links, i)
        dqs = []
        for h in range(heads):
            kh = head_lanes(qkv_ref, width + HD * h, k_extra)
            qh = head_lanes(q_ref, HD * h, q_extra)
            vh = head_lanes(qkv_ref, 2 * width + HD * h)
            doh = head_lanes(d_ref, HD * h)
            oh = head_lanes(out_ref, HD * h)
            inner = jnp.sum((doh.astype(jnp.float32) * oh.astype(jnp.float32)).T, axis=0, keepdims=True)
            lse = lse_ref[i, h : h + 1, :]
            for kb in range(total // 256):
                s_t = dot(kh[256 * kb : 256 * kb + 256], qh, NT)
                dp_t = dot(vh[256 * kb : 256 * kb + 256], doh, NT)
                for js in range(8):
                    st = 8 * kb + js
                    start = strip_start(qq, js, keys[kb])
                    s = s_t[32 * js : 32 * js + 32] * (scale * LOG2E) + wall[h, :, pl.ds(start, QB)]
                    p = jnp.exp2(s - lse)
                    ds = p * (dp_t[32 * js : 32 * js + 32] - inner)
                    p_scr[h % 2, 32 * st : 32 * st + 32] = p.astype(jnp.bfloat16)
                    s_scr[h % 2, 32 * st : 32 * st + 32] = ds.astype(jnp.bfloat16)
                    acc[h, :, pl.ds(start, QB)] += ds
            p_b, ds_b = p_scr[h % 2], s_scr[h % 2]
            dv_scr[h] += dot(p_b, doh, NN)
            dk_scr[h] += dot(ds_b, qh, NN)
            dq_t = dot(kh, ds_b, TN) * scale
            dqs.append(dq_t.T[:, :HD].astype(jnp.bfloat16))
        dq_scr[at] = jnp.concatenate(dqs, axis=1)
        event(i)
        return carry

    lax.fori_loop(0, total // QB, block, 0)
    parts = [dq_scr[...]]
    parts += [(dk_scr[h, :, :HD] * scale).astype(jnp.bfloat16) for h in range(heads)]
    parts += [dv_scr[h, :, :HD].astype(jnp.bfloat16) for h in range(heads)]
    dqkv_ref[...] = jnp.concatenate(parts, axis=1)


def bwd_kernel(order, scale, bits, fold, layers, summed, qkv_ref, do_ref, o_ref, lse_ref, mask_ref, wall_hbm, gfc_hbm, *refs):
    refs = list(refs)
    take = lambda k: [refs.pop(0) for _ in range(k)]
    blocks = take(len(layers))
    sent_2, kept_2 = take(2) if fold else (None, None)
    y_ref, hid_ref = take(2) if summed else (None, None)
    dqkv_ref, acc_hbm = take(2)
    fc_out, fin_out = take(2) if fold else (None, None)
    places = [take(2) for _ in range(len(layers) + (1 if fold else 0))]
    (act_ref,) = take(1) if summed else (None,)
    wall, acc, p_scr, s_scr, dq_scr, dk_scr, dv_scr = take(7)
    if fold:
        gfc, land0, land1, sent, land_2 = take(5)
    if summed:
        (low,) = take(1)
    load_sem, store_sem, send_sem, recv_sem = refs
    loads = [start_load(wall_hbm, wall, load_sem.at[0])]
    if fold:
        loads.append(start_load(gfc_hbm, gfc, load_sem.at[1]))
    links = Links(send_sem, recv_sem, bits)
    links.enter()
    returns = [Return(links, layer, src, *at) for layer, src, at in zip(layers, blocks, places)]
    if fold:
        finish = DpFinish(links, sent_2, kept_2, land_2)
        finish.start()
        last = Return(links, 1, fin_out, *places[-1])
        reduce = DpReduce(links, gfc, land0, land1, sent)
    if summed:
        rows = hid_ref.shape[0]
        part = lambda b: y_ref.at[pl.ds(b * rows, rows)]
        to_sib = links.make(part(3), low.at[0], SIBLING)
        near = links.make(part(1), low.at[1], SIBLING)
        to_partner = links.make(low.at[2], low.at[3], PARTNER)
        to_sib.start()
        near.start()
    acc[...] = jnp.zeros_like(acc)
    dk_scr[...] = jnp.zeros_like(dk_scr)
    dv_scr[...] = jnp.zeros_like(dv_scr)
    if fold:
        loads[1].wait()
        reduce.start()
    if summed:
        to_sib.wait_recv()
        low[2] = (part(2)[...].astype(jnp.float32) + low[0].astype(jnp.float32)).astype(jnp.bfloat16)
        to_partner.start()
    for back in returns:
        back.start()
    loads[0].wait()

    def finished():
        finish.done(fin_out)
        last.start()

    def event(i):
        if fold:
            pl.when(i == 0)(finished)

    attn_back(
        links, order, scale, qkv_ref, do_ref, o_ref, lse_ref, mask_ref[...], wall, acc, p_scr, s_scr, dq_scr, dk_scr, dv_scr,
        dqkv_ref, event,
    )
    stores = [start_load(acc, acc_hbm, store_sem.at[0])]
    if fold:
        reduce.middle()
    if summed:
        near.wait_recv()
        to_partner.wait_recv()
        act = hid_ref[...] + part(0)[...].astype(jnp.float32) + low[1].astype(jnp.float32) + low[3].astype(jnp.float32)
        act_ref[...] = act.astype(jnp.bfloat16)
    if fold:
        reduce.done(fc_out)
        last.done()
    for back in returns:
        back.done()
    links.leave()
    for store in stores:
        store.wait()


def bwd_chain(ident, fold, qkv, do, o, lse, mask_pad, wall, gfc, finish, returns, order, scale, summed=None):
    total, wide = qkv.shape
    heads = wall.shape[0]
    bits = 2
    n, columns = gfc.shape[2:]
    bf16, f32 = jnp.bfloat16, jnp.float32
    out = jax.ShapeDtypeStruct
    layers = [layer for layer, _ in returns]
    blocks = [block for _, block in returns]
    outs = [out((total, wide), bf16), out(wall.shape, f32)]
    specs = [VM, HB]
    if fold:
        outs += [out((n, columns), bf16)] * 2
        specs += [VM] * 2
    for block in blocks + ([finish[0]] if fold else []):
        outs += [out(block.shape, block.dtype)] * 2
        specs += [HB] * 2
    scratch = [
        pltpu.VMEM(wall.shape, f32),
        pltpu.VMEM(wall.shape, f32),
        pltpu.VMEM((2, total, QB), bf16),
        pltpu.VMEM((2, total, QB), bf16),
        pltpu.VMEM((total, heads * HD), bf16),
        pltpu.VMEM((heads, total, 128), f32),
        pltpu.VMEM((heads, total, 128), f32),
    ]
    if fold:
        scratch += [pltpu.VMEM(gfc.shape, bf16), *DpReduce.scratch(n, columns), pltpu.VMEM((n, columns), bf16)]
    more = list(finish) if fold else []
    if summed is not None:
        more += list(summed)
        rows, width = summed[1].shape
        outs.append(out((rows, width), bf16))
        specs.append(VM)
        scratch.append(pltpu.VMEM((4, rows, width), bf16))
    copies = len(layers) * Return.COPIES + (DpReduce.COPIES + DpFinish.COPIES + Return.COPIES if fold else 0) + (3 if summed else 0)
    res = pl.pallas_call(
        functools.partial(bwd_kernel, order, scale, bits, fold, layers, summed is not None),
        in_specs=[VM] * 5 + [HB] * 2 + [VM] * (len(blocks) + len(more)),
        out_specs=specs,
        out_shape=outs,
        scratch_shapes=scratch
        + [pltpu.SemaphoreType.DMA((2,)), pltpu.SemaphoreType.DMA((1,)), *comm_scratch(max(copies, 1))],
        compiler_params=params(ident),
        cost_estimate=pl.CostEstimate(flops=24 << 30, bytes_accessed=20 << 20, transcendentals=0),
    )(qkv, do, o, lse, mask_pad, wall, gfc, *blocks, *more)
    res = list(res)
    dqkv, acc = res[:2]
    res = res[2:]
    fc, fin = (res.pop(0), res.pop(0)) if fold else (None, None)
    got = [(res[2 * k], res[2 * k + 1]) for k in range(len(layers) + (1 if fold else 0))]
    act = res[-1] if summed is not None else None
    return dqkv, acc, fc, fin, got, act


class SumHops:
    def __init__(self, links, buf, land, hops):
        self.links, self.buf, self.land, self.hops, self.k = links, buf, land, hops, 0

    def send(self):
        if self.k < len(self.hops):
            self.copy = self.links.send(self.buf, self.land.at[self.k], self.hops[self.k], track=False)

    def take(self):
        self.copy.wait_recv()
        self.copy.wait_send()
        self.buf[...] = self.buf[...] + self.land[self.k]
        self.k += 1
        self.send()


def end_kernel(order, scale, bits, fold, layers, flags_ref, qkv_ref, do_ref, o_ref, lse_ref, mask_ref,
               x_ref, dh_ref, ln_ref, lab_ref, small_ref, rel1_ref,
               wall_hbm, wq_hbm, n1_hbm, da_hbm, fc_hbm, *refs):
    refs = list(refs)
    take = lambda k: [refs.pop(0) for _ in range(k)]
    blocks = take(len(layers))
    sent_2, kept_2 = take(2) if fold else (None, None)
    gin_ref, small_out, rel_out, q_out = take(4)
    fc_out, fin_out = take(2) if fold else (None, None)
    (all_fc,) = (None,) if fold else take(1)
    places = [take(2) for _ in range(len(layers) + (4 if fold else 1))]
    acc, dqkv_ref, gq, fc, gin_low, low1 = take(6)
    rel, rel_land, rel_near, smalls, small_land, norm_land, small_near = take(7)
    if fold:
        lands_q, lands_f, (land_2,) = take(3), take(3), take(1)
    load_sem, send_sem, recv_sem = refs
    small, out_lab = flags_ref[0], flags_ref[1]
    rows, width = x_ref.shape
    heads = rel.shape[1]
    hidden = fc_hbm.shape[-1]
    load_f = start_load(fc_hbm, fc.at[:, :, :, pl.ds(0, hidden)], load_sem.at[1])
    links = Links(send_sem, recv_sem, bits)
    home, away = links.home, jnp.logical_not(links.home)
    links.enter()
    give = list(zip(layers, blocks)) + [(0, gin_low)] + ([(0, fc_out), (0, q_out), (0, fin_out)] if fold else [])
    returns = [Return(links, layer, src, *at) for (layer, src), at in zip(give, places)]
    early = len(layers)
    for back in returns[:early]:
        back.start()
    if fold:
        finish = DpFinish(links, sent_2, kept_2, land_2)
        finish.start()
        reduce_f = DpReduce(links, fc, *lands_f)
        reduce_q = DpReduce(links, gq, *lands_q)

    def proj_grad(rows_buf):
        start_load(da_hbm, rows_buf, load_sem.at[4]).wait()
        slab_grad(fc, hidden, rows_buf[...], o_ref[...])

    pl.run_scoped(proj_grad, pltpu.VMEM(da_hbm.shape, jnp.bfloat16))
    load_f.wait()
    if fold:
        reduce_f.start()
    acc[...] = jnp.zeros_like(acc)

    def finished():
        finish.done(fin_out)
        returns[early + 3].start()

    def event(i):
        if fold:
            pl.when(i == 0)(finished)

    def attention(wall, p_scr, s_scr, dq_scr, dk_scr, dv_scr):
        load_w = start_load(wall_hbm, wall, load_sem.at[0])
        dk_scr[...] = jnp.zeros_like(dk_scr)
        dv_scr[...] = jnp.zeros_like(dv_scr)
        load_w.wait()
        attn_back(
            links, order, scale, qkv_ref, do_ref, o_ref, lse_ref, mask_ref[...], wall, acc, p_scr, s_scr, dq_scr, dk_scr,
            dv_scr, dqkv_ref, event,
        )

    total = qkv_ref.shape[0]
    vmem, bf16, f32 = pltpu.VMEM, jnp.bfloat16, jnp.float32
    pl.run_scoped(
        attention,
        vmem(wall_hbm.shape, f32),
        vmem((2, total, QB), bf16),
        vmem((2, total, QB), bf16),
        vmem((total, heads * HD), bf16),
        vmem((heads, total, 128), f32),
        vmem((heads, total, 128), f32),
    )
    lw = o_ref.shape[1]

    def rest(wq, rows_buf, wide1):
        s1 = Scatter(links, low1, wide1)
        load_q = start_load(wq_hbm, wq, load_sem.at[2])
        load_n = start_load(n1_hbm, rows_buf, load_sem.at[3])
        load_q.wait()
        for i in range(NCH):
            scatter_product(s1, i, lambda b: block_rows(dqkv_ref, b, i, rows), wq[...], rows)
            if i:
                s1.middle(i - 1)
        s1.middle(NCH - 1)
        load_n.wait()
        slab_grad(gq, 0, rows_buf[...], dqkv_ref[...])
        if fold:
            reduce_f.middle()
            reduce_q.start()
        cols = jnp.sum(dqkv_ref[...].astype(jnp.float32), axis=0, keepdims=True)
        mine = jnp.concatenate([cols[:, :lw], cols[:, 2 * lw :]], axis=1)
        images = (smalls.shape[0] - 8) // 2
        number = 2 * lax.axis_index("dp") + links.pair
        here = lax.broadcasted_iota(jnp.int32, (images, 2 * lw), 0) == number
        smalls[...] = small_ref[...]
        smalls[8 : 8 + images, 0 : 2 * lw] = jnp.where(here, jnp.broadcast_to(mine, (images, 2 * lw)), 0.0)
        lab = lab_ref[...]
        hi_mask, lo_hot = _labels_hi_lo(lab)
        rel[1] = rel1_ref[...]

        def heads_of(a, b):
            def one(h, carry):
                rel[0, h] = wall_grad(small, out_lab, lab, hi_mask, lo_hot, acc.at[h])
                return carry

            lax.fori_loop(a, b, one, 0)

        hops = [ACROSS] + [("dp", b) for b in range(bits)]
        small_hops = SumHops(links, smalls, small_land, hops)
        rel_hops = SumHops(links, rel, rel_land, hops)
        heads_of(0, heads // 2)
        if fold:
            reduce_f.done(fc_out)
            returns[early + 1].start()
        late = None
        for i in range(NCH):
            at = chunk(i, rows)
            dx, dgain, dshift = norm_back(x_ref[at].astype(jnp.float32), s1.done(i), ln_ref[0:1])
            gin = dh_ref[at] + dx
            gin_ref[at] = gin
            gin_low[at] = gin.astype(jnp.bfloat16)
            both = jnp.concatenate([dgain, dshift], axis=0)
            late = both if late is None else late + both
        smalls[0:2] = late
        small_hops.send()
        heads_of(heads // 2, heads)
        rel_hops.send()
        returns[early].start()
        if fold:
            reduce_q.middle()
            reduce_q.done(q_out)
            returns[early + 2].start()
        else:
            q_out[...] = gq[...]
            all_fc[...] = fc[...]
        for _ in range(bits + 1):
            small_hops.take()
            rel_hops.take()
        images_at = pl.ds(8, smalls.shape[0] - 8)
        rel_copy = links.send(rel.at[1 - links.c], rel_near, SIBLING, home)
        small_copy = links.send(smalls.at[images_at], small_near, SIBLING, home)
        norm_hops = SumHops(links, smalls.at[pl.ds(0, 8)], norm_land, [PARTNER, SIBLING])
        norm_hops.send()

        @pl.when(home)
        def _():
            rel_out[...] = rel[links.c]
            small_out[images_at] = smalls[images_at]

        @pl.when(away)
        def _():
            rel_copy.wait_recv()
            small_copy.wait_recv()
            rel_out[...] = rel_near[...]
            small_out[images_at] = small_near[...]

        norm_hops.take()
        norm_hops.take()
        small_out[0:8] = smalls[0:8]
        for back in returns:
            back.done()
        links.leave()

    pl.run_scoped(rest, vmem(wq_hbm.shape, bf16), vmem(n1_hbm.shape, bf16), vmem((2, rows, width), f32))


def end_chain(ndp, flags, qkv, do, o, lse, mask_pad, x, dh, ln, lab, smalls, rel1, wall, wq, n1, da, fc, finish, returns, order, scale):
    rows, width = x.shape
    heads = wall.shape[0]
    total, wide = qkv.shape
    bits = ndp.bit_length() - 1
    fold = bits == 2
    n, hidden = fc.shape[2:]
    fc_cols = hidden + o.shape[1]
    count = smalls.shape[0]
    hops = bits + 1
    bf16, f32 = jnp.bfloat16, jnp.float32
    out = jax.ShapeDtypeStruct
    layers = [layer for layer, _ in returns]
    blocks = [block for _, block in returns]
    landed = [out(block.shape, bf16) for block in blocks] + [out((rows, width), bf16)]
    outs = [
        out((rows, width), f32),
        out((count, width), f32),
        out((heads, 32, 128), f32),
        out((n, wide) if fold else (2, 2, n, wide), bf16),
    ]
    if fold:
        outs += [out((n, fc_cols), bf16), out((n, hidden), bf16)]
        landed += [out((n, fc_cols), bf16), out((n, wide), bf16), out((n, hidden), bf16)]
        blocks += list(finish)
    else:
        outs.append(out((2, 2, n, fc_cols), bf16))
    copies = Scatter.COPIES + len(landed) * Return.COPIES + 2 * DpReduce.COPIES + DpFinish.COPIES + 2 * hops + 4
    res = pl.pallas_call(
        functools.partial(end_kernel, order, scale, bits, fold, layers),
        in_specs=[pl.BlockSpec(memory_space=pltpu.SMEM)] + [VM] * 11 + [HB] * (5 + len(layers)) + ([VM] * 2 if fold else []),
        out_specs=[VM] * len(outs) + [HB] * (2 * len(landed)),
        out_shape=outs + [shape for shape in landed for _ in range(2)],
        scratch_shapes=[
            pltpu.VMEM(wall.shape, f32),
            pltpu.VMEM((total, wide), bf16),
            pltpu.VMEM((2, 2, n, wide), bf16),
            pltpu.VMEM((2, 2, n, fc_cols), bf16),
            pltpu.VMEM((rows, width), bf16),
            pltpu.VMEM((6, rows, width), bf16),
            pltpu.VMEM((2, heads, 32, 128), f32),
            pltpu.VMEM((hops, 2, heads, 32, 128), f32),
            pltpu.VMEM((heads, 32, 128), f32),
            pltpu.VMEM((count, width), f32),
            pltpu.VMEM((hops, count, width), f32),
            pltpu.VMEM((2, 8, width), f32),
            pltpu.VMEM((count - 8, width), f32),
            *(
                DpReduce.scratch(n, wide) + DpReduce.scratch(n, fc_cols) + [pltpu.VMEM((n, hidden), bf16)]
                if fold
                else []
            ),
            pltpu.SemaphoreType.DMA((5,)),
            *comm_scratch(copies),
        ],
        compiler_params=params(4),
        cost_estimate=pl.CostEstimate(flops=90 << 30, bytes_accessed=24 << 20, transcendentals=0),
    )(flags, qkv, do, o, lse, mask_pad, x, dh, ln, lab, smalls, rel1, wall, wq, n1, da, fc, *blocks)
    res = list(res)
    got = [(res[len(outs) + 2 * k], res[len(outs) + 2 * k + 1]) for k in range(len(landed))]
    return res[: len(outs)], got


AXES = ("dp", "section", "tensor")
ORDER = (0, 2, 1, 3)


def local(
    inputs,
    time_emb,
    lengths,
    key_mask,
    rel_index,
    w_qkv,
    w_time,
    w_proj,
    w_fc1,
    w_fc2,
    rel_table,
    norm_gains,
    norm_biases,
    cotangent,
):
    bf16, f32 = jnp.bfloat16, jnp.float32
    _, rows, width = inputs.shape
    seq_len = key_mask.shape[1]
    heads, buckets = rel_table.shape[1:]
    local_width = w_proj.shape[2]
    scale = 1.0 / math.sqrt(HD)
    ndp = lax.axis_size("dp")
    d = lax.axis_index("dp")
    c = lax.axis_index("section")
    z = lax.axis_index("tensor")
    pair = z // 2
    home = c == pair
    first = c == 0
    t = z % 2 + 2 * c

    def move(x, to, name="move"):
        pairs = []
        for dd in range(ndp):
            for cc in range(2):
                for zz in range(4):
                    dst = to(dd, cc, zz)
                    if dst is not None:
                        pairs.append(((dd * 2 + cc) * 4 + zz, (dst[0] * 2 + dst[1]) * 4 + dst[2]))
        with jax.named_scope(name):
            return lax.ppermute(x, AXES, pairs)

    def partner(x):
        return move(x, lambda dd, cc, zz: (dd, cc, zz ^ 1), "partner")

    def sibling(x):
        return move(x, lambda dd, cc, zz: (dd, 1 - cc, zz), "sibling")

    def across(x):
        return move(x, lambda dd, cc, zz: (dd, cc, zz ^ 2), "across")

    def dp_scatter(x, bits):
        n = x.shape[1]
        left = sorted(bits, reverse=True)
        v = x.reshape((2,) * len(left) + (-1, n))
        for b in bits:
            axis = left.index(b)
            left.remove(b)
            mine = (d >> b) & 1
            send = lax.dynamic_index_in_dim(v, 1 - mine, axis, keepdims=False)
            keep = lax.dynamic_index_in_dim(v, mine, axis, keepdims=False)
            got = move(send, lambda dd, cc, zz, b=b: (dd ^ (1 << b), cc, zz), "g_dp")
            v = keep.astype(f32) + got.astype(f32)
            if left:
                v = v.astype(bf16)
        return v

    def by_bits(w):
        return w.reshape(2, 2, -1, w.shape[-1])

    table = jnp.pad(rel_table[0], ((0, 0), (0, 4096 - buckets))).reshape(heads, 32, 128)
    time_all = jnp.einsum("id,dcn->icn", time_emb, w_time[0], preferred_element_type=f32)
    gap = jnp.zeros((2, local_width), f32)
    time_rows = jnp.concatenate([time_all[:, 0], gap, time_all[:, 1], gap], axis=1)
    small_pack = jnp.concatenate([norm_gains[0], norm_biases[0], time_rows, jnp.zeros((2, width), f32)], axis=0)
    own = [by_bits(w) for w in (jnp.concatenate([w_qkv[0, :, j] for j in range(3)], axis=1), w_proj[0], w_fc1[0], w_fc2[0])]
    label_lanes = label_row(rel_index)
    out_label = rel_index[1, seq_len - 1, seq_len - 1].reshape(1)

    length = lax.dynamic_index_in_dim(lengths, pair, 0, keepdims=False)
    small = (length < seq_len).astype(jnp.int32)
    scalars = jnp.stack([z % 2, c] + [jnp.int32(j) for j in ORDER])
    flags = jnp.concatenate([small.reshape(1), out_label])
    mask = lax.dynamic_index_in_dim(key_mask, pair, 0, keepdims=False).reshape(4, rows)
    mask = jnp.concatenate([lax.dynamic_index_in_dim(mask, t ^ j, 0, keepdims=False) for j in ORDER])
    lane = jnp.arange(128 - HD)[None, :]
    mask_pad = jnp.where((lane == 0) & (mask[:, None] == 0), -1e30, 0.0).astype(bf16)

    def gather_rows(x):
        far = partner(x)
        near = sibling(x)
        return jnp.concatenate([x, near, far, sibling(far)], axis=0)

    def scatter_rows(far, near):
        a = sibling(far[rows:].astype(bf16))
        rz = partner((far[:rows] + a.astype(f32)).astype(bf16))
        rs = sibling(near[rows:].astype(bf16))
        return near[:rows] + rs.astype(f32) + rz.astype(f32)

    def times_t(x, w):
        return lax.dot_general(x, w, (((1,), (1,)), ((), ())), preferred_element_type=f32)

    def grad_of(x, y):
        return lax.dot_general(x, y, (((0,), (0,)), ((), ())), preferred_element_type=f32).astype(bf16)

    half = 2 * rows

    def reduced(x):
        with jax.named_scope("g_sum"):
            return lax.psum_scatter(x, "dp", scatter_dimension=0, tiled=True)

    def reduced_late(x):
        if ndp & (ndp - 1):
            return reduced(x)
        bits = list(range(ndp.bit_length() - 1))
        cut = 4 * 128
        return jnp.concatenate(
            [dp_scatter(x[:, :cut], bits), dp_scatter(x[:, cut:], bits[::-1])], axis=1
        ).astype(bf16)

    def column_sums(dqkv):
        sums = jnp.sum(dqkv.astype(f32), axis=0)
        return jnp.concatenate([sums[:local_width], sums[2 * local_width :]])

    def tie(*values):
        return lax.optimization_barrier(values)

    def by_core(pairs):
        return jnp.where(first, pairs[0], pairs[1])

    def near_of(x, layer):
        return move(x, lambda dd, cc, zz: (dd, layer, zz) if cc == zz // 2 and cc != layer else None, "d_near")

    def far_of(x, layer):
        return move(x, lambda dd, cc, zz: (dd, layer, zz ^ 2) if cc != zz // 2 else None, "d_far")

    live = ((t * rows + jnp.arange(rows)) < length).astype(f32)[:, None]
    res = start_chain(flags, inputs, cotangent, mask_pad, label_lanes, table, small_pack, *own, ORDER, scale)
    x0, cot, packs, lse0, o0, n1_0, qkv0 = res[:7]
    walls, got0 = res[7:9], res[9:]
    n1_0 = n1_0.reshape(seq_len, width)

    def whole(w):
        return w.reshape(width, w.shape[-1])

    gains = [packs[l, 0:2] for l in range(2)]
    shifts = [packs[l, 2:4] for l in range(2)]
    ln_mid = jnp.stack([gains[0][1], shifts[0][1], gains[1][0], shifts[1][0]])
    wq0, wp0 = whole(got0[0]), whole(got0[1])
    term1 = lax.dynamic_index_in_dim(packs[1], 4 + pair, 0, keepdims=True)[:, : 3 * local_width]
    hid0, act0, dy1, o1, lse1, n2_0, u0, g0, n1_1, qkv1, dm1, fc_w0, got1 = mid_chain(
        x0, o0, ln_mid, cot, live, term1, mask_pad, wp0, got0[2], got0[3], walls[1], own, ORDER, scale
    )
    w10, w20 = whole(fc_w0[0]), whole(fc_w0[1])
    wq1, wp1 = whole(got1[0]), whole(got1[1])

    fold = ndp == 4
    ln_turn = jnp.stack([gains[1][1], shifts[1][1]])
    dh1, norms1, y1, hid1, do1, da1, fc1_1, fc2_1 = turn_chain(
        ndp, act0, o1, dy1, ln_turn, dm1, wp1, own[2:], got1[2:]
    )
    dqkv1, dwall1, sum_fc1_1, sum_fc2_1, landed, act1 = bwd_chain(
        6, fold, qkv1, do1, o1, lse1, mask_pad, walls[1], fc1_1, fc2_1, [(0, act0)], ORDER, scale, (y1, hid1)
    )
    got_act0, got_fc2_1 = landed[0], landed[-1]
    ln_back = jnp.stack([gains[1][0], gains[0][1]])
    give = [(1, act1)] + ([(1, sum_fc1_1)] if fold else [])
    gin1, dh0, norms10, do0, da0, fc1_0, fc2_0, qp1, rel1, sums1, landed = back_chain(
        ndp, flags, act0, dh1, hid0, ln_back, dqkv1, o1, label_lanes,
        wq1, wp0, w10, w20, u0, g0, n2_0, n1_1, da1, dwall1, give,
    )
    got_act1, got_fc1_1, got_gin1 = landed[0], landed[len(landed) - 2], landed[-1]
    number = 2 * d + pair
    sums_rows = lax.dynamic_update_slice(
        jnp.zeros((2 * ndp, width), f32), sums1, (number, jnp.int32(width - 2 * local_width))
    )
    mine = lax.dynamic_index_in_dim(time_emb, pair, 0, keepdims=True).astype(f32)
    emb_rows = lax.dynamic_update_slice(jnp.zeros((2 * ndp, width), f32), mine, (number, jnp.int32(0)))
    smalls = jnp.concatenate(
        [jnp.zeros((2, width), f32), norms10[2:], norms10[:2], norms1, sums_rows, emb_rows], axis=0
    )
    give = [(1, qp1)] if fold else []
    (gin0, smalls, rel, q0, *more), landed = end_chain(
        ndp, flags, qkv0, do0, o0, lse0, mask_pad, x0, dh0, gains[0][0:1], label_lanes, smalls, rel1,
        walls[0], wq0, n1_0, da0, by_bits(fc1_0), fc2_0, give, ORDER, scale,
    )
    norms, sums_all = smalls[:8], smalls[8:]

    def total(mine, got):
        return jnp.where(home, mine, got[0]).astype(f32) + got[1].astype(f32)

    hidden_units = w_fc1.shape[2]
    wide = 3 * local_width
    if fold:
        got_qp1, got_gin0, got_f0, got_q0, got_fc2_0 = landed
        f0, sum_fc2_0 = more
        f0, qp1 = total(f0, got_f0), total(qp1, got_qp1)
        layer0 = (total(q0, got_q0), f0[:, hidden_units:], f0[:, :hidden_units], total(sum_fc2_0, got_fc2_0))
        layer1 = (qp1[:, :wide], qp1[:, wide:], total(sum_fc1_1, got_fc1_1), total(sum_fc2_1, got_fc2_1))
    else:
        (got_gin0,) = landed

        def summed(x, layer):
            x = reduced(whole(x))
            return total(x, (near_of(x, layer), far_of(x, layer)))

        f0, qp1 = summed(more[0], 0), summed(qp1, 1)
        layer0 = (summed(q0, 0), f0[:, hidden_units:], f0[:, :hidden_units], summed(fc2_0[1], 0))
        layer1 = (qp1[:, :wide], qp1[:, wide:], summed(fc1_1, 1), summed(fc2_1[1], 1))
    grad_q, grad_p, grad_fc1, grad_fc2 = [by_core(pair_of) for pair_of in zip(layer0, layer1)]

    def by_image(same, other):
        return jnp.stack([jnp.where(pair == 0, same, other), jnp.where(pair == 0, other, same)])[None]

    acts = by_image(
        jnp.where(home, by_core((act0, act1)), by_core((got_act0[0], got_act1[0]))), by_core((got_act0[1], got_act1[1]))
    )
    same = jnp.where(home, by_core((gin0, gin1)), by_core((got_gin0[0], got_gin1[0])).astype(f32))
    input_grads = by_image(same, by_core((got_gin0[1], got_gin1[1])).astype(f32))

    rel_grad = rel.reshape(heads, 4096)[:, :buckets]
    norms_mine = jnp.where(first, norms[:4], norms[4:]).reshape(2, 2, width)
    cols = width // (4 * ndp)
    norms_mine = lax.dynamic_slice_in_dim(norms_mine, (d * 4 + z) * cols, cols, 2)
    emb_of = sums_all[2 * ndp :]
    sums_mine = jnp.where(first, sums_all[: 2 * ndp, : 2 * local_width], sums_all[: 2 * ndp, 2 * local_width :])
    emb_mine = lax.dynamic_slice_in_dim(emb_of, d * (width // ndp), width // ndp, 1)
    grad_time = lax.dot_general(
        emb_mine, sums_mine, (((0,), (0,)), ((), ())), precision=lax.Precision.HIGHEST, preferred_element_type=f32
    ).reshape(width // ndp, 2, local_width)
    return (
        acts,
        input_grads,
        grad_q.reshape(width // ndp, 3, local_width)[None],
        grad_time[None],
        grad_p[None],
        grad_fc1[None],
        grad_fc2[None],
        rel_grad[None],
        norms_mine[:, 0][None],
        norms_mine[:, 1][None],
    )


def solution(mesh):
    return jax.shard_map(
        local,
        mesh=mesh,
        in_specs=(
            P("dp", "tensor", None),
            P("dp", None),
            P("dp"),
            P("dp", None),
            P(),
            P("section", None, None, "tensor"),
            P("section", None, None, "tensor"),
            P("section", None, "tensor"),
            P("section", None, "tensor"),
            P("section", None, "tensor"),
            P("section", "tensor", None),
            P("section", None, None),
            P("section", None, None),
            P("dp", "tensor", None),
        ),
        out_specs=(
            P("section", "dp", "tensor", None),
            P("section", "dp", "tensor", None),
            P("section", "dp", None, "tensor"),
            P("section", "dp", None, "tensor"),
            P("section", "dp", "tensor"),
            P("section", "dp", "tensor"),
            P("section", "dp", "tensor"),
            P("section", "tensor", None),
            P("section", None, ("dp", "tensor")),
            P("section", None, ("dp", "tensor")),
        ),
        check_vma=False,
    )
```

```python
import functools
import math

import jax
import jax.numpy as jnp
from jax import lax
from jax.experimental import pallas as pl
from jax.experimental.pallas import tpu as pltpu
from jax.sharding import PartitionSpec as P

LOG2E = 1.4426950408889634
HIGHEST = lax.Precision.HIGHEST
PLANE = 7 * 256
WALL = 8 * PLANE


def _labels_hi_lo(lab):
    hi = lax.shift_right_logical(lab, 6)
    lo = jnp.bitwise_and(lab, 63)
    iota = lax.broadcasted_iota(jnp.int32, (64, lab.shape[1]), 0)
    group = 2 * jnp.bitwise_and(iota, 31) + lax.shift_right_logical(iota, 5)
    return group == hi, jnp.where(iota == lo, 1.0, 0.0)


def build_wall(small, out_lab, lab, hi_mask, lo_hot, table, wall_ref):
    table = jnp.concatenate([table[:, :64], table[:, 64:]], axis=0)
    rows = lax.dot_general(table, lo_hot, (((1,), (0,)), ((), ())), precision=HIGHEST, preferred_element_type=jnp.float32)
    flat = jnp.sum(jnp.where(hi_mask, rows, 0.0), axis=0, keepdims=True) * LOG2E
    outside = jnp.sum(jnp.where(lab == out_lab, flat, 0.0), axis=1, keepdims=True)
    wide = jnp.broadcast_to(flat, (32, 4096))
    wide = pltpu.roll(wide, 4096 - 31, 1, stride=1, stride_axis=0)
    lane = lax.broadcasted_iota(jnp.int32, (32, 128), 1)
    tight = []
    for g in range(16):
        a = wide[:, 256 * g : 256 * g + 128]
        b = wide[:, 256 * g + 128 : 256 * g + 256]
        piece = jnp.where(lane < 32, a, pltpu.roll(a, 96, 1))
        other = jnp.where(lane < 96, pltpu.roll(b, 64, 1), pltpu.roll(b, 32, 1))
        tight.append(jnp.where(lane < 64, piece, other))
    w0 = jnp.concatenate(tight, axis=1)
    lane16 = lane[:16]
    tight16 = []
    for g in range(8):
        lo_v = w0[:16, 256 * g : 256 * g + 128]
        hi_v = w0[:16, 256 * g + 128 : 256 * g + 256]
        acc = lo_v
        for k in range(1, 4):
            acc = jnp.where(lane16 >= 16 * k, pltpu.roll(lo_v, 128 - 16 * k, 1), acc)
        for k in range(4):
            acc = jnp.where(lane16 >= 64 + 16 * k, pltpu.roll(hi_v, (64 - 16 * k) % 128, 1), acc)
        tight16.append(acc)
    w16 = jnp.concatenate(tight16, axis=1)
    beyond = jnp.broadcast_to(outside, (32, 768))
    tiny = small == 1
    for j in range(8):
        big = w0 if j == 7 else pltpu.roll(w0, 2048 - 32 * (7 - j), 1)
        inner = [pltpu.roll(w16, 1024 - 16 * (31 - 2 * j - k), 1)[:, :256] for k in range(2)]
        inner = jnp.concatenate(inner, axis=0)
        at = j * PLANE
        wall_ref[:, at : at + 768] = jnp.where(tiny, beyond, big[:, :768])
        wall_ref[:, at + 768 : at + 1024] = jnp.where(tiny, inner, big[:, 768:1024])
        wall_ref[:, at + 1024 : at + PLANE] = jnp.where(tiny, beyond, big[:, 1024:PLANE])


def wall_grad(small, out_lab, lab, hi_mask, lo_hot, acc_ref):
    tiny = small == 1
    w0 = jnp.zeros((32, 2048), jnp.float32)
    w16 = jnp.zeros((16, 1024), jnp.float32)
    beyond = jnp.zeros((32, 768), jnp.float32)
    for j in range(8):
        at = j * PLANE
        piece = jnp.concatenate([acc_ref[:, at : at + PLANE], jnp.zeros((32, 256), jnp.float32)], axis=1)
        w0 = w0 + (piece if j == 7 else pltpu.roll(piece, 32 * (7 - j), 1))
        beyond = beyond + acc_ref[:, at + 1024 : at + PLANE]
        for k in range(2):
            inner = acc_ref[16 * k : 16 * k + 16, at + 768 : at + 1024]
            inner = jnp.concatenate([inner, jnp.zeros((16, 768), jnp.float32)], axis=1)
            w16 = w16 + pltpu.roll(inner, 16 * (31 - 2 * j - k), 1)
    w0 = jnp.where(tiny, 0.0, w0)
    w16 = jnp.where(tiny, w16, 0.0)
    outside = jnp.sum(jnp.sum(jnp.where(tiny, beyond, 0.0), axis=0, keepdims=True), axis=1, keepdims=True)
    lane = lax.broadcasted_iota(jnp.int32, (32, 128), 1)
    lane16 = lane[:16]
    wide = []
    for g in range(32):
        src = w0[:, 128 * (g // 2) : 128 * (g // 2) + 128]
        k = 2 * (g % 2)
        first = src if k == 0 else pltpu.roll(src, 128 - 32 * k, 1)
        second = pltpu.roll(src, (64 - 32 * (k + 1)) % 128, 1)
        piece = jnp.where(lane < 32, first, jnp.where((lane >= 64) & (lane < 96), second, 0.0))
        src16 = w16[:, 128 * (g // 4) : 128 * (g // 4) + 128]
        k = 2 * (g % 4)
        first = src16 if k == 0 else pltpu.roll(src16, 128 - 16 * k, 1)
        second = pltpu.roll(src16, (64 - 16 * (k + 1)) % 128, 1)
        piece16 = jnp.where(lane16 < 16, first, jnp.where((lane16 >= 64) & (lane16 < 80), second, 0.0))
        wide.append(piece + jnp.concatenate([piece16, jnp.zeros((16, 128), jnp.float32)], axis=0))
    wide = jnp.concatenate(wide, axis=1)
    back = 31 - lax.broadcasted_iota(jnp.int32, (32, 4096), 0)
    for k in range(5):
        wide = jnp.where(jnp.bitwise_and(back, 1 << k) > 0, pltpu.roll(wide, 1 << k, 1), wide)
    flat = jnp.sum(wide, axis=0, keepdims=True)
    flat = flat + jnp.where(lab == out_lab, outside, 0.0)
    spread = jnp.where(hi_mask, jnp.broadcast_to(flat, (64, 4096)), 0.0)
    res = lax.dot_general(spread, lo_hot, (((1,), (1,)), ((), ())), precision=HIGHEST, preferred_element_type=jnp.float32)
    return jnp.concatenate([res[:32], res[32:]], axis=1)


def label_row(rel_index):
    side = 32
    a = rel_index[0, 1023].reshape(side, side)
    b = rel_index[0, 0].reshape(side, side)
    c = rel_index[0, 992].reshape(side, side)
    d = rel_index[0, 31].reshape(side, side)
    top = jnp.concatenate([a, c[:, 1:]], axis=1)
    low = jnp.concatenate([d[1:], b[1:, 1:]], axis=1)
    grid = jnp.flip(jnp.concatenate([top, low], axis=0), (0, 1))
    return jnp.pad(grid, ((0, 1), (0, 1)), constant_values=4095).reshape(1, 4096)


NT = (((1,), (1,)), ((), ()))
TN = (((0,), (0,)), ((), ()))
NN = (((1,), (0,)), ((), ()))
HD = 72
QB = 256


def dot(a, b, dims):
    return lax.dot_general(a, b, dims, preferred_element_type=jnp.float32)


def head_lanes(x, at, extra=None):
    rows = x.shape[0]
    part = x[:, at : at + HD]
    if extra is None:
        pad = jnp.zeros((rows, 128 - HD), x.dtype)
    else:
        pad = extra
    return jnp.concatenate([part, pad], axis=1)


def quarter(r, c, rel):
    return lax.rem(r + rel % 2, 2) + 2 * lax.rem(c + rel // 2, 2)


def strip_start(q_quarter, jj, kq):
    return pl.multiple_of(PLANE * jj + 256 * (q_quarter - kq + 3), 256)


def attn_block(q_quarter, key_quarters, scale, q_ref, kv_ref, k_extra, wall_ref, lse_ref, s_scr, p_scr):
    heads = wall_ref.shape[0]
    width = heads * HD
    nstrip = kv_ref.shape[0] // 32
    lane = lax.broadcasted_iota(jnp.int32, (QB, 128 - HD), 1)
    q_extra = jnp.where(lane == 0, 1.0, 0.0).astype(jnp.bfloat16)
    outs = []
    for h in range(heads):
        kh = head_lanes(kv_ref, width + HD * h, k_extra)
        qh = head_lanes(q_ref, HD * h, q_extra)
        vh = head_lanes(kv_ref, 2 * width + HD * h)
        s_scr[h % 2] = dot(kh, qh, NT)
        top = None
        for st in range(nstrip):
            start = strip_start(q_quarter, st % 8, key_quarters[st // 8])
            s = s_scr[h % 2, 32 * st : 32 * st + 32] * (scale * LOG2E) + wall_ref[h, :, pl.ds(start, QB)]
            s_scr[h % 2, 32 * st : 32 * st + 32] = s
            top = s if top is None else jnp.maximum(top, s)
        row_max = jnp.max(top, axis=0, keepdims=True)
        total = None
        for st in range(nstrip):
            p = jnp.exp2(s_scr[h % 2, 32 * st : 32 * st + 32] - row_max)
            p_scr[h % 2, 32 * st : 32 * st + 32] = p.astype(jnp.bfloat16)
            total = p if total is None else total + p
        row_sum = jnp.sum(total, axis=0, keepdims=True)
        o_t = dot(vh, p_scr[h % 2], TN) * (1.0 / row_sum)
        lse_ref[h : h + 1, :] = row_max + jnp.log2(row_sum)
        outs.append(o_t.T[:, :HD].astype(jnp.bfloat16))
    return jnp.concatenate(outs, axis=1)


EPSILON = 1e-05
NCH = 2
GELU_C = math.sqrt(2.0 / math.pi)


def normed(x):
    center = x - jnp.mean(x, axis=-1, keepdims=True)
    spread = jnp.mean(center * center, axis=-1, keepdims=True)
    r = lax.rsqrt(spread + EPSILON)
    return center * r, r


def norm_back(x, dy, gain):
    xhat, r = normed(x)
    dxhat = dy * gain
    dx = r * (
        dxhat
        - jnp.mean(dxhat, axis=-1, keepdims=True)
        - xhat * jnp.mean(dxhat * xhat, axis=-1, keepdims=True)
    )
    return dx, jnp.sum(dy * xhat, axis=0, keepdims=True), jnp.sum(dy, axis=0, keepdims=True)


def gelu_both(u):
    th = jnp.tanh(GELU_C * (u + 0.044715 * u * u * u))
    half = 0.5 * (1.0 + th)
    slope = half + 0.5 * u * (1.0 - th * th) * GELU_C * (1.0 + 3 * 0.044715 * u * u)
    return u * half, slope


class Links:
    def __init__(self, send_sem, recv_sem, bits=0):
        z, c = lax.axis_index("tensor"), lax.axis_index("section")
        self.z, self.c = z, c
        self.pair = z // 2
        self.r = lax.rem(z, 2)
        self.home = c == self.pair
        across = z + 2 - 4 * self.pair
        self.ids = {
            PARTNER: {"tensor": z + 1 - 2 * self.r},
            SIBLING: {"section": 1 - c},
            FAR: {"tensor": across, "section": self.pair},
            HOME: {"section": self.pair},
        }
        self.greet = [self.ids[PARTNER], self.ids[SIBLING]]
        self.dp_bit = []
        if bits:
            d = lax.axis_index("dp")
            for b in range(bits):
                bit = lax.rem(d // (1 << b), 2)
                self.dp_bit.append(bit)
                self.ids["dp", b] = {"dp": d + (1 - 2 * bit) * (1 << b)}
                self.greet.append(self.ids["dp", b])
            self.greet += [{"tensor": across}, {"tensor": across, "section": 1 - c}]
        self.ids[ACROSS] = {"tensor": across}
        for layer in range(2):
            self.ids["return", layer] = {"tensor": across, "section": layer}
        self.send_sem, self.recv_sem = send_sem, recv_sem
        self.used = 0
        self.started = []

    def enter(self):
        barrier = pltpu.get_barrier_semaphore()
        for where in self.greet:
            pl.semaphore_signal(barrier, inc=1, device_id=where, device_id_type=pl.DeviceIdType.MESH)
        pl.semaphore_wait(barrier, len(self.greet))

    def make(self, src, dst, to, cond=None, track=True):
        k = self.used
        self.used += 1
        assert k < self.send_sem.shape[0]
        copy = pltpu.make_async_remote_copy(
            src_ref=src,
            dst_ref=dst,
            send_sem=self.send_sem.at[k],
            recv_sem=self.recv_sem.at[k],
            device_id=self.ids[to],
            device_id_type=pl.DeviceIdType.MESH,
        )
        if track:
            self.started.append((copy, cond))
        return copy

    def send(self, src, dst, to, cond=None, track=True):
        copy = self.make(src, dst, to, cond, track)
        when(cond, copy.start)
        return copy

    def leave(self):
        for copy, cond in self.started:
            when(cond, copy.wait_send)


def when(cond, do):
    if cond is None:
        do()
    else:
        pl.when(cond)(lambda: do())


PARTNER, SIBLING, FAR, HOME, ACROSS = "partner", "sibling", "far", "home", "across"


class Spread:
    COPIES = 2

    def __init__(self, links, layer, src, out, sem):
        self.links, self.layer, self.src, self.out, self.sem = links, layer, src, out, sem

    def start(self):
        links = self.links
        mine = links.c == self.layer
        keeps = links.pair == self.layer
        self.local = pltpu.make_async_copy(self.src, self.out, self.sem)
        when(mine & keeps, self.local.start)
        self.near = links.send(self.src, self.out, HOME, mine & jnp.logical_not(keeps))
        self.far = links.send(self.src, self.out, FAR, mine)

    def done(self):
        links = self.links
        keeps = links.pair == self.layer
        when(links.home & keeps, self.local.wait)
        when(links.home & jnp.logical_not(keeps), self.near.wait_recv)
        when(jnp.logical_not(links.home), self.far.wait_recv)


def bits_region(links, gathered, cols=None):
    index = []
    for b in reversed(range(len(links.dp_bit))):
        index.append(pl.ds(0, 2) if b in gathered else links.dp_bit[b])
    return tuple(index) + (() if cols is None else (slice(None), cols))


class Deliver:
    COPIES = 2

    def __init__(self, links, layer, src, out, sem=None):
        self.links, self.layer, self.src, self.out, self.sem = links, layer, src, out, sem

    def start(self):
        links = self.links
        mine = links.c == self.layer
        keeps = links.pair == self.layer
        if self.sem is not None:
            self.local = pltpu.make_async_copy(self.src, self.out, self.sem)
            when(mine & keeps, self.local.start)
        at = bits_region(links, ())
        self.far = links.send(self.src.at[at], self.out.at[at], FAR, mine)
        self.near = links.send(self.src, self.out, HOME, mine & jnp.logical_not(keeps))

    def done(self):
        links = self.links
        keeps = links.pair == self.layer
        if self.sem is not None:
            when(links.home & keeps, self.local.wait)
        when(links.home & jnp.logical_not(keeps), self.near.wait_recv)
        when(jnp.logical_not(links.home), self.far.wait_recv)


class Exchange:
    def __init__(self, links, buf):
        self.links, self.buf = links, buf
        columns = buf.shape[-1]
        cut = columns // 256 * 128
        order = list(range(len(links.dp_bit)))
        self.halves = [(pl.ds(0, cut), order), (pl.ds(cut, columns - cut), order[::-1])]
        self.away = jnp.logical_not(links.home)
        self.last = None

    @staticmethod
    def copies(bits):
        return 2 * bits

    def step(self, s):
        self.done()
        self.last = []
        for cols, order in self.halves:
            at = bits_region(self.links, order[:s], cols)
            self.last.append(self.links.send(self.buf.at[at], self.buf.at[at], ("dp", order[s]), self.away))

    def done(self):
        for copy in self.last or ():
            when(self.away, copy.wait_recv)


class Part:
    def __init__(self, links, layer, own, got, dst, sem):
        at = bits_region(links, ())
        keeps = links.pair == layer
        self.ways = (
            (links.home & keeps, pltpu.make_async_copy(own, dst, sem)),
            (links.home & jnp.logical_not(keeps), pltpu.make_async_copy(got, dst, sem)),
            (jnp.logical_not(links.home), pltpu.make_async_copy(got.at[at], dst.at[at], sem)),
        )

    def start(self):
        for cond, copy in self.ways:
            when(cond, copy.start)
        return self

    def wait(self):
        for cond, copy in self.ways:
            when(cond, copy.wait)


class PartStore:
    def __init__(self, links, layer, src, dst, sem):
        at = bits_region(links, ())
        self.ways = (
            (links.home & (links.pair != layer), pltpu.make_async_copy(src, dst, sem)),
            (jnp.logical_not(links.home), pltpu.make_async_copy(src.at[at], dst.at[at], sem)),
        )

    def start(self):
        for cond, copy in self.ways:
            when(cond, copy.start)
        return self

    def wait(self):
        for cond, copy in self.ways:
            when(cond, copy.wait)


def chunk(i, rows):
    return pl.ds(i * (rows // NCH), rows // NCH)


class Scatter:
    COPIES = 3 * NCH

    def __init__(self, links, low, wide):
        self.links, self.low, self.wide = links, low, wide
        self.rows = low.shape[1]
        self.copies = {}

    def far(self, i, p2, p3):
        at = chunk(i, self.rows)
        self.low[0, at] = p3.astype(jnp.bfloat16)
        self.copies["a", i] = self.links.send(self.low.at[0, at], self.low.at[3, at], SIBLING)
        self.wide[0, at] = p2

    def middle(self, i):
        at = chunk(i, self.rows)
        self.copies["a", i].wait_recv()
        self.low[1, at] = (self.wide[0, at] + self.low[3, at].astype(jnp.float32)).astype(jnp.bfloat16)
        self.copies["z", i] = self.links.send(self.low.at[1, at], self.low.at[4, at], PARTNER)

    def near(self, i, p0, p1):
        at = chunk(i, self.rows)
        self.low[2, at] = p1.astype(jnp.bfloat16)
        self.copies["b", i] = self.links.send(self.low.at[2, at], self.low.at[5, at], SIBLING)
        self.wide[1, at] = p0

    def release(self):
        for copy in self.copies.values():
            copy.wait_send()
        self.links.started = [s for s in self.links.started if all(s[0] is not c for c in self.copies.values())]
        self.copies = {}

    def done(self, i):
        at = chunk(i, self.rows)
        self.copies["b", i].wait_recv()
        self.copies["z", i].wait_recv()
        return self.wide[1, at] + self.low[5, at].astype(jnp.float32) + self.low[4, at].astype(jnp.float32)


class Gather:
    COPIES = 3 * NCH

    def __init__(self, links, buf):
        self.links, self.buf = links, buf
        self.rows = buf.shape[1]
        self.copies = {}

    def send(self, i, x):
        at = chunk(i, self.rows)
        self.buf[0, at] = x
        self.copies["z", i] = self.links.send(self.buf.at[0, at], self.buf.at[2, at], PARTNER)
        self.copies["s", i] = self.links.send(self.buf.at[0, at], self.buf.at[1, at], SIBLING)

    def forward(self, i):
        at = chunk(i, self.rows)
        self.copies["z", i].wait_recv()
        self.copies["f", i] = self.links.send(self.buf.at[2, at], self.buf.at[3, at], SIBLING)

    def done(self, i):
        self.copies["s", i].wait_recv()
        self.copies["f", i].wait_recv()
        at = chunk(i, self.rows)
        n = self.rows // NCH
        return jnp.concatenate([self.buf[b, at] for b in range(4)], axis=0)


class DpReduce:
    COPIES = 4

    def __init__(self, links, buf, land0, land1=None, sent=None):
        self.links, self.buf, self.land0, self.land1, self.sent = links, buf, land0, land1, sent
        columns = buf.shape[-1]
        cut = columns // 256 * 128
        self.cols = (pl.ds(0, cut), pl.ds(cut, columns - cut))
        self.orders = ((0, 1), (1, 0))
        self.mine = links.dp_bit
        self.other = [1 - bit for bit in links.dp_bit]
        self.first, self.second = [], []
        for (b0, b1), h, cols in zip(self.orders, range(2), self.cols):
            at = self.place(h, self.other[b0], pl.ds(0, 2))
            self.first.append(links.make(buf.at[at + (slice(None), cols)], land0.at[:, :, cols], ("dp", b0)))
            if land1 is not None:
                self.second.append(links.make(sent.at[0, :, cols], land1.at[0, :, cols], ("dp", b1)))

    @staticmethod
    def scratch(n, columns):
        return [pltpu.VMEM((k, n, columns), jnp.bfloat16) for k in (2, 1, 1)]

    def place(self, h, first, second):
        return (second, first) if self.orders[h][0] == 0 else (first, second)

    def start(self):
        for copy in self.first:
            copy.start()

    def half(self, h, cols):
        b0, b1 = self.orders[h]
        self.first[h].wait_recv()
        sums = []
        for second in (self.other[b1], self.mine[b1]):
            own = self.buf[self.place(h, self.mine[b0], second) + (slice(None), cols)]
            sums.append(own.astype(jnp.float32) + self.land0[second, :, cols].astype(jnp.float32))
        return sums

    def split(self, sent, kept):
        for h, cols in enumerate(self.cols):
            sums = self.half(h, cols)
            sent[:, cols] = sums[0].astype(jnp.bfloat16)
            kept[:, cols] = sums[1].astype(jnp.bfloat16)

    def middle(self):
        for h, cols in enumerate(self.cols):
            b0, b1 = self.orders[h]
            sums = self.half(h, cols)
            self.sent[0, :, cols] = sums[0].astype(jnp.bfloat16)
            self.buf[self.place(h, self.mine[b0], self.mine[b1]) + (slice(None), cols)] = sums[1].astype(jnp.bfloat16)
            self.second[h].start()

    def done(self, out):
        for h, cols in enumerate(self.cols):
            self.second[h].wait_recv()
            b0, b1 = self.orders[h]
            own = self.buf[self.place(h, self.mine[b0], self.mine[b1]) + (slice(None), cols)]
            out[:, cols] = (own.astype(jnp.float32) + self.land1[0, :, cols].astype(jnp.float32)).astype(out.dtype)


class DpFinish:
    COPIES = 2

    def __init__(self, links, sent, kept, land):
        self.kept, self.land = kept, land
        columns = sent.shape[-1]
        cut = columns // 256 * 128
        self.cols = (pl.ds(0, cut), pl.ds(cut, columns - cut))
        self.copies = [
            links.make(sent.at[:, cols], land.at[:, cols], ("dp", b)) for cols, b in zip(self.cols, (1, 0))
        ]

    def start(self):
        for copy in self.copies:
            copy.start()

    def done(self, out):
        for copy, cols in zip(self.copies, self.cols):
            copy.wait_recv()
            out[:, cols] = (self.kept[:, cols].astype(jnp.float32) + self.land[:, cols].astype(jnp.float32)).astype(out.dtype)


class Return:
    COPIES = 2

    def __init__(self, links, layer, src, near, far):
        self.links, self.layer = links, layer
        self.home, self.away = links.home, jnp.logical_not(links.home)
        self.here = links.c == layer
        self.near_cond = self.home & jnp.logical_not(self.here)
        self.near = links.make(src, near, SIBLING, self.near_cond)
        self.far = links.make(src, far, ("return", layer), self.away)

    def start(self):
        when(self.near_cond, self.near.start)
        when(self.away, self.far.start)

    def done(self):
        when(self.here & self.away, self.near.wait_recv)
        when(self.here, self.far.wait_recv)


def start_load(src, dst, sem):
    copy = pltpu.make_async_copy(src, dst, sem)
    copy.start()
    return copy


def block_rows(ref, b, i, rows):
    n = rows // NCH
    return ref[pl.ds(b * rows + i * n, n)]


def put_rows(ref, value, i, rows):
    n = rows // NCH
    for b in range(4):
        ref[pl.ds(b * rows + i * n, n)] = value[b * n : (b + 1) * n]


def weight_grad(out, col, x, y):
    width = x.shape[1]
    step = 384
    for k in range(0, width, step):
        out[k : k + step, col : col + y.shape[1]] = dot(x[:, k : k + step], y, TN).astype(out.dtype)


def flat(ref):
    return ref[...].reshape(-1, ref.shape[-1])


def scatter_product(scatter, i, lhs, weight, rows):
    p = dot(jnp.concatenate([lhs(2), lhs(3)], axis=0), weight, NT)
    n = rows // NCH
    scatter.far(i, p[:n], p[n:])
    p = dot(jnp.concatenate([lhs(0), lhs(1)], axis=0), weight, NT)
    scatter.near(i, p[:n], p[n:])


def slab_grad(out, col, x, y):
    n = out.shape[2]
    width = x.shape[1]
    step = 384
    for k in range(0, width, step):
        res = dot(x[:, k : k + step], y, TN).astype(out.dtype)
        at = k
        while at < k + step:
            slab = at // n
            stop = min(k + step, (slab + 1) * n)
            out[slab // 2, slab % 2, at - slab * n : stop - slab * n, col : col + y.shape[1]] = res[at - k : stop - k]
            at = stop


def block_quarter(links, i):
    return lax.rem(links.r + i // 2, 2) + 2 * lax.rem(links.c + lax.rem(i, 2), 2)


def mid_kernel(order, scale, bits, x_ref, o_ref, ln_ref, cot_ref, live_ref, term_ref, mask_ref,
               wp_hbm, got1_hbm, got2_hbm, wall_hbm, own_q, own_p, own_1, own_2,
               hid_ref, act_ref, dy_ref, o1_ref, lse_ref,
               n2_hbm, u_hbm, g_hbm, n1_hbm, qkv_hbm, dm_hbm, w1_out, w2_out, next_q, next_p, next_1, next_2,
               wp, w1, w2, got_q, got_p, got_1, got_2, wall, u_buf, g_buf, qkv, gat1, gat2, gat3, low, wide, s_scr, p_scr,
               load_sem, store_sem, send_sem, recv_sem):
    rows, width = x_ref.shape
    n = rows // NCH
    links = Links(send_sem, recv_sem, bits)
    load_p = start_load(wp_hbm, wp, load_sem.at[0])
    load_1 = Part(links, 0, own_1, got1_hbm, w1, load_sem.at[1]).start()
    load_2 = Part(links, 0, own_2, got2_hbm, w2, load_sem.at[2]).start()
    load_w = start_load(wall_hbm, wall, load_sem.at[3])
    links.enter()
    ex1, ex2 = Exchange(links, w1), Exchange(links, w2)
    exq, exp = Exchange(links, got_q), Exchange(links, got_p)
    get_q, get_p = Deliver(links, 1, own_q, got_q, load_sem.at[4]), Deliver(links, 1, own_p, got_p, load_sem.at[5])
    get_1, get_2 = Deliver(links, 1, own_1, got_1), Deliver(links, 1, own_2, got_2)
    s1, s2 = Scatter(links, low, wide), Scatter(links, low, wide)
    g1, g2, g3 = Gather(links, gat1), Gather(links, gat2), Gather(links, gat3)
    load_p.wait()
    for i in range(NCH):
        scatter_product(s1, i, lambda b: block_rows(o_ref, b, i, rows), wp[...], rows)
    load_1.wait()
    ex1.step(0)
    load_2.wait()
    ex2.step(0)
    for i in range(NCH):
        s1.middle(i)
    for s in range(1, bits):
        ex1.step(s)
    get_q.start()
    get_p.start()
    for i in range(NCH):
        h = x_ref[chunk(i, rows)].astype(jnp.float32) + s1.done(i)
        hid_ref[chunk(i, rows)] = h
        g1.send(i, (normed(h)[0] * ln_ref[0:1] + ln_ref[1:2]).astype(jnp.bfloat16))
        if i == 0:
            for s in range(1, bits):
                ex2.step(s)
    s1.release()

    def mlp(i):
        u = dot(g1.done(i), w1[...].reshape(width, -1), NN)
        put_rows(u_buf, u.astype(jnp.bfloat16), i, rows)
        g = gelu_both(u)[0].astype(jnp.bfloat16)
        put_rows(g_buf, g, i, rows)
        if i == 0:
            ex2.done()
        scatter_product(s2, i, lambda b: g[b * n : (b + 1) * n], w2[...].reshape(width, -1), rows)

    g1.forward(0)
    ex1.done()
    for i in range(NCH):
        mlp(i)
        if i + 1 < NCH:
            g1.forward(i + 1)
        s2.middle(i)
    stores = [
        start_load(src, dst, store_sem.at[k])
        for k, (src, dst) in enumerate(((gat1, n2_hbm), (u_buf, u_hbm), (g_buf, g_hbm), (w1, w1_out), (w2, w2_out)))
    ]
    get_q.done()
    exq.step(0)
    for i in range(NCH):
        act = (hid_ref[chunk(i, rows)] + s2.done(i)).astype(jnp.bfloat16)
        act_ref[chunk(i, rows)] = act
        g2.send(i, (normed(act.astype(jnp.float32))[0] * ln_ref[2:3] + ln_ref[3:4]).astype(jnp.bfloat16))
    for i in range(NCH):
        at = chunk(i, rows)
        dy = cot_ref[at].astype(jnp.float32) * live_ref[at]
        dy_ref[at] = dy
        g3.send(i, dy.astype(jnp.bfloat16))
    get_1.start()
    get_2.start()
    for s in range(1, bits):
        exq.step(s)
    get_p.done()
    exp.step(0)
    for i in range(NCH):
        g2.forward(i)
    exq.done()
    weight = got_q[...].reshape(width, -1)
    for i in range(NCH):
        part = (dot(g2.done(i), weight, NN) + term_ref[0:1]).astype(jnp.bfloat16)
        put_rows(qkv, part, i, rows)
    for s in range(1, bits):
        exp.step(s)
    stores += [
        start_load(src, dst, store_sem.at[5 + k])
        for k, (src, dst) in enumerate(((gat2, n1_hbm), (qkv, qkv_hbm), (got_q, next_q)))
    ]
    load_w.wait()
    keys = [quarter(links.r, links.c, j) for j in order]

    def block(i, carry):
        at = pl.ds(pl.multiple_of(i * QB, QB), QB)
        o1_ref[at] = attn_block(
            block_quarter(links, i), keys, scale, qkv.at[at], qkv, mask_ref[...], wall, lse_ref.at[i], s_scr, p_scr
        )
        return carry

    lax.fori_loop(0, 4, block, 0)
    for i in range(NCH):
        g3.forward(i)
    exp.done()
    stores.append(start_load(got_p, next_p, store_sem.at[8]))
    for i in range(NCH):
        g3.copies["s", i].wait_recv()
        g3.copies["f", i].wait_recv()
    stores.append(start_load(gat3, dm_hbm, store_sem.at[9]))
    for k, (get, src, dst) in enumerate(((get_1, got_1, next_1), (get_2, got_2, next_2))):
        get.done()
        stores.append(PartStore(links, 1, src, dst, store_sem.at[10 + k]).start())
    links.leave()
    for store in stores:
        store.wait()


VM = pl.BlockSpec(memory_space=pltpu.VMEM)
HB = pl.BlockSpec(memory_space=pl.ANY)


def comm_scratch(copies):
    return [pltpu.SemaphoreType.DMA((copies,)), pltpu.SemaphoreType.DMA((copies,))]


def scatter_scratch(rows, width):
    return [pltpu.VMEM((6, rows, width), jnp.bfloat16), pltpu.VMEM((2, rows, width), jnp.float32)]


def params(ident):
    return pltpu.CompilerParams(collective_id=ident, has_side_effects=True, vmem_limit_bytes=52 << 20)


def mid_chain(x, o, ln, cot, live, term, mask_pad, wp, w1, w2, wall, own, order, scale):
    rows, width = x.shape
    hidden = w1.shape[-1]
    bits = w1.ndim - 2
    heads = wall.shape[0]
    wide = own[0].shape[-1]
    bf16, f32 = jnp.bfloat16, jnp.float32
    out = jax.ShapeDtypeStruct
    res = pl.pallas_call(
        functools.partial(mid_kernel, order, scale, bits),
        in_specs=[VM] * 7 + [HB] * 8,
        out_specs=[VM] * 5 + [HB] * 12,
        out_shape=[
            out((rows, width), f32),
            out((rows, width), bf16),
            out((rows, width), f32),
            out((4 * rows, heads * HD), bf16),
            out((4, heads, QB), f32),
            out((4, rows, width), bf16),
            out((4 * rows, hidden), bf16),
            out((4 * rows, hidden), bf16),
            out((4, rows, width), bf16),
            out((4 * rows, wide), bf16),
            out((4, rows, width), bf16),
        ]
        + [out(w.shape, bf16) for w in (w1, w2, *own)],
        scratch_shapes=[
            *[pltpu.VMEM(w.shape, bf16) for w in (wp, w1, w2, *own)],
            pltpu.VMEM(wall.shape, f32),
            pltpu.VMEM((4 * rows, hidden), bf16),
            pltpu.VMEM((4 * rows, hidden), bf16),
            pltpu.VMEM((4 * rows, wide), bf16),
            pltpu.VMEM((4, rows, width), bf16),
            pltpu.VMEM((4, rows, width), bf16),
            pltpu.VMEM((4, rows, width), bf16),
            *scatter_scratch(rows, width),
            pltpu.VMEM((2, 4 * rows, QB), f32),
            pltpu.VMEM((2, 4 * rows, QB), bf16),
            pltpu.SemaphoreType.DMA((6,)),
            pltpu.SemaphoreType.DMA((12,)),
            *comm_scratch(2 * Scatter.COPIES + 3 * Gather.COPIES + 4 * Deliver.COPIES + 4 * Exchange.copies(bits)),
        ],
        compiler_params=params(1),
        cost_estimate=pl.CostEstimate(flops=60 << 30, bytes_accessed=24 << 20, transcendentals=0),
    )(x, o, ln, cot, live, term, mask_pad, wp, w1, w2, wall, *own)
    hid, act, dy, o1, lse, n2, u, g, n1, qkv, dm = res[:11]
    rest = lambda v: v.reshape(4 * rows, width)
    return hid, act, dy, o1, lse, rest(n2), u, g, rest(n1), qkv, rest(dm), res[11:13], res[13:]


def turn_kernel(bits, fold, x_ref, o_ref, dy_ref, ln_ref, dm_hbm, wp_hbm, own1, own2, got1, got2,
                dh_ref, norm_ref, hid_ref, do_ref, fc2_sent, fc2_ref, y_hbm, da_hbm, fc1_hbm,
                wp, w1, w2, dm, g_buf, du_buf, y_buf, fc1, fc2, gat1, gat2, low, wide, *refs):
    lands, (load_sem, store_sem, send_sem, recv_sem) = refs[:-4], refs[-4:]
    rows, width = x_ref.shape
    n = rows // NCH
    links = Links(send_sem, recv_sem, bits)
    loads = [
        start_load(wp_hbm, wp, load_sem.at[0]),
        Part(links, 1, own1, got1, w1, load_sem.at[1]).start(),
        Part(links, 1, own2, got2, w2, load_sem.at[2]).start(),
        start_load(dm_hbm, dm, load_sem.at[3]),
    ]
    links.enter()
    ex1, ex2 = Exchange(links, w1), Exchange(links, w2)
    s1, s2 = Scatter(links, low, wide), Scatter(links, low, wide)
    g1, g2 = Gather(links, gat1), Gather(links, gat2)
    loads[0].wait()
    for i in range(NCH):
        scatter_product(s1, i, lambda b: block_rows(o_ref, b, i, rows), wp[...], rows)
    loads[1].wait()
    ex1.step(0)
    loads[2].wait()
    ex2.step(0)
    for i in range(NCH):
        s1.middle(i)
    for s in range(1, bits):
        ex1.step(s)
    for i in range(NCH):
        h = x_ref[chunk(i, rows)].astype(jnp.float32) + s1.done(i)
        hid_ref[chunk(i, rows)] = h
        g1.send(i, (normed(h)[0] * ln_ref[0:1] + ln_ref[1:2]).astype(jnp.bfloat16))
        if i == 0:
            for s in range(1, bits):
                ex2.step(s)
    s1.release()
    loads[3].wait()

    def mlp(i):
        u = dot(g1.done(i), w1[...].reshape(width, -1), NN)
        g, slope = gelu_both(u)
        put_rows(g_buf, g.astype(jnp.bfloat16), i, rows)
        dmi = jnp.concatenate([block_rows(dm, b, i, rows) for b in range(4)], axis=0)
        du = (dot(dmi, w2[...].reshape(width, -1), NN) * slope).astype(jnp.bfloat16)
        put_rows(du_buf, du, i, rows)
        scatter_product(s2, i, lambda b: du[b * n : (b + 1) * n], w1[...].reshape(width, -1), rows)

    g1.forward(0)
    ex1.done()
    ex2.done()
    for i in range(NCH):
        mlp(i)
        if i + 1 < NCH:
            g1.forward(i + 1)
        s2.middle(i)
    slab_grad(fc2, 0, dm[...], g_buf[...])
    if fold:
        reduce = DpReduce(links, fc2, lands[0])
        reduce.start()
    sums = None
    for i in range(NCH):
        at = chunk(i, rows)
        dx, dgain, dshift = norm_back(hid_ref[at], s2.done(i), ln_ref[0:1])
        dh = dy_ref[at] + dx
        dh_ref[at] = dh
        g2.send(i, dh.astype(jnp.bfloat16))
        both = jnp.concatenate([dgain, dshift], axis=0)
        sums = both if sums is None else sums + both
    norm_ref[...] = sums
    slab_grad(fc1, 0, flat(gat1), du_buf[...])
    stores = [start_load(fc1, fc1_hbm, store_sem.at[0])]
    g2.forward(0)
    for b in range(4):
        y = dot(g_buf[pl.ds(b * rows, rows)], w2[...].reshape(width, -1), NT)
        y_buf[pl.ds(b * rows, rows)] = y.astype(jnp.bfloat16)
    stores.append(start_load(y_buf, y_hbm, store_sem.at[1]))
    for i in range(1, NCH):
        g2.forward(i)
    for i in range(NCH):
        put_rows(do_ref, dot(g2.done(i), wp[...], NN).astype(jnp.bfloat16), i, rows)
    stores.append(start_load(gat2, da_hbm, store_sem.at[2]))
    if fold:
        reduce.split(fc2_sent, fc2_ref)
    else:
        fc2_ref[...] = fc2[...]
    links.leave()
    for store in stores:
        store.wait()


def turn_chain(ndp, x, o, dy, ln, dm, wp, own, got):
    rows, width = x.shape
    hidden = own[0].shape[-1]
    bits = own[0].ndim - 2
    fold = ndp == 4
    lw = wp.shape[1]
    n = width // 4
    bf16, f32 = jnp.bfloat16, jnp.float32
    out = jax.ShapeDtypeStruct
    res = pl.pallas_call(
        functools.partial(turn_kernel, bits, fold),
        in_specs=[VM, VM, VM, VM] + [HB] * 6,
        out_specs=[VM] * 6 + [HB] * 3,
        out_shape=[
            out((rows, width), f32),
            out((2, width), f32),
            out((rows, width), f32),
            out((4 * rows, lw), bf16),
            out((n, hidden), bf16),
            out((n, hidden) if fold else (2, 2, n, hidden), bf16),
            out((4 * rows, width), bf16),
            out((4, rows, width), bf16),
            out((2, 2, n, hidden), bf16),
        ],
        scratch_shapes=[
            pltpu.VMEM(wp.shape, bf16),
            pltpu.VMEM(own[0].shape, bf16),
            pltpu.VMEM(own[1].shape, bf16),
            pltpu.VMEM((4 * rows, width), bf16),
            pltpu.VMEM((4 * rows, hidden), bf16),
            pltpu.VMEM((4 * rows, hidden), bf16),
            pltpu.VMEM((4 * rows, width), bf16),
            pltpu.VMEM((2, 2, n, hidden), bf16),
            pltpu.VMEM((2, 2, n, hidden), bf16),
            pltpu.VMEM((4, rows, width), bf16),
            pltpu.VMEM((4, rows, width), bf16),
            *scatter_scratch(rows, width),
            *(DpReduce.scratch(n, hidden)[:1] if fold else []),
            pltpu.SemaphoreType.DMA((4,)),
            pltpu.SemaphoreType.DMA((3,)),
            *comm_scratch(2 * Scatter.COPIES + 2 * Gather.COPIES + 2 * Exchange.copies(bits) + DpReduce.COPIES),
        ],
        compiler_params=params(2),
        cost_estimate=pl.CostEstimate(flops=60 << 30, bytes_accessed=24 << 20, transcendentals=0),
    )(x, o, dy, ln, dm, wp, *own, *got)
    dh, norms, hid, do, sent, fc2, y, da, fc1 = res
    return dh, norms, y, hid, do, da.reshape(4 * rows, width), fc1, (sent, fc2)


def back_kernel(bits, fold, layers, flags_ref, x_ref, dh1_ref, hid_ref, ln_ref, dqkv_ref, o1_ref, lab_ref,
                wq_hbm, wp_hbm, w1_hbm, w2_hbm, u_hbm, g_hbm, n2_hbm, n1_hbm, da1_hbm, dwall_hbm, *refs):
    refs = list(refs)
    take = lambda k: [refs.pop(0) for _ in range(k)]
    blocks = take(len(layers))
    gin_ref, dh_ref, norm_ref, do_ref, da_hbm, fc1_hbm, fc2_sent, fc2_out, qp_out, rel_out, sum_out = take(11)
    places = [take(2) for _ in range(len(layers) + 1)]
    wq, wp, w1, w2, u_buf, g_buf, fc2, gqp, strips, gin_low, gat1, gat2, low, wide = take(14)
    if fold:
        lands_qp, lands_fc = take(3), take(1)
    load_sem, store_sem, send_sem, recv_sem = refs
    small, out_lab = flags_ref[0], flags_ref[1]
    rows, width = x_ref.shape
    n = rows // NCH
    hidden = w1.shape[1]
    heads = rel_out.shape[0]
    lw = o1_ref.shape[1]
    load = lambda k, src, dst: start_load(src, dst, load_sem.at[k])
    load_q, load_n1, load_da = load(0, wq_hbm, wq), load(1, n1_hbm, u_buf), load(2, da1_hbm, g_buf)
    load_1, load_2, load_p = load(3, w1_hbm, w1), load(4, w2_hbm, w2), load(5, wp_hbm, wp)
    load_strip = load(6, dwall_hbm.at[0], strips)
    links = Links(send_sem, recv_sem, bits)
    links.enter()
    blocks.append(gin_low)
    layers = layers + [1]
    returns = [Return(links, layer, src, *at) for layer, src, at in zip(layers, blocks, places)]
    for back in returns[:-1]:
        back.start()
    s1, s2 = Scatter(links, low, wide), Scatter(links, low, wide)
    g1, g2 = Gather(links, gat1), Gather(links, gat2)
    load_q.wait()
    for i in range(NCH):
        scatter_product(s1, i, lambda b: block_rows(dqkv_ref, b, i, rows), wq[...], rows)
        if i:
            s1.middle(i - 1)
    s1.middle(NCH - 1)
    load_n1.wait()
    slab_grad(gqp, 0, u_buf[...], dqkv_ref[...])
    load_da.wait()
    slab_grad(gqp, dqkv_ref.shape[1], g_buf[...], o1_ref[...])
    load_u, load_g = load(8, u_hbm, u_buf), load(9, g_hbm, g_buf)
    if fold:
        reduce = DpReduce(links, gqp, *lands_qp)
        reduce.start()
    cols = jnp.sum(dqkv_ref[...].astype(jnp.float32), axis=0, keepdims=True)
    sum_out[...] = jnp.concatenate([cols[:, :lw], cols[:, 2 * lw :]], axis=1)
    sums1 = None
    for i in range(NCH):
        at = chunk(i, rows)
        dx, dgain, dshift = norm_back(x_ref[at].astype(jnp.float32), s1.done(i), ln_ref[0:1])
        gin = dh1_ref[at] + dx
        gin_ref[at] = gin
        gin_low[at] = gin.astype(jnp.bfloat16)
        g1.send(i, gin_low[at])
        both = jnp.concatenate([dgain, dshift], axis=0)
        sums1 = both if sums1 is None else sums1 + both
    returns[-1].start()
    lab = lab_ref[...]
    hi_mask, lo_hot = _labels_hi_lo(lab)

    def bias_head(h, load_strip):
        load_strip.wait()
        rel_out[h] = wall_grad(small, out_lab, lab, hi_mask, lo_hot, strips)
        return load(6, dwall_hbm.at[h + 1], strips) if h + 1 < heads else None

    load_strip = bias_head(0, load_strip)
    load_strip = bias_head(1, load_strip)
    s1.release()
    load_1.wait()
    load_2.wait()
    load_u.wait()

    def mlp(i):
        dmi = g1.done(i)
        ui = jnp.concatenate([block_rows(u_buf, b, i, rows) for b in range(4)], axis=0).astype(jnp.float32)
        du = (dot(dmi, w2[...], NN) * gelu_both(ui)[1]).astype(jnp.bfloat16)
        put_rows(u_buf, du, i, rows)
        scatter_product(s2, i, lambda b: du[b * n : (b + 1) * n], w1[...], rows)

    g1.forward(0)
    for i in range(NCH):
        mlp(i)
        if i + 1 < NCH:
            g1.forward(i + 1)
        s2.middle(i)
    if fold:
        reduce.middle()
    load_g.wait()
    slab_grad(fc2, 0, flat(gat1), g_buf[...])
    if fold:
        reduce_2 = DpReduce(links, fc2, *lands_fc)
        reduce_2.start()
    load_n2 = load(10, n2_hbm, g_buf)
    sums2 = None
    for i in range(NCH):
        at = chunk(i, rows)
        dx, dgain, dshift = norm_back(hid_ref[at], s2.done(i), ln_ref[1:2])
        dh = gin_ref[at].astype(jnp.bfloat16).astype(jnp.float32) + dx
        dh_ref[at] = dh
        g2.send(i, dh.astype(jnp.bfloat16))
        both = jnp.concatenate([dgain, dshift], axis=0)
        sums2 = both if sums2 is None else sums2 + both
    norm_ref[...] = jnp.concatenate([sums1, sums2], axis=0)
    load_n2.wait()
    weight_grad(w2, 0, g_buf[...], u_buf[...])
    stores = [start_load(w2, fc1_hbm, store_sem.at[0])]
    load_strip = bias_head(2, load_strip)
    load_p.wait()
    g2.forward(0)
    bias_head(3, load_strip)
    for i in range(1, NCH):
        g2.forward(i)
    for i in range(NCH):
        put_rows(do_ref, dot(g2.done(i), wp[...], NN).astype(jnp.bfloat16), i, rows)
    stores.append(start_load(gat2, da_hbm, store_sem.at[2]))
    if fold:
        reduce.done(qp_out)
        reduce_2.split(fc2_sent, fc2_out)
    else:
        qp_out[...] = gqp[...]
        fc2_out[...] = fc2[...]
    for back in returns:
        back.done()
    links.leave()
    for store in stores:
        store.wait()


def back_chain(ndp, flags, x, dh1, hid, ln, dqkv, o1, lab, wq, wp, w1, w2, u, g, n2, n1, da1, dwall, returns):
    rows, width = x.shape
    hidden = w1.shape[1]
    lw = wp.shape[1]
    heads = dwall.shape[0]
    fold = ndp == 4
    bits = 2
    n = width // 4
    qp_cols = wq.shape[1] + lw
    bf16, f32 = jnp.bfloat16, jnp.float32
    out = jax.ShapeDtypeStruct
    layers = [layer for layer, _ in returns]
    blocks = [block for _, block in returns]
    copies = 2 * Scatter.COPIES + 2 * Gather.COPIES + 2 * DpReduce.COPIES + (len(layers) + 1) * Return.COPIES
    res = pl.pallas_call(
        functools.partial(back_kernel, bits, fold, layers),
        in_specs=[pl.BlockSpec(memory_space=pltpu.SMEM)] + [VM] * 7 + [HB] * (10 + len(blocks)),
        out_specs=[VM, VM, VM, VM, HB, HB, VM, VM, VM, VM, VM] + [HB] * (2 * len(blocks) + 2),
        out_shape=[
            out((rows, width), f32),
            out((rows, width), f32),
            out((4, width), f32),
            out((4 * rows, lw), bf16),
            out((4, rows, width), bf16),
            out((width, hidden), bf16),
            out((n, hidden), bf16),
            out((n, hidden) if fold else (2, 2, n, hidden), bf16),
            out((n, qp_cols) if fold else (2, 2, n, qp_cols), bf16),
            out((heads, 32, 128), f32),
            out((1, 2 * lw), f32),
        ]
        + [out(block.shape, block.dtype) for block in blocks for _ in range(2)]
        + [out((rows, width), bf16)] * 2,
        scratch_shapes=[
            pltpu.VMEM(wq.shape, bf16),
            pltpu.VMEM(wp.shape, bf16),
            pltpu.VMEM(w1.shape, bf16),
            pltpu.VMEM(w2.shape, bf16),
            pltpu.VMEM((4 * rows, hidden), bf16),
            pltpu.VMEM((4 * rows, hidden), bf16),
            pltpu.VMEM((2, 2, n, hidden), bf16),
            pltpu.VMEM((2, 2, n, qp_cols), bf16),
            pltpu.VMEM(dwall.shape[1:], f32),
            pltpu.VMEM((rows, width), bf16),
            pltpu.VMEM((4, rows, width), bf16),
            pltpu.VMEM((4, rows, width), bf16),
            *scatter_scratch(rows, width),
            *(DpReduce.scratch(n, qp_cols) + DpReduce.scratch(n, hidden)[:1] if fold else []),
            pltpu.SemaphoreType.DMA((11,)),
            pltpu.SemaphoreType.DMA((3,)),
            *comm_scratch(copies),
        ],
        compiler_params=params(3),
        cost_estimate=pl.CostEstimate(flops=60 << 30, bytes_accessed=24 << 20, transcendentals=0),
    )(flags, x, dh1, hid, ln, dqkv, o1, lab, wq, wp, w1, w2, u, g, n2, n1, da1, dwall, *blocks)
    gin, dh, norms, do, da, fc1, sent, fc2, qp, rel, sums = res[:11]
    got = [(res[11 + 2 * k], res[12 + 2 * k]) for k in range(len(layers) + 1)]
    return gin, dh, norms, do, da.reshape(4 * rows, width), fc1, (sent, fc2), qp, rel, sums, got


def start_kernel(order, scale, bits, flags_ref, x_hbm, cot_hbm, mask_ref, lab_ref, tab_hbm, pack_hbm,
                 wq_hbm, wp_hbm, w1_hbm, w2_hbm,
                 x_ref, cot_ref, pack_ref, lse_ref, o_ref, n1_hbm, qkv_hbm, wall0_hbm, wall1_hbm,
                 wq0_hbm, wp0_hbm, w10_hbm, w20_hbm,
                 tab, wq, wp, qkv, wall, gat1, s_scr, p_scr, load_sem, store_sem, send_sem, recv_sem):
    small, out_lab = flags_ref[0], flags_ref[1]
    rows, width = x_ref.shape
    wide = qkv.shape[1]
    heads = wall.shape[1]
    links = Links(send_sem, recv_sem, bits)
    pair, home = links.pair, links.home
    own_x = pltpu.make_async_copy(x_hbm.at[pair], x_ref, load_sem.at[0])
    when(home, own_x.start)
    own_cot = pltpu.make_async_copy(cot_hbm.at[pair], cot_ref, load_sem.at[7])
    when(home, own_cot.start)
    links.enter()
    packs = [Spread(links, l, pack_hbm, pack_ref.at[l], load_sem.at[1 + l]) for l in range(2)]
    tabs = [Spread(links, l, tab_hbm, tab.at[l], load_sem.at[3 + l]) for l in range(2)]
    tabs[0].start()
    packs[0].start()
    far_x = links.send(x_hbm.at[1 - pair], x_ref, FAR, home)
    tabs[1].start()
    packs[1].start()
    get_q = Deliver(links, 0, wq_hbm, wq, load_sem.at[5])
    get_p = Deliver(links, 0, wp_hbm, wp, load_sem.at[6])
    get_1, get_2 = Deliver(links, 0, w1_hbm, w10_hbm), Deliver(links, 0, w2_hbm, w20_hbm)
    ex_q, ex_p = Exchange(links, wq), Exchange(links, wp)
    get_q.start()
    lab = lab_ref[...]
    hi_mask, lo_hot = _labels_hi_lo(lab)

    def build(l):
        def one(h, carry):
            build_wall(small, out_lab, lab, hi_mask, lo_hot, tab[l, h], wall.at[l, h])
            return carry

        lax.fori_loop(0, heads, one, 0)

    tabs[0].done()
    build(0)
    stores = [start_load(wall.at[0], wall0_hbm, store_sem.at[0])]
    packs[0].done()
    when(home, own_x.wait)
    when(jnp.logical_not(home), far_x.wait_recv)
    g1 = Gather(links, gat1)
    for i in range(NCH):
        at = chunk(i, rows)
        xhat = normed(x_ref[at].astype(jnp.float32))[0]
        g1.send(i, (xhat * pack_ref[0, 0:1] + pack_ref[0, 2:3]).astype(jnp.bfloat16))
    get_p.start()
    get_1.start()
    get_2.start()
    far_cot = links.send(cot_hbm.at[1 - pair], cot_ref, FAR, home)
    tabs[1].done()
    build(1)
    stores.append(start_load(wall.at[1], wall1_hbm, store_sem.at[5]))
    get_q.done()
    ex_q.step(0)
    for i in range(NCH):
        g1.forward(i)
    for s in range(1, bits):
        ex_q.step(s)
    for i in range(NCH):
        g1.copies["s", i].wait_recv()
        g1.copies["f", i].wait_recv()
    stores.append(start_load(gat1, n1_hbm, store_sem.at[1]))
    packs[1].done()
    get_p.done()
    ex_q.done()
    ex_p.step(0)
    stores.append(start_load(wq, wq0_hbm, store_sem.at[2]))
    term = pack_ref[0, pl.ds(4 + pair, 1)][:, :wide]
    weight = wq[...].reshape(width, wide)
    for b in range(4):
        qkv[pl.ds(b * rows, rows)] = (dot(gat1[b], weight, NN) + term).astype(jnp.bfloat16)
    stores.append(start_load(qkv, qkv_hbm, store_sem.at[3]))
    for s in range(1, bits):
        ex_p.step(s)
    keys = [quarter(links.r, links.c, j) for j in order]

    def block(i, carry):
        at = pl.ds(pl.multiple_of(i * QB, QB), QB)
        qq = lax.rem(links.r + i // 2, 2) + 2 * lax.rem(links.c + lax.rem(i, 2), 2)
        o_ref[at] = attn_block(
            qq, keys, scale, qkv.at[at], qkv, mask_ref[...], wall.at[0], lse_ref.at[i], s_scr, p_scr
        )
        return carry

    lax.fori_loop(0, 4, block, 0)
    ex_p.done()
    stores.append(start_load(wp, wp0_hbm, store_sem.at[4]))
    get_1.done()
    get_2.done()
    when(home, own_cot.wait)
    when(jnp.logical_not(home), far_cot.wait_recv)
    links.leave()
    for store in stores:
        store.wait()


def start_chain(flags, x, cot, mask_pad, lab, table, pack, wq, wp, w1, w2, order, scale):
    bits = wq.ndim - 2
    _, rows, width = x.shape
    heads = table.shape[0]
    wide = wq.shape[-1]
    bf16, f32 = jnp.bfloat16, jnp.float32
    out = jax.ShapeDtypeStruct
    copies = 2 + 4 * Spread.COPIES + 4 * Deliver.COPIES + 2 * Exchange.copies(bits) + Gather.COPIES
    return pl.pallas_call(
        functools.partial(start_kernel, order, scale, bits),
        in_specs=[pl.BlockSpec(memory_space=pltpu.SMEM), HB, HB, VM, VM, HB, HB, HB, HB, HB, HB],
        out_specs=[VM] * 5 + [HB] * 8,
        out_shape=[
            out((rows, width), bf16),
            out((rows, width), bf16),
            out((2,) + pack.shape, f32),
            out((4, heads, QB), f32),
            out((4 * rows, heads * HD), bf16),
            out((4, rows, width), bf16),
            out((4 * rows, wide), bf16),
            out((heads, 32, WALL), f32),
            out((heads, 32, WALL), f32),
            *[out(w.shape, bf16) for w in (wq, wp, w1, w2)],
        ],
        scratch_shapes=[
            pltpu.VMEM((2,) + table.shape, f32),
            *[pltpu.VMEM(w.shape, bf16) for w in (wq, wp)],
            pltpu.VMEM((4 * rows, wide), bf16),
            pltpu.VMEM((2, heads, 32, WALL), f32),
            pltpu.VMEM((4, rows, width), bf16),
            pltpu.VMEM((2, 4 * rows, QB), f32),
            pltpu.VMEM((2, 4 * rows, QB), bf16),
            pltpu.SemaphoreType.DMA((8,)),
            pltpu.SemaphoreType.DMA((6,)),
            *comm_scratch(copies),
        ],
        compiler_params=params(0),
        cost_estimate=pl.CostEstimate(flops=80 << 30, bytes_accessed=24 << 20, transcendentals=0),
    )(flags, x, cot, mask_pad, lab, table, pack, wq, wp, w1, w2)


def attn_back(links, order, scale, qkv_ref, do_ref, o_ref, lse_ref, k_extra, wall, acc, p_scr, s_scr, dq_scr, dk_scr, dv_scr,
              dqkv_ref, event):
    heads = wall.shape[0]
    width = heads * HD
    total = qkv_ref.shape[0]
    keys = [quarter(links.r, links.c, j) for j in order]
    lane = lax.broadcasted_iota(jnp.int32, (QB, 128 - HD), 1)
    q_extra = jnp.where(lane == 0, 1.0, 0.0).astype(jnp.bfloat16)

    def block(i, carry):
        at = pl.ds(pl.multiple_of(i * QB, QB), QB)
        q_ref, d_ref, out_ref = qkv_ref.at[at], do_ref.at[at], o_ref.at[at]
        qq = block_quarter(links, i)
        dqs = []
        for h in range(heads):
            kh = head_lanes(qkv_ref, width + HD * h, k_extra)
            qh = head_lanes(q_ref, HD * h, q_extra)
            vh = head_lanes(qkv_ref, 2 * width + HD * h)
            doh = head_lanes(d_ref, HD * h)
            oh = head_lanes(out_ref, HD * h)
            inner = jnp.sum((doh.astype(jnp.float32) * oh.astype(jnp.float32)).T, axis=0, keepdims=True)
            lse = lse_ref[i, h : h + 1, :]
            for kb in range(total // 256):
                s_t = dot(kh[256 * kb : 256 * kb + 256], qh, NT)
                dp_t = dot(vh[256 * kb : 256 * kb + 256], doh, NT)
                for js in range(8):
                    st = 8 * kb + js
                    start = strip_start(qq, js, keys[kb])
                    s = s_t[32 * js : 32 * js + 32] * (scale * LOG2E) + wall[h, :, pl.ds(start, QB)]
                    p = jnp.exp2(s - lse)
                    ds = p * (dp_t[32 * js : 32 * js + 32] - inner)
                    p_scr[h % 2, 32 * st : 32 * st + 32] = p.astype(jnp.bfloat16)
                    s_scr[h % 2, 32 * st : 32 * st + 32] = ds.astype(jnp.bfloat16)
                    acc[h, :, pl.ds(start, QB)] += ds
            p_b, ds_b = p_scr[h % 2], s_scr[h % 2]
            dv_scr[h] += dot(p_b, doh, NN)
            dk_scr[h] += dot(ds_b, qh, NN)
            dq_t = dot(kh, ds_b, TN) * scale
            dqs.append(dq_t.T[:, :HD].astype(jnp.bfloat16))
        dq_scr[at] = jnp.concatenate(dqs, axis=1)
        event(i)
        return carry

    lax.fori_loop(0, total // QB, block, 0)
    parts = [dq_scr[...]]
    parts += [(dk_scr[h, :, :HD] * scale).astype(jnp.bfloat16) for h in range(heads)]
    parts += [dv_scr[h, :, :HD].astype(jnp.bfloat16) for h in range(heads)]
    dqkv_ref[...] = jnp.concatenate(parts, axis=1)


def bwd_kernel(order, scale, bits, fold, layers, summed, qkv_ref, do_ref, o_ref, lse_ref, mask_ref, wall_hbm, gfc_hbm, *refs):
    refs = list(refs)
    take = lambda k: [refs.pop(0) for _ in range(k)]
    blocks = take(len(layers))
    sent_2, kept_2 = take(2) if fold else (None, None)
    y_ref, hid_ref = take(2) if summed else (None, None)
    dqkv_ref, acc_hbm = take(2)
    fc_out, fin_out = take(2) if fold else (None, None)
    places = [take(2) for _ in range(len(layers) + (1 if fold else 0))]
    (act_ref,) = take(1) if summed else (None,)
    wall, acc, p_scr, s_scr, dq_scr, dk_scr, dv_scr = take(7)
    if fold:
        gfc, land0, land1, sent, land_2 = take(5)
    if summed:
        (low,) = take(1)
    load_sem, store_sem, send_sem, recv_sem = refs
    loads = [start_load(wall_hbm, wall, load_sem.at[0])]
    if fold:
        loads.append(start_load(gfc_hbm, gfc, load_sem.at[1]))
    links = Links(send_sem, recv_sem, bits)
    links.enter()
    returns = [Return(links, layer, src, *at) for layer, src, at in zip(layers, blocks, places)]
    if fold:
        finish = DpFinish(links, sent_2, kept_2, land_2)
        finish.start()
        last = Return(links, 1, fin_out, *places[-1])
        reduce = DpReduce(links, gfc, land0, land1, sent)
    if summed:
        rows = hid_ref.shape[0]
        part = lambda b: y_ref.at[pl.ds(b * rows, rows)]
        to_sib = links.make(part(3), low.at[0], SIBLING)
        near = links.make(part(1), low.at[1], SIBLING)
        to_partner = links.make(low.at[2], low.at[3], PARTNER)
        to_sib.start()
        near.start()
    acc[...] = jnp.zeros_like(acc)
    dk_scr[...] = jnp.zeros_like(dk_scr)
    dv_scr[...] = jnp.zeros_like(dv_scr)
    if fold:
        loads[1].wait()
        reduce.start()
    if summed:
        to_sib.wait_recv()
        low[2] = (part(2)[...].astype(jnp.float32) + low[0].astype(jnp.float32)).astype(jnp.bfloat16)
        to_partner.start()
    for back in returns:
        back.start()
    loads[0].wait()

    def finished():
        finish.done(fin_out)
        last.start()

    def event(i):
        if fold:
            pl.when(i == 0)(finished)

    attn_back(
        links, order, scale, qkv_ref, do_ref, o_ref, lse_ref, mask_ref[...], wall, acc, p_scr, s_scr, dq_scr, dk_scr, dv_scr,
        dqkv_ref, event,
    )
    stores = [start_load(acc, acc_hbm, store_sem.at[0])]
    if fold:
        reduce.middle()
    if summed:
        near.wait_recv()
        to_partner.wait_recv()
        act = hid_ref[...] + part(0)[...].astype(jnp.float32) + low[1].astype(jnp.float32) + low[3].astype(jnp.float32)
        act_ref[...] = act.astype(jnp.bfloat16)
    if fold:
        reduce.done(fc_out)
        last.done()
    for back in returns:
        back.done()
    links.leave()
    for store in stores:
        store.wait()


def bwd_chain(ident, fold, qkv, do, o, lse, mask_pad, wall, gfc, finish, returns, order, scale, summed=None):
    total, wide = qkv.shape
    heads = wall.shape[0]
    bits = 2
    n, columns = gfc.shape[2:]
    bf16, f32 = jnp.bfloat16, jnp.float32
    out = jax.ShapeDtypeStruct
    layers = [layer for layer, _ in returns]
    blocks = [block for _, block in returns]
    outs = [out((total, wide), bf16), out(wall.shape, f32)]
    specs = [VM, HB]
    if fold:
        outs += [out((n, columns), bf16)] * 2
        specs += [VM] * 2
    for block in blocks + ([finish[0]] if fold else []):
        outs += [out(block.shape, block.dtype)] * 2
        specs += [HB] * 2
    scratch = [
        pltpu.VMEM(wall.shape, f32),
        pltpu.VMEM(wall.shape, f32),
        pltpu.VMEM((2, total, QB), bf16),
        pltpu.VMEM((2, total, QB), bf16),
        pltpu.VMEM((total, heads * HD), bf16),
        pltpu.VMEM((heads, total, 128), f32),
        pltpu.VMEM((heads, total, 128), f32),
    ]
    if fold:
        scratch += [pltpu.VMEM(gfc.shape, bf16), *DpReduce.scratch(n, columns), pltpu.VMEM((n, columns), bf16)]
    more = list(finish) if fold else []
    if summed is not None:
        more += list(summed)
        rows, width = summed[1].shape
        outs.append(out((rows, width), bf16))
        specs.append(VM)
        scratch.append(pltpu.VMEM((4, rows, width), bf16))
    copies = len(layers) * Return.COPIES + (DpReduce.COPIES + DpFinish.COPIES + Return.COPIES if fold else 0) + (3 if summed else 0)
    res = pl.pallas_call(
        functools.partial(bwd_kernel, order, scale, bits, fold, layers, summed is not None),
        in_specs=[VM] * 5 + [HB] * 2 + [VM] * (len(blocks) + len(more)),
        out_specs=specs,
        out_shape=outs,
        scratch_shapes=scratch
        + [pltpu.SemaphoreType.DMA((2,)), pltpu.SemaphoreType.DMA((1,)), *comm_scratch(max(copies, 1))],
        compiler_params=params(ident),
        cost_estimate=pl.CostEstimate(flops=24 << 30, bytes_accessed=20 << 20, transcendentals=0),
    )(qkv, do, o, lse, mask_pad, wall, gfc, *blocks, *more)
    res = list(res)
    dqkv, acc = res[:2]
    res = res[2:]
    fc, fin = (res.pop(0), res.pop(0)) if fold else (None, None)
    got = [(res[2 * k], res[2 * k + 1]) for k in range(len(layers) + (1 if fold else 0))]
    act = res[-1] if summed is not None else None
    return dqkv, acc, fc, fin, got, act


class SumHops:
    def __init__(self, links, buf, land, hops):
        self.links, self.buf, self.land, self.hops, self.k = links, buf, land, hops, 0

    def send(self):
        if self.k < len(self.hops):
            self.copy = self.links.send(self.buf, self.land.at[self.k], self.hops[self.k], track=False)

    def take(self):
        self.copy.wait_recv()
        self.copy.wait_send()
        self.buf[...] = self.buf[...] + self.land[self.k]
        self.k += 1
        self.send()


def end_kernel(order, scale, bits, fold, layers, flags_ref, qkv_ref, do_ref, o_ref, lse_ref, mask_ref,
               x_ref, dh_ref, ln_ref, lab_ref, small_ref, rel1_ref,
               wall_hbm, wq_hbm, n1_hbm, da_hbm, fc_hbm, *refs):
    refs = list(refs)
    take = lambda k: [refs.pop(0) for _ in range(k)]
    blocks = take(len(layers))
    sent_2, kept_2 = take(2) if fold else (None, None)
    gin_ref, small_out, rel_out, q_out = take(4)
    fc_out, fin_out = take(2) if fold else (None, None)
    (all_fc,) = (None,) if fold else take(1)
    places = [take(2) for _ in range(len(layers) + (4 if fold else 1))]
    acc, dqkv_ref, gq, fc, gin_low, low1 = take(6)
    rel, rel_land, rel_near, smalls, small_land, norm_land, small_near = take(7)
    if fold:
        lands_q, lands_f, (land_2,) = take(3), take(3), take(1)
    load_sem, send_sem, recv_sem = refs
    small, out_lab = flags_ref[0], flags_ref[1]
    rows, width = x_ref.shape
    heads = rel.shape[1]
    hidden = fc_hbm.shape[-1]
    load_f = start_load(fc_hbm, fc.at[:, :, :, pl.ds(0, hidden)], load_sem.at[1])
    links = Links(send_sem, recv_sem, bits)
    home, away = links.home, jnp.logical_not(links.home)
    links.enter()
    give = list(zip(layers, blocks)) + [(0, gin_low)] + ([(0, fc_out), (0, q_out), (0, fin_out)] if fold else [])
    returns = [Return(links, layer, src, *at) for (layer, src), at in zip(give, places)]
    early = len(layers)
    for back in returns[:early]:
        back.start()
    if fold:
        finish = DpFinish(links, sent_2, kept_2, land_2)
        finish.start()
        reduce_f = DpReduce(links, fc, *lands_f)
        reduce_q = DpReduce(links, gq, *lands_q)

    def proj_grad(rows_buf):
        start_load(da_hbm, rows_buf, load_sem.at[4]).wait()
        slab_grad(fc, hidden, rows_buf[...], o_ref[...])

    pl.run_scoped(proj_grad, pltpu.VMEM(da_hbm.shape, jnp.bfloat16))
    load_f.wait()
    if fold:
        reduce_f.start()
    acc[...] = jnp.zeros_like(acc)

    def finished():
        finish.done(fin_out)
        returns[early + 3].start()

    def event(i):
        if fold:
            pl.when(i == 0)(finished)

    def attention(wall, p_scr, s_scr, dq_scr, dk_scr, dv_scr):
        load_w = start_load(wall_hbm, wall, load_sem.at[0])
        dk_scr[...] = jnp.zeros_like(dk_scr)
        dv_scr[...] = jnp.zeros_like(dv_scr)
        load_w.wait()
        attn_back(
            links, order, scale, qkv_ref, do_ref, o_ref, lse_ref, mask_ref[...], wall, acc, p_scr, s_scr, dq_scr, dk_scr,
            dv_scr, dqkv_ref, event,
        )

    total = qkv_ref.shape[0]
    vmem, bf16, f32 = pltpu.VMEM, jnp.bfloat16, jnp.float32
    pl.run_scoped(
        attention,
        vmem(wall_hbm.shape, f32),
        vmem((2, total, QB), bf16),
        vmem((2, total, QB), bf16),
        vmem((total, heads * HD), bf16),
        vmem((heads, total, 128), f32),
        vmem((heads, total, 128), f32),
    )
    lw = o_ref.shape[1]

    def rest(wq, rows_buf, wide1):
        s1 = Scatter(links, low1, wide1)
        load_q = start_load(wq_hbm, wq, load_sem.at[2])
        load_n = start_load(n1_hbm, rows_buf, load_sem.at[3])
        load_q.wait()
        for i in range(NCH):
            scatter_product(s1, i, lambda b: block_rows(dqkv_ref, b, i, rows), wq[...], rows)
            if i:
                s1.middle(i - 1)
        s1.middle(NCH - 1)
        load_n.wait()
        slab_grad(gq, 0, rows_buf[...], dqkv_ref[...])
        if fold:
            reduce_f.middle()
            reduce_q.start()
        cols = jnp.sum(dqkv_ref[...].astype(jnp.float32), axis=0, keepdims=True)
        mine = jnp.concatenate([cols[:, :lw], cols[:, 2 * lw :]], axis=1)
        images = (smalls.shape[0] - 8) // 2
        number = 2 * lax.axis_index("dp") + links.pair
        here = lax.broadcasted_iota(jnp.int32, (images, 2 * lw), 0) == number
        smalls[...] = small_ref[...]
        smalls[8 : 8 + images, 0 : 2 * lw] = jnp.where(here, jnp.broadcast_to(mine, (images, 2 * lw)), 0.0)
        lab = lab_ref[...]
        hi_mask, lo_hot = _labels_hi_lo(lab)
        rel[1] = rel1_ref[...]

        def heads_of(a, b):
            def one(h, carry):
                rel[0, h] = wall_grad(small, out_lab, lab, hi_mask, lo_hot, acc.at[h])
                return carry

            lax.fori_loop(a, b, one, 0)

        hops = [ACROSS] + [("dp", b) for b in range(bits)]
        small_hops = SumHops(links, smalls, small_land, hops)
        rel_hops = SumHops(links, rel, rel_land, hops)
        heads_of(0, heads // 2)
        if fold:
            reduce_f.done(fc_out)
            returns[early + 1].start()
        late = None
        for i in range(NCH):
            at = chunk(i, rows)
            dx, dgain, dshift = norm_back(x_ref[at].astype(jnp.float32), s1.done(i), ln_ref[0:1])
            gin = dh_ref[at] + dx
            gin_ref[at] = gin
            gin_low[at] = gin.astype(jnp.bfloat16)
            both = jnp.concatenate([dgain, dshift], axis=0)
            late = both if late is None else late + both
        smalls[0:2] = late
        small_hops.send()
        heads_of(heads // 2, heads)
        rel_hops.send()
        returns[early].start()
        if fold:
            reduce_q.middle()
            reduce_q.done(q_out)
            returns[early + 2].start()
        else:
            q_out[...] = gq[...]
            all_fc[...] = fc[...]
        for _ in range(bits + 1):
            small_hops.take()
            rel_hops.take()
        images_at = pl.ds(8, smalls.shape[0] - 8)
        rel_copy = links.send(rel.at[1 - links.c], rel_near, SIBLING, home)
        small_copy = links.send(smalls.at[images_at], small_near, SIBLING, home)
        norm_hops = SumHops(links, smalls.at[pl.ds(0, 8)], norm_land, [PARTNER, SIBLING])
        norm_hops.send()

        @pl.when(home)
        def _():
            rel_out[...] = rel[links.c]
            small_out[images_at] = smalls[images_at]

        @pl.when(away)
        def _():
            rel_copy.wait_recv()
            small_copy.wait_recv()
            rel_out[...] = rel_near[...]
            small_out[images_at] = small_near[...]

        norm_hops.take()
        norm_hops.take()
        small_out[0:8] = smalls[0:8]
        for back in returns:
            back.done()
        links.leave()

    pl.run_scoped(rest, vmem(wq_hbm.shape, bf16), vmem(n1_hbm.shape, bf16), vmem((2, rows, width), f32))


def end_chain(ndp, flags, qkv, do, o, lse, mask_pad, x, dh, ln, lab, smalls, rel1, wall, wq, n1, da, fc, finish, returns, order, scale):
    rows, width = x.shape
    heads = wall.shape[0]
    total, wide = qkv.shape
    bits = ndp.bit_length() - 1
    fold = bits == 2
    n, hidden = fc.shape[2:]
    fc_cols = hidden + o.shape[1]
    count = smalls.shape[0]
    hops = bits + 1
    bf16, f32 = jnp.bfloat16, jnp.float32
    out = jax.ShapeDtypeStruct
    layers = [layer for layer, _ in returns]
    blocks = [block for _, block in returns]
    landed = [out(block.shape, bf16) for block in blocks] + [out((rows, width), bf16)]
    outs = [
        out((rows, width), f32),
        out((count, width), f32),
        out((heads, 32, 128), f32),
        out((n, wide) if fold else (2, 2, n, wide), bf16),
    ]
    if fold:
        outs += [out((n, fc_cols), bf16), out((n, hidden), bf16)]
        landed += [out((n, fc_cols), bf16), out((n, wide), bf16), out((n, hidden), bf16)]
        blocks += list(finish)
    else:
        outs.append(out((2, 2, n, fc_cols), bf16))
    copies = Scatter.COPIES + len(landed) * Return.COPIES + 2 * DpReduce.COPIES + DpFinish.COPIES + 2 * hops + 4
    res = pl.pallas_call(
        functools.partial(end_kernel, order, scale, bits, fold, layers),
        in_specs=[pl.BlockSpec(memory_space=pltpu.SMEM)] + [VM] * 11 + [HB] * (5 + len(layers)) + ([VM] * 2 if fold else []),
        out_specs=[VM] * len(outs) + [HB] * (2 * len(landed)),
        out_shape=outs + [shape for shape in landed for _ in range(2)],
        scratch_shapes=[
            pltpu.VMEM(wall.shape, f32),
            pltpu.VMEM((total, wide), bf16),
            pltpu.VMEM((2, 2, n, wide), bf16),
            pltpu.VMEM((2, 2, n, fc_cols), bf16),
            pltpu.VMEM((rows, width), bf16),
            pltpu.VMEM((6, rows, width), bf16),
            pltpu.VMEM((2, heads, 32, 128), f32),
            pltpu.VMEM((hops, 2, heads, 32, 128), f32),
            pltpu.VMEM((heads, 32, 128), f32),
            pltpu.VMEM((count, width), f32),
            pltpu.VMEM((hops, count, width), f32),
            pltpu.VMEM((2, 8, width), f32),
            pltpu.VMEM((count - 8, width), f32),
            *(
                DpReduce.scratch(n, wide) + DpReduce.scratch(n, fc_cols) + [pltpu.VMEM((n, hidden), bf16)]
                if fold
                else []
            ),
            pltpu.SemaphoreType.DMA((5,)),
            *comm_scratch(copies),
        ],
        compiler_params=params(4),
        cost_estimate=pl.CostEstimate(flops=90 << 30, bytes_accessed=24 << 20, transcendentals=0),
    )(flags, qkv, do, o, lse, mask_pad, x, dh, ln, lab, smalls, rel1, wall, wq, n1, da, fc, *blocks)
    res = list(res)
    got = [(res[len(outs) + 2 * k], res[len(outs) + 2 * k + 1]) for k in range(len(landed))]
    return res[: len(outs)], got


AXES = ("dp", "section", "tensor")
ORDER = (0, 2, 1, 3)


def local(
    inputs,
    time_emb,
    lengths,
    key_mask,
    rel_index,
    w_qkv,
    w_time,
    w_proj,
    w_fc1,
    w_fc2,
    rel_table,
    norm_gains,
    norm_biases,
    cotangent,
):
    bf16, f32 = jnp.bfloat16, jnp.float32
    _, rows, width = inputs.shape
    seq_len = key_mask.shape[1]
    heads, buckets = rel_table.shape[1:]
    local_width = w_proj.shape[2]
    scale = 1.0 / math.sqrt(HD)
    ndp = lax.axis_size("dp")
    d = lax.axis_index("dp")
    c = lax.axis_index("section")
    z = lax.axis_index("tensor")
    pair = z // 2
    home = c == pair
    first = c == 0
    t = z % 2 + 2 * c

    def move(x, to, name="move"):
        pairs = []
        for dd in range(ndp):
            for cc in range(2):
                for zz in range(4):
                    dst = to(dd, cc, zz)
                    if dst is not None:
                        pairs.append(((dd * 2 + cc) * 4 + zz, (dst[0] * 2 + dst[1]) * 4 + dst[2]))
        with jax.named_scope(name):
            return lax.ppermute(x, AXES, pairs)

    def partner(x):
        return move(x, lambda dd, cc, zz: (dd, cc, zz ^ 1), "partner")

    def sibling(x):
        return move(x, lambda dd, cc, zz: (dd, 1 - cc, zz), "sibling")

    def across(x):
        return move(x, lambda dd, cc, zz: (dd, cc, zz ^ 2), "across")

    def dp_scatter(x, bits):
        n = x.shape[1]
        left = sorted(bits, reverse=True)
        v = x.reshape((2,) * len(left) + (-1, n))
        for b in bits:
            axis = left.index(b)
            left.remove(b)
            mine = (d >> b) & 1
            send = lax.dynamic_index_in_dim(v, 1 - mine, axis, keepdims=False)
            keep = lax.dynamic_index_in_dim(v, mine, axis, keepdims=False)
            got = move(send, lambda dd, cc, zz, b=b: (dd ^ (1 << b), cc, zz), "g_dp")
            v = keep.astype(f32) + got.astype(f32)
            if left:
                v = v.astype(bf16)
        return v

    def by_bits(w):
        return w.reshape(2, 2, -1, w.shape[-1])

    table = jnp.pad(rel_table[0], ((0, 0), (0, 4096 - buckets))).reshape(heads, 32, 128)
    time_all = jnp.einsum("id,dcn->icn", time_emb, w_time[0], preferred_element_type=f32)
    gap = jnp.zeros((2, local_width), f32)
    time_rows = jnp.concatenate([time_all[:, 0], gap, time_all[:, 1], gap], axis=1)
    small_pack = jnp.concatenate([norm_gains[0], norm_biases[0], time_rows, jnp.zeros((2, width), f32)], axis=0)
    own = [by_bits(w) for w in (jnp.concatenate([w_qkv[0, :, j] for j in range(3)], axis=1), w_proj[0], w_fc1[0], w_fc2[0])]
    label_lanes = label_row(rel_index)
    out_label = rel_index[1, seq_len - 1, seq_len - 1].reshape(1)

    length = lax.dynamic_index_in_dim(lengths, pair, 0, keepdims=False)
    small = (length < seq_len).astype(jnp.int32)
    scalars = jnp.stack([z % 2, c] + [jnp.int32(j) for j in ORDER])
    flags = jnp.concatenate([small.reshape(1), out_label])
    mask = lax.dynamic_index_in_dim(key_mask, pair, 0, keepdims=False).reshape(4, rows)
    mask = jnp.concatenate([lax.dynamic_index_in_dim(mask, t ^ j, 0, keepdims=False) for j in ORDER])
    lane = jnp.arange(128 - HD)[None, :]
    mask_pad = jnp.where((lane == 0) & (mask[:, None] == 0), -1e30, 0.0).astype(bf16)

    def gather_rows(x):
        far = partner(x)
        near = sibling(x)
        return jnp.concatenate([x, near, far, sibling(far)], axis=0)

    def scatter_rows(far, near):
        a = sibling(far[rows:].astype(bf16))
        rz = partner((far[:rows] + a.astype(f32)).astype(bf16))
        rs = sibling(near[rows:].astype(bf16))
        return near[:rows] + rs.astype(f32) + rz.astype(f32)

    def times_t(x, w):
        return lax.dot_general(x, w, (((1,), (1,)), ((), ())), preferred_element_type=f32)

    def grad_of(x, y):
        return lax.dot_general(x, y, (((0,), (0,)), ((), ())), preferred_element_type=f32).astype(bf16)

    half = 2 * rows

    def reduced(x):
        with jax.named_scope("g_sum"):
            return lax.psum_scatter(x, "dp", scatter_dimension=0, tiled=True)

    def reduced_late(x):
        if ndp & (ndp - 1):
            return reduced(x)
        bits = list(range(ndp.bit_length() - 1))
        cut = 4 * 128
        return jnp.concatenate(
            [dp_scatter(x[:, :cut], bits), dp_scatter(x[:, cut:], bits[::-1])], axis=1
        ).astype(bf16)

    def column_sums(dqkv):
        sums = jnp.sum(dqkv.astype(f32), axis=0)
        return jnp.concatenate([sums[:local_width], sums[2 * local_width :]])

    def tie(*values):
        return lax.optimization_barrier(values)

    def by_core(pairs):
        return jnp.where(first, pairs[0], pairs[1])

    def near_of(x, layer):
        return move(x, lambda dd, cc, zz: (dd, layer, zz) if cc == zz // 2 and cc != layer else None, "d_near")

    def far_of(x, layer):
        return move(x, lambda dd, cc, zz: (dd, layer, zz ^ 2) if cc != zz // 2 else None, "d_far")

    live = ((t * rows + jnp.arange(rows)) < length).astype(f32)[:, None]
    res = start_chain(flags, inputs, cotangent, mask_pad, label_lanes, table, small_pack, *own, ORDER, scale)
    x0, cot, packs, lse0, o0, n1_0, qkv0 = res[:7]
    walls, got0 = res[7:9], res[9:]
    n1_0 = n1_0.reshape(seq_len, width)

    def whole(w):
        return w.reshape(width, w.shape[-1])

    gains = [packs[l, 0:2] for l in range(2)]
    shifts = [packs[l, 2:4] for l in range(2)]
    ln_mid = jnp.stack([gains[0][1], shifts[0][1], gains[1][0], shifts[1][0]])
    wq0, wp0 = whole(got0[0]), whole(got0[1])
    term1 = lax.dynamic_index_in_dim(packs[1], 4 + pair, 0, keepdims=True)[:, : 3 * local_width]
    hid0, act0, dy1, o1, lse1, n2_0, u0, g0, n1_1, qkv1, dm1, fc_w0, got1 = mid_chain(
        x0, o0, ln_mid, cot, live, term1, mask_pad, wp0, got0[2], got0[3], walls[1], own, ORDER, scale
    )
    w10, w20 = whole(fc_w0[0]), whole(fc_w0[1])
    wq1, wp1 = whole(got1[0]), whole(got1[1])

    fold = ndp == 4
    ln_turn = jnp.stack([gains[1][1], shifts[1][1]])
    dh1, norms1, y1, hid1, do1, da1, fc1_1, fc2_1 = turn_chain(
        ndp, act0, o1, dy1, ln_turn, dm1, wp1, own[2:], got1[2:]
    )
    dqkv1, dwall1, sum_fc1_1, sum_fc2_1, landed, act1 = bwd_chain(
        6, fold, qkv1, do1, o1, lse1, mask_pad, walls[1], fc1_1, fc2_1, [(0, act0)], ORDER, scale, (y1, hid1)
    )
    got_act0, got_fc2_1 = landed[0], landed[-1]
    ln_back = jnp.stack([gains[1][0], gains[0][1]])
    give = [(1, act1)] + ([(1, sum_fc1_1)] if fold else [])
    gin1, dh0, norms10, do0, da0, fc1_0, fc2_0, qp1, rel1, sums1, landed = back_chain(
        ndp, flags, act0, dh1, hid0, ln_back, dqkv1, o1, label_lanes,
        wq1, wp0, w10, w20, u0, g0, n2_0, n1_1, da1, dwall1, give,
    )
    got_act1, got_fc1_1, got_gin1 = landed[0], landed[len(landed) - 2], landed[-1]
    number = 2 * d + pair
    sums_rows = lax.dynamic_update_slice(
        jnp.zeros((2 * ndp, width), f32), sums1, (number, jnp.int32(width - 2 * local_width))
    )
    mine = lax.dynamic_index_in_dim(time_emb, pair, 0, keepdims=True).astype(f32)
    emb_rows = lax.dynamic_update_slice(jnp.zeros((2 * ndp, width), f32), mine, (number, jnp.int32(0)))
    smalls = jnp.concatenate(
        [jnp.zeros((2, width), f32), norms10[2:], norms10[:2], norms1, sums_rows, emb_rows], axis=0
    )
    give = [(1, qp1)] if fold else []
    (gin0, smalls, rel, q0, *more), landed = end_chain(
        ndp, flags, qkv0, do0, o0, lse0, mask_pad, x0, dh0, gains[0][0:1], label_lanes, smalls, rel1,
        walls[0], wq0, n1_0, da0, by_bits(fc1_0), fc2_0, give, ORDER, scale,
    )
    norms, sums_all = smalls[:8], smalls[8:]

    def total(mine, got):
        return jnp.where(home, mine, got[0]).astype(f32) + got[1].astype(f32)

    hidden_units = w_fc1.shape[2]
    wide = 3 * local_width
    if fold:
        got_qp1, got_gin0, got_f0, got_q0, got_fc2_0 = landed
        f0, sum_fc2_0 = more
        f0, qp1 = total(f0, got_f0), total(qp1, got_qp1)
        layer0 = (total(q0, got_q0), f0[:, hidden_units:], f0[:, :hidden_units], total(sum_fc2_0, got_fc2_0))
        layer1 = (qp1[:, :wide], qp1[:, wide:], total(sum_fc1_1, got_fc1_1), total(sum_fc2_1, got_fc2_1))
    else:
        (got_gin0,) = landed

        def summed(x, layer):
            x = reduced(whole(x))
            return total(x, (near_of(x, layer), far_of(x, layer)))

        f0, qp1 = summed(more[0], 0), summed(qp1, 1)
        layer0 = (summed(q0, 0), f0[:, hidden_units:], f0[:, :hidden_units], summed(fc2_0[1], 0))
        layer1 = (qp1[:, :wide], qp1[:, wide:], summed(fc1_1, 1), summed(fc2_1[1], 1))
    grad_q, grad_p, grad_fc1, grad_fc2 = [by_core(pair_of) for pair_of in zip(layer0, layer1)]

    def by_image(same, other):
        return jnp.stack([jnp.where(pair == 0, same, other), jnp.where(pair == 0, other, same)])[None]

    acts = by_image(
        jnp.where(home, by_core((act0, act1)), by_core((got_act0[0], got_act1[0]))), by_core((got_act0[1], got_act1[1]))
    )
    same = jnp.where(home, by_core((gin0, gin1)), by_core((got_gin0[0], got_gin1[0])).astype(f32))
    input_grads = by_image(same, by_core((got_gin0[1], got_gin1[1])).astype(f32))

    rel_grad = rel.reshape(heads, 4096)[:, :buckets]
    norms_mine = jnp.where(first, norms[:4], norms[4:]).reshape(2, 2, width)
    cols = width // (4 * ndp)
    norms_mine = lax.dynamic_slice_in_dim(norms_mine, (d * 4 + z) * cols, cols, 2)
    emb_of = sums_all[2 * ndp :]
    sums_mine = jnp.where(first, sums_all[: 2 * ndp, : 2 * local_width], sums_all[: 2 * ndp, 2 * local_width :])
    emb_mine = lax.dynamic_slice_in_dim(emb_of, d * (width // ndp), width // ndp, 1)
    grad_time = lax.dot_general(
        emb_mine, sums_mine, (((0,), (0,)), ((), ())), precision=lax.Precision.HIGHEST, preferred_element_type=f32
    ).reshape(width // ndp, 2, local_width)
    return (
        acts,
        input_grads,
        jnp.stack([grad_q[:, j * local_width : (j + 1) * local_width] for j in range(3)], axis=1)[None],
        grad_time[None],
        grad_p[None],
        grad_fc1[None],
        grad_fc2[None],
        rel_grad[None],
        norms_mine[:, 0][None],
        norms_mine[:, 1][None],
    )


def solution(mesh):
    return jax.shard_map(
        local,
        mesh=mesh,
        in_specs=(
            P("dp", "tensor", None),
            P("dp", None),
            P("dp"),
            P("dp", None),
            P(),
            P("section", None, None, "tensor"),
            P("section", None, None, "tensor"),
            P("section", None, "tensor"),
            P("section", None, "tensor"),
            P("section", None, "tensor"),
            P("section", "tensor", None),
            P("section", None, None),
            P("section", None, None),
            P("dp", "tensor", None),
        ),
        out_specs=(
            P("section", "dp", "tensor", None),
            P("section", "dp", "tensor", None),
            P("section", "dp", None, "tensor"),
            P("section", "dp", None, "tensor"),
            P("section", "dp", "tensor"),
            P("section", "dp", "tensor"),
            P("section", "dp", "tensor"),
            P("section", "tensor", None),
            P("section", None, ("dp", "tensor")),
            P("section", None, ("dp", "tensor")),
        ),
        check_vma=False,
    )
```

```python
import functools
import math

import jax
import jax.numpy as jnp
from jax import lax
from jax.experimental import pallas as pl
from jax.experimental.pallas import tpu as pltpu
from jax.sharding import PartitionSpec as P

LOG2E = 1.4426950408889634
HIGHEST = lax.Precision.HIGHEST
PLANE = 7 * 256
WALL = 8 * PLANE


def _labels_hi_lo(lab):
    hi = lax.shift_right_logical(lab, 6)
    lo = jnp.bitwise_and(lab, 63)
    iota = lax.broadcasted_iota(jnp.int32, (64, lab.shape[1]), 0)
    group = 2 * jnp.bitwise_and(iota, 31) + lax.shift_right_logical(iota, 5)
    return group == hi, jnp.where(iota == lo, 1.0, 0.0)


def build_wall(small, out_lab, lab, hi_mask, lo_hot, table, wall_ref):
    table = jnp.concatenate([table[:, :64], table[:, 64:]], axis=0)
    rows = lax.dot_general(table, lo_hot, (((1,), (0,)), ((), ())), precision=HIGHEST, preferred_element_type=jnp.float32)
    flat = jnp.sum(jnp.where(hi_mask, rows, 0.0), axis=0, keepdims=True) * LOG2E
    outside = jnp.sum(jnp.where(lab == out_lab, flat, 0.0), axis=1, keepdims=True)
    wide = jnp.broadcast_to(flat, (32, 4096))
    wide = pltpu.roll(wide, 4096 - 31, 1, stride=1, stride_axis=0)
    lane = lax.broadcasted_iota(jnp.int32, (32, 128), 1)
    tight = []
    for g in range(16):
        a = wide[:, 256 * g : 256 * g + 128]
        b = wide[:, 256 * g + 128 : 256 * g + 256]
        piece = jnp.where(lane < 32, a, pltpu.roll(a, 96, 1))
        other = jnp.where(lane < 96, pltpu.roll(b, 64, 1), pltpu.roll(b, 32, 1))
        tight.append(jnp.where(lane < 64, piece, other))
    w0 = jnp.concatenate(tight, axis=1)
    lane16 = lane[:16]
    tight16 = []
    for g in range(8):
        lo_v = w0[:16, 256 * g : 256 * g + 128]
        hi_v = w0[:16, 256 * g + 128 : 256 * g + 256]
        acc = lo_v
        for k in range(1, 4):
            acc = jnp.where(lane16 >= 16 * k, pltpu.roll(lo_v, 128 - 16 * k, 1), acc)
        for k in range(4):
            acc = jnp.where(lane16 >= 64 + 16 * k, pltpu.roll(hi_v, (64 - 16 * k) % 128, 1), acc)
        tight16.append(acc)
    w16 = jnp.concatenate(tight16, axis=1)
    beyond = jnp.broadcast_to(outside, (32, 768))
    tiny = small == 1
    for j in range(8):
        big = w0 if j == 7 else pltpu.roll(w0, 2048 - 32 * (7 - j), 1)
        inner = [pltpu.roll(w16, 1024 - 16 * (31 - 2 * j - k), 1)[:, :256] for k in range(2)]
        inner = jnp.concatenate(inner, axis=0)
        at = j * PLANE
        wall_ref[:, at : at + 768] = jnp.where(tiny, beyond, big[:, :768])
        wall_ref[:, at + 768 : at + 1024] = jnp.where(tiny, inner, big[:, 768:1024])
        wall_ref[:, at + 1024 : at + PLANE] = jnp.where(tiny, beyond, big[:, 1024:PLANE])


def wall_grad(small, out_lab, lab, hi_mask, lo_hot, acc_ref):
    tiny = small == 1
    w0 = jnp.zeros((32, 2048), jnp.float32)
    w16 = jnp.zeros((16, 1024), jnp.float32)
    beyond = jnp.zeros((32, 768), jnp.float32)
    for j in range(8):
        at = j * PLANE
        piece = jnp.concatenate([acc_ref[:, at : at + PLANE], jnp.zeros((32, 256), jnp.float32)], axis=1)
        w0 = w0 + (piece if j == 7 else pltpu.roll(piece, 32 * (7 - j), 1))
        beyond = beyond + acc_ref[:, at + 1024 : at + PLANE]
        for k in range(2):
            inner = acc_ref[16 * k : 16 * k + 16, at + 768 : at + 1024]
            inner = jnp.concatenate([inner, jnp.zeros((16, 768), jnp.float32)], axis=1)
            w16 = w16 + pltpu.roll(inner, 16 * (31 - 2 * j - k), 1)
    w0 = jnp.where(tiny, 0.0, w0)
    w16 = jnp.where(tiny, w16, 0.0)
    outside = jnp.sum(jnp.sum(jnp.where(tiny, beyond, 0.0), axis=0, keepdims=True), axis=1, keepdims=True)
    lane = lax.broadcasted_iota(jnp.int32, (32, 128), 1)
    lane16 = lane[:16]
    wide = []
    for g in range(32):
        src = w0[:, 128 * (g // 2) : 128 * (g // 2) + 128]
        k = 2 * (g % 2)
        first = src if k == 0 else pltpu.roll(src, 128 - 32 * k, 1)
        second = pltpu.roll(src, (64 - 32 * (k + 1)) % 128, 1)
        piece = jnp.where(lane < 32, first, jnp.where((lane >= 64) & (lane < 96), second, 0.0))
        src16 = w16[:, 128 * (g // 4) : 128 * (g // 4) + 128]
        k = 2 * (g % 4)
        first = src16 if k == 0 else pltpu.roll(src16, 128 - 16 * k, 1)
        second = pltpu.roll(src16, (64 - 16 * (k + 1)) % 128, 1)
        piece16 = jnp.where(lane16 < 16, first, jnp.where((lane16 >= 64) & (lane16 < 80), second, 0.0))
        wide.append(piece + jnp.concatenate([piece16, jnp.zeros((16, 128), jnp.float32)], axis=0))
    wide = jnp.concatenate(wide, axis=1)
    back = 31 - lax.broadcasted_iota(jnp.int32, (32, 4096), 0)
    for k in range(5):
        wide = jnp.where(jnp.bitwise_and(back, 1 << k) > 0, pltpu.roll(wide, 1 << k, 1), wide)
    flat = jnp.sum(wide, axis=0, keepdims=True)
    flat = flat + jnp.where(lab == out_lab, outside, 0.0)
    spread = jnp.where(hi_mask, jnp.broadcast_to(flat, (64, 4096)), 0.0)
    res = lax.dot_general(spread, lo_hot, (((1,), (1,)), ((), ())), precision=HIGHEST, preferred_element_type=jnp.float32)
    return jnp.concatenate([res[:32], res[32:]], axis=1)


def label_row(rel_index):
    side = 32
    a = rel_index[0, 1023].reshape(side, side)
    b = rel_index[0, 0].reshape(side, side)
    c = rel_index[0, 992].reshape(side, side)
    d = rel_index[0, 31].reshape(side, side)
    top = jnp.concatenate([a, c[:, 1:]], axis=1)
    low = jnp.concatenate([d[1:], b[1:, 1:]], axis=1)
    grid = jnp.flip(jnp.concatenate([top, low], axis=0), (0, 1))
    return jnp.pad(grid, ((0, 1), (0, 1)), constant_values=4095).reshape(1, 4096)


NT = (((1,), (1,)), ((), ()))
TN = (((0,), (0,)), ((), ()))
NN = (((1,), (0,)), ((), ()))
HD = 72
QB = 256


def dot(a, b, dims):
    return lax.dot_general(a, b, dims, preferred_element_type=jnp.float32)


def head_lanes(x, at, extra=None):
    rows = x.shape[0]
    part = x[:, at : at + HD]
    if extra is None:
        pad = jnp.zeros((rows, 128 - HD), x.dtype)
    else:
        pad = extra
    return jnp.concatenate([part, pad], axis=1)


def quarter(r, c, rel):
    return lax.rem(r + rel % 2, 2) + 2 * lax.rem(c + rel // 2, 2)


def strip_start(q_quarter, jj, kq):
    return pl.multiple_of(PLANE * jj + 256 * (q_quarter - kq + 3), 256)


def attn_block(q_quarter, key_quarters, scale, q_ref, kv_ref, k_extra, wall_ref, lse_ref, s_scr, p_scr):
    heads = wall_ref.shape[0]
    width = heads * HD
    nstrip = kv_ref.shape[0] // 32
    lane = lax.broadcasted_iota(jnp.int32, (QB, 128 - HD), 1)
    q_extra = jnp.where(lane == 0, 1.0, 0.0).astype(jnp.bfloat16)
    outs = []
    for h in range(heads):
        kh = head_lanes(kv_ref, width + HD * h, k_extra)
        qh = head_lanes(q_ref, HD * h, q_extra)
        vh = head_lanes(kv_ref, 2 * width + HD * h)
        s_scr[h % 2] = dot(kh, qh, NT)
        top = None
        for st in range(nstrip):
            start = strip_start(q_quarter, st % 8, key_quarters[st // 8])
            s = s_scr[h % 2, 32 * st : 32 * st + 32] * (scale * LOG2E) + wall_ref[h, :, pl.ds(start, QB)]
            s_scr[h % 2, 32 * st : 32 * st + 32] = s
            top = s if top is None else jnp.maximum(top, s)
        row_max = jnp.max(top, axis=0, keepdims=True)
        total = None
        for st in range(nstrip):
            p = jnp.exp2(s_scr[h % 2, 32 * st : 32 * st + 32] - row_max)
            p_scr[h % 2, 32 * st : 32 * st + 32] = p.astype(jnp.bfloat16)
            total = p if total is None else total + p
        row_sum = jnp.sum(total, axis=0, keepdims=True)
        o_t = dot(vh, p_scr[h % 2], TN) * (1.0 / row_sum)
        lse_ref[h : h + 1, :] = row_max + jnp.log2(row_sum)
        outs.append(o_t.T[:, :HD].astype(jnp.bfloat16))
    return jnp.concatenate(outs, axis=1)


EPSILON = 1e-05
NCH = 2
GELU_C = math.sqrt(2.0 / math.pi)


def normed(x):
    center = x - jnp.mean(x, axis=-1, keepdims=True)
    spread = jnp.mean(center * center, axis=-1, keepdims=True)
    r = lax.rsqrt(spread + EPSILON)
    return center * r, r


def norm_back(x, dy, gain):
    xhat, r = normed(x)
    dxhat = dy * gain
    dx = r * (
        dxhat
        - jnp.mean(dxhat, axis=-1, keepdims=True)
        - xhat * jnp.mean(dxhat * xhat, axis=-1, keepdims=True)
    )
    return dx, jnp.sum(dy * xhat, axis=0, keepdims=True), jnp.sum(dy, axis=0, keepdims=True)


def gelu_both(u):
    th = jnp.tanh(GELU_C * (u + 0.044715 * u * u * u))
    half = 0.5 * (1.0 + th)
    slope = half + 0.5 * u * (1.0 - th * th) * GELU_C * (1.0 + 3 * 0.044715 * u * u)
    return u * half, slope


class Links:
    def __init__(self, send_sem, recv_sem, bits=0):
        z, c = lax.axis_index("tensor"), lax.axis_index("section")
        self.z, self.c = z, c
        self.pair = z // 2
        self.r = lax.rem(z, 2)
        self.home = c == self.pair
        across = z + 2 - 4 * self.pair
        self.ids = {
            PARTNER: {"tensor": z + 1 - 2 * self.r},
            SIBLING: {"section": 1 - c},
            FAR: {"tensor": across, "section": self.pair},
            HOME: {"section": self.pair},
        }
        self.greet = [self.ids[PARTNER], self.ids[SIBLING]]
        self.dp_bit = []
        if bits:
            d = lax.axis_index("dp")
            for b in range(bits):
                bit = lax.rem(d // (1 << b), 2)
                self.dp_bit.append(bit)
                self.ids["dp", b] = {"dp": d + (1 - 2 * bit) * (1 << b)}
                self.greet.append(self.ids["dp", b])
            self.greet += [{"tensor": across}, {"tensor": across, "section": 1 - c}]
        self.ids[ACROSS] = {"tensor": across}
        for layer in range(2):
            self.ids["return", layer] = {"tensor": across, "section": layer}
        self.send_sem, self.recv_sem = send_sem, recv_sem
        self.used = 0
        self.started = []

    def enter(self):
        barrier = pltpu.get_barrier_semaphore()
        for where in self.greet:
            pl.semaphore_signal(barrier, inc=1, device_id=where, device_id_type=pl.DeviceIdType.MESH)
        pl.semaphore_wait(barrier, len(self.greet))

    def make(self, src, dst, to, cond=None, track=True):
        k = self.used
        self.used += 1
        assert k < self.send_sem.shape[0]
        copy = pltpu.make_async_remote_copy(
            src_ref=src,
            dst_ref=dst,
            send_sem=self.send_sem.at[k],
            recv_sem=self.recv_sem.at[k],
            device_id=self.ids[to],
            device_id_type=pl.DeviceIdType.MESH,
        )
        if track:
            self.started.append((copy, cond))
        return copy

    def send(self, src, dst, to, cond=None, track=True):
        copy = self.make(src, dst, to, cond, track)
        when(cond, copy.start)
        return copy

    def leave(self):
        for copy, cond in self.started:
            when(cond, copy.wait_send)


def when(cond, do):
    if cond is None:
        do()
    else:
        pl.when(cond)(lambda: do())


PARTNER, SIBLING, FAR, HOME, ACROSS = "partner", "sibling", "far", "home", "across"


class Spread:
    COPIES = 2

    def __init__(self, links, layer, src, out, sem):
        self.links, self.layer, self.src, self.out, self.sem = links, layer, src, out, sem

    def start(self):
        links = self.links
        mine = links.c == self.layer
        keeps = links.pair == self.layer
        self.local = pltpu.make_async_copy(self.src, self.out, self.sem)
        when(mine & keeps, self.local.start)
        self.near = links.send(self.src, self.out, HOME, mine & jnp.logical_not(keeps))
        self.far = links.send(self.src, self.out, FAR, mine)

    def done(self):
        links = self.links
        keeps = links.pair == self.layer
        when(links.home & keeps, self.local.wait)
        when(links.home & jnp.logical_not(keeps), self.near.wait_recv)
        when(jnp.logical_not(links.home), self.far.wait_recv)


def bits_region(links, gathered, cols=None):
    index = []
    for b in reversed(range(len(links.dp_bit))):
        index.append(pl.ds(0, 2) if b in gathered else links.dp_bit[b])
    return tuple(index) + (() if cols is None else (slice(None), cols))


class Deliver:
    COPIES = 2

    def __init__(self, links, layer, src, out, sem=None):
        self.links, self.layer, self.src, self.out, self.sem = links, layer, src, out, sem

    def start(self):
        links = self.links
        mine = links.c == self.layer
        keeps = links.pair == self.layer
        if self.sem is not None:
            self.local = pltpu.make_async_copy(self.src, self.out, self.sem)
            when(mine & keeps, self.local.start)
        at = bits_region(links, ())
        self.far = links.send(self.src.at[at], self.out.at[at], FAR, mine)
        self.near = links.send(self.src, self.out, HOME, mine & jnp.logical_not(keeps))

    def done(self):
        links = self.links
        keeps = links.pair == self.layer
        if self.sem is not None:
            when(links.home & keeps, self.local.wait)
        when(links.home & jnp.logical_not(keeps), self.near.wait_recv)
        when(jnp.logical_not(links.home), self.far.wait_recv)


class Exchange:
    def __init__(self, links, buf):
        self.links, self.buf = links, buf
        columns = buf.shape[-1]
        cut = columns // 256 * 128
        order = list(range(len(links.dp_bit)))
        self.halves = [(pl.ds(0, cut), order), (pl.ds(cut, columns - cut), order[::-1])]
        self.away = jnp.logical_not(links.home)
        self.last = None

    @staticmethod
    def copies(bits):
        return 2 * bits

    def step(self, s):
        self.done()
        self.last = []
        for cols, order in self.halves:
            at = bits_region(self.links, order[:s], cols)
            self.last.append(self.links.send(self.buf.at[at], self.buf.at[at], ("dp", order[s]), self.away))

    def done(self):
        for copy in self.last or ():
            when(self.away, copy.wait_recv)


class Part:
    def __init__(self, links, layer, own, got, dst, sem):
        at = bits_region(links, ())
        keeps = links.pair == layer
        self.ways = (
            (links.home & keeps, pltpu.make_async_copy(own, dst, sem)),
            (links.home & jnp.logical_not(keeps), pltpu.make_async_copy(got, dst, sem)),
            (jnp.logical_not(links.home), pltpu.make_async_copy(got.at[at], dst.at[at], sem)),
        )

    def start(self):
        for cond, copy in self.ways:
            when(cond, copy.start)
        return self

    def wait(self):
        for cond, copy in self.ways:
            when(cond, copy.wait)


class PartStore:
    def __init__(self, links, layer, src, dst, sem):
        at = bits_region(links, ())
        self.ways = (
            (links.home & (links.pair != layer), pltpu.make_async_copy(src, dst, sem)),
            (jnp.logical_not(links.home), pltpu.make_async_copy(src.at[at], dst.at[at], sem)),
        )

    def start(self):
        for cond, copy in self.ways:
            when(cond, copy.start)
        return self

    def wait(self):
        for cond, copy in self.ways:
            when(cond, copy.wait)


def chunk(i, rows):
    return pl.ds(i * (rows // NCH), rows // NCH)


class Scatter:
    COPIES = 3 * NCH

    def __init__(self, links, low, wide):
        self.links, self.low, self.wide = links, low, wide
        self.rows = low.shape[1]
        self.copies = {}

    def far(self, i, p2, p3):
        at = chunk(i, self.rows)
        self.low[0, at] = p3.astype(jnp.bfloat16)
        self.copies["a", i] = self.links.send(self.low.at[0, at], self.low.at[3, at], SIBLING)
        self.wide[0, at] = p2

    def middle(self, i):
        at = chunk(i, self.rows)
        self.copies["a", i].wait_recv()
        self.low[1, at] = (self.wide[0, at] + self.low[3, at].astype(jnp.float32)).astype(jnp.bfloat16)
        self.copies["z", i] = self.links.send(self.low.at[1, at], self.low.at[4, at], PARTNER)

    def near(self, i, p0, p1):
        at = chunk(i, self.rows)
        self.low[2, at] = p1.astype(jnp.bfloat16)
        self.copies["b", i] = self.links.send(self.low.at[2, at], self.low.at[5, at], SIBLING)
        self.wide[1, at] = p0

    def release(self):
        for copy in self.copies.values():
            copy.wait_send()
        self.links.started = [s for s in self.links.started if all(s[0] is not c for c in self.copies.values())]
        self.copies = {}

    def done(self, i):
        at = chunk(i, self.rows)
        self.copies["b", i].wait_recv()
        self.copies["z", i].wait_recv()
        return self.wide[1, at] + self.low[5, at].astype(jnp.float32) + self.low[4, at].astype(jnp.float32)


class Gather:
    COPIES = 3 * NCH

    def __init__(self, links, buf):
        self.links, self.buf = links, buf
        self.rows = buf.shape[1]
        self.copies = {}

    def send(self, i, x):
        at = chunk(i, self.rows)
        self.buf[0, at] = x
        self.copies["z", i] = self.links.send(self.buf.at[0, at], self.buf.at[2, at], PARTNER)
        self.copies["s", i] = self.links.send(self.buf.at[0, at], self.buf.at[1, at], SIBLING)

    def forward(self, i):
        at = chunk(i, self.rows)
        self.copies["z", i].wait_recv()
        self.copies["f", i] = self.links.send(self.buf.at[2, at], self.buf.at[3, at], SIBLING)

    def done(self, i):
        self.copies["s", i].wait_recv()
        self.copies["f", i].wait_recv()
        at = chunk(i, self.rows)
        n = self.rows // NCH
        return jnp.concatenate([self.buf[b, at] for b in range(4)], axis=0)


class DpReduce:
    COPIES = 4

    def __init__(self, links, buf, land0, land1=None, sent=None):
        self.links, self.buf, self.land0, self.land1, self.sent = links, buf, land0, land1, sent
        columns = buf.shape[-1]
        cut = columns // 256 * 128
        self.cols = (pl.ds(0, cut), pl.ds(cut, columns - cut))
        self.orders = ((0, 1), (1, 0))
        self.mine = links.dp_bit
        self.other = [1 - bit for bit in links.dp_bit]
        self.first, self.second = [], []
        for (b0, b1), h, cols in zip(self.orders, range(2), self.cols):
            at = self.place(h, self.other[b0], pl.ds(0, 2))
            self.first.append(links.make(buf.at[at + (slice(None), cols)], land0.at[:, :, cols], ("dp", b0)))
            if land1 is not None:
                self.second.append(links.make(sent.at[0, :, cols], land1.at[0, :, cols], ("dp", b1)))

    @staticmethod
    def scratch(n, columns):
        return [pltpu.VMEM((k, n, columns), jnp.bfloat16) for k in (2, 1, 1)]

    def place(self, h, first, second):
        return (second, first) if self.orders[h][0] == 0 else (first, second)

    def start(self):
        for copy in self.first:
            copy.start()

    def half(self, h, cols):
        b0, b1 = self.orders[h]
        self.first[h].wait_recv()
        sums = []
        for second in (self.other[b1], self.mine[b1]):
            own = self.buf[self.place(h, self.mine[b0], second) + (slice(None), cols)]
            sums.append(own.astype(jnp.float32) + self.land0[second, :, cols].astype(jnp.float32))
        return sums

    def split(self, sent, kept):
        for h, cols in enumerate(self.cols):
            sums = self.half(h, cols)
            sent[:, cols] = sums[0].astype(jnp.bfloat16)
            kept[:, cols] = sums[1].astype(jnp.bfloat16)

    def middle(self):
        for h, cols in enumerate(self.cols):
            b0, b1 = self.orders[h]
            sums = self.half(h, cols)
            self.sent[0, :, cols] = sums[0].astype(jnp.bfloat16)
            self.buf[self.place(h, self.mine[b0], self.mine[b1]) + (slice(None), cols)] = sums[1].astype(jnp.bfloat16)
            self.second[h].start()

    def done(self, out):
        for h, cols in enumerate(self.cols):
            self.second[h].wait_recv()
            b0, b1 = self.orders[h]
            own = self.buf[self.place(h, self.mine[b0], self.mine[b1]) + (slice(None), cols)]
            out[:, cols] = (own.astype(jnp.float32) + self.land1[0, :, cols].astype(jnp.float32)).astype(out.dtype)


class DpFinish:
    COPIES = 2

    def __init__(self, links, sent, kept, land):
        self.kept, self.land = kept, land
        columns = sent.shape[-1]
        cut = columns // 256 * 128
        self.cols = (pl.ds(0, cut), pl.ds(cut, columns - cut))
        self.copies = [
            links.make(sent.at[:, cols], land.at[:, cols], ("dp", b)) for cols, b in zip(self.cols, (1, 0))
        ]

    def start(self):
        for copy in self.copies:
            copy.start()

    def done(self, out):
        for copy, cols in zip(self.copies, self.cols):
            copy.wait_recv()
            out[:, cols] = (self.kept[:, cols].astype(jnp.float32) + self.land[:, cols].astype(jnp.float32)).astype(out.dtype)


class Return:
    COPIES = 2

    def __init__(self, links, layer, src, near, far):
        self.links, self.layer = links, layer
        self.home, self.away = links.home, jnp.logical_not(links.home)
        self.here = links.c == layer
        self.near_cond = self.home & jnp.logical_not(self.here)
        self.near = links.make(src, near, SIBLING, self.near_cond)
        self.far = links.make(src, far, ("return", layer), self.away)

    def start(self):
        when(self.near_cond, self.near.start)
        when(self.away, self.far.start)

    def done(self):
        when(self.here & self.away, self.near.wait_recv)
        when(self.here, self.far.wait_recv)


def start_load(src, dst, sem):
    copy = pltpu.make_async_copy(src, dst, sem)
    copy.start()
    return copy


def block_rows(ref, b, i, rows):
    n = rows // NCH
    return ref[pl.ds(b * rows + i * n, n)]


def put_rows(ref, value, i, rows):
    n = rows // NCH
    for b in range(4):
        ref[pl.ds(b * rows + i * n, n)] = value[b * n : (b + 1) * n]


def weight_grad(out, col, x, y):
    width = x.shape[1]
    step = 384
    for k in range(0, width, step):
        out[k : k + step, col : col + y.shape[1]] = dot(x[:, k : k + step], y, TN).astype(out.dtype)


def flat(ref):
    return ref[...].reshape(-1, ref.shape[-1])


def scatter_product(scatter, i, lhs, weight, rows):
    p = dot(jnp.concatenate([lhs(2), lhs(3)], axis=0), weight, NT)
    n = rows // NCH
    scatter.far(i, p[:n], p[n:])
    p = dot(jnp.concatenate([lhs(0), lhs(1)], axis=0), weight, NT)
    scatter.near(i, p[:n], p[n:])


def slab_grad(out, col, x, y):
    n = out.shape[2]
    width = x.shape[1]
    step = 384
    for k in range(0, width, step):
        res = dot(x[:, k : k + step], y, TN).astype(out.dtype)
        at = k
        while at < k + step:
            slab = at // n
            stop = min(k + step, (slab + 1) * n)
            out[slab // 2, slab % 2, at - slab * n : stop - slab * n, col : col + y.shape[1]] = res[at - k : stop - k]
            at = stop


def block_quarter(links, i):
    return lax.rem(links.r + i // 2, 2) + 2 * lax.rem(links.c + lax.rem(i, 2), 2)


def mid_kernel(order, scale, bits, x_ref, o_ref, ln_ref, cot_ref, live_ref, term_ref, mask_ref,
               wp_hbm, got1_hbm, got2_hbm, wall_hbm, own_q, own_p, own_1, own_2,
               hid_ref, act_ref, dy_ref, o1_ref, lse_ref,
               n2_hbm, u_hbm, g_hbm, n1_hbm, qkv_hbm, dm_hbm, w1_out, w2_out, next_q, next_p, next_1, next_2,
               wp, w1, w2, got_q, got_p, got_1, got_2, wall, u_buf, g_buf, qkv, gat1, gat2, gat3, low, wide, s_scr, p_scr,
               load_sem, store_sem, send_sem, recv_sem):
    rows, width = x_ref.shape
    n = rows // NCH
    links = Links(send_sem, recv_sem, bits)
    load_p = start_load(wp_hbm, wp, load_sem.at[0])
    load_1 = Part(links, 0, own_1, got1_hbm, w1, load_sem.at[1]).start()
    load_2 = Part(links, 0, own_2, got2_hbm, w2, load_sem.at[2]).start()
    load_w = start_load(wall_hbm, wall, load_sem.at[3])
    links.enter()
    ex1, ex2 = Exchange(links, w1), Exchange(links, w2)
    exq, exp = Exchange(links, got_q), Exchange(links, got_p)
    get_q, get_p = Deliver(links, 1, own_q, got_q, load_sem.at[4]), Deliver(links, 1, own_p, got_p, load_sem.at[5])
    get_1, get_2 = Deliver(links, 1, own_1, got_1), Deliver(links, 1, own_2, got_2)
    s1, s2 = Scatter(links, low, wide), Scatter(links, low, wide)
    g1, g2, g3 = Gather(links, gat1), Gather(links, gat2), Gather(links, gat3)
    load_p.wait()
    for i in range(NCH):
        scatter_product(s1, i, lambda b: block_rows(o_ref, b, i, rows), wp[...], rows)
    load_1.wait()
    ex1.step(0)
    load_2.wait()
    ex2.step(0)
    for i in range(NCH):
        s1.middle(i)
    for s in range(1, bits):
        ex1.step(s)
    get_q.start()
    get_p.start()
    for i in range(NCH):
        h = x_ref[chunk(i, rows)].astype(jnp.float32) + s1.done(i)
        hid_ref[chunk(i, rows)] = h
        g1.send(i, (normed(h)[0] * ln_ref[0:1] + ln_ref[1:2]).astype(jnp.bfloat16))
        if i == 0:
            for s in range(1, bits):
                ex2.step(s)
    s1.release()

    def mlp(i):
        u = dot(g1.done(i), w1[...].reshape(width, -1), NN)
        put_rows(u_buf, u.astype(jnp.bfloat16), i, rows)
        g = gelu_both(u)[0].astype(jnp.bfloat16)
        put_rows(g_buf, g, i, rows)
        if i == 0:
            ex2.done()
        scatter_product(s2, i, lambda b: g[b * n : (b + 1) * n], w2[...].reshape(width, -1), rows)

    g1.forward(0)
    ex1.done()
    for i in range(NCH):
        mlp(i)
        if i + 1 < NCH:
            g1.forward(i + 1)
        s2.middle(i)
    stores = [
        start_load(src, dst, store_sem.at[k])
        for k, (src, dst) in enumerate(((gat1, n2_hbm), (u_buf, u_hbm), (g_buf, g_hbm), (w1, w1_out), (w2, w2_out)))
    ]
    get_q.done()
    exq.step(0)
    for i in range(NCH):
        act = (hid_ref[chunk(i, rows)] + s2.done(i)).astype(jnp.bfloat16)
        act_ref[chunk(i, rows)] = act
        g2.send(i, (normed(act.astype(jnp.float32))[0] * ln_ref[2:3] + ln_ref[3:4]).astype(jnp.bfloat16))
    for i in range(NCH):
        at = chunk(i, rows)
        dy = cot_ref[at].astype(jnp.float32) * live_ref[at]
        dy_ref[at] = dy
        g3.send(i, dy.astype(jnp.bfloat16))
    get_1.start()
    get_2.start()
    for s in range(1, bits):
        exq.step(s)
    get_p.done()
    exp.step(0)
    for i in range(NCH):
        g2.forward(i)
    exq.done()
    weight = got_q[...].reshape(width, -1)
    for i in range(NCH):
        part = (dot(g2.done(i), weight, NN) + term_ref[0:1]).astype(jnp.bfloat16)
        put_rows(qkv, part, i, rows)
    for s in range(1, bits):
        exp.step(s)
    stores += [
        start_load(src, dst, store_sem.at[5 + k])
        for k, (src, dst) in enumerate(((gat2, n1_hbm), (qkv, qkv_hbm), (got_q, next_q)))
    ]
    load_w.wait()
    keys = [quarter(links.r, links.c, j) for j in order]

    def block(i, carry):
        at = pl.ds(pl.multiple_of(i * QB, QB), QB)
        o1_ref[at] = attn_block(
            block_quarter(links, i), keys, scale, qkv.at[at], qkv, mask_ref[...], wall, lse_ref.at[i], s_scr, p_scr
        )
        return carry

    lax.fori_loop(0, 4, block, 0)
    for i in range(NCH):
        g3.forward(i)
    exp.done()
    stores.append(start_load(got_p, next_p, store_sem.at[8]))
    for i in range(NCH):
        g3.copies["s", i].wait_recv()
        g3.copies["f", i].wait_recv()
    stores.append(start_load(gat3, dm_hbm, store_sem.at[9]))
    for k, (get, src, dst) in enumerate(((get_1, got_1, next_1), (get_2, got_2, next_2))):
        get.done()
        stores.append(PartStore(links, 1, src, dst, store_sem.at[10 + k]).start())
    links.leave()
    for store in stores:
        store.wait()


VM = pl.BlockSpec(memory_space=pltpu.VMEM)
HB = pl.BlockSpec(memory_space=pl.ANY)


def comm_scratch(copies):
    return [pltpu.SemaphoreType.DMA((copies,)), pltpu.SemaphoreType.DMA((copies,))]


def scatter_scratch(rows, width):
    return [pltpu.VMEM((6, rows, width), jnp.bfloat16), pltpu.VMEM((2, rows, width), jnp.float32)]


def params(ident):
    return pltpu.CompilerParams(collective_id=ident, has_side_effects=True, vmem_limit_bytes=52 << 20)


def mid_chain(x, o, ln, cot, live, term, mask_pad, wp, w1, w2, wall, own, order, scale):
    rows, width = x.shape
    hidden = w1.shape[-1]
    bits = w1.ndim - 2
    heads = wall.shape[0]
    wide = own[0].shape[-1]
    bf16, f32 = jnp.bfloat16, jnp.float32
    out = jax.ShapeDtypeStruct
    res = pl.pallas_call(
        functools.partial(mid_kernel, order, scale, bits),
        in_specs=[VM] * 7 + [HB] * 8,
        out_specs=[VM] * 5 + [HB] * 12,
        out_shape=[
            out((rows, width), f32),
            out((rows, width), bf16),
            out((rows, width), f32),
            out((4 * rows, heads * HD), bf16),
            out((4, heads, QB), f32),
            out((4, rows, width), bf16),
            out((4 * rows, hidden), bf16),
            out((4 * rows, hidden), bf16),
            out((4, rows, width), bf16),
            out((4 * rows, wide), bf16),
            out((4, rows, width), bf16),
        ]
        + [out(w.shape, bf16) for w in (w1, w2, *own)],
        scratch_shapes=[
            *[pltpu.VMEM(w.shape, bf16) for w in (wp, w1, w2, *own)],
            pltpu.VMEM(wall.shape, f32),
            pltpu.VMEM((4 * rows, hidden), bf16),
            pltpu.VMEM((4 * rows, hidden), bf16),
            pltpu.VMEM((4 * rows, wide), bf16),
            pltpu.VMEM((4, rows, width), bf16),
            pltpu.VMEM((4, rows, width), bf16),
            pltpu.VMEM((4, rows, width), bf16),
            *scatter_scratch(rows, width),
            pltpu.VMEM((2, 4 * rows, QB), f32),
            pltpu.VMEM((2, 4 * rows, QB), bf16),
            pltpu.SemaphoreType.DMA((6,)),
            pltpu.SemaphoreType.DMA((12,)),
            *comm_scratch(2 * Scatter.COPIES + 3 * Gather.COPIES + 4 * Deliver.COPIES + 4 * Exchange.copies(bits)),
        ],
        compiler_params=params(1),
        cost_estimate=pl.CostEstimate(flops=60 << 30, bytes_accessed=24 << 20, transcendentals=0),
    )(x, o, ln, cot, live, term, mask_pad, wp, w1, w2, wall, *own)
    hid, act, dy, o1, lse, n2, u, g, n1, qkv, dm = res[:11]
    rest = lambda v: v.reshape(4 * rows, width)
    return hid, act, dy, o1, lse, rest(n2), u, g, rest(n1), qkv, rest(dm), res[11:13], res[13:]


def turn_kernel(bits, fold, x_ref, o_ref, dy_ref, ln_ref, dm_hbm, wp_hbm, own1, own2, got1, got2,
                dh_ref, norm_ref, hid_ref, do_ref, fc2_sent, fc2_ref, y_hbm, da_hbm, fc1_hbm,
                wp, w1, w2, dm, g_buf, du_buf, y_buf, fc1, fc2, gat1, gat2, low, wide, *refs):
    lands, (load_sem, store_sem, send_sem, recv_sem) = refs[:-4], refs[-4:]
    rows, width = x_ref.shape
    n = rows // NCH
    links = Links(send_sem, recv_sem, bits)
    loads = [
        start_load(wp_hbm, wp, load_sem.at[0]),
        Part(links, 1, own1, got1, w1, load_sem.at[1]).start(),
        Part(links, 1, own2, got2, w2, load_sem.at[2]).start(),
        start_load(dm_hbm, dm, load_sem.at[3]),
    ]
    links.enter()
    ex1, ex2 = Exchange(links, w1), Exchange(links, w2)
    s1, s2 = Scatter(links, low, wide), Scatter(links, low, wide)
    g1, g2 = Gather(links, gat1), Gather(links, gat2)
    loads[0].wait()
    for i in range(NCH):
        scatter_product(s1, i, lambda b: block_rows(o_ref, b, i, rows), wp[...], rows)
    loads[1].wait()
    ex1.step(0)
    loads[2].wait()
    ex2.step(0)
    for i in range(NCH):
        s1.middle(i)
    for s in range(1, bits):
        ex1.step(s)
    for i in range(NCH):
        h = x_ref[chunk(i, rows)].astype(jnp.float32) + s1.done(i)
        hid_ref[chunk(i, rows)] = h
        g1.send(i, (normed(h)[0] * ln_ref[0:1] + ln_ref[1:2]).astype(jnp.bfloat16))
        if i == 0:
            for s in range(1, bits):
                ex2.step(s)
    s1.release()
    loads[3].wait()

    def mlp(i):
        u = dot(g1.done(i), w1[...].reshape(width, -1), NN)
        g, slope = gelu_both(u)
        put_rows(g_buf, g.astype(jnp.bfloat16), i, rows)
        dmi = jnp.concatenate([block_rows(dm, b, i, rows) for b in range(4)], axis=0)
        du = (dot(dmi, w2[...].reshape(width, -1), NN) * slope).astype(jnp.bfloat16)
        put_rows(du_buf, du, i, rows)
        scatter_product(s2, i, lambda b: du[b * n : (b + 1) * n], w1[...].reshape(width, -1), rows)

    g1.forward(0)
    ex1.done()
    ex2.done()
    for i in range(NCH):
        mlp(i)
        if i + 1 < NCH:
            g1.forward(i + 1)
        s2.middle(i)
    slab_grad(fc2, 0, dm[...], g_buf[...])
    if fold:
        reduce = DpReduce(links, fc2, lands[0])
        reduce.start()
    sums = None
    for i in range(NCH):
        at = chunk(i, rows)
        dx, dgain, dshift = norm_back(hid_ref[at], s2.done(i), ln_ref[0:1])
        dh = dy_ref[at] + dx
        dh_ref[at] = dh
        g2.send(i, dh.astype(jnp.bfloat16))
        both = jnp.concatenate([dgain, dshift], axis=0)
        sums = both if sums is None else sums + both
    norm_ref[...] = sums
    slab_grad(fc1, 0, flat(gat1), du_buf[...])
    stores = [start_load(fc1, fc1_hbm, store_sem.at[0])]
    g2.forward(0)
    for b in range(4):
        y = dot(g_buf[pl.ds(b * rows, rows)], w2[...].reshape(width, -1), NT)
        y_buf[pl.ds(b * rows, rows)] = y.astype(jnp.bfloat16)
    stores.append(start_load(y_buf, y_hbm, store_sem.at[1]))
    for i in range(1, NCH):
        g2.forward(i)
    for i in range(NCH):
        put_rows(do_ref, dot(g2.done(i), wp[...], NN).astype(jnp.bfloat16), i, rows)
    stores.append(start_load(gat2, da_hbm, store_sem.at[2]))
    if fold:
        reduce.split(fc2_sent, fc2_ref)
    else:
        fc2_ref[...] = fc2[...]
    links.leave()
    for store in stores:
        store.wait()


def turn_chain(ndp, x, o, dy, ln, dm, wp, own, got):
    rows, width = x.shape
    hidden = own[0].shape[-1]
    bits = own[0].ndim - 2
    fold = ndp == 4
    lw = wp.shape[1]
    n = width // 4
    bf16, f32 = jnp.bfloat16, jnp.float32
    out = jax.ShapeDtypeStruct
    res = pl.pallas_call(
        functools.partial(turn_kernel, bits, fold),
        in_specs=[VM, VM, VM, VM] + [HB] * 6,
        out_specs=[VM] * 6 + [HB] * 3,
        out_shape=[
            out((rows, width), f32),
            out((2, width), f32),
            out((rows, width), f32),
            out((4 * rows, lw), bf16),
            out((n, hidden), bf16),
            out((n, hidden) if fold else (2, 2, n, hidden), bf16),
            out((4 * rows, width), bf16),
            out((4, rows, width), bf16),
            out((2, 2, n, hidden), bf16),
        ],
        scratch_shapes=[
            pltpu.VMEM(wp.shape, bf16),
            pltpu.VMEM(own[0].shape, bf16),
            pltpu.VMEM(own[1].shape, bf16),
            pltpu.VMEM((4 * rows, width), bf16),
            pltpu.VMEM((4 * rows, hidden), bf16),
            pltpu.VMEM((4 * rows, hidden), bf16),
            pltpu.VMEM((4 * rows, width), bf16),
            pltpu.VMEM((2, 2, n, hidden), bf16),
            pltpu.VMEM((2, 2, n, hidden), bf16),
            pltpu.VMEM((4, rows, width), bf16),
            pltpu.VMEM((4, rows, width), bf16),
            *scatter_scratch(rows, width),
            *(DpReduce.scratch(n, hidden)[:1] if fold else []),
            pltpu.SemaphoreType.DMA((4,)),
            pltpu.SemaphoreType.DMA((3,)),
            *comm_scratch(2 * Scatter.COPIES + 2 * Gather.COPIES + 2 * Exchange.copies(bits) + DpReduce.COPIES),
        ],
        compiler_params=params(2),
        cost_estimate=pl.CostEstimate(flops=60 << 30, bytes_accessed=24 << 20, transcendentals=0),
    )(x, o, dy, ln, dm, wp, *own, *got)
    dh, norms, hid, do, sent, fc2, y, da, fc1 = res
    return dh, norms, y, hid, do, da.reshape(4 * rows, width), fc1, (sent, fc2)


def back_kernel(bits, fold, layers, flags_ref, x_ref, dh1_ref, hid_ref, ln_ref, dqkv_ref, o1_ref, lab_ref,
                wq_hbm, wp_hbm, w1_hbm, w2_hbm, u_hbm, g_hbm, n2_hbm, n1_hbm, da1_hbm, dwall_hbm, *refs):
    refs = list(refs)
    take = lambda k: [refs.pop(0) for _ in range(k)]
    blocks = take(len(layers))
    gin_ref, dh_ref, norm_ref, do_ref, da_hbm, fc1_hbm, fc2_sent, fc2_out, qp_out, rel_out, sum_out = take(11)
    places = [take(2) for _ in range(len(layers) + 1)]
    wq, wp, w1, w2, u_buf, g_buf, fc2, gqp, strips, gin_low, gat1, gat2, low, wide = take(14)
    if fold:
        lands_qp, lands_fc = take(3), take(1)
    load_sem, store_sem, send_sem, recv_sem = refs
    small, out_lab = flags_ref[0], flags_ref[1]
    rows, width = x_ref.shape
    n = rows // NCH
    hidden = w1.shape[1]
    heads = rel_out.shape[0]
    lw = o1_ref.shape[1]
    load = lambda k, src, dst: start_load(src, dst, load_sem.at[k])
    load_q, load_n1, load_da = load(0, wq_hbm, wq), load(1, n1_hbm, u_buf), load(2, da1_hbm, g_buf)
    load_1, load_2, load_p = load(3, w1_hbm, w1), load(4, w2_hbm, w2), load(5, wp_hbm, wp)
    load_strip = load(6, dwall_hbm.at[0], strips)
    links = Links(send_sem, recv_sem, bits)
    links.enter()
    blocks.append(gin_low)
    layers = layers + [1]
    returns = [Return(links, layer, src, *at) for layer, src, at in zip(layers, blocks, places)]
    for back in returns[:-1]:
        back.start()
    s1, s2 = Scatter(links, low, wide), Scatter(links, low, wide)
    g1, g2 = Gather(links, gat1), Gather(links, gat2)
    load_q.wait()
    for i in range(NCH):
        scatter_product(s1, i, lambda b: block_rows(dqkv_ref, b, i, rows), wq[...], rows)
        if i:
            s1.middle(i - 1)
    s1.middle(NCH - 1)
    load_n1.wait()
    slab_grad(gqp, 0, u_buf[...], dqkv_ref[...])
    load_da.wait()
    slab_grad(gqp, dqkv_ref.shape[1], g_buf[...], o1_ref[...])
    load_u, load_g = load(8, u_hbm, u_buf), load(9, g_hbm, g_buf)
    if fold:
        reduce = DpReduce(links, gqp, *lands_qp)
        reduce.start()
    cols = jnp.sum(dqkv_ref[...].astype(jnp.float32), axis=0, keepdims=True)
    sum_out[...] = jnp.concatenate([cols[:, :lw], cols[:, 2 * lw :]], axis=1)
    sums1 = None
    for i in range(NCH):
        at = chunk(i, rows)
        dx, dgain, dshift = norm_back(x_ref[at].astype(jnp.float32), s1.done(i), ln_ref[0:1])
        gin = dh1_ref[at] + dx
        gin_ref[at] = gin
        gin_low[at] = gin.astype(jnp.bfloat16)
        g1.send(i, gin_low[at])
        both = jnp.concatenate([dgain, dshift], axis=0)
        sums1 = both if sums1 is None else sums1 + both
    returns[-1].start()
    lab = lab_ref[...]
    hi_mask, lo_hot = _labels_hi_lo(lab)

    def bias_head(h, load_strip):
        load_strip.wait()
        rel_out[h] = wall_grad(small, out_lab, lab, hi_mask, lo_hot, strips)
        return load(6, dwall_hbm.at[h + 1], strips) if h + 1 < heads else None

    load_strip = bias_head(0, load_strip)
    load_strip = bias_head(1, load_strip)
    s1.release()
    load_1.wait()
    load_2.wait()
    load_u.wait()

    def mlp(i):
        dmi = g1.done(i)
        ui = jnp.concatenate([block_rows(u_buf, b, i, rows) for b in range(4)], axis=0).astype(jnp.float32)
        du = (dot(dmi, w2[...], NN) * gelu_both(ui)[1]).astype(jnp.bfloat16)
        put_rows(u_buf, du, i, rows)
        scatter_product(s2, i, lambda b: du[b * n : (b + 1) * n], w1[...], rows)

    g1.forward(0)
    for i in range(NCH):
        mlp(i)
        if i + 1 < NCH:
            g1.forward(i + 1)
        s2.middle(i)
    if fold:
        reduce.middle()
    load_g.wait()
    slab_grad(fc2, 0, flat(gat1), g_buf[...])
    if fold:
        reduce_2 = DpReduce(links, fc2, *lands_fc)
        reduce_2.start()
    load_n2 = load(10, n2_hbm, g_buf)
    sums2 = None
    for i in range(NCH):
        at = chunk(i, rows)
        dx, dgain, dshift = norm_back(hid_ref[at], s2.done(i), ln_ref[1:2])
        dh = gin_ref[at].astype(jnp.bfloat16).astype(jnp.float32) + dx
        dh_ref[at] = dh
        g2.send(i, dh.astype(jnp.bfloat16))
        both = jnp.concatenate([dgain, dshift], axis=0)
        sums2 = both if sums2 is None else sums2 + both
    norm_ref[...] = jnp.concatenate([sums1, sums2], axis=0)
    load_n2.wait()
    weight_grad(w2, 0, g_buf[...], u_buf[...])
    stores = [start_load(w2, fc1_hbm, store_sem.at[0])]
    load_strip = bias_head(2, load_strip)
    load_p.wait()
    g2.forward(0)
    bias_head(3, load_strip)
    for i in range(1, NCH):
        g2.forward(i)
    for i in range(NCH):
        put_rows(do_ref, dot(g2.done(i), wp[...], NN).astype(jnp.bfloat16), i, rows)
    stores.append(start_load(gat2, da_hbm, store_sem.at[2]))
    if fold:
        reduce.done(qp_out)
        reduce_2.split(fc2_sent, fc2_out)
    else:
        qp_out[...] = gqp[...]
        fc2_out[...] = fc2[...]
    for back in returns:
        back.done()
    links.leave()
    for store in stores:
        store.wait()


def back_chain(ndp, flags, x, dh1, hid, ln, dqkv, o1, lab, wq, wp, w1, w2, u, g, n2, n1, da1, dwall, returns):
    rows, width = x.shape
    hidden = w1.shape[1]
    lw = wp.shape[1]
    heads = dwall.shape[0]
    fold = ndp == 4
    bits = 2
    n = width // 4
    qp_cols = wq.shape[1] + lw
    bf16, f32 = jnp.bfloat16, jnp.float32
    out = jax.ShapeDtypeStruct
    layers = [layer for layer, _ in returns]
    blocks = [block for _, block in returns]
    copies = 2 * Scatter.COPIES + 2 * Gather.COPIES + 2 * DpReduce.COPIES + (len(layers) + 1) * Return.COPIES
    res = pl.pallas_call(
        functools.partial(back_kernel, bits, fold, layers),
        in_specs=[pl.BlockSpec(memory_space=pltpu.SMEM)] + [VM] * 7 + [HB] * (10 + len(blocks)),
        out_specs=[VM, VM, VM, VM, HB, HB, VM, VM, VM, VM, VM] + [HB] * (2 * len(blocks) + 2),
        out_shape=[
            out((rows, width), f32),
            out((rows, width), f32),
            out((4, width), f32),
            out((4 * rows, lw), bf16),
            out((4, rows, width), bf16),
            out((width, hidden), bf16),
            out((n, hidden), bf16),
            out((n, hidden) if fold else (2, 2, n, hidden), bf16),
            out((n, qp_cols) if fold else (2, 2, n, qp_cols), bf16),
            out((heads, 32, 128), f32),
            out((1, 2 * lw), f32),
        ]
        + [out(block.shape, block.dtype) for block in blocks for _ in range(2)]
        + [out((rows, width), bf16)] * 2,
        scratch_shapes=[
            pltpu.VMEM(wq.shape, bf16),
            pltpu.VMEM(wp.shape, bf16),
            pltpu.VMEM(w1.shape, bf16),
            pltpu.VMEM(w2.shape, bf16),
            pltpu.VMEM((4 * rows, hidden), bf16),
            pltpu.VMEM((4 * rows, hidden), bf16),
            pltpu.VMEM((2, 2, n, hidden), bf16),
            pltpu.VMEM((2, 2, n, qp_cols), bf16),
            pltpu.VMEM(dwall.shape[1:], f32),
            pltpu.VMEM((rows, width), bf16),
            pltpu.VMEM((4, rows, width), bf16),
            pltpu.VMEM((4, rows, width), bf16),
            *scatter_scratch(rows, width),
            *(DpReduce.scratch(n, qp_cols) + DpReduce.scratch(n, hidden)[:1] if fold else []),
            pltpu.SemaphoreType.DMA((11,)),
            pltpu.SemaphoreType.DMA((3,)),
            *comm_scratch(copies),
        ],
        compiler_params=params(3),
        cost_estimate=pl.CostEstimate(flops=60 << 30, bytes_accessed=24 << 20, transcendentals=0),
    )(flags, x, dh1, hid, ln, dqkv, o1, lab, wq, wp, w1, w2, u, g, n2, n1, da1, dwall, *blocks)
    gin, dh, norms, do, da, fc1, sent, fc2, qp, rel, sums = res[:11]
    got = [(res[11 + 2 * k], res[12 + 2 * k]) for k in range(len(layers) + 1)]
    return gin, dh, norms, do, da.reshape(4 * rows, width), fc1, (sent, fc2), qp, rel, sums, got


def start_kernel(order, scale, bits, flags_ref, x_hbm, cot_hbm, mask_ref, lab_ref, tab_hbm, pack_hbm,
                 wq_hbm, wp_hbm, w1_hbm, w2_hbm,
                 x_ref, cot_ref, pack_ref, lse_ref, o_ref, n1_hbm, qkv_hbm, wall0_hbm, wall1_hbm,
                 wq0_hbm, wp0_hbm, w10_hbm, w20_hbm,
                 tab, wq, wp, qkv, wall, gat1, s_scr, p_scr, load_sem, store_sem, send_sem, recv_sem):
    small, out_lab = flags_ref[0], flags_ref[1]
    rows, width = x_ref.shape
    wide = qkv.shape[1]
    heads = wall.shape[1]
    links = Links(send_sem, recv_sem, bits)
    pair, home = links.pair, links.home
    own_x = pltpu.make_async_copy(x_hbm.at[pair], x_ref, load_sem.at[0])
    when(home, own_x.start)
    own_cot = pltpu.make_async_copy(cot_hbm.at[pair], cot_ref, load_sem.at[7])
    when(home, own_cot.start)
    links.enter()
    packs = [Spread(links, l, pack_hbm, pack_ref.at[l], load_sem.at[1 + l]) for l in range(2)]
    tabs = [Spread(links, l, tab_hbm, tab.at[l], load_sem.at[3 + l]) for l in range(2)]
    tabs[0].start()
    packs[0].start()
    far_x = links.send(x_hbm.at[1 - pair], x_ref, FAR, home)
    tabs[1].start()
    packs[1].start()
    get_q = Deliver(links, 0, wq_hbm, wq, load_sem.at[5])
    get_p = Deliver(links, 0, wp_hbm, wp, load_sem.at[6])
    get_1, get_2 = Deliver(links, 0, w1_hbm, w10_hbm), Deliver(links, 0, w2_hbm, w20_hbm)
    ex_q, ex_p = Exchange(links, wq), Exchange(links, wp)
    get_q.start()
    lab = lab_ref[...]
    hi_mask, lo_hot = _labels_hi_lo(lab)

    def build(l):
        def one(h, carry):
            build_wall(small, out_lab, lab, hi_mask, lo_hot, tab[l, h], wall.at[l, h])
            return carry

        lax.fori_loop(0, heads, one, 0)

    tabs[0].done()
    build(0)
    stores = [start_load(wall.at[0], wall0_hbm, store_sem.at[0])]
    packs[0].done()
    when(home, own_x.wait)
    when(jnp.logical_not(home), far_x.wait_recv)
    g1 = Gather(links, gat1)
    for i in range(NCH):
        at = chunk(i, rows)
        xhat = normed(x_ref[at].astype(jnp.float32))[0]
        g1.send(i, (xhat * pack_ref[0, 0:1] + pack_ref[0, 2:3]).astype(jnp.bfloat16))
    get_p.start()
    get_1.start()
    get_2.start()
    far_cot = links.send(cot_hbm.at[1 - pair], cot_ref, FAR, home)
    tabs[1].done()
    build(1)
    stores.append(start_load(wall.at[1], wall1_hbm, store_sem.at[5]))
    get_q.done()
    ex_q.step(0)
    for i in range(NCH):
        g1.forward(i)
    for s in range(1, bits):
        ex_q.step(s)
    for i in range(NCH):
        g1.copies["s", i].wait_recv()
        g1.copies["f", i].wait_recv()
    stores.append(start_load(gat1, n1_hbm, store_sem.at[1]))
    packs[1].done()
    get_p.done()
    ex_q.done()
    ex_p.step(0)
    stores.append(start_load(wq, wq0_hbm, store_sem.at[2]))
    term = pack_ref[0, pl.ds(4 + pair, 1)][:, :wide]
    weight = wq[...].reshape(width, wide)
    for b in range(4):
        qkv[pl.ds(b * rows, rows)] = (dot(gat1[b], weight, NN) + term).astype(jnp.bfloat16)
    stores.append(start_load(qkv, qkv_hbm, store_sem.at[3]))
    for s in range(1, bits):
        ex_p.step(s)
    keys = [quarter(links.r, links.c, j) for j in order]

    def block(i, carry):
        at = pl.ds(pl.multiple_of(i * QB, QB), QB)
        qq = lax.rem(links.r + i // 2, 2) + 2 * lax.rem(links.c + lax.rem(i, 2), 2)
        o_ref[at] = attn_block(
            qq, keys, scale, qkv.at[at], qkv, mask_ref[...], wall.at[0], lse_ref.at[i], s_scr, p_scr
        )
        return carry

    lax.fori_loop(0, 4, block, 0)
    ex_p.done()
    stores.append(start_load(wp, wp0_hbm, store_sem.at[4]))
    get_1.done()
    get_2.done()
    when(home, own_cot.wait)
    when(jnp.logical_not(home), far_cot.wait_recv)
    links.leave()
    for store in stores:
        store.wait()


def start_chain(flags, x, cot, mask_pad, lab, table, pack, wq, wp, w1, w2, order, scale):
    bits = wq.ndim - 2
    _, rows, width = x.shape
    heads = table.shape[0]
    wide = wq.shape[-1]
    bf16, f32 = jnp.bfloat16, jnp.float32
    out = jax.ShapeDtypeStruct
    copies = 2 + 4 * Spread.COPIES + 4 * Deliver.COPIES + 2 * Exchange.copies(bits) + Gather.COPIES
    return pl.pallas_call(
        functools.partial(start_kernel, order, scale, bits),
        in_specs=[pl.BlockSpec(memory_space=pltpu.SMEM), HB, HB, VM, VM, HB, HB, HB, HB, HB, HB],
        out_specs=[VM] * 5 + [HB] * 8,
        out_shape=[
            out((rows, width), bf16),
            out((rows, width), bf16),
            out((2,) + pack.shape, f32),
            out((4, heads, QB), f32),
            out((4 * rows, heads * HD), bf16),
            out((4, rows, width), bf16),
            out((4 * rows, wide), bf16),
            out((heads, 32, WALL), f32),
            out((heads, 32, WALL), f32),
            *[out(w.shape, bf16) for w in (wq, wp, w1, w2)],
        ],
        scratch_shapes=[
            pltpu.VMEM((2,) + table.shape, f32),
            *[pltpu.VMEM(w.shape, bf16) for w in (wq, wp)],
            pltpu.VMEM((4 * rows, wide), bf16),
            pltpu.VMEM((2, heads, 32, WALL), f32),
            pltpu.VMEM((4, rows, width), bf16),
            pltpu.VMEM((2, 4 * rows, QB), f32),
            pltpu.VMEM((2, 4 * rows, QB), bf16),
            pltpu.SemaphoreType.DMA((8,)),
            pltpu.SemaphoreType.DMA((6,)),
            *comm_scratch(copies),
        ],
        compiler_params=params(0),
        cost_estimate=pl.CostEstimate(flops=80 << 30, bytes_accessed=24 << 20, transcendentals=0),
    )(flags, x, cot, mask_pad, lab, table, pack, wq, wp, w1, w2)


def attn_back(links, order, scale, qkv_ref, do_ref, o_ref, lse_ref, k_extra, wall, acc, p_scr, s_scr, dq_scr, dk_scr, dv_scr,
              dqkv_ref, event):
    heads = wall.shape[0]
    width = heads * HD
    total = qkv_ref.shape[0]
    keys = [quarter(links.r, links.c, j) for j in order]
    lane = lax.broadcasted_iota(jnp.int32, (QB, 128 - HD), 1)
    q_extra = jnp.where(lane == 0, 1.0, 0.0).astype(jnp.bfloat16)

    def block(i, carry):
        at = pl.ds(pl.multiple_of(i * QB, QB), QB)
        q_ref, d_ref, out_ref = qkv_ref.at[at], do_ref.at[at], o_ref.at[at]
        qq = block_quarter(links, i)
        dqs = []
        for h in range(heads):
            kh = head_lanes(qkv_ref, width + HD * h, k_extra)
            qh = head_lanes(q_ref, HD * h, q_extra)
            vh = head_lanes(qkv_ref, 2 * width + HD * h)
            doh = head_lanes(d_ref, HD * h)
            oh = head_lanes(out_ref, HD * h)
            inner = jnp.sum((doh.astype(jnp.float32) * oh.astype(jnp.float32)).T, axis=0, keepdims=True)
            lse = lse_ref[i, h : h + 1, :]
            for kb in range(total // 256):
                s_t = dot(kh[256 * kb : 256 * kb + 256], qh, NT)
                dp_t = dot(vh[256 * kb : 256 * kb + 256], doh, NT)
                for js in range(8):
                    st = 8 * kb + js
                    start = strip_start(qq, js, keys[kb])
                    s = s_t[32 * js : 32 * js + 32] * (scale * LOG2E) + wall[h, :, pl.ds(start, QB)]
                    p = jnp.exp2(s - lse)
                    ds = p * (dp_t[32 * js : 32 * js + 32] - inner)
                    p_scr[h % 2, 32 * st : 32 * st + 32] = p.astype(jnp.bfloat16)
                    s_scr[h % 2, 32 * st : 32 * st + 32] = ds.astype(jnp.bfloat16)
                    acc[h, :, pl.ds(start, QB)] += ds
            p_b, ds_b = p_scr[h % 2], s_scr[h % 2]
            dv_scr[h] += dot(p_b, doh, NN)
            dk_scr[h] += dot(ds_b, qh, NN)
            dq_t = dot(kh, ds_b, TN) * scale
            dqs.append(dq_t.T[:, :HD].astype(jnp.bfloat16))
        dq_scr[at] = jnp.concatenate(dqs, axis=1)
        event(i)
        return carry

    lax.fori_loop(0, total // QB, block, 0)
    parts = [dq_scr[...]]
    parts += [(dk_scr[h, :, :HD] * scale).astype(jnp.bfloat16) for h in range(heads)]
    parts += [dv_scr[h, :, :HD].astype(jnp.bfloat16) for h in range(heads)]
    dqkv_ref[...] = jnp.concatenate(parts, axis=1)


def bwd_kernel(order, scale, bits, fold, layers, summed, qkv_ref, do_ref, o_ref, lse_ref, mask_ref, wall_hbm, gfc_hbm, *refs):
    refs = list(refs)
    take = lambda k: [refs.pop(0) for _ in range(k)]
    blocks = take(len(layers))
    sent_2, kept_2 = take(2) if fold else (None, None)
    y_ref, hid_ref = take(2) if summed else (None, None)
    dqkv_ref, acc_hbm = take(2)
    fc_out, fin_out = take(2) if fold else (None, None)
    places = [take(2) for _ in range(len(layers) + (1 if fold else 0))]
    (act_ref,) = take(1) if summed else (None,)
    wall, acc, p_scr, s_scr, dq_scr, dk_scr, dv_scr = take(7)
    if fold:
        gfc, land0, land1, sent, land_2 = take(5)
    if summed:
        (low,) = take(1)
    load_sem, store_sem, send_sem, recv_sem = refs
    loads = [start_load(wall_hbm, wall, load_sem.at[0])]
    if fold:
        loads.append(start_load(gfc_hbm, gfc, load_sem.at[1]))
    links = Links(send_sem, recv_sem, bits)
    links.enter()
    returns = [Return(links, layer, src, *at) for layer, src, at in zip(layers, blocks, places)]
    if fold:
        finish = DpFinish(links, sent_2, kept_2, land_2)
        finish.start()
        last = Return(links, 1, fin_out, *places[-1])
        reduce = DpReduce(links, gfc, land0, land1, sent)
    if summed:
        rows = hid_ref.shape[0]
        part = lambda b: y_ref.at[pl.ds(b * rows, rows)]
        to_sib = links.make(part(3), low.at[0], SIBLING)
        near = links.make(part(1), low.at[1], SIBLING)
        to_partner = links.make(low.at[2], low.at[3], PARTNER)
        to_sib.start()
        near.start()
    acc[...] = jnp.zeros_like(acc)
    dk_scr[...] = jnp.zeros_like(dk_scr)
    dv_scr[...] = jnp.zeros_like(dv_scr)
    if fold:
        loads[1].wait()
        reduce.start()
    if summed:
        to_sib.wait_recv()
        low[2] = (part(2)[...].astype(jnp.float32) + low[0].astype(jnp.float32)).astype(jnp.bfloat16)
        to_partner.start()
    for back in returns:
        back.start()
    loads[0].wait()

    def finished():
        finish.done(fin_out)
        last.start()

    def event(i):
        if fold:
            pl.when(i == 0)(finished)

    attn_back(
        links, order, scale, qkv_ref, do_ref, o_ref, lse_ref, mask_ref[...], wall, acc, p_scr, s_scr, dq_scr, dk_scr, dv_scr,
        dqkv_ref, event,
    )
    stores = [start_load(acc, acc_hbm, store_sem.at[0])]
    if fold:
        reduce.middle()
    if summed:
        near.wait_recv()
        to_partner.wait_recv()
        act = hid_ref[...] + part(0)[...].astype(jnp.float32) + low[1].astype(jnp.float32) + low[3].astype(jnp.float32)
        act_ref[...] = act.astype(jnp.bfloat16)
    if fold:
        reduce.done(fc_out)
        last.done()
    for back in returns:
        back.done()
    links.leave()
    for store in stores:
        store.wait()


def bwd_chain(ident, fold, qkv, do, o, lse, mask_pad, wall, gfc, finish, returns, order, scale, summed=None):
    total, wide = qkv.shape
    heads = wall.shape[0]
    bits = 2
    n, columns = gfc.shape[2:]
    bf16, f32 = jnp.bfloat16, jnp.float32
    out = jax.ShapeDtypeStruct
    layers = [layer for layer, _ in returns]
    blocks = [block for _, block in returns]
    outs = [out((total, wide), bf16), out(wall.shape, f32)]
    specs = [VM, HB]
    if fold:
        outs += [out((n, columns), bf16)] * 2
        specs += [VM] * 2
    for block in blocks + ([finish[0]] if fold else []):
        outs += [out(block.shape, block.dtype)] * 2
        specs += [HB] * 2
    scratch = [
        pltpu.VMEM(wall.shape, f32),
        pltpu.VMEM(wall.shape, f32),
        pltpu.VMEM((2, total, QB), bf16),
        pltpu.VMEM((2, total, QB), bf16),
        pltpu.VMEM((total, heads * HD), bf16),
        pltpu.VMEM((heads, total, 128), f32),
        pltpu.VMEM((heads, total, 128), f32),
    ]
    if fold:
        scratch += [pltpu.VMEM(gfc.shape, bf16), *DpReduce.scratch(n, columns), pltpu.VMEM((n, columns), bf16)]
    more = list(finish) if fold else []
    if summed is not None:
        more += list(summed)
        rows, width = summed[1].shape
        outs.append(out((rows, width), bf16))
        specs.append(VM)
        scratch.append(pltpu.VMEM((4, rows, width), bf16))
    copies = len(layers) * Return.COPIES + (DpReduce.COPIES + DpFinish.COPIES + Return.COPIES if fold else 0) + (3 if summed else 0)
    res = pl.pallas_call(
        functools.partial(bwd_kernel, order, scale, bits, fold, layers, summed is not None),
        in_specs=[VM] * 5 + [HB] * 2 + [VM] * (len(blocks) + len(more)),
        out_specs=specs,
        out_shape=outs,
        scratch_shapes=scratch
        + [pltpu.SemaphoreType.DMA((2,)), pltpu.SemaphoreType.DMA((1,)), *comm_scratch(max(copies, 1))],
        compiler_params=params(ident),
        cost_estimate=pl.CostEstimate(flops=24 << 30, bytes_accessed=20 << 20, transcendentals=0),
    )(qkv, do, o, lse, mask_pad, wall, gfc, *blocks, *more)
    res = list(res)
    dqkv, acc = res[:2]
    res = res[2:]
    fc, fin = (res.pop(0), res.pop(0)) if fold else (None, None)
    got = [(res[2 * k], res[2 * k + 1]) for k in range(len(layers) + (1 if fold else 0))]
    act = res[-1] if summed is not None else None
    return dqkv, acc, fc, fin, got, act


class SumHops:
    def __init__(self, links, buf, land, hops):
        self.links, self.buf, self.land, self.hops, self.k = links, buf, land, hops, 0

    def send(self):
        if self.k < len(self.hops):
            self.copy = self.links.send(self.buf, self.land.at[self.k], self.hops[self.k], track=False)

    def take(self):
        self.copy.wait_recv()
        self.copy.wait_send()
        self.buf[...] = self.buf[...] + self.land[self.k]
        self.k += 1
        self.send()


def end_kernel(order, scale, bits, fold, layers, flags_ref, qkv_ref, do_ref, o_ref, lse_ref, mask_ref,
               x_ref, dh_ref, ln_ref, lab_ref, small_ref, rel1_ref,
               wall_hbm, wq_hbm, n1_hbm, da_hbm, fc_hbm, *refs):
    refs = list(refs)
    take = lambda k: [refs.pop(0) for _ in range(k)]
    blocks = take(len(layers))
    sent_2, kept_2 = take(2) if fold else (None, None)
    gin_ref, small_out, rel_out, q_out = take(4)
    fc_out, fin_out = take(2) if fold else (None, None)
    (all_fc,) = (None,) if fold else take(1)
    places = [take(2) for _ in range(len(layers) + (4 if fold else 1))]
    acc, dqkv_ref, gq, fc, gin_low, low1 = take(6)
    rel, rel_land, rel_near, smalls, small_land, norm_land, small_near = take(7)
    if fold:
        lands_q, lands_f, (land_2,) = take(3), take(3), take(1)
    load_sem, send_sem, recv_sem = refs
    small, out_lab = flags_ref[0], flags_ref[1]
    rows, width = x_ref.shape
    heads = rel.shape[1]
    hidden = fc_hbm.shape[-1]
    load_f = start_load(fc_hbm, fc.at[:, :, :, pl.ds(0, hidden)], load_sem.at[1])
    links = Links(send_sem, recv_sem, bits)
    home, away = links.home, jnp.logical_not(links.home)
    links.enter()
    give = list(zip(layers, blocks)) + [(0, gin_low)] + ([(0, fc_out), (0, q_out), (0, fin_out)] if fold else [])
    returns = [Return(links, layer, src, *at) for (layer, src), at in zip(give, places)]
    early = len(layers)
    for back in returns[:early]:
        back.start()
    if fold:
        finish = DpFinish(links, sent_2, kept_2, land_2)
        finish.start()
        reduce_f = DpReduce(links, fc, *lands_f)
        reduce_q = DpReduce(links, gq, *lands_q)

    def proj_grad(rows_buf):
        start_load(da_hbm, rows_buf, load_sem.at[4]).wait()
        slab_grad(fc, hidden, rows_buf[...], o_ref[...])

    pl.run_scoped(proj_grad, pltpu.VMEM(da_hbm.shape, jnp.bfloat16))
    load_f.wait()
    if fold:
        reduce_f.start()
    acc[...] = jnp.zeros_like(acc)

    def finished():
        finish.done(fin_out)
        returns[early + 3].start()

    def event(i):
        if fold:
            pl.when(i == 0)(finished)

    def attention(wall, p_scr, s_scr, dq_scr, dk_scr, dv_scr):
        load_w = start_load(wall_hbm, wall, load_sem.at[0])
        dk_scr[...] = jnp.zeros_like(dk_scr)
        dv_scr[...] = jnp.zeros_like(dv_scr)
        load_w.wait()
        attn_back(
            links, order, scale, qkv_ref, do_ref, o_ref, lse_ref, mask_ref[...], wall, acc, p_scr, s_scr, dq_scr, dk_scr,
            dv_scr, dqkv_ref, event,
        )

    total = qkv_ref.shape[0]
    vmem, bf16, f32 = pltpu.VMEM, jnp.bfloat16, jnp.float32
    pl.run_scoped(
        attention,
        vmem(wall_hbm.shape, f32),
        vmem((2, total, QB), bf16),
        vmem((2, total, QB), bf16),
        vmem((total, heads * HD), bf16),
        vmem((heads, total, 128), f32),
        vmem((heads, total, 128), f32),
    )
    lw = o_ref.shape[1]

    def rest(wq, rows_buf, wide1):
        s1 = Scatter(links, low1, wide1)
        load_q = start_load(wq_hbm, wq, load_sem.at[2])
        load_n = start_load(n1_hbm, rows_buf, load_sem.at[3])
        load_q.wait()
        for i in range(NCH):
            scatter_product(s1, i, lambda b: block_rows(dqkv_ref, b, i, rows), wq[...], rows)
            if i:
                s1.middle(i - 1)
        s1.middle(NCH - 1)
        load_n.wait()
        slab_grad(gq, 0, rows_buf[...], dqkv_ref[...])
        if fold:
            reduce_f.middle()
            reduce_q.start()
        cols = jnp.sum(dqkv_ref[...].astype(jnp.float32), axis=0, keepdims=True)
        mine = jnp.concatenate([cols[:, :lw], cols[:, 2 * lw :]], axis=1)
        images = (smalls.shape[0] - 8) // 2
        number = 2 * lax.axis_index("dp") + links.pair
        here = lax.broadcasted_iota(jnp.int32, (images, 2 * lw), 0) == number
        smalls[...] = small_ref[...]
        smalls[8 : 8 + images, 0 : 2 * lw] = jnp.where(here, jnp.broadcast_to(mine, (images, 2 * lw)), 0.0)
        lab = lab_ref[...]
        hi_mask, lo_hot = _labels_hi_lo(lab)
        rel[1] = rel1_ref[...]

        def heads_of(a, b):
            def one(h, carry):
                rel[0, h] = wall_grad(small, out_lab, lab, hi_mask, lo_hot, acc.at[h])
                return carry

            lax.fori_loop(a, b, one, 0)

        hops = [ACROSS] + [("dp", b) for b in range(bits)]
        small_hops = SumHops(links, smalls, small_land, hops)
        rel_hops = SumHops(links, rel, rel_land, hops)
        heads_of(0, heads // 2)
        if fold:
            reduce_f.done(fc_out)
            returns[early + 1].start()
        late = None
        for i in range(NCH):
            at = chunk(i, rows)
            dx, dgain, dshift = norm_back(x_ref[at].astype(jnp.float32), s1.done(i), ln_ref[0:1])
            gin = dh_ref[at] + dx
            gin_ref[at] = gin
            gin_low[at] = gin.astype(jnp.bfloat16)
            both = jnp.concatenate([dgain, dshift], axis=0)
            late = both if late is None else late + both
        smalls[0:2] = late
        small_hops.send()
        heads_of(heads // 2, heads)
        rel_hops.send()
        returns[early].start()
        if fold:
            reduce_q.middle()
            reduce_q.done(q_out)
            returns[early + 2].start()
        else:
            q_out[...] = gq[...]
            all_fc[...] = fc[...]
        for _ in range(bits + 1):
            small_hops.take()
            rel_hops.take()
        images_at = pl.ds(8, smalls.shape[0] - 8)
        rel_copy = links.send(rel.at[1 - links.c], rel_near, SIBLING, home)
        small_copy = links.send(smalls.at[images_at], small_near, SIBLING, home)
        norm_hops = SumHops(links, smalls.at[pl.ds(0, 8)], norm_land, [PARTNER, SIBLING])
        norm_hops.send()

        @pl.when(home)
        def _():
            rel_out[...] = rel[links.c]
            small_out[images_at] = smalls[images_at]

        @pl.when(away)
        def _():
            rel_copy.wait_recv()
            small_copy.wait_recv()
            rel_out[...] = rel_near[...]
            small_out[images_at] = small_near[...]

        norm_hops.take()
        norm_hops.take()
        small_out[0:8] = smalls[0:8]
        for back in returns:
            back.done()
        links.leave()

    pl.run_scoped(rest, vmem(wq_hbm.shape, bf16), vmem(n1_hbm.shape, bf16), vmem((2, rows, width), f32))


def end_chain(ndp, flags, qkv, do, o, lse, mask_pad, x, dh, ln, lab, smalls, rel1, wall, wq, n1, da, fc, finish, returns, order, scale):
    rows, width = x.shape
    heads = wall.shape[0]
    total, wide = qkv.shape
    bits = ndp.bit_length() - 1
    fold = bits == 2
    n, hidden = fc.shape[2:]
    fc_cols = hidden + o.shape[1]
    count = smalls.shape[0]
    hops = bits + 1
    bf16, f32 = jnp.bfloat16, jnp.float32
    out = jax.ShapeDtypeStruct
    layers = [layer for layer, _ in returns]
    blocks = [block for _, block in returns]
    landed = [out(block.shape, bf16) for block in blocks] + [out((rows, width), bf16)]
    outs = [
        out((rows, width), f32),
        out((count, width), f32),
        out((heads, 32, 128), f32),
        out((n, wide) if fold else (2, 2, n, wide), bf16),
    ]
    if fold:
        outs += [out((n, fc_cols), bf16), out((n, hidden), bf16)]
        landed += [out((n, fc_cols), bf16), out((n, wide), bf16), out((n, hidden), bf16)]
        blocks += list(finish)
    else:
        outs.append(out((2, 2, n, fc_cols), bf16))
    copies = Scatter.COPIES + len(landed) * Return.COPIES + 2 * DpReduce.COPIES + DpFinish.COPIES + 2 * hops + 4
    res = pl.pallas_call(
        functools.partial(end_kernel, order, scale, bits, fold, layers),
        in_specs=[pl.BlockSpec(memory_space=pltpu.SMEM)] + [VM] * 11 + [HB] * (5 + len(layers)) + ([VM] * 2 if fold else []),
        out_specs=[VM] * len(outs) + [HB] * (2 * len(landed)),
        out_shape=outs + [shape for shape in landed for _ in range(2)],
        scratch_shapes=[
            pltpu.VMEM(wall.shape, f32),
            pltpu.VMEM((total, wide), bf16),
            pltpu.VMEM((2, 2, n, wide), bf16),
            pltpu.VMEM((2, 2, n, fc_cols), bf16),
            pltpu.VMEM((rows, width), bf16),
            pltpu.VMEM((6, rows, width), bf16),
            pltpu.VMEM((2, heads, 32, 128), f32),
            pltpu.VMEM((hops, 2, heads, 32, 128), f32),
            pltpu.VMEM((heads, 32, 128), f32),
            pltpu.VMEM((count, width), f32),
            pltpu.VMEM((hops, count, width), f32),
            pltpu.VMEM((2, 8, width), f32),
            pltpu.VMEM((count - 8, width), f32),
            *(
                DpReduce.scratch(n, wide) + DpReduce.scratch(n, fc_cols) + [pltpu.VMEM((n, hidden), bf16)]
                if fold
                else []
            ),
            pltpu.SemaphoreType.DMA((5,)),
            *comm_scratch(copies),
        ],
        compiler_params=params(4),
        cost_estimate=pl.CostEstimate(flops=90 << 30, bytes_accessed=24 << 20, transcendentals=0),
    )(flags, qkv, do, o, lse, mask_pad, x, dh, ln, lab, smalls, rel1, wall, wq, n1, da, fc, *blocks)
    res = list(res)
    got = [(res[len(outs) + 2 * k], res[len(outs) + 2 * k + 1]) for k in range(len(landed))]
    return res[: len(outs)], got


AXES = ("dp", "section", "tensor")
ORDER = (0, 2, 1, 3)


def local(
    inputs,
    time_emb,
    lengths,
    key_mask,
    rel_index,
    w_qkv,
    w_time,
    w_proj,
    w_fc1,
    w_fc2,
    rel_table,
    norm_gains,
    norm_biases,
    cotangent,
):
    bf16, f32 = jnp.bfloat16, jnp.float32
    _, rows, width = inputs.shape
    seq_len = key_mask.shape[1]
    heads, buckets = rel_table.shape[1:]
    local_width = w_proj.shape[2]
    scale = 1.0 / math.sqrt(HD)
    ndp = lax.axis_size("dp")
    d = lax.axis_index("dp")
    c = lax.axis_index("section")
    z = lax.axis_index("tensor")
    pair = z // 2
    home = c == pair
    first = c == 0
    t = z % 2 + 2 * c

    def move(x, to, name="move"):
        pairs = []
        for dd in range(ndp):
            for cc in range(2):
                for zz in range(4):
                    dst = to(dd, cc, zz)
                    if dst is not None:
                        pairs.append(((dd * 2 + cc) * 4 + zz, (dst[0] * 2 + dst[1]) * 4 + dst[2]))
        with jax.named_scope(name):
            return lax.ppermute(x, AXES, pairs)

    def partner(x):
        return move(x, lambda dd, cc, zz: (dd, cc, zz ^ 1), "partner")

    def sibling(x):
        return move(x, lambda dd, cc, zz: (dd, 1 - cc, zz), "sibling")

    def across(x):
        return move(x, lambda dd, cc, zz: (dd, cc, zz ^ 2), "across")

    def dp_scatter(x, bits):
        n = x.shape[1]
        left = sorted(bits, reverse=True)
        v = x.reshape((2,) * len(left) + (-1, n))
        for b in bits:
            axis = left.index(b)
            left.remove(b)
            mine = (d >> b) & 1
            send = lax.dynamic_index_in_dim(v, 1 - mine, axis, keepdims=False)
            keep = lax.dynamic_index_in_dim(v, mine, axis, keepdims=False)
            got = move(send, lambda dd, cc, zz, b=b: (dd ^ (1 << b), cc, zz), "g_dp")
            v = keep.astype(f32) + got.astype(f32)
            if left:
                v = v.astype(bf16)
        return v

    def by_bits(w):
        return w.reshape(2, 2, -1, w.shape[-1])

    table = jnp.pad(rel_table[0], ((0, 0), (0, 4096 - buckets))).reshape(heads, 32, 128)
    time_all = jnp.einsum("id,dcn->icn", time_emb, w_time[0], preferred_element_type=f32)
    gap = jnp.zeros((2, local_width), f32)
    time_rows = jnp.concatenate([time_all[:, 0], gap, time_all[:, 1], gap], axis=1)
    small_pack = jnp.concatenate([norm_gains[0], norm_biases[0], time_rows, jnp.zeros((2, width), f32)], axis=0)
    own = [by_bits(w) for w in (jnp.concatenate([w_qkv[0, :, j] for j in range(3)], axis=1), w_proj[0], w_fc1[0], w_fc2[0])]
    label_lanes = label_row(rel_index)
    out_label = rel_index[1, seq_len - 1, seq_len - 1].reshape(1)

    length = lax.dynamic_index_in_dim(lengths, pair, 0, keepdims=False)
    small = (length < seq_len).astype(jnp.int32)
    scalars = jnp.stack([z % 2, c] + [jnp.int32(j) for j in ORDER])
    flags = jnp.concatenate([small.reshape(1), out_label])
    mask = lax.dynamic_index_in_dim(key_mask, pair, 0, keepdims=False).reshape(4, rows)
    mask = jnp.concatenate([lax.dynamic_index_in_dim(mask, t ^ j, 0, keepdims=False) for j in ORDER])
    lane = jnp.arange(128 - HD)[None, :]
    mask_pad = jnp.where((lane == 0) & (mask[:, None] == 0), -1e30, 0.0).astype(bf16)

    def gather_rows(x):
        far = partner(x)
        near = sibling(x)
        return jnp.concatenate([x, near, far, sibling(far)], axis=0)

    def scatter_rows(far, near):
        a = sibling(far[rows:].astype(bf16))
        rz = partner((far[:rows] + a.astype(f32)).astype(bf16))
        rs = sibling(near[rows:].astype(bf16))
        return near[:rows] + rs.astype(f32) + rz.astype(f32)

    def times_t(x, w):
        return lax.dot_general(x, w, (((1,), (1,)), ((), ())), preferred_element_type=f32)

    def grad_of(x, y):
        return lax.dot_general(x, y, (((0,), (0,)), ((), ())), preferred_element_type=f32).astype(bf16)

    half = 2 * rows

    def reduced(x):
        with jax.named_scope("g_sum"):
            return lax.psum_scatter(x, "dp", scatter_dimension=0, tiled=True)

    def reduced_late(x):
        if ndp & (ndp - 1):
            return reduced(x)
        bits = list(range(ndp.bit_length() - 1))
        cut = 4 * 128
        return jnp.concatenate(
            [dp_scatter(x[:, :cut], bits), dp_scatter(x[:, cut:], bits[::-1])], axis=1
        ).astype(bf16)

    def column_sums(dqkv):
        sums = jnp.sum(dqkv.astype(f32), axis=0)
        return jnp.concatenate([sums[:local_width], sums[2 * local_width :]])

    def tie(*values):
        return lax.optimization_barrier(values)

    def by_core(pairs):
        return jnp.where(first, pairs[0], pairs[1])

    def near_of(x, layer):
        return move(x, lambda dd, cc, zz: (dd, layer, zz) if cc == zz // 2 and cc != layer else None, "d_near")

    def far_of(x, layer):
        return move(x, lambda dd, cc, zz: (dd, layer, zz ^ 2) if cc != zz // 2 else None, "d_far")

    live = ((t * rows + jnp.arange(rows)) < length).astype(f32)[:, None]
    res = start_chain(flags, inputs, cotangent, mask_pad, label_lanes, table, small_pack, *own, ORDER, scale)
    x0, cot, packs, lse0, o0, n1_0, qkv0 = res[:7]
    walls, got0 = res[7:9], res[9:]
    n1_0 = n1_0.reshape(seq_len, width)

    def whole(w):
        return w.reshape(width, w.shape[-1])

    gains = [packs[l, 0:2] for l in range(2)]
    shifts = [packs[l, 2:4] for l in range(2)]
    ln_mid = jnp.stack([gains[0][1], shifts[0][1], gains[1][0], shifts[1][0]])
    wq0, wp0 = whole(got0[0]), whole(got0[1])
    term1 = lax.dynamic_index_in_dim(packs[1], 4 + pair, 0, keepdims=True)[:, : 3 * local_width]
    hid0, act0, dy1, o1, lse1, n2_0, u0, g0, n1_1, qkv1, dm1, fc_w0, got1 = mid_chain(
        x0, o0, ln_mid, cot, live, term1, mask_pad, wp0, got0[2], got0[3], walls[1], own, ORDER, scale
    )
    w10, w20 = whole(fc_w0[0]), whole(fc_w0[1])
    wq1, wp1 = whole(got1[0]), whole(got1[1])

    fold = ndp == 4
    ln_turn = jnp.stack([gains[1][1], shifts[1][1]])
    dh1, norms1, y1, hid1, do1, da1, fc1_1, fc2_1 = turn_chain(
        ndp, act0, o1, dy1, ln_turn, dm1, wp1, own[2:], got1[2:]
    )
    dqkv1, dwall1, sum_fc1_1, sum_fc2_1, landed, act1 = bwd_chain(
        6, fold, qkv1, do1, o1, lse1, mask_pad, walls[1], fc1_1, fc2_1, [(0, act0)], ORDER, scale, (y1, hid1)
    )
    got_act0, got_fc2_1 = landed[0], landed[-1]
    ln_back = jnp.stack([gains[1][0], gains[0][1]])
    give = [(1, act1)] + ([(1, sum_fc1_1)] if fold else [])
    gin1, dh0, norms10, do0, da0, fc1_0, fc2_0, qp1, rel1, sums1, landed = back_chain(
        ndp, flags, act0, dh1, hid0, ln_back, dqkv1, o1, label_lanes,
        wq1, wp0, w10, w20, u0, g0, n2_0, n1_1, da1, dwall1, give,
    )
    got_act1, got_fc1_1, got_gin1 = landed[0], landed[len(landed) - 2], landed[-1]
    number = 2 * d + pair
    sums_rows = lax.dynamic_update_slice(
        jnp.zeros((2 * ndp, width), f32), sums1, (number, jnp.int32(width - 2 * local_width))
    )
    mine = lax.dynamic_index_in_dim(time_emb, pair, 0, keepdims=True).astype(f32)
    emb_rows = lax.dynamic_update_slice(jnp.zeros((2 * ndp, width), f32), mine, (number, jnp.int32(0)))
    smalls = jnp.concatenate(
        [jnp.zeros((2, width), f32), norms10[2:], norms10[:2], norms1, sums_rows, emb_rows], axis=0
    )
    give = [(1, qp1)] if fold else []
    (gin0, smalls, rel, q0, *more), landed = end_chain(
        ndp, flags, qkv0, do0, o0, lse0, mask_pad, x0, dh0, gains[0][0:1], label_lanes, smalls, rel1,
        walls[0], wq0, n1_0, da0, by_bits(fc1_0), fc2_0, give, ORDER, scale,
    )
    norms, sums_all = smalls[:8], smalls[8:]

    def total(mine, got):
        return jnp.where(home, mine, got[0]).astype(f32) + got[1].astype(f32)

    hidden_units = w_fc1.shape[2]
    wide = 3 * local_width
    if fold:
        got_qp1, got_gin0, got_f0, got_q0, got_fc2_0 = landed
        f0, sum_fc2_0 = more
        f0, qp1 = total(f0, got_f0), total(qp1, got_qp1)
        layer0 = (total(q0, got_q0), f0[:, hidden_units:], f0[:, :hidden_units], total(sum_fc2_0, got_fc2_0))
        layer1 = (qp1[:, :wide], qp1[:, wide:], total(sum_fc1_1, got_fc1_1), total(sum_fc2_1, got_fc2_1))
    else:
        (got_gin0,) = landed

        def summed(x, layer):
            x = reduced(whole(x))
            return total(x, (near_of(x, layer), far_of(x, layer)))

        f0, qp1 = summed(more[0], 0), summed(qp1, 1)
        layer0 = (summed(q0, 0), f0[:, hidden_units:], f0[:, :hidden_units], summed(fc2_0[1], 0))
        layer1 = (qp1[:, :wide], qp1[:, wide:], summed(fc1_1, 1), summed(fc2_1[1], 1))
    grad_q, grad_p, grad_fc1, grad_fc2 = [by_core(pair_of) for pair_of in zip(layer0, layer1)]

    def by_image(same, other):
        return jnp.stack([jnp.where(pair == 0, same, other), jnp.where(pair == 0, other, same)])[None]

    acts = by_image(
        jnp.where(home, by_core((act0, act1)), by_core((got_act0[0], got_act1[0]))), by_core((got_act0[1], got_act1[1]))
    )
    same = jnp.where(home, by_core((gin0, gin1)), by_core((got_gin0[0], got_gin1[0])).astype(f32))
    input_grads = by_image(same, by_core((got_gin0[1], got_gin1[1])).astype(f32))

    rel_grad = rel.reshape(heads, 4096)[:, :buckets]
    norms_mine = jnp.where(first, norms[:4], norms[4:]).reshape(2, 2, width)
    cols = width // (4 * ndp)
    norms_mine = lax.dynamic_slice_in_dim(norms_mine, (d * 4 + z) * cols, cols, 2)
    emb_of = sums_all[2 * ndp :]
    sums_mine = jnp.where(first, sums_all[: 2 * ndp, : 2 * local_width], sums_all[: 2 * ndp, 2 * local_width :])
    emb_mine = lax.dynamic_slice_in_dim(emb_of, d * (width // ndp), width // ndp, 1)
    grad_time = jnp.stack(
        [
            lax.dot_general(
                emb_mine,
                sums_mine[:, j * local_width : (j + 1) * local_width],
                (((0,), (0,)), ((), ())),
                precision=lax.Precision.HIGHEST,
                preferred_element_type=f32,
            )
            for j in range(2)
        ],
        axis=1,
    )
    return (
        acts,
        input_grads,
        jnp.stack([grad_q[:, j * local_width : (j + 1) * local_width] for j in range(3)], axis=1)[None],
        grad_time[None],
        grad_p[None],
        grad_fc1[None],
        grad_fc2[None],
        rel_grad[None],
        norms_mine[:, 0][None],
        norms_mine[:, 1][None],
    )


def solution(mesh):
    return jax.shard_map(
        local,
        mesh=mesh,
        in_specs=(
            P("dp", "tensor", None),
            P("dp", None),
            P("dp"),
            P("dp", None),
            P(),
            P("section", None, None, "tensor"),
            P("section", None, None, "tensor"),
            P("section", None, "tensor"),
            P("section", None, "tensor"),
            P("section", None, "tensor"),
            P("section", "tensor", None),
            P("section", None, None),
            P("section", None, None),
            P("dp", "tensor", None),
        ),
        out_specs=(
            P("section", "dp", "tensor", None),
            P("section", "dp", "tensor", None),
            P("section", "dp", None, "tensor"),
            P("section", "dp", None, "tensor"),
            P("section", "dp", "tensor"),
            P("section", "dp", "tensor"),
            P("section", "dp", "tensor"),
            P("section", "tensor", None),
            P("section", None, ("dp", "tensor")),
            P("section", None, ("dp", "tensor")),
        ),
        check_vma=False,
    )
```
